32 devices in a mesh: parts: 2 (over y), shard: 16 (over z, x, core).
Axes of the slice: x: 2, y: 2, z: 4, core: 2. Of those that a mesh axis runs over, the one named last changes fastest.
Arguments:
- entity_table: bfloat16 [32768, 200], P('shard'), may hold values from -6 to 6
- relation_table: bfloat16 [1387, 200], replicated, may hold values from -6 to 6
- filters: bfloat16 [48, 9, 9], replicated, may hold values from -0.625 to 0.625
- proj_weight: bfloat16 [19200, 200], replicated, may hold values from -0.046875 to 0.046875
- chequer_perm: int32 [400], replicated, may hold values from 0 to 399, each once
- head_owner: int32 [4096, 1], P(('parts', 'shard')), parts along dimension 0, may hold values from 0 to 15; in each aligned block of 128 rows (0 to 127, 128 to 255, ...) at most 16 rows name the same one
- head_row: int32 [4096], P(('parts', 'shard')), parts along dimension 0, may hold values from 0 to 2047
- rel_ids: int32 [4096], P(('parts', 'shard')), parts along dimension 0, may hold values from 0 to 1386
- pos_index: int32 [4096], P(('parts', 'shard')), parts along dimension 0, may hold values from 0 to 4095
- tail_owner: int32 [8192, 1], P('parts'), parts along dimension 0, may hold values from 0 to 15; in each aligned block of 4096 rows (0 to 4095, 4096 to 8191, ...) at most 512 rows name the same one
- tail_row: int32 [8192], P('parts'), parts along dimension 0, may hold values from 0 to 2047
Outputs:
- entity_grad: float32 [65536, 200], P(('parts', 'shard')), parts along dimension 0
- relation_grad: float32 [2774, 200], P('parts'), parts along dimension 0
- filter_grad: float32 [96, 9, 9], P('parts'), parts along dimension 0
- proj_grad: float32 [38400, 200], P(('parts', 'shard')), parts along dimension 0
The draws below stay inside these ranges and needn't reach their ends.
There are 2 independent parts, one for each index of `parts`. The reference program is written for one: setup_inputs(seed, part) draws one part's arguments, and reference() takes and returns one part's arrays. A program takes and returns all parts, laid end to end along the dimension named above; an argument that names none is the same for every part. Nothing has to cross between parts.
Inputs may be any that keep to these rules, and one draw needn't show every extreme that they name: `head_owner`: the queries of one device name one owner at most 16 times; some device names some owner exactly 16 times. `tail_owner`: at most 512 candidates name one owner; some owner is named exactly 512 times. `chequer_perm`: each of 0 to 399 appears once.
All inputs are finite; a program needn't handle non-finite values.
Results may differ from the reference program's by a relative error of at most 0.0014.
Values may be sent and summed in bfloat16 or wider, within the bound.
No kernel may reach another device: no remote copies, remote signals or barrier semaphores. Data moves between devices by JAX's collectives and lax.ppermute only.
A program may use at most 192 MiB of HBM per device.

```python
import math
import jax
import jax.numpy as jnp
import numpy as np
from jax import lax

D = 200
REL = 1387
FILT = 48
KS = 9
IMG_H = 20
CAND = 4096
Q_DEV = 128
ENT_DEV = 2048
OWNERS = 16
IMG_W = 20
FLAT = 19200
QUERIES = 2048
ENTITIES = 32768
HCAP = 16
TCAP = 512


def plant(values, key, least, high):
    spot = [jax.random.randint(jax.random.fold_in(key, axis), (), 0, length) for axis, length in enumerate(values.shape)]
    widest = values.shape.index(max(values.shape))
    next_to = spot[:widest] + [(spot[widest] + 1) % values.shape[widest]] + spot[widest + 1:]
    return values.at[tuple(spot)].set(least).at[tuple(next_to)].set(high)


def levels(rng, shape, pieces, least, top_value):
    factor_of = 1.0
    for position, shards_of in pieces:
        draws = jax.random.uniform(jax.random.fold_in(jax.random.fold_in(rng, 6), position), (shards_of,), jnp.float32, least / len(pieces), top_value / len(pieces))
        factor_of = factor_of * jnp.repeat(jnp.exp(draws), shape[position] // shards_of).reshape((-1,) + (1,) * (len(shape) - 1 - position))
    return factor_of


def rank_bounds(count, skew):
    loads = [(1 << 20) // math.isqrt(grade ** skew) + 1 for grade in range(1, count + 1)]
    width = 1 + sum(loads) // (1 << 30)
    return np.cumsum(np.array([max(1, weight // width) for weight in loads]))


def ranked_ids(rng, dims, number_of, skew):
    grid = rank_bounds(number_of, skew)
    ticket = jax.random.randint(jax.random.fold_in(rng, 1), dims, 0, int(grid[number_of - 1]))
    standing = jnp.searchsorted(jnp.asarray(grid, jnp.int32), ticket, side="right")
    return jax.random.permutation(jax.random.fold_in(rng, 2), number_of)[standing].astype(jnp.int32)


def routed_block(rng, own, number, rows, count, top, bound, lean):
    sequence = jax.random.permutation(rng, count)
    packed, ordinary = shares(count, rows * top, bound, lean, True), shares(count, rows * top, bound, lean, False)
    places = jnp.arange(count)

    def named(sizes, rotation):
        used = int((sizes > 0).sum())
        fixed = max(1, used // 4)
        shifted = fixed + (places - fixed + rotation * (used - fixed)) % max(1, count - fixed)
        return jnp.zeros((count,), jnp.int32).at[sequence[jnp.where(places < fixed, places, shifted)]].set(jnp.asarray(sizes, jnp.int32))

    sizes = jnp.where(number % 4 == 0, named(packed, number // 4), named(ordinary, number - number // 4 - 1))
    mixed = jax.random.permutation(jax.random.fold_in(own, 3), count)
    giver, sink = mixed[0:count // 2 * 2:2], mixed[1:count // 2 * 2:2]
    slack = jnp.minimum(sizes[giver] - 1, bound - sizes[sink]) // 2
    slack = jnp.where((giver == sequence[0]) | (sink == sequence[0]) | (sizes[sink] == 0), 0, jnp.maximum(slack, 0))
    shifted = jax.random.randint(jax.random.fold_in(own, 4), (count // 2,), 0, 1 << 20) % (slack + 1)
    sizes = sizes.at[giver].add(-shifted).at[sink].add(shifted)
    items = jnp.searchsorted(jnp.cumsum(sizes), jnp.arange(rows * top), side="right").astype(jnp.int32)
    grid = items.reshape(top, rows).T
    grid = grid[jax.random.permutation(jax.random.fold_in(own, 1), rows)]
    rotation = jax.random.randint(jax.random.fold_in(own, 2), (rows, 1), 0, top)
    return jnp.take_along_axis(grid, (jnp.arange(top)[None, :] + rotation) % top, axis=1)


def shares(amount, total, reach, lean, full):
    portions = [(1 << 20) // math.isqrt(grade ** lean) + 1 for grade in range(1, amount + 1)]
    largest = reach if full else min(reach, max(-(-total // amount), total * portions[0] // sum(portions)))
    least = 1 if total - largest >= amount - 1 else 0
    counts, surplus = [largest] + [least] * (amount - 1), total - largest - least * (amount - 1)
    while surplus > 0:
        free = [i for i in range(1, amount) if counts[i] < largest] or [i for i in range(1, amount) if counts[i] < reach]
        mass, remaining = sum([portions[i] for i in free]), surplus
        for i in free:
            extra = min(reach - counts[i], max(1, remaining * portions[i] // mass), surplus)
            counts[i] = counts[i] + extra
            surplus = surplus - extra
    return np.array(counts)


def scatter_about(key, extent, scale, bound, shards=(), held_as=jnp.bfloat16):
    array = scale * jax.random.normal(key, extent, jnp.float32)
    if shards:
        array = array * levels(key, extent, shards, -0.22, 0.18)
    return jnp.clip(array, -bound, bound).astype(held_as)


def setup_inputs(seed: int = 0, part: int = 0) -> dict:
    key_of = jax.random.split(jax.random.key(seed), 12)
    own_keys = jax.random.split(jax.random.fold_in(key_of[11], part), 12)
    entity_table = scatter_about(key_of[0], (ENTITIES, D), 1.0, 6.0, ((0, 16),))
    relation_table = scatter_about(key_of[1], (REL, D), 1.0, 6.0)
    filters = scatter_about(key_of[2], (FILT, KS, KS), (KS * KS) ** -0.5, 0.625)
    proj_weight = scatter_about(key_of[3], (FLAT, D), FLAT ** -0.5, 0.046875)
    chequer_perm = jax.random.permutation(key_of[4], 2 * D).astype(jnp.int32)
    head_owner_keys = jax.random.split(jax.random.fold_in(own_keys[5], 1), QUERIES // Q_DEV)
    head_owner_turns = jax.random.permutation(jax.random.fold_in(own_keys[5], 3), QUERIES // Q_DEV)
    head_owner = jax.vmap(lambda own, number: routed_block(jax.random.fold_in(own_keys[5], 2), own, number, Q_DEV, OWNERS, 1, HCAP, 2))(head_owner_keys, head_owner_turns).reshape((QUERIES, 1))
    head_row = plant(jax.random.randint(own_keys[6], (QUERIES,), 0, ENT_DEV), jax.random.fold_in(own_keys[6], 1), 0, ENT_DEV - 1).astype(jnp.int32)
    rel_ids = plant(ranked_ids(own_keys[7], (QUERIES,), REL, 2), jax.random.fold_in(own_keys[7], 3), 0, REL - 1).astype(jnp.int32)
    pos_index = plant(jax.random.randint(own_keys[8], (QUERIES,), 0, CAND), jax.random.fold_in(own_keys[8], 1), 0, CAND - 1).astype(jnp.int32)
    tail_owner_keys = jax.random.split(jax.random.fold_in(own_keys[9], 1), CAND // CAND)
    tail_owner_turns = jax.random.permutation(jax.random.fold_in(own_keys[9], 3), CAND // CAND)
    tail_owner = jax.vmap(lambda own, number: routed_block(jax.random.fold_in(own_keys[9], 2), own, number, CAND, OWNERS, 1, TCAP, 2))(tail_owner_keys, tail_owner_turns).reshape((CAND, 1))
    tail_row = plant(jax.random.randint(own_keys[10], (CAND,), 0, ENT_DEV), jax.random.fold_in(own_keys[10], 1), 0, ENT_DEV - 1).astype(jnp.int32)
    return {"entity_table": entity_table, "relation_table": relation_table, "filters": filters, "proj_weight": proj_weight, "chequer_perm": chequer_perm, "head_owner": head_owner, "head_row": head_row, "rel_ids": rel_ids, "pos_index": pos_index, "tail_owner": tail_owner, "tail_row": tail_row}


loss_weight = 0.015625
smooth = 0.1

def wrap_pad(pair_image, rim_width):
    return jnp.pad(pair_image, ((0, 0), (rim_width, rim_width), (rim_width, rim_width)), mode='wrap')

def conv_forward(pair_image, filters):
    rim_width = filters.shape[-1] // 2
    padded = wrap_pad(pair_image, rim_width)[:, None]
    return lax.conv_general_dilated(padded, filters[:, None], (1, 1), 'VALID', dimension_numbers=('NCHW', 'OIHW', 'NCHW'), preferred_element_type=jnp.float32)

def conv_backward(pair_image, filters, feat_grad):
    kernel_size = filters.shape[-1]
    rim_width = kernel_size // 2
    img_height = pair_image.shape[1]
    img_width = pair_image.shape[2]
    padded = wrap_pad(pair_image, rim_width)
    filter_part = lax.conv_general_dilated(padded[None], feat_grad, (1, 1), 'VALID', dimension_numbers=('NCHW', 'IOHW', 'NCHW'), preferred_element_type=jnp.float32)[0]
    flipped = filters[:, ::-1, ::-1][None]
    spread = lax.conv_general_dilated(feat_grad, flipped, (1, 1), ((kernel_size - 1, kernel_size - 1), (kernel_size - 1, kernel_size - 1)), dimension_numbers=('NCHW', 'OIHW', 'NCHW'), preferred_element_type=jnp.float32)[:, 0]
    row_block = spread[:, rim_width:rim_width + img_height]
    row_block = row_block.at[:, :rim_width].add(spread[:, rim_width + img_height:])
    row_block = row_block.at[:, img_height - rim_width:].add(spread[:, :rim_width])
    col_block = row_block[:, :, rim_width:rim_width + img_width]
    col_block = col_block.at[:, :, :rim_width].add(row_block[:, :, rim_width + img_width:])
    col_block = col_block.at[:, :, img_width - rim_width:].add(row_block[:, :, :rim_width])
    return (filter_part, col_block)

def make_image(head_vec, rel_vec, positions):
    joined = jnp.concatenate([head_vec, rel_vec], axis=1)
    return joined[:, positions].reshape(joined.shape[0], IMG_H, IMG_W)

def front(pair_image, filters, proj_weight):
    conv_pre = conv_forward(pair_image, filters)
    features = jax.nn.silu(conv_pre).astype(jnp.bfloat16).reshape(conv_pre.shape[0], -1)
    query_vec = jnp.dot(features, proj_weight, preferred_element_type=jnp.float32).astype(jnp.bfloat16)
    return (conv_pre, features, query_vec)

def feature_grad(query_grad, proj_weight, conv_pre):
    linear = lax.dot_general(query_grad, proj_weight, (((1,), (1,)), ((), ())), preferred_element_type=jnp.float32)
    gate_sig = jax.nn.sigmoid(conv_pre)
    slope = gate_sig * (1.0 + conv_pre * (1.0 - gate_sig))
    return (linear.reshape(conv_pre.shape) * slope).astype(jnp.bfloat16)

def reference(entity_table, relation_table, filters, proj_weight, chequer_perm, head_owner, head_row, rel_ids, pos_index, tail_owner, tail_row):
    tail_ids = (tail_owner[:, 0] * ENT_DEV + tail_row).astype(jnp.int32)
    tail_vec = entity_table[tail_ids]
    head_ids = (head_owner[:, 0] * ENT_DEV + head_row).astype(jnp.int32)
    inverse = jnp.argsort(chequer_perm)
    blocks = QUERIES // Q_DEV
    cand_index = jnp.arange(CAND, dtype=jnp.int32)

    def block_step(totals, inputs):
        tail_sum, proj_sum, filt_sum, rel_sum = totals
        block_heads, block_rels, block_pos = inputs
        pair_image = make_image(entity_table[block_heads], relation_table[block_rels], chequer_perm)
        conv_pre, features, query_vec = front(pair_image, filters, proj_weight)
        score = lax.dot_general(query_vec, tail_vec, (((1,), (1,)), ((), ())), preferred_element_type=jnp.float32)
        target = smooth / CAND + (1.0 - smooth) * (cand_index[None, :] == block_pos[:, None]).astype(jnp.float32)
        score_grad = ((jax.nn.sigmoid(score) - target) * loss_weight).astype(jnp.bfloat16)
        query_grad = jnp.dot(score_grad, tail_vec, preferred_element_type=jnp.float32).astype(jnp.bfloat16)
        tail_sum = tail_sum + lax.dot_general(score_grad, query_vec, (((0,), (0,)), ((), ())), preferred_element_type=jnp.float32)
        proj_sum = proj_sum + lax.dot_general(features, query_grad, (((0,), (0,)), ((), ())), preferred_element_type=jnp.float32)
        feat_grad = feature_grad(query_grad, proj_weight, conv_pre)
        filter_part, image_grad = conv_backward(pair_image, filters, feat_grad)
        pair_grad = image_grad.reshape(image_grad.shape[0], -1)[:, inverse]
        rel_sum = rel_sum + jax.ops.segment_sum(pair_grad[:, D:], block_rels, num_segments=REL)
        return ((tail_sum, proj_sum, filt_sum + filter_part, rel_sum), pair_grad[:, :D])
    start = (jnp.zeros((CAND, D), jnp.float32), jnp.zeros((FLAT, D), jnp.float32), jnp.zeros((FILT, KS, KS), jnp.float32), jnp.zeros((REL, D), jnp.float32))
    inputs = (head_ids.reshape(blocks, Q_DEV), rel_ids.reshape(blocks, Q_DEV), pos_index.reshape(blocks, Q_DEV))
    totals, head_grads = lax.scan(block_step, start, inputs)
    tail_sum, proj_sum, filt_sum, rel_sum = totals
    entity_grad = jax.ops.segment_sum(head_grads.reshape(QUERIES, D), head_ids, num_segments=ENTITIES)
    entity_grad = entity_grad + jax.ops.segment_sum(tail_sum, tail_ids, num_segments=ENTITIES)
    return (entity_grad, rel_sum, filt_sum, proj_sum)
```

```python
import functools
import math

import jax
import jax.numpy as jnp
import numpy as np
from jax import lax
from jax.experimental import pallas as pl
from jax.experimental.pallas import tpu as pltpu
from jax.sharding import PartitionSpec as P

IMG = 20
BAND = 4
GROUPS = IMG // BAND
BAND_OUT = BAND * IMG
LANES = 256

loss_weight = 0.015625
smooth = 0.1

f32 = jnp.float32
bf16 = jnp.bfloat16
i32 = jnp.int32

NN = (((1,), (0,)), ((), ()))
NT = (((1,), (1,)), ((), ()))
TN = (((0,), (0,)), ((), ()))


def mm(a, b, dims=NN):
    return lax.dot_general(a, b, dims, preferred_element_type=f32)


def iota(shape, axis):
    return lax.broadcasted_iota(i32, shape, axis)


def onehot(mask):
    return jnp.where(mask, 1.0, 0.0).astype(bf16)


def split(value):
    high = value.astype(bf16)
    return high, (value - high.astype(f32)).astype(bf16)


def sigmoid(v):
    return 0.5 * jnp.tanh(0.5 * v) + 0.5


def params(*semantics, mib=40):
    return pltpu.CompilerParams(
        dimension_semantics=semantics or None, vmem_limit_bytes=mib << 20
    )


def cost(flops, nbytes, trans=0):
    return pl.CostEstimate(flops=int(flops), bytes_accessed=int(nbytes), transcendentals=int(trans))


def whole(shape):
    return pl.BlockSpec(shape, lambda *_: (0,) * len(shape))


SMEM = pl.BlockSpec(memory_space=pltpu.SMEM)


def band_codes(ks):
    codes = np.full((IMG, LANES), -1, np.int32)
    for j in range(IMG):
        for r in range(ks):
            for x in range(IMG):
                b = (x - j + ks // 2) % IMG
                if b < ks:
                    codes[j, r * IMG + x] = r * ks + b
    return codes


def band_kernel(codes_ref, filt_ref, out_ref, scr):
    count, taps = filt_ref.shape
    filt = filt_ref[...]
    for j in range(IMG):
        pick = onehot(iota((taps, LANES), 0) == codes_ref[j : j + 1, :])
        row = mm(filt, pick)
        for di in range(BAND):
            scr[:, di * IMG + j, :] = row if di == 0 else pltpu.roll(row, di * IMG, 1)
    out_ref[...] = scr[...].reshape(count * BAND_OUT, LANES).astype(bf16)


def build_band(filters):
    count, ks, _ = filters.shape
    codes = jnp.asarray(band_codes(ks))
    return pl.pallas_call(
        band_kernel,
        out_shape=jax.ShapeDtypeStruct((count * BAND_OUT, LANES), bf16),
        scratch_shapes=[pltpu.VMEM((count, BAND_OUT, LANES), f32)],
        compiler_params=params(),
        cost_estimate=cost(4e7, 4e6),
        name="band",
    )(codes, filters.reshape(count, ks * ks))


def pack_kernel(shift, me_ref, owner_ref, row_ref, table_ref, tails_ref, tails_t_ref, cand_ref, srow_ref):
    cap = tails_ref.shape[0]
    lines = owner_ref.shape[0]
    mine = owner_ref[...] == me_ref[0]
    mine_b = onehot(mine)
    before = onehot(iota((128, 128), 0) < iota((128, 128), 1))
    rank = mm(mine_b, before)
    totals = mm(mine_b, jnp.ones((128, 128), bf16))
    upper = jnp.where(iota((lines, lines), 1) < iota((lines, lines), 0), 1.0, 0.0).astype(bf16)
    offset = mm(upper, totals.astype(bf16))
    key = jnp.where(mine, (rank + offset).astype(i32), -1)
    code = row_ref[...] * (1 << shift) + iota((lines, 128), 0) * 128 + iota((lines, 128), 1) + 1
    code = code.astype(f32)
    slots = iota((cap, 128), 0)
    total = jnp.zeros((cap, 128), f32)
    for r in range(lines):
        total = total + jnp.where(slots == key[r : r + 1, :], code[r : r + 1, :], 0.0)
    found = jnp.sum(total, axis=1, keepdims=True).astype(i32) - 1
    live = found >= 0
    srow = jnp.where(live, lax.shift_right_arithmetic(found, shift), -1)
    cand_ref[...] = jnp.where(live, found & ((1 << shift) - 1), -1)
    srow_ref[...] = srow
    pick = onehot(iota((cap, table_ref.shape[0]), 1) == srow)
    tails = mm(pick, table_ref[...])
    tails_ref[...] = tails.astype(bf16)
    tails_t_ref[...] = tails.T.astype(bf16)


def pack_tails(me, tail_owners, tail_row, table, cap):
    cand = tail_row.shape[0]
    shift = int(math.log2(cand))
    assert 1 << shift == cand and cand * table.shape[0] < 1 << 24 and cand % 128 == 0
    width = table.shape[1]
    return pl.pallas_call(
        functools.partial(pack_kernel, shift),
        in_specs=[SMEM] + [pl.BlockSpec(memory_space=pltpu.VMEM)] * 3,
        out_shape=[
            jax.ShapeDtypeStruct((cap, width), bf16),
            jax.ShapeDtypeStruct((width, cap), bf16),
            jax.ShapeDtypeStruct((cap, 1), i32),
            jax.ShapeDtypeStruct((cap, 1), i32),
        ],
        compiler_params=params(),
        cost_estimate=cost(1e9, 2e6),
        name="pack_tails",
    )(me, tail_owners.reshape(-1, 128), tail_row.reshape(-1, 128), table)


def found_kernel(cap, me_ref, owner_ref, row_ref, table_ref, found_ref, want_ref, scr):
    count, queries = owner_ref.shape
    mine = owner_ref[...] == me_ref[0]
    before = onehot(iota((queries, queries), 0) < iota((queries, queries), 1))
    rank = mm(onehot(mine), before)
    key = jnp.where(mine, rank.astype(i32), -1)
    code = (row_ref[...] + 1).astype(f32)
    slots = iota((cap, queries), 0)
    for d in range(count):
        picked = jnp.where(slots == key[d : d + 1, :], code[d : d + 1, :], 0.0)
        scr[d * cap : (d + 1) * cap, :] = jnp.sum(picked, axis=1, keepdims=True)
    want = scr[...].astype(i32) - 1
    want_ref[...] = want
    pick = onehot(iota((count * cap, table_ref.shape[0]), 1) == want)
    found_ref[...] = mm(pick, table_ref[...]).astype(bf16)


def find_heads(me, owners, rows, table, cap):
    count = owners.shape[0]
    width = table.shape[1]
    return pl.pallas_call(
        functools.partial(found_kernel, cap),
        in_specs=[SMEM] + [pl.BlockSpec(memory_space=pltpu.VMEM)] * 3,
        out_shape=[
            jax.ShapeDtypeStruct((count * cap, width), bf16),
            jax.ShapeDtypeStruct((count * cap, 1), i32),
        ],
        scratch_shapes=[pltpu.VMEM((count * cap, 1), f32)],
        compiler_params=params(),
        cost_estimate=cost(3e8, 2e6),
        name="find_heads",
    )(me, owners, rows, table)


def pos_kernel(cap, core_ref, owner_ref, pos_ref, out_ref):
    cand = owner_ref.shape[1]
    pos = pos_ref[...]
    queries = pos.shape[0]
    step = min(512, cand)
    owner = jnp.zeros((queries, 1), f32)
    for c in range(0, cand, step):
        here = iota((queries, step), 1) + c
        value = owner_ref[:, c : c + step].astype(f32)
        owner = owner + jnp.sum(jnp.where(here == pos, value, 0.0), axis=1, keepdims=True)
    owner = owner.astype(i32)
    ahead = jnp.zeros((queries, 1), f32)
    for c in range(0, cand, step):
        here = iota((queries, step), 1) + c
        same = (owner_ref[:, c : c + step] == owner) & (here < pos)
        ahead = ahead + jnp.sum(jnp.where(same, 1.0, 0.0), axis=1, keepdims=True)
    slot = lax.shift_right_arithmetic(owner, 1) * cap + ahead.astype(i32)
    out_ref[...] = jnp.where((owner & 1) == core_ref[0], slot, -1)


def pos_slots(core, tail_owners, pos_col, cap):
    return pl.pallas_call(
        functools.partial(pos_kernel, cap),
        in_specs=[SMEM] + [pl.BlockSpec(memory_space=pltpu.VMEM)] * 2,
        out_shape=jax.ShapeDtypeStruct(pos_col.shape, i32),
        compiler_params=params(),
        cost_estimate=cost(1e7, 1e5),
        name="pos_slots",
    )(core, tail_owners.reshape(1, -1), pos_col)


def front_kernel(
    cap, fetched_ref, ocol_ref, orow_ref, rel_ref, rtab_ref, win_ref, band_ref, w_ref,
    pre_ref, pwin_ref, qv_ref, hvt_ref, qvt_ref, hv, rv, acc,
):
    g = pl.program_id(0)
    queries, width = hv.shape

    @pl.when(g == 0)
    def _():
        ocol = ocol_ref[...]
        same = (ocol == orow_ref[...]) & (iota((queries, queries), 1) < iota((queries, queries), 0))
        rank = jnp.sum(jnp.where(same, 1.0, 0.0), axis=1, keepdims=True)
        slot = ocol * cap + rank.astype(i32)
        pick = onehot(iota((queries, fetched_ref.shape[0]), 1) == slot)
        head = mm(pick, fetched_ref[...])
        hv[...] = head.astype(bf16)
        hvt_ref[...] = head.T.astype(bf16)
        rpick = onehot(iota((queries, rtab_ref.shape[0]), 1) == rel_ref[...])
        rv[...] = mm(rpick, rtab_ref[...]).astype(bf16)
        acc[...] = jnp.zeros_like(acc)

    win = win_ref[0]
    entry = iota((width, LANES), 0)
    image = mm(hv[...], onehot(entry == win)) + mm(rv[...], onehot(entry + width == win))
    image = image.astype(bf16)
    pwin_ref[0] = image
    count = w_ref.shape[0]
    chunk = math.gcd(count, 16)
    total = acc[...]
    for c in range(0, count, chunk):
        rows = pl.ds(c * BAND_OUT, chunk * BAND_OUT)
        pre = mm(image, band_ref[rows, :], NT)
        pre_ref[0, :, rows] = pre
        feats = (pre * sigmoid(pre)).astype(bf16)
        weight = w_ref[c : c + chunk, 0].reshape(chunk * BAND_OUT, width)
        total = total + mm(feats, weight)
    acc[...] = total

    @pl.when(g == GROUPS - 1)
    def _():
        query = acc[...]
        qv_ref[...] = query.astype(bf16)
        qvt_ref[...] = query.T.astype(bf16)


def front(fetched, ocol, orow, rel_col, relation_table, windows, band, weight, cap):
    queries = ocol.shape[0]
    width = weight.shape[-1]
    count = weight.shape[0]
    lanes = count * BAND_OUT
    return pl.pallas_call(
        functools.partial(front_kernel, cap),
        grid=(GROUPS,),
        in_specs=[
            whole(fetched.shape),
            whole(ocol.shape),
            whole(orow.shape),
            whole(rel_col.shape),
            whole(relation_table.shape),
            pl.BlockSpec((1, 1, LANES), lambda g: (g, 0, 0)),
            whole(band.shape),
            pl.BlockSpec((count, 1, BAND_OUT, width), lambda g: (0, g, 0, 0)),
        ],
        out_specs=[
            pl.BlockSpec((1, queries, lanes), lambda g: (g, 0, 0)),
            pl.BlockSpec((1, queries, LANES), lambda g: (g, 0, 0)),
            whole((queries, width)),
            whole((width, queries)),
            whole((width, queries)),
        ],
        out_shape=[
            jax.ShapeDtypeStruct((GROUPS, queries, lanes), f32),
            jax.ShapeDtypeStruct((GROUPS, queries, LANES), bf16),
            jax.ShapeDtypeStruct((queries, width), bf16),
            jax.ShapeDtypeStruct((width, queries), bf16),
            jax.ShapeDtypeStruct((width, queries), bf16),
        ],
        scratch_shapes=[
            pltpu.VMEM((queries, width), bf16),
            pltpu.VMEM((queries, width), bf16),
            pltpu.VMEM((queries, width), f32),
        ],
        compiler_params=params("arbitrary"),
        cost_estimate=cost(4e9, 2.4e7, 2.5e6),
        name="front",
    )(fetched, ocol, orow, rel_col, relation_table, windows, band, weight)


def score_kernel(cand, qv_ref, pos_ref, tails_ref, own_ref, other_ref, acc):
    step = pl.program_id(0)

    @pl.when(step == 0)
    def _():
        acc[...] = jnp.zeros_like(acc)

    blocks, _, cap = tails_ref.shape
    qv = qv_ref[...]
    queries = qv.shape[0]
    total = acc[...]
    for b in range(blocks):
        tails = tails_ref[b]
        score = mm(qv, tails)
        here = iota((queries, cap), 1) + (step * blocks + b) * cap
        target = jnp.where(here == pos_ref[...], 1.0 - smooth + smooth / cand, smooth / cand)
        grad = ((sigmoid(score) - target) * loss_weight).astype(bf16)
        total = total + mm(grad, tails, NT)
    acc[...] = total

    @pl.when(step == pl.num_programs(0) - 1)
    def _():
        own_ref[...] = acc[: queries // 2, :]
        other_ref[...] = acc[queries // 2 :, :]


def score_part(qv2, pos2, tails, cand):
    owners, width, cap = tails.shape
    queries = qv2.shape[0]
    blocks = math.gcd(owners, max(1, 2048 // cap))
    half = jax.ShapeDtypeStruct((queries // 2, width), f32)
    return pl.pallas_call(
        functools.partial(score_kernel, cand),
        grid=(owners // blocks,),
        in_specs=[
            whole(qv2.shape),
            whole(pos2.shape),
            pl.BlockSpec((blocks, width, cap), lambda s: (s, 0, 0)),
        ],
        out_specs=[whole(half.shape), whole(half.shape)],
        out_shape=[half, half],
        scratch_shapes=[pltpu.VMEM((queries, width), f32)],
        compiler_params=params("arbitrary"),
        cost_estimate=cost(1e9, 2e6, 1e6),
        name="score",
    )(qv2, pos2, tails)


def back_kernel(
    cap, qg_ref, ocol_ref, orow_ref, win_ref, band_ref, w_ref, pre_ref, pwin_ref,
    relt_ref, out_ref, corr_ref, hacc, racc,
):
    g = pl.program_id(0)
    queries, width = hacc.shape

    @pl.when(g == 0)
    def _():
        hacc[...] = jnp.zeros_like(hacc)
        racc[...] = jnp.zeros_like(racc)
        corr_ref[...] = jnp.zeros_like(corr_ref)

    qg = qg_ref[...]
    image = pwin_ref[0]
    count = w_ref.shape[0]
    chunk = math.gcd(count, 16)
    spread = jnp.zeros((queries, LANES), f32)
    for c in range(0, count, chunk):
        rows = pl.ds(c * BAND_OUT, chunk * BAND_OUT)
        weight = w_ref[c : c + chunk, 0].reshape(chunk * BAND_OUT, width)
        linear = mm(qg, weight, NT)
        v = pre_ref[0, :, rows]
        s = sigmoid(v)
        grad = (linear * (s * (1.0 + v * (1.0 - s)))).astype(bf16)
        spread = spread + mm(grad, band_ref[rows, :])
        corr_ref[:, rows] += mm(image, grad, TN)
    win = win_ref[0]
    entry = iota((width, LANES), 0)
    hpick = onehot(entry == win)
    rpick = onehot(entry + width == win)
    high, low = split(spread)
    hacc[...] += mm(high, hpick, NT) + mm(low, hpick, NT)
    racc[...] += mm(rpick, high, NT) + mm(rpick, low, NT)

    @pl.when(g == GROUPS - 1)
    def _():
        relt_ref[...] = racc[...]
        orow = orow_ref[...]
        same = (ocol_ref[...] == orow) & (iota((queries, queries), 0) < iota((queries, queries), 1))
        rank = jnp.sum(jnp.where(same, 1.0, 0.0), axis=0, keepdims=True)
        slot = orow * cap + rank.astype(i32)
        pick = onehot(iota((out_ref.shape[0], queries), 0) == slot)
        out_ref[...] = mm(pick, hacc[...].astype(bf16)).astype(bf16)


def back(qg, ocol, orow, windows, band, weight, pre, pwin, slots, cap):
    queries, width = qg.shape
    count = weight.shape[0]
    lanes = count * BAND_OUT
    return pl.pallas_call(
        functools.partial(back_kernel, cap),
        grid=(GROUPS,),
        in_specs=[
            whole(qg.shape),
            whole(ocol.shape),
            whole(orow.shape),
            pl.BlockSpec((1, 1, LANES), lambda g: (g, 0, 0)),
            whole(band.shape),
            pl.BlockSpec((count, 1, BAND_OUT, width), lambda g: (0, g, 0, 0)),
            pl.BlockSpec((1, queries, lanes), lambda g: (g, 0, 0)),
            pl.BlockSpec((1, queries, LANES), lambda g: (g, 0, 0)),
        ],
        out_specs=[
            whole((width, queries)),
            whole((slots, width)),
            whole((LANES, lanes)),
        ],
        out_shape=[
            jax.ShapeDtypeStruct((width, queries), f32),
            jax.ShapeDtypeStruct((slots, width), bf16),
            jax.ShapeDtypeStruct((LANES, lanes), f32),
        ],
        scratch_shapes=[pltpu.VMEM((queries, width), f32), pltpu.VMEM((width, queries), f32)],
        compiler_params=params("arbitrary", mib=48),
        cost_estimate=cost(6e9, 2.8e7, 2.5e6),
        name="back",
    )(qg, ocol, orow, windows, band, weight, pre, pwin)


def diag_kernel(ks, corr_ref, out_ref, scr):
    lanes = corr_ref.shape[1]
    count = out_ref.shape[1]
    lane = iota((1, lanes), 1)
    unit = lane - (lane // BAND_OUT) * BAND_OUT
    di = unit // IMG
    j = unit - di * IMG
    xs = iota((IMG, lanes), 0)
    near = [((j + (b - ks // 2) + IMG) % IMG) == xs for b in range(ks)]
    for a in range(ks):
        rows = jnp.zeros((IMG, lanes), f32)
        for d in range(BAND):
            first = (d + a) * IMG
            rows = jnp.where(di == d, corr_ref[first : first + IMG, :], rows)
        for b in range(ks):
            scr[a * ks + b : a * ks + b + 1, :] = jnp.sum(
                jnp.where(near[b], rows, 0.0), axis=0, keepdims=True
            )
    member = onehot(iota((lanes, count), 0) // BAND_OUT == iota((lanes, count), 1))
    high, low = split(scr[...])
    out_ref[...] = mm(high, member) + mm(low, member)


def filter_sums(corr, count, ks):
    lanes = corr.shape[1]
    return pl.pallas_call(
        functools.partial(diag_kernel, ks),
        out_shape=jax.ShapeDtypeStruct((ks * ks, count), f32),
        scratch_shapes=[pltpu.VMEM((ks * ks, lanes), f32)],
        compiler_params=params(mib=48),
        cost_estimate=cost(3e7, 4e6),
        name="filter_sums",
    )(corr)


def tail_kernel(cand, tails_ref, scand_ref, qvt_ref, pos_ref, own_ref, other_ref, acc):
    step = pl.program_id(0)

    @pl.when(step == 0)
    def _():
        acc[...] = jnp.zeros_like(acc)

    blocks = qvt_ref.shape[0]
    qvt = jnp.concatenate([qvt_ref[b, 0] for b in range(blocks)], axis=1)
    pos = jnp.concatenate([pos_ref[b] for b in range(blocks)], axis=1)
    score = mm(tails_ref[...], qvt)
    target = jnp.where(scand_ref[...] == pos, 1.0 - smooth + smooth / cand, smooth / cand)
    grad = ((sigmoid(score) - target) * loss_weight).astype(bf16)
    acc[...] += mm(grad, qvt, NT)

    @pl.when(step == pl.num_programs(0) - 1)
    def _():
        cap = own_ref.shape[0]
        own_ref[...] = acc[:cap, :]
        other_ref[...] = acc[cap:, :]


def tail_part(tails2, scand2, gathered, which, pos, cand):
    owners, _, width, queries = gathered.shape
    cap = tails2.shape[0] // 2
    blocks = 2 if owners % 2 == 0 else 1
    half = jax.ShapeDtypeStruct((cap, width), f32)
    return pl.pallas_call(
        functools.partial(tail_kernel, cand),
        grid=(owners // blocks,),
        in_specs=[
            whole(tails2.shape),
            whole(scand2.shape),
            pl.BlockSpec((blocks, 1, width, queries), lambda s: (s, which, 0, 0)),
            pl.BlockSpec((blocks, 1, queries), lambda s: (s, 0, 0)),
        ],
        out_specs=[whole(half.shape), whole(half.shape)],
        out_shape=[half, half],
        scratch_shapes=[pltpu.VMEM((2 * cap, width), f32)],
        compiler_params=params("arbitrary"),
        cost_estimate=cost(2e9, 3e6, 1e6),
        name="tail_grad",
    )(tails2, scand2, gathered, pos)


def proj_kernel(
    rtab_ref, win_ref, band_ref, hvt_ref, qgt_ref, rel_ref, own_ref, other_ref, hmat, rmat, acc
):
    step = pl.program_id(0)
    width = rtab_ref.shape[0]
    rels = rtab_ref.shape[1]

    @pl.when(step == 0)
    def _():
        acc[...] = jnp.zeros_like(acc)
        entry = iota((width, LANES), 0)
        for g in range(GROUPS):
            hmat[g] = mm(band_ref[...], onehot(entry == win_ref[g]), NT).astype(bf16)
            rmat[g] = mm(band_ref[...], onehot(entry + width == win_ref[g]), NT).astype(bf16)

    blocks = hvt_ref.shape[0]
    hvt = jnp.concatenate([hvt_ref[b, 0] for b in range(blocks)], axis=1)
    qgt = jnp.concatenate([qgt_ref[b, 0] for b in range(blocks)], axis=1)
    rel = jnp.concatenate([rel_ref[b] for b in range(blocks)], axis=1)
    rvt = mm(rtab_ref[...], onehot(iota((rels, rel.shape[1]), 0) == rel)).astype(bf16)
    for g in range(GROUPS):
        pre = mm(hmat[g], hvt) + mm(rmat[g], rvt)
        feats = (pre * sigmoid(pre)).astype(bf16)
        acc[g] += mm(feats, qgt, NT)

    @pl.when(step == pl.num_programs(0) - 1)
    def _():
        half = own_ref.shape[0]
        for f in range(half):
            for g in range(GROUPS):
                own_ref[f, g] = acc[g, f * BAND_OUT : (f + 1) * BAND_OUT, :]
                other_ref[f, g] = acc[g, (half + f) * BAND_OUT : (half + f + 1) * BAND_OUT, :]


def proj_part(rtab_t, windows, band2, gathered, rel_rows):
    owners, _, width, queries = gathered.shape
    rows = band2.shape[0]
    blocks = 2 if owners % 2 == 0 else 1
    half = jax.ShapeDtypeStruct((rows // BAND_OUT // 2, GROUPS, BAND_OUT, width), f32)
    return pl.pallas_call(
        proj_kernel,
        grid=(owners // blocks,),
        in_specs=[
            whole(rtab_t.shape),
            whole(windows.shape),
            whole(band2.shape),
            pl.BlockSpec((blocks, 1, width, queries), lambda s: (s, 0, 0, 0)),
            pl.BlockSpec((blocks, 1, width, queries), lambda s: (s, 2, 0, 0)),
            pl.BlockSpec((blocks, 1, queries), lambda s: (s, 0, 0)),
        ],
        out_specs=[whole(half.shape), whole(half.shape)],
        out_shape=[half, half],
        scratch_shapes=[
            pltpu.VMEM((GROUPS, rows, width), bf16),
            pltpu.VMEM((GROUPS, rows, width), bf16),
            pltpu.VMEM((GROUPS, rows, width), f32),
        ],
        compiler_params=params("arbitrary"),
        cost_estimate=cost(6e9, 6e6, 2.5e6),
        name="proj_grad",
    )(rtab_t, windows, band2, gathered, gathered, rel_rows)


def proj_columns(first, cols, filters, chequer_perm, relation_table, gathered, rel_rows):
    ks = filters.shape[-1]
    rim = ks // 2
    flat = IMG * IMG
    column = first + jnp.arange(cols, dtype=i32)
    f = column // flat
    i = (column % flat) // IMG
    j = column % IMG
    spot = jnp.arange(flat, dtype=i32)
    a = (spot[:, None] // IMG - i[None, :] + rim) % IMG
    b = (spot[:, None] % IMG - j[None, :] + rim) % IMG
    tap = filters[f[None, :], jnp.minimum(a, ks - 1), jnp.minimum(b, ks - 1)]
    matrix = jnp.where((a < ks) & (b < ks), tap, jnp.zeros((), bf16))
    owners, _, width, queries = gathered.shape
    head = gathered[:, 0].transpose(0, 2, 1).reshape(owners * queries, width)
    qg = gathered[:, 2].transpose(0, 2, 1).reshape(owners * queries, width)
    joined = jnp.concatenate([head, relation_table[rel_rows.reshape(-1)]], axis=1)
    pre = mm(joined[:, chequer_perm], matrix)
    return mm((pre * sigmoid(pre)).astype(bf16), qg, TN)


def rel_kernel(relt_ref, rel_ref, out_ref):
    step = pl.program_id(0)

    @pl.when(step == 0)
    def _():
        out_ref[...] = jnp.zeros_like(out_ref)

    blocks = relt_ref.shape[0]
    grads = jnp.concatenate([relt_ref[b] for b in range(blocks)], axis=1)
    rel = jnp.concatenate([rel_ref[b] for b in range(blocks)], axis=1)
    pick = onehot(iota((out_ref.shape[0], rel.shape[1]), 0) == rel)
    high, low = split(grads)
    out_ref[...] += mm(pick, high, NT) + mm(pick, low, NT)


def rel_part(relt, rel_rows, rels):
    owners, width, queries = relt.shape
    blocks = 2 if owners % 2 == 0 else 1
    return pl.pallas_call(
        rel_kernel,
        grid=(owners // blocks,),
        in_specs=[
            pl.BlockSpec((blocks, width, queries), lambda s: (s, 0, 0)),
            pl.BlockSpec((blocks, 1, queries), lambda s: (s, 0, 0)),
        ],
        out_specs=whole((rels, width)),
        out_shape=jax.ShapeDtypeStruct((rels, width), f32),
        compiler_params=params("arbitrary"),
        cost_estimate=cost(2e9, 3e6),
        name="rel_grad",
    )(relt, rel_rows)


def entity_kernel(want_ref, incoming_ref, srow_ref, own_ref, recv_ref, out_ref):
    rows = out_ref.shape[0]
    first = pl.program_id(0) * rows
    here = iota((rows, want_ref.shape[1]), 0) + first
    total = mm(onehot(here == want_ref[...]), incoming_ref[...])
    here = iota((rows, srow_ref.shape[1]), 0) + first
    pick = onehot(here == srow_ref[...])
    high, low = split(own_ref[...] + recv_ref[...])
    out_ref[...] = total + mm(pick, high) + mm(pick, low)


def entity_sum(want, incoming, srow, own, recv, rows):
    width = own.shape[1]
    block = math.gcd(rows, 512)
    return pl.pallas_call(
        entity_kernel,
        grid=(rows // block,),
        in_specs=[whole(want.shape), whole(incoming.shape), whole(srow.shape), whole(own.shape), whole(recv.shape)],
        out_specs=pl.BlockSpec((block, width), lambda s: (s, 0)),
        out_shape=jax.ShapeDtypeStruct((rows, width), f32),
        compiler_params=params("arbitrary"),
        cost_estimate=cost(1.5e9, 4e6),
        name="entity_grad",
    )(want, incoming, srow, own, recv)


def shards(
    entity_table,
    relation_table,
    filters,
    proj_weight,
    chequer_perm,
    head_owner,
    head_row,
    rel_ids,
    pos_index,
    tail_owner,
    tail_row,
):
    count = lax.axis_size("shard")
    me = lax.axis_index("shard")
    core = me & 1
    partner = me ^ 1
    queries = head_row.shape[0]
    cand = tail_row.shape[0]
    rows, width = entity_table.shape
    rels = relation_table.shape[0]
    filts, ks, _ = filters.shape
    head_cap = 2 * queries // count
    tail_cap = 2 * cand // count
    same_core = [list(range(c, count, 2)) for c in range(2)]
    swap = [(d, d ^ 1) for d in range(count)]

    def gather_core(x):
        return lax.all_gather(x, "shard", axis=0, axis_index_groups=same_core)

    def to_partner(x):
        return lax.ppermute(x, "shard", swap)

    me1 = me.reshape(1)
    heads = head_owner[:, 0]
    numbers = lax.all_gather(jnp.stack([heads, head_row, rel_ids, pos_index]), "shard", axis=0)
    tail_owners = tail_owner[:, 0]
    tails, tails_t, slot_cand, slot_row = pack_tails(me1, tail_owners, tail_row, entity_table, tail_cap)
    core_tails = gather_core(tails_t)
    tails2 = jnp.concatenate([tails, to_partner(tails)], axis=0)
    scand2 = jnp.concatenate([slot_cand, to_partner(slot_cand)], axis=0)

    found, want = find_heads(me1, numbers[:, 0], numbers[:, 1], entity_table, head_cap)
    fetched = lax.all_to_all(
        found.reshape(count, head_cap, width), "shard", split_axis=0, concat_axis=0, tiled=True
    ).reshape(count * head_cap, width)
    band = build_band(filters)
    extended = jnp.concatenate([chequer_perm[-BAND_OUT:], chequer_perm, chequer_perm[:BAND_OUT]])
    reach = BAND + ks - 1
    windows = jnp.stack([extended[g * BAND_OUT : g * BAND_OUT + reach * IMG] for g in range(GROUPS)])
    windows = jnp.pad(windows, ((0, 0), (0, LANES - reach * IMG)), constant_values=-1)[:, None]
    weight = proj_weight.reshape(filts, GROUPS, BAND_OUT, width)
    mates = numbers.reshape(count // 2, 2, 4, queries)
    core_numbers = lax.dynamic_index_in_dim(mates, core, 1, keepdims=False)
    rel_rows = core_numbers[:, 2:3]
    pos_rows = core_numbers[:, 3:4]
    pos2 = jnp.concatenate([pos_index, lax.dynamic_index_in_dim(numbers, partner, 0, keepdims=False)[3]])
    pos2 = pos_slots(core.reshape(1), tail_owners, pos2[:, None], tail_cap)
    ocol = heads[:, None]
    orow = heads[None, :]
    pre, pwin, qv, hvt, qvt = front(
        fetched, ocol, orow, rel_ids[:, None], relation_table, windows, band, weight, head_cap
    )

    qv2 = jnp.concatenate([qv, to_partner(qv)], axis=0)
    own, other = score_part(qv2, pos2, core_tails, cand)
    qg = (own + to_partner(other)).astype(bf16)
    gathered = gather_core(jnp.stack([hvt, qvt, qg.T]))

    relt, outgoing, corr = back(
        qg, ocol, orow, windows, band, weight, pre, pwin, count * head_cap, head_cap
    )
    incoming = lax.all_to_all(
        outgoing.reshape(count, head_cap, width), "shard", split_axis=0, concat_axis=0, tiled=True
    ).reshape(count * head_cap, width)
    relt_all = gather_core(relt)
    filter_grad = lax.psum(filter_sums(corr, filts, ks), "shard").T.reshape(filts, ks, ks)

    own, other = tail_part(tails2, scand2, gathered, 1, pos_rows, cand)
    entity_grad = entity_sum(
        want.reshape(1, -1), incoming, slot_row.reshape(1, -1), own, to_partner(other), rows
    )

    cols = filts * IMG * IMG // count
    if cols % (IMG * IMG) == 0:
        unit = cols // (IMG * IMG) * BAND_OUT
        band2 = jnp.concatenate(
            [lax.dynamic_slice_in_dim(band, d * unit, unit, axis=0) for d in (me, partner)]
        )
        own, other = proj_part(relation_table.T, windows, band2, gathered, rel_rows)
        own, other = own.reshape(cols, width), other.reshape(cols, width)
    else:
        own, other = (
            proj_columns(d * cols, cols, filters, chequer_perm, relation_table, gathered, rel_rows)
            for d in (me, partner)
        )
    proj_grad = own + to_partner(other)

    part = rel_part(relt_all, rel_rows, rels)
    relation_grad = part + to_partner(part)
    return (entity_grad, relation_grad, filter_grad, proj_grad)


def solution(mesh):
    placed = (
        P("shard", None),
        P(),
        P(),
        P(),
        P(),
        P(("parts", "shard"), None),
        P(("parts", "shard")),
        P(("parts", "shard")),
        P(("parts", "shard")),
        P("parts", None),
        P("parts"),
    )
    return jax.shard_map(
        shards,
        mesh=mesh,
        in_specs=placed,
        out_specs=(
            P(("parts", "shard"), None),
            P("parts", None),
            P("parts", None, None),
            P(("parts", "shard"), None),
        ),
        check_vma=False,
    )
```

```python
import functools
import math

import jax
import jax.numpy as jnp
import numpy as np
from jax import lax
from jax.experimental import pallas as pl
from jax.experimental.pallas import tpu as pltpu
from jax.sharding import PartitionSpec as P

IMG = 20
BAND = 4
GROUPS = IMG // BAND
BAND_OUT = BAND * IMG
LANES = 256

loss_weight = 0.015625
smooth = 0.1

f32 = jnp.float32
bf16 = jnp.bfloat16
i32 = jnp.int32

NN = (((1,), (0,)), ((), ()))
NT = (((1,), (1,)), ((), ()))
TN = (((0,), (0,)), ((), ()))


def mm(a, b, dims=NN):
    return lax.dot_general(a, b, dims, preferred_element_type=f32)


def iota(shape, axis):
    return lax.broadcasted_iota(i32, shape, axis)


def onehot(mask):
    return jnp.where(mask, 1.0, 0.0).astype(bf16)


def split(value):
    high = value.astype(bf16)
    return high, (value - high.astype(f32)).astype(bf16)


def sigmoid(v):
    return 0.5 * jnp.tanh(0.5 * v) + 0.5


def params(*semantics, mib=40):
    return pltpu.CompilerParams(
        dimension_semantics=semantics or None, vmem_limit_bytes=mib << 20
    )


def cost(flops, nbytes, trans=0):
    return pl.CostEstimate(flops=int(flops), bytes_accessed=int(nbytes), transcendentals=int(trans))


def whole(shape):
    return pl.BlockSpec(shape, lambda *_: (0,) * len(shape))


SMEM = pl.BlockSpec(memory_space=pltpu.SMEM)


def band_codes(ks):
    codes = np.full((IMG, LANES), -1, np.int32)
    for j in range(IMG):
        for r in range(ks):
            for x in range(IMG):
                b = (x - j + ks // 2) % IMG
                if b < ks:
                    codes[j, r * IMG + x] = r * ks + b
    return codes


def band_kernel(codes_ref, filt_ref, out_ref, out_t_ref, scr):
    count, taps = filt_ref.shape
    filt = filt_ref[...]
    for j in range(IMG):
        pick = onehot(iota((taps, LANES), 0) == codes_ref[j : j + 1, :])
        row = mm(filt, pick)
        for di in range(BAND):
            scr[:, di * IMG + j, :] = row if di == 0 else pltpu.roll(row, di * IMG, 1)
    full = scr[...].reshape(count * BAND_OUT, LANES)
    out_ref[...] = full.astype(bf16)
    out_t_ref[...] = full.T.astype(bf16)


def build_band(filters, codes):
    count, ks, _ = filters.shape
    return pl.pallas_call(
        band_kernel,
        out_shape=[
            jax.ShapeDtypeStruct((count * BAND_OUT, LANES), bf16),
            jax.ShapeDtypeStruct((LANES, count * BAND_OUT), bf16),
        ],
        scratch_shapes=[pltpu.VMEM((count, BAND_OUT, LANES), f32)],
        compiler_params=params(mib=24),
        cost_estimate=cost(4e7, 4e6),
        name="band",
    )(codes, filters.reshape(count, ks * ks))


VMEM = pl.BlockSpec(memory_space=pltpu.VMEM)


def pieces(refs):
    return [ref.at[i] for ref in refs for i in range(ref.shape[0])]


def pairs(blocks):
    step = 2 if len(blocks) % 2 == 0 else 1
    return [blocks[i : i + step] for i in range(0, len(blocks), step)]


def lanes_of(blocks, rows=slice(None)):
    return jnp.concatenate([b[rows, :] for b in blocks], axis=1)


def pack_kernel(shift, me_ref, owner_ref, row_ref, table_ref, tails_ref, tails_t_ref, cand_ref, srow_ref):
    cap = tails_ref.shape[0]
    lines = owner_ref.shape[0]
    mine = owner_ref[...] == me_ref[0]
    mine_b = onehot(mine)
    before = onehot(iota((128, 128), 0) < iota((128, 128), 1))
    rank = mm(mine_b, before)
    totals = mm(mine_b, jnp.ones((128, 128), bf16))
    upper = onehot(iota((lines, lines), 1) < iota((lines, lines), 0))
    offset = mm(upper, totals.astype(bf16))
    key = jnp.where(mine, (rank + offset).astype(i32), -1)
    code = row_ref[...] * (1 << shift) + iota((lines, 128), 0) * 128 + iota((lines, 128), 1) + 1
    code = code.astype(f32)
    slots = iota((cap, 128), 0)
    total = jnp.zeros((cap, 128), f32)
    for r in range(lines):
        total = total + jnp.where(slots == key[r : r + 1, :], code[r : r + 1, :], 0.0)
    found = jnp.sum(total, axis=1, keepdims=True).astype(i32) - 1
    live = found >= 0
    srow = jnp.where(live, lax.shift_right_arithmetic(found, shift), -1)
    cand_ref[...] = jnp.where(live, found & ((1 << shift) - 1), -1)
    srow_ref[...] = srow
    pick = onehot(iota((cap, table_ref.shape[1]), 1) == srow)
    tails_ref[...] = mm(pick, table_ref[...], NT).astype(bf16)
    tails_t_ref[0] = mm(table_ref[...], pick, NT).astype(bf16)


def pack_tails(me, tail_owners, tail_row, table_t, cap):
    cand = tail_row.shape[0]
    shift = int(math.log2(cand))
    width, rows = table_t.shape
    assert 1 << shift == cand and cand * rows < 1 << 24 and cand % 128 == 0
    return pl.pallas_call(
        functools.partial(pack_kernel, shift),
        in_specs=[SMEM] + [VMEM] * 3,
        out_shape=[
            jax.ShapeDtypeStruct((cap, width), bf16),
            jax.ShapeDtypeStruct((1, width, cap), bf16),
            jax.ShapeDtypeStruct((cap, 1), i32),
            jax.ShapeDtypeStruct((cap, 1), i32),
        ],
        compiler_params=params(mib=16),
        cost_estimate=cost(1e9, 2e6),
        name="pack_tails",
    )(me, tail_owners.reshape(-1, 128), tail_row.reshape(-1, 128), table_t)


def found_kernel(cap, count, me_ref, table_ref, *refs):
    outs, (want_ref, scr) = refs[count:-2], refs[-2:]
    numbers = pieces(refs[:count])
    queries = numbers[0].shape[1]
    owners = jnp.concatenate([b[0:1, :] for b in numbers], axis=0)
    mine = owners == me_ref[0]
    before = onehot(iota((queries, queries), 0) < iota((queries, queries), 1))
    rank = mm(onehot(mine), before)
    key = jnp.where(mine, rank.astype(i32), -1)
    slots = iota((cap, queries), 0)
    for d, block in enumerate(numbers):
        code = (block[1:2, :] + 1).astype(f32)
        picked = jnp.where(slots == key[d : d + 1, :], code, 0.0)
        scr[d * cap : (d + 1) * cap, :] = jnp.sum(picked, axis=1, keepdims=True)
    want = scr[...].astype(i32) - 1
    want_ref[...] = want
    pick = onehot(iota((len(numbers) * cap, table_ref.shape[1]), 1) == want)
    found = mm(pick, table_ref[...], NT).astype(bf16)
    for d, out in enumerate(pieces(outs)):
        out[...] = found[d * cap : (d + 1) * cap, :]


def find_heads(me, numbers, table_t, cap):
    width = table_t.shape[0]
    sizes = [x.shape[0] for x in numbers]
    slots = sum(sizes) * cap
    *found, want = pl.pallas_call(
        functools.partial(found_kernel, cap, len(numbers)),
        in_specs=[SMEM] + [VMEM] * (1 + len(numbers)),
        out_shape=[jax.ShapeDtypeStruct((s, cap, width), bf16) for s in sizes]
        + [jax.ShapeDtypeStruct((slots, 1), i32)],
        scratch_shapes=[pltpu.VMEM((slots, 1), f32)],
        compiler_params=params(mib=16),
        cost_estimate=cost(3e8, 2e6),
        name="find_heads",
    )(me, table_t, *numbers)
    return found, want


def pos_kernel(cap, me_ref, owner_ref, own_ref, other_ref, out_ref):
    cand = owner_ref.shape[1]
    queries = own_ref.shape[2]
    eye = iota((queries, queries), 0) == iota((queries, queries), 1)
    step = min(512, cand)
    for part, ref in enumerate((own_ref, other_ref)):
        row = ref[0, 3:4, :].astype(f32)
        pos = jnp.sum(jnp.where(eye, row, 0.0), axis=1, keepdims=True).astype(i32)
        owner = jnp.zeros((queries, step), f32)
        for c in range(0, cand, step):
            here = iota((queries, step), 1) + c
            value = owner_ref[:, c : c + step].astype(f32)
            owner = owner + jnp.where(here == pos, value, 0.0)
        owner = jnp.sum(owner, axis=1, keepdims=True).astype(i32)
        ahead = jnp.zeros((queries, step), f32)
        for c in range(0, cand, step):
            here = iota((queries, step), 1) + c
            same = (owner_ref[:, c : c + step] == owner) & (here < pos)
            ahead = ahead + jnp.where(same, 1.0, 0.0)
        ahead = jnp.sum(ahead, axis=1, keepdims=True).astype(i32)
        away = owner ^ me_ref[0]
        slot = lax.shift_right_arithmetic(away, 1) * cap + ahead
        out_ref[part * queries : (part + 1) * queries, :] = jnp.where((away & 1) == 0, slot, -1)


def pos_slots(me, tail_owners, own, other, cap):
    queries = own.shape[2]
    return pl.pallas_call(
        functools.partial(pos_kernel, cap),
        in_specs=[SMEM] + [VMEM] * 3,
        out_shape=jax.ShapeDtypeStruct((2 * queries, 1), i32),
        compiler_params=params(mib=8),
        cost_estimate=cost(1e7, 1e5),
        name="pos_slots",
    )(me, tail_owners.reshape(1, -1), own, other)


def slot_picks(cap, slots, me, orow):
    count = slots // cap
    queries = orow.shape[1]
    away = orow ^ me
    member = iota((count, queries), 0) == away
    before = onehot(iota((queries, queries), 0) < iota((queries, queries), 1))
    rank = mm(onehot(member), before)
    rank = jnp.sum(jnp.where(member, rank, 0.0), axis=0, keepdims=True).astype(i32)
    return onehot(iota((slots, queries), 0) == away * cap + rank)


def front_kernel(cap, count, me_ref, orow_ref, rel_ref, rtab_ref, ext_ref, band_ref, w_ref, *refs):
    fetched, (pre_ref, img_ref, qv_ref, hvt_ref, qvt_ref, feats, acc, ext) = refs[:count], refs[count:]
    s = pl.program_id(0)
    width, queries = acc.shape

    @pl.when(s == 0)
    def _():
        rows = jnp.concatenate([b[...] for b in pieces(fetched)], axis=0)
        pick = slot_picks(cap, rows.shape[0], me_ref[0], orow_ref[...])
        hvt = mm(rows, pick, TN).astype(bf16)
        hvt_ref[0] = hvt
        rels = rtab_ref.shape[1]
        rvt = mm(rtab_ref[...], onehot(iota((rels, queries), 0) == rel_ref[...])).astype(bf16)
        entry = iota((width, ext_ref.shape[1]), 0)
        image = mm(onehot(entry == ext_ref[...]), hvt, TN)
        image = image + mm(onehot(entry + width == ext_ref[...]), rvt, TN)
        ext[...] = image.astype(bf16)
        for g in range(GROUPS):
            img_ref[:, g * queries : (g + 1) * queries] = ext[g * BAND_OUT : g * BAND_OUT + LANES, :]
        acc[...] = jnp.zeros_like(acc)

    units = band_ref.shape[0] // BAND_OUT
    flat = GROUPS * BAND_OUT
    pre = mm(band_ref[...], img_ref[...])
    act = (pre * sigmoid(pre)).astype(bf16)
    for f in range(units):
        for g in range(GROUPS):
            rows = slice(f * flat + g * BAND_OUT, f * flat + (g + 1) * BAND_OUT)
            part = slice(f * BAND_OUT, (f + 1) * BAND_OUT)
            lanes = slice(g * queries, (g + 1) * queries)
            pre_ref[rows, :] = pre[part, lanes]
            feats[rows, :] = act[part, lanes]
    acc[...] += mm(w_ref[...], feats[...])

    @pl.when(s == pl.num_programs(0) - 1)
    def _():
        query = acc[...]
        qvt_ref[0] = query.astype(bf16)
        qv_ref[...] = query.T.astype(bf16)


def filter_block(filts):
    return math.gcd(filts, 8)


def front(me, fetched, orow, rel_row, rtab_t, ext, band, weight_t, cap):
    queries = orow.shape[1]
    width, flat = weight_t.shape
    filts = band.shape[0] // BAND_OUT
    units = filter_block(filts)
    cols = flat // filts * units
    return pl.pallas_call(
        functools.partial(front_kernel, cap, len(fetched)),
        grid=(filts // units,),
        in_specs=[
            SMEM,
            whole(orow.shape),
            whole(rel_row.shape),
            whole(rtab_t.shape),
            whole(ext.shape),
            pl.BlockSpec((units * BAND_OUT, LANES), lambda s: (s, 0)),
            pl.BlockSpec((width, cols), lambda s: (0, s)),
        ]
        + [whole(x.shape) for x in fetched],
        out_specs=[
            pl.BlockSpec((cols, queries), lambda s: (s, 0)),
            whole((LANES, GROUPS * queries)),
            whole((queries, width)),
            whole((1, width, queries)),
            whole((1, width, queries)),
        ],
        out_shape=[
            jax.ShapeDtypeStruct((flat, queries), f32),
            jax.ShapeDtypeStruct((LANES, GROUPS * queries), bf16),
            jax.ShapeDtypeStruct((queries, width), bf16),
            jax.ShapeDtypeStruct((1, width, queries), bf16),
            jax.ShapeDtypeStruct((1, width, queries), bf16),
        ],
        scratch_shapes=[
            pltpu.VMEM((cols, queries), bf16),
            pltpu.VMEM((width, queries), f32),
            pltpu.VMEM((ext.shape[1], queries), bf16),
        ],
        compiler_params=params("arbitrary", mib=24),
        cost_estimate=cost(4e9, 2.4e7, 2.5e6),
        name="front",
    )(me, orow, rel_row, rtab_t, ext, band, weight_t, *fetched)


def score_kernel(cand, count, pos_ref, mine_ref, mate_ref, *refs):
    tails, (own_ref, other_ref) = pieces(refs[:count]), refs[count:]
    qv = jnp.concatenate([mine_ref[...], mate_ref[...]], axis=0)
    queries = qv.shape[0]
    cap = tails[0].shape[1]
    total = jnp.zeros(qv.shape, f32)
    for b, ref in enumerate(tails):
        block = ref[...]
        score = mm(qv, block)
        here = iota((queries, cap), 1) + b * cap
        target = jnp.where(here == pos_ref[...], 1.0 - smooth + smooth / cand, smooth / cand)
        grad = ((sigmoid(score) - target) * loss_weight).astype(bf16)
        total = total + mm(grad, block, NT)
    own_ref[...] = total[: queries // 2, :]
    other_ref[...] = total[queries // 2 :, :]


def score_part(qv, mate, pos2, tails, cand):
    half = jax.ShapeDtypeStruct(qv.shape, f32)
    return pl.pallas_call(
        functools.partial(score_kernel, cand, len(tails)),
        out_shape=[half, half],
        compiler_params=params(mib=16),
        cost_estimate=cost(1e9, 2e6, 1e6),
        name="score",
    )(pos2, qv, mate, *tails)


def back_kernel(
    cap, taps, count, me_ref, orow_ref, ext_ref, codes_ref, own_ref, recv_ref, img_ref, bandt_ref, w_ref, pre_ref,
    *refs,
):
    outs, (qgt_out, sums_ref, qgt, fgrad, spread, corr, ext) = refs[:count], refs[count:]
    s = pl.program_id(0)
    width, queries = qgt.shape

    @pl.when(s == 0)
    def _():
        qgt[...] = (own_ref[...] + recv_ref[...]).T.astype(bf16)
        qgt_out[0] = qgt[...]
        spread[...] = jnp.zeros_like(spread)

    units = bandt_ref.shape[1] // BAND_OUT
    flat = GROUPS * BAND_OUT
    for f in range(units):
        cols = slice(f * flat, (f + 1) * flat)
        linear = mm(w_ref[:, cols], qgt[...], TN)
        v = pre_ref[cols, :]
        sig = sigmoid(v)
        grad = (linear * (sig * (1.0 + v * (1.0 - sig)))).astype(bf16)
        for g in range(GROUPS):
            fgrad[f * BAND_OUT : (f + 1) * BAND_OUT, g * queries : (g + 1) * queries] = grad[
                g * BAND_OUT : (g + 1) * BAND_OUT, :
            ]
    spread[...] += mm(bandt_ref[...], fgrad[...])
    corr[pl.ds(s * units, units)] = mm(fgrad[...], img_ref[...], NT).reshape(units, BAND_OUT, LANES)

    @pl.when(s == pl.num_programs(0) - 1)
    def _():
        filts = corr.shape[0]
        ext[...] = jnp.zeros_like(ext)
        for g in range(GROUPS):
            ext[g * BAND_OUT : g * BAND_OUT + LANES, :] += spread[:, g * queries : (g + 1) * queries]
        entry = iota((width, ext.shape[0]), 0)
        high, low = split(ext[...])
        hpick = onehot(entry == ext_ref[...])
        rpick = onehot(entry + width == ext_ref[...])
        hgrad = (mm(hpick, high) + mm(hpick, low)).astype(bf16)
        sums_ref[0, :width, :] = mm(rpick, high) + mm(rpick, low)
        total = jnp.zeros((taps, filts), f32)
        for j in range(IMG):
            rows = corr[:, j, :]
            for di in range(1, BAND):
                rows = rows + pltpu.roll(corr[:, di * IMG + j, :], LANES - di * IMG, 1)
            pick = onehot(iota((taps, LANES), 0) == codes_ref[j : j + 1, :])
            rhigh, rlow = split(rows)
            total = total + mm(pick, rhigh, NT) + mm(pick, rlow, NT)
        rest = sums_ref.shape[1] - width
        sums_ref[0, width:, :] = jnp.zeros((rest, queries), f32)
        sums_ref[0, width : width + taps, :filts] = total
        blocks = pieces(outs)
        pick = slot_picks(cap, len(blocks) * cap, me_ref[0], orow_ref[...])
        rows = mm(pick, hgrad, NT).astype(bf16)
        for d, out in enumerate(blocks):
            out[...] = rows[d * cap : (d + 1) * cap, :]


def sums_rows(width, taps):
    return -(-(width + taps) // 8) * 8


def back(me, own, recv, orow, ext, codes, img, band_t, weight_t, pre, sizes, cap, taps):
    queries, width = own.shape
    flat = weight_t.shape[1]
    filts = band_t.shape[1] // BAND_OUT
    units = filter_block(filts)
    cols = flat // filts * units
    rows = sums_rows(width, taps)
    assert filts <= queries
    *outgoing, qgt, sums = pl.pallas_call(
        functools.partial(back_kernel, cap, taps, len(sizes)),
        grid=(filts // units,),
        in_specs=[
            SMEM,
            whole(orow.shape),
            whole(ext.shape),
            whole(codes.shape),
            whole(own.shape),
            whole(recv.shape),
            whole(img.shape),
            pl.BlockSpec((LANES, units * BAND_OUT), lambda s: (0, s)),
            pl.BlockSpec((width, cols), lambda s: (0, s)),
            pl.BlockSpec((cols, queries), lambda s: (s, 0)),
        ],
        out_specs=[whole((n, cap, width)) for n in sizes]
        + [whole((1, width, queries)), whole((1, rows, queries))],
        out_shape=[jax.ShapeDtypeStruct((n, cap, width), bf16) for n in sizes]
        + [
            jax.ShapeDtypeStruct((1, width, queries), bf16),
            jax.ShapeDtypeStruct((1, rows, queries), f32),
        ],
        scratch_shapes=[
            pltpu.VMEM((width, queries), bf16),
            pltpu.VMEM((units * BAND_OUT, GROUPS * queries), bf16),
            pltpu.VMEM((LANES, GROUPS * queries), f32),
            pltpu.VMEM((filts, BAND_OUT, LANES), f32),
            pltpu.VMEM((ext.shape[1], queries), f32),
        ],
        compiler_params=params("arbitrary", mib=28),
        cost_estimate=cost(6e9, 2e7, 2.5e6),
        name="back",
    )(me, orow, ext, codes, own, recv, img, band_t, weight_t, pre)
    return outgoing, qgt, sums


def tail_kernel(cand, count, tails_ref, mate_ref, scand_ref, mcand_ref, *refs):
    numbers, vectors = pieces(refs[:count]), pieces(refs[count : 2 * count])
    own_ref, other_ref = refs[2 * count :]
    tails = jnp.concatenate([tails_ref[...], mate_ref[...]], axis=0)
    scand = jnp.concatenate([scand_ref[...], mcand_ref[...]], axis=0)
    cap = tails_ref.shape[0]
    own = jnp.zeros(own_ref.shape, f32)
    other = jnp.zeros(own_ref.shape, f32)
    for nums, vecs in zip(pairs(numbers), pairs(vectors)):
        qvt = lanes_of(vecs)
        pos = lanes_of(nums, slice(3, 4))
        score = mm(tails, qvt)
        target = jnp.where(scand == pos, 1.0 - smooth + smooth / cand, smooth / cand)
        grad = ((sigmoid(score) - target) * loss_weight).astype(bf16)
        own = own + mm(qvt, grad[:cap, :], NT)
        other = other + mm(qvt, grad[cap:, :], NT)
    own_ref[...] = own
    other_ref[...] = other


def tail_part(tails, mate, scand, mcand, numbers, vectors, cand):
    cap, width = tails.shape
    half = jax.ShapeDtypeStruct((width, cap), f32)
    return pl.pallas_call(
        functools.partial(tail_kernel, cand, len(numbers)),
        out_shape=[half, half],
        compiler_params=params(mib=24),
        cost_estimate=cost(2e9, 3e6, 1e6),
        name="tail_grad",
    )(tails, mate, scand, mcand, *numbers, *vectors)


def proj_kernel(count, rtab_ref, ext_ref, band_ref, mate_ref, *refs):
    numbers = pieces(refs[:count])
    heads = pieces(refs[count : 2 * count])
    grads = pieces(refs[2 * count : 3 * count])
    own_ref, other_ref, pick, hmat, rmat = refs[3 * count :]
    width, rels = rtab_ref.shape
    units = band_ref.shape[0] // BAND_OUT
    flat = GROUPS * BAND_OUT
    cols = units * flat
    entry = iota((width, ext_ref.shape[1]), 0)
    for part, mat in ((0, hmat), (width, rmat)):
        pick[...] = jnp.where(entry + part == ext_ref[...], 1.0, 0.0).T.astype(bf16)
        for k, source in enumerate((band_ref, mate_ref)):
            for g in range(GROUPS):
                rows = mm(source[...], pick[g * BAND_OUT : g * BAND_OUT + LANES, :]).astype(bf16)
                for f in range(units):
                    first = k * cols + f * flat + g * BAND_OUT
                    mat[first : first + BAND_OUT, :] = rows[f * BAND_OUT : (f + 1) * BAND_OUT, :]
    for k, out in enumerate((own_ref, other_ref)):
        out[...] = jnp.zeros_like(out)
    for nums, hs, gs in zip(pairs(numbers), pairs(heads), pairs(grads)):
        hvt = lanes_of(hs)
        qgt = lanes_of(gs)
        rel = lanes_of(nums, slice(2, 3))
        rvt = mm(rtab_ref[...], onehot(iota((rels, rel.shape[1]), 0) == rel)).astype(bf16)
        for k, out in enumerate((own_ref, other_ref)):
            rows = slice(k * cols, (k + 1) * cols)
            pre = mm(hmat[rows, :], hvt) + mm(rmat[rows, :], rvt)
            out[...] += mm(qgt, (pre * sigmoid(pre)).astype(bf16), NT)


def proj_part(rtab_t, ext, band, mate, numbers, heads, grads):
    width = rtab_t.shape[0]
    rows = band.shape[0]
    cols = rows * GROUPS
    half = jax.ShapeDtypeStruct((width, cols), f32)
    return pl.pallas_call(
        functools.partial(proj_kernel, len(numbers)),
        out_shape=[half, half],
        scratch_shapes=[
            pltpu.VMEM((ext.shape[1], width), bf16),
            pltpu.VMEM((2 * cols, width), bf16),
            pltpu.VMEM((2 * cols, width), bf16),
        ],
        compiler_params=params(mib=28),
        cost_estimate=cost(6e9, 6e6, 2.5e6),
        name="proj_grad",
    )(rtab_t, ext, band, mate, *numbers, *heads, *grads)


def proj_columns(first, cols, filters, chequer_perm, relation_table, numbers, heads, grads):
    ks = filters.shape[-1]
    rim = ks // 2
    flat = IMG * IMG
    column = first + jnp.arange(cols, dtype=i32)
    f = column // flat
    i = (column % flat) // IMG
    j = column % IMG
    spot = jnp.arange(flat, dtype=i32)
    a = (spot[:, None] // IMG - i[None, :] + rim) % IMG
    b = (spot[:, None] % IMG - j[None, :] + rim) % IMG
    tap = filters[f[None, :], jnp.minimum(a, ks - 1), jnp.minimum(b, ks - 1)]
    matrix = jnp.where((a < ks) & (b < ks), tap, jnp.zeros((), bf16))
    width = heads.shape[1]
    head = heads.transpose(0, 2, 1).reshape(-1, width)
    qg = grads.transpose(0, 2, 1).reshape(-1, width)
    joined = jnp.concatenate([head, relation_table[numbers[:, 2].reshape(-1)]], axis=1)
    pre = mm(joined[:, chequer_perm], matrix)
    return mm(qg, (pre * sigmoid(pre)).astype(bf16), TN)


def rel_kernel(count, width, taps, *refs):
    numbers, sums = pieces(refs[:count]), pieces(refs[count : 2 * count])
    rel_ref, filt_ref = refs[2 * count :]
    total = jnp.zeros(rel_ref.shape, f32)
    filt = jnp.zeros(filt_ref.shape, f32)
    for nums, parts in zip(pairs(numbers), pairs(sums)):
        rel = lanes_of(nums, slice(2, 3))
        pick = onehot(iota((rel_ref.shape[1], rel.shape[1]), 0) == rel)
        high, low = split(lanes_of(parts, slice(0, width)))
        total = total + mm(high, pick, NT) + mm(low, pick, NT)
        for part in parts:
            filt = filt + part[width:, :]
    rel_ref[...] = total
    filt_ref[...] = filt


def rel_part(numbers, sums, width, rels, taps):
    rows, queries = sums[0].shape[1:]
    return pl.pallas_call(
        functools.partial(rel_kernel, len(numbers), width, taps),
        out_shape=[
            jax.ShapeDtypeStruct((width, rels), f32),
            jax.ShapeDtypeStruct((rows - width, queries), f32),
        ],
        compiler_params=params(mib=24),
        cost_estimate=cost(2e9, 3e6),
        name="rel_grad",
    )(*numbers, *sums)


def entity_kernel(count, want_ref, srow_ref, own_ref, recv_ref, *refs):
    incoming, out_ref = refs[:count], refs[count]
    rows = out_ref.shape[1]
    grads = jnp.concatenate([b[...] for b in pieces(incoming)], axis=0)
    total = mm(grads, onehot(iota((want_ref.shape[0], rows), 1) == want_ref[...]), TN)
    pick = onehot(iota((srow_ref.shape[0], rows), 1) == srow_ref[...])
    high, low = split(own_ref[...] + recv_ref[...])
    out_ref[...] = total + mm(high, pick) + mm(low, pick)


def entity_sum(want, srow, own, recv, incoming, rows):
    return pl.pallas_call(
        functools.partial(entity_kernel, len(incoming)),
        out_shape=jax.ShapeDtypeStruct((own.shape[0], rows), f32),
        compiler_params=params(mib=24),
        cost_estimate=cost(1.5e9, 4e6),
        name="entity_grad",
    )(want, srow, own, recv, *incoming)


def shards(
    entity_table,
    relation_table,
    filters,
    proj_weight,
    chequer_perm,
    head_owner,
    head_row,
    rel_ids,
    pos_index,
    tail_owner,
    tail_row,
):
    count = lax.axis_size("shard")
    me = lax.axis_index("shard")
    assert count & (count - 1) == 0
    direct = count <= 16
    order = me ^ jnp.arange(count, dtype=i32)
    core_order = (me >> 1) ^ jnp.arange(count // 2, dtype=i32)
    queries = head_row.shape[0]
    cand = tail_row.shape[0]
    rows, width = entity_table.shape
    rels = relation_table.shape[0]
    filts, ks, _ = filters.shape
    head_cap = 2 * queries // count
    tail_cap = 2 * cand // count
    same_core = [list(range(c, count, 2)) for c in range(2)]

    def swap(x, r):
        return lax.ppermute(x, "shard", [(d, d ^ r) for d in range(count)])

    def gather_all(x):
        if direct:
            return [x] + [swap(x, r) for r in range(1, count)]
        return [lax.all_gather(x, "shard", axis=0, tiled=True)[order]]

    def gather_core(x):
        if direct:
            far = [x] + [swap(x, r) for r in range(4, count, 4)]
            return [b for block in far for b in (block, swap(block, 2))]
        every = lax.all_gather(x, "shard", axis=0, axis_index_groups=same_core, tiled=True)
        return [every[core_order]]

    def exchange(blocks):
        if direct:
            return blocks[:1] + [swap(b, r) for r, b in enumerate(blocks) if r]
        sent = lax.all_to_all(blocks[0][order], "shard", split_axis=0, concat_axis=0, tiled=True)
        return [sent[order]]

    me1 = me.reshape(1)
    heads = head_owner[:, 0]
    tail_owners = tail_owner[:, 0]
    table_t, rtab_t, weight_t = entity_table.T, relation_table.T, proj_weight.T
    numbers = gather_all(jnp.stack([heads, head_row, rel_ids, pos_index])[None])
    core_numbers = numbers[::2] if direct else [numbers[0][::2]]
    mate_numbers = numbers[1] if direct else numbers[0][1:2]
    own_numbers = numbers[0] if direct else numbers[0][:1]

    found, want = find_heads(me1, numbers, table_t, head_cap)
    fetched = exchange(found)
    tails, tails_t, slot_cand, slot_row = pack_tails(me1, tail_owners, tail_row, table_t, tail_cap)
    core_tails = gather_core(tails_t)
    mate_tails, mate_cand = swap(tails, 1), swap(slot_cand, 1)
    pos2 = pos_slots(me1, tail_owners, own_numbers, mate_numbers, tail_cap)

    codes = jnp.asarray(band_codes(ks))
    band, band_t = build_band(filters, codes)
    extra = BAND_OUT * (GROUPS - 1) + LANES - IMG * IMG - BAND_OUT
    ext = jnp.concatenate([chequer_perm[-BAND_OUT:], chequer_perm, chequer_perm[:extra]])[None]
    orow = heads[None, :]
    pre, img, qv, hvt, qvt = front(
        me1, fetched, orow, rel_ids[None, :], rtab_t, ext, band, weight_t, head_cap
    )

    own, other = score_part(qv, swap(qv, 1), pos2, core_tails, cand)
    outgoing, qgt, sums = back(
        me1, own, swap(other, 1), orow, ext, codes, img, band_t, weight_t, pre,
        [x.shape[0] for x in found], head_cap, ks * ks,
    )
    incoming = exchange(outgoing)
    core_sums = gather_core(sums)
    core_hvt, core_qvt, core_qgt = gather_core(hvt), gather_core(qvt), gather_core(qgt)

    own, other = tail_part(tails, mate_tails, slot_cand, mate_cand, core_numbers, core_qvt, cand)
    entity_grad = entity_sum(want, slot_row, own, swap(other, 1), incoming, rows).T

    cols = filts * IMG * IMG // count
    if direct and cols % (IMG * IMG) == 0:
        unit = cols // (IMG * IMG) * BAND_OUT
        mine, mate = (
            lax.dynamic_slice_in_dim(band, d * unit, unit, axis=0) for d in (me, me ^ 1)
        )
        own, other = proj_part(rtab_t, ext, mine, mate, core_numbers, core_hvt, core_qgt)
    else:
        own, other = (
            proj_columns(
                d * cols, cols, filters, chequer_perm, relation_table,
                jnp.concatenate(core_numbers), jnp.concatenate(core_hvt), jnp.concatenate(core_qgt),
            )
            for d in (me, me ^ 1)
        )
    proj_grad = (own + swap(other, 1)).T

    part, filt = rel_part(core_numbers, core_sums, width, rels, ks * ks)
    relation_grad = (part + swap(part, 1)).T
    filter_grad = (filt + swap(filt, 1))[: ks * ks, :filts].T.reshape(filts, ks, ks)
    return (entity_grad, relation_grad, filter_grad, proj_grad)


def solution(mesh):
    placed = (
        P("shard", None),
        P(),
        P(),
        P(),
        P(),
        P(("parts", "shard"), None),
        P(("parts", "shard")),
        P(("parts", "shard")),
        P(("parts", "shard")),
        P("parts", None),
        P("parts"),
    )
    return jax.shard_map(
        shards,
        mesh=mesh,
        in_specs=placed,
        out_specs=(
            P(("parts", "shard"), None),
            P("parts", None),
            P("parts", None, None),
            P(("parts", "shard"), None),
        ),
        check_vma=False,
    )
```

```python
import functools
import math

import jax
import jax.numpy as jnp
import numpy as np
from jax import lax
from jax.experimental import pallas as pl
from jax.experimental.pallas import tpu as pltpu
from jax.sharding import PartitionSpec as P

IMG = 20
BAND = 4
GROUPS = IMG // BAND
BAND_OUT = BAND * IMG
LANES = 256

loss_weight = 0.015625
smooth = 0.1

f32 = jnp.float32
bf16 = jnp.bfloat16
i32 = jnp.int32

NN = (((1,), (0,)), ((), ()))
NT = (((1,), (1,)), ((), ()))
TN = (((0,), (0,)), ((), ()))


def mm(a, b, dims=NN):
    return lax.dot_general(a, b, dims, preferred_element_type=f32)


def iota(shape, axis):
    return lax.broadcasted_iota(i32, shape, axis)


def onehot(mask):
    return jnp.where(mask, 1.0, 0.0).astype(bf16)


def split(value):
    high = value.astype(bf16)
    return high, (value - high.astype(f32)).astype(bf16)


def sigmoid(v):
    return 0.5 * jnp.tanh(0.5 * v) + 0.5


def params(*semantics, mib=40):
    return pltpu.CompilerParams(
        dimension_semantics=semantics or None, vmem_limit_bytes=mib << 20
    )


def cost(flops, nbytes, trans=0):
    return pl.CostEstimate(flops=int(flops), bytes_accessed=int(nbytes), transcendentals=int(trans))


def whole(shape):
    return pl.BlockSpec(shape, lambda *_: (0,) * len(shape))


SMEM = pl.BlockSpec(memory_space=pltpu.SMEM)


def band_codes(ks):
    codes = np.full((IMG, LANES), -1, np.int32)
    for j in range(IMG):
        for r in range(ks):
            for x in range(IMG):
                b = (x - j + ks // 2) % IMG
                if b < ks:
                    codes[j, r * IMG + x] = r * ks + b
    return codes


def band_kernel(codes_ref, filt_ref, out_ref, out_t_ref, scr):
    count, taps = filt_ref.shape
    filt = filt_ref[...]
    for j in range(IMG):
        pick = onehot(iota((taps, LANES), 0) == codes_ref[j : j + 1, :])
        row = mm(filt, pick)
        for di in range(BAND):
            scr[:, di * IMG + j, :] = row if di == 0 else pltpu.roll(row, di * IMG, 1)
    full = scr[...].reshape(count * BAND_OUT, LANES)
    out_ref[...] = full.astype(bf16)
    out_t_ref[...] = full.T.astype(bf16)


def build_band(filters, codes):
    count, ks, _ = filters.shape
    return pl.pallas_call(
        band_kernel,
        out_shape=[
            jax.ShapeDtypeStruct((count * BAND_OUT, LANES), bf16),
            jax.ShapeDtypeStruct((LANES, count * BAND_OUT), bf16),
        ],
        scratch_shapes=[pltpu.VMEM((count, BAND_OUT, LANES), f32)],
        compiler_params=params(mib=24),
        cost_estimate=cost(4e7, 4e6),
        name="band",
    )(codes, filters.reshape(count, ks * ks))


VMEM = pl.BlockSpec(memory_space=pltpu.VMEM)


def pairs(count):
    step = 2 if count % 2 == 0 else 1
    return [range(i, i + step) for i in range(0, count, step)]


def beside(blocks):
    return jnp.concatenate(list(blocks), axis=1)


def pack_kernel(shift, me_ref, owner_ref, row_ref, table_ref, tails_ref, tails_t_ref, cand_ref, srow_ref):
    cap = tails_ref.shape[0]
    lines = owner_ref.shape[0]
    mine = owner_ref[...] == me_ref[0]
    mine_b = onehot(mine)
    before = onehot(iota((128, 128), 0) < iota((128, 128), 1))
    rank = mm(mine_b, before)
    totals = mm(mine_b, jnp.ones((128, 128), bf16))
    upper = onehot(iota((lines, lines), 1) < iota((lines, lines), 0))
    offset = mm(upper, totals.astype(bf16))
    key = jnp.where(mine, (rank + offset).astype(i32), -1)
    code = row_ref[...] * (1 << shift) + iota((lines, 128), 0) * 128 + iota((lines, 128), 1) + 1
    code = code.astype(f32)
    slots = iota((cap, 128), 0)
    total = jnp.zeros((cap, 128), f32)
    for r in range(lines):
        total = total + jnp.where(slots == key[r : r + 1, :], code[r : r + 1, :], 0.0)
    found = jnp.sum(total, axis=1, keepdims=True).astype(i32) - 1
    live = found >= 0
    srow = jnp.where(live, lax.shift_right_arithmetic(found, shift), -1)
    cand_ref[...] = jnp.where(live, found & ((1 << shift) - 1), -1)
    srow_ref[...] = srow
    pick = onehot(iota((cap, table_ref.shape[1]), 1) == srow)
    tails_ref[...] = mm(pick, table_ref[...], NT).astype(bf16)
    tails_t_ref[0] = mm(table_ref[...], pick, NT).astype(bf16)


def pack_tails(me, tail_owners, tail_row, table_t, cap):
    cand = tail_row.shape[0]
    shift = int(math.log2(cand))
    width, rows = table_t.shape
    assert 1 << shift == cand and cand * rows < 1 << 24 and cand % 128 == 0
    return pl.pallas_call(
        functools.partial(pack_kernel, shift),
        in_specs=[SMEM] + [VMEM] * 3,
        out_shape=[
            jax.ShapeDtypeStruct((cap, width), bf16),
            jax.ShapeDtypeStruct((1, width, cap), bf16),
            jax.ShapeDtypeStruct((cap, 1), i32),
            jax.ShapeDtypeStruct((cap, 1), i32),
        ],
        compiler_params=params(mib=16),
        cost_estimate=cost(1e9, 2e6),
        name="pack_tails",
    )(me, tail_owners.reshape(-1, 128), tail_row.reshape(-1, 128), table_t)


def found_kernel(cap, me_ref, table_ref, numbers_ref, found_ref, want_ref, scr):
    count, _, queries = numbers_ref.shape
    owners = jnp.concatenate([numbers_ref[d, 0:1, :] for d in range(count)], axis=0)
    mine = owners == me_ref[0]
    before = onehot(iota((queries, queries), 0) < iota((queries, queries), 1))
    rank = mm(onehot(mine), before)
    key = jnp.where(mine, rank.astype(i32), -1)
    slots = iota((cap, queries), 0)
    for d in range(count):
        code = (numbers_ref[d, 1:2, :] + 1).astype(f32)
        picked = jnp.where(slots == key[d : d + 1, :], code, 0.0)
        scr[d * cap : (d + 1) * cap, :] = jnp.sum(picked, axis=1, keepdims=True)
    want = scr[...].astype(i32) - 1
    want_ref[...] = want
    pick = onehot(iota((count * cap, table_ref.shape[1]), 1) == want)
    found = mm(pick, table_ref[...], NT).astype(bf16)
    for d in range(count):
        found_ref[d] = found[d * cap : (d + 1) * cap, :]


def find_heads(me, numbers, table_t, cap):
    width = table_t.shape[0]
    count = numbers.shape[0]
    return pl.pallas_call(
        functools.partial(found_kernel, cap),
        in_specs=[SMEM] + [VMEM] * 2,
        out_shape=[
            jax.ShapeDtypeStruct((count, cap, width), bf16),
            jax.ShapeDtypeStruct((count * cap, 1), i32),
        ],
        scratch_shapes=[pltpu.VMEM((count * cap, 1), f32)],
        compiler_params=params(mib=16),
        cost_estimate=cost(3e8, 2e6),
        name="find_heads",
    )(me, table_t, numbers)


def pos_kernel(cap, owner_ref, pos_ref, out_ref):
    cand = owner_ref.shape[1]
    queries = pos_ref.shape[1]
    eye = iota((queries, queries), 0) == iota((queries, queries), 1)
    step = min(512, cand)
    row = pos_ref[...].astype(f32)
    pos = jnp.sum(jnp.where(eye, row, 0.0), axis=1, keepdims=True).astype(i32)
    owner = jnp.zeros((queries, step), f32)
    for c in range(0, cand, step):
        here = iota((queries, step), 1) + c
        value = owner_ref[:, c : c + step].astype(f32)
        owner = owner + jnp.where(here == pos, value, 0.0)
    owner = jnp.sum(owner, axis=1, keepdims=True).astype(i32)
    ahead = jnp.zeros((queries, step), f32)
    for c in range(0, cand, step):
        here = iota((queries, step), 1) + c
        same = (owner_ref[:, c : c + step] == owner) & (here < pos)
        ahead = ahead + jnp.where(same, 1.0, 0.0)
    ahead = jnp.sum(ahead, axis=1, keepdims=True).astype(i32)
    out_ref[...] = owner * cap + ahead


def pos_slots(tail_owners, pos_index, cap):
    queries = pos_index.shape[0]
    return pl.pallas_call(
        functools.partial(pos_kernel, cap),
        out_shape=jax.ShapeDtypeStruct((queries, 1), i32),
        compiler_params=params(mib=8),
        cost_estimate=cost(1e7, 1e5),
        name="pos_slots",
    )(tail_owners.reshape(1, -1), pos_index.reshape(1, -1))


def slot_picks(cap, slots, orow):
    count = slots // cap
    queries = orow.shape[1]
    member = iota((count, queries), 0) == orow
    before = onehot(iota((queries, queries), 0) < iota((queries, queries), 1))
    rank = mm(onehot(member), before)
    rank = jnp.sum(jnp.where(member, rank, 0.0), axis=0, keepdims=True).astype(i32)
    return onehot(iota((slots, queries), 0) == orow * cap + rank)


def front_kernel(
    cap, fetched_ref, orow_ref, rel_ref, rtab_ref, ext_ref, band_ref, w_ref,
    pre_ref, img_ref, qv_ref, vecs_ref, feats, acc, ext,
):
    s = pl.program_id(0)
    width, queries = acc.shape

    @pl.when(s == 0)
    def _():
        rows = jnp.concatenate([fetched_ref[d] for d in range(fetched_ref.shape[0])], axis=0)
        pick = slot_picks(cap, rows.shape[0], orow_ref[...])
        hvt = mm(rows, pick, TN).astype(bf16)
        for d in range(vecs_ref.shape[0]):
            vecs_ref[d, 0] = hvt
        rels = rtab_ref.shape[1]
        rvt = mm(rtab_ref[...], onehot(iota((rels, queries), 0) == rel_ref[...])).astype(bf16)
        entry = iota((width, ext_ref.shape[1]), 0)
        image = mm(onehot(entry == ext_ref[...]), hvt, TN)
        image = image + mm(onehot(entry + width == ext_ref[...]), rvt, TN)
        ext[...] = image.astype(bf16)
        for g in range(GROUPS):
            img_ref[:, g * queries : (g + 1) * queries] = ext[g * BAND_OUT : g * BAND_OUT + LANES, :]
        acc[...] = jnp.zeros_like(acc)

    units = band_ref.shape[0] // BAND_OUT
    flat = GROUPS * BAND_OUT
    pre = mm(band_ref[...], img_ref[...])
    act = (pre * sigmoid(pre)).astype(bf16)
    for f in range(units):
        for g in range(GROUPS):
            rows = slice(f * flat + g * BAND_OUT, f * flat + (g + 1) * BAND_OUT)
            part = slice(f * BAND_OUT, (f + 1) * BAND_OUT)
            lanes = slice(g * queries, (g + 1) * queries)
            pre_ref[rows, :] = pre[part, lanes]
            feats[rows, :] = act[part, lanes]
    acc[...] += mm(w_ref[...], feats[...])

    @pl.when(s == pl.num_programs(0) - 1)
    def _():
        query = acc[...]
        qv_ref[...] = query.T.astype(bf16)
        qvt = query.astype(bf16)
        for d in range(vecs_ref.shape[0]):
            vecs_ref[d, 1] = qvt


def filter_block(filts):
    return math.gcd(filts, 8)


def front(fetched, orow, rel_row, rtab_t, ext, band, weight_t, cap, copies):
    queries = orow.shape[1]
    width, flat = weight_t.shape
    filts = band.shape[0] // BAND_OUT
    units = filter_block(filts)
    cols = flat // filts * units
    return pl.pallas_call(
        functools.partial(front_kernel, cap),
        grid=(filts // units,),
        in_specs=[
            whole(fetched.shape),
            whole(orow.shape),
            whole(rel_row.shape),
            whole(rtab_t.shape),
            whole(ext.shape),
            pl.BlockSpec((units * BAND_OUT, LANES), lambda s: (s, 0)),
            pl.BlockSpec((width, cols), lambda s: (0, s)),
        ],
        out_specs=[
            pl.BlockSpec((cols, queries), lambda s: (s, 0)),
            whole((LANES, GROUPS * queries)),
            whole((queries, width)),
            whole((copies, 2, width, queries)),
        ],
        out_shape=[
            jax.ShapeDtypeStruct((flat, queries), f32),
            jax.ShapeDtypeStruct((LANES, GROUPS * queries), bf16),
            jax.ShapeDtypeStruct((queries, width), bf16),
            jax.ShapeDtypeStruct((copies, 2, width, queries), bf16),
        ],
        scratch_shapes=[
            pltpu.VMEM((cols, queries), bf16),
            pltpu.VMEM((width, queries), f32),
            pltpu.VMEM((ext.shape[1], queries), bf16),
        ],
        compiler_params=params("arbitrary", mib=24),
        cost_estimate=cost(4e9, 2.4e7, 2.5e6),
        name="front",
    )(fetched, orow, rel_row, rtab_t, ext, band, weight_t)


def score_kernel(cand, pos_ref, qv_ref, tails_ref, out_ref):
    qv = qv_ref[...]
    queries = qv.shape[0]
    owners, _, cap = tails_ref.shape
    total = jnp.zeros(qv.shape, f32)
    for b in range(owners):
        block = tails_ref[b]
        score = mm(qv, block)
        here = iota((queries, cap), 1) + b * cap
        target = jnp.where(here == pos_ref[...], 1.0 - smooth + smooth / cand, smooth / cand)
        grad = ((sigmoid(score) - target) * loss_weight).astype(bf16)
        total = total + mm(grad, block, NT)
    qgt = total.T.astype(bf16)
    for d in range(out_ref.shape[0]):
        out_ref[d] = qgt


def score_part(qv, pos, tails, cand, copies):
    queries, width = qv.shape
    return pl.pallas_call(
        functools.partial(score_kernel, cand),
        out_shape=jax.ShapeDtypeStruct((copies, width, queries), bf16),
        compiler_params=params(mib=20),
        cost_estimate=cost(1e9, 3e6, 5e5),
        name="score",
    )(pos, qv, tails)


def back_kernel(
    cap, taps, orow_ref, ext_ref, codes_ref, qgt_ref, img_ref, bandt_ref, w_ref, pre_ref,
    out_ref, sums_ref, fgrad, spread, corr, ext,
):
    s = pl.program_id(0)
    _, width, queries = qgt_ref.shape

    @pl.when(s == 0)
    def _():
        spread[...] = jnp.zeros_like(spread)

    units = bandt_ref.shape[1] // BAND_OUT
    flat = GROUPS * BAND_OUT
    linear = mm(w_ref[...], qgt_ref[0], TN)
    for f in range(units):
        cols = slice(f * flat, (f + 1) * flat)
        v = pre_ref[cols, :]
        sig = sigmoid(v)
        grad = (linear[cols, :] * (sig * (1.0 + v * (1.0 - sig)))).astype(bf16)
        for g in range(GROUPS):
            fgrad[f * BAND_OUT : (f + 1) * BAND_OUT, g * queries : (g + 1) * queries] = grad[
                g * BAND_OUT : (g + 1) * BAND_OUT, :
            ]
    spread[...] += mm(bandt_ref[...], fgrad[...])
    corr[pl.ds(s * units, units)] = mm(fgrad[...], img_ref[...], NT).reshape(units, BAND_OUT, LANES)

    @pl.when(s == pl.num_programs(0) - 1)
    def _():
        filts = corr.shape[0]
        ext[...] = jnp.zeros_like(ext)
        for g in range(GROUPS):
            ext[g * BAND_OUT : g * BAND_OUT + LANES, :] += spread[:, g * queries : (g + 1) * queries]
        entry = iota((width, ext.shape[0]), 0)
        high, low = split(ext[...])
        hpick = onehot(entry == ext_ref[...])
        rpick = onehot(entry + width == ext_ref[...])
        hgrad = (mm(hpick, high) + mm(hpick, low)).astype(bf16)
        rgrad = mm(rpick, high) + mm(rpick, low)
        total = jnp.zeros((taps, filts), f32)
        for j in range(IMG):
            rows = corr[:, j, :]
            for di in range(1, BAND):
                rows = rows + pltpu.roll(corr[:, di * IMG + j, :], LANES - di * IMG, 1)
            pick = onehot(iota((taps, LANES), 0) == codes_ref[j : j + 1, :])
            rhigh, rlow = split(rows)
            total = total + mm(pick, rhigh, NT) + mm(pick, rlow, NT)
        rest = jnp.zeros((sums_ref.shape[1] - width, queries), f32)
        for d in range(sums_ref.shape[0]):
            sums_ref[d, :width, :] = rgrad
            sums_ref[d, width:, :] = rest
            sums_ref[d, width : width + taps, :filts] = total
        blocks = out_ref.shape[0]
        pick = slot_picks(cap, blocks * cap, orow_ref[...])
        rows = mm(pick, hgrad, NT).astype(bf16)
        for d in range(blocks):
            out_ref[d] = rows[d * cap : (d + 1) * cap, :]


def sums_rows(width, taps):
    return -(-(width + taps) // 8) * 8


def back(qgt, orow, ext, codes, img, band_t, weight_t, pre, count, cap, taps, copies):
    _, width, queries = qgt.shape
    flat = weight_t.shape[1]
    filts = band_t.shape[1] // BAND_OUT
    units = filter_block(filts)
    cols = flat // filts * units
    rows = sums_rows(width, taps)
    assert filts <= queries
    return pl.pallas_call(
        functools.partial(back_kernel, cap, taps),
        grid=(filts // units,),
        in_specs=[
            whole(orow.shape),
            whole(ext.shape),
            whole(codes.shape),
            whole((1, width, queries)),
            whole(img.shape),
            pl.BlockSpec((LANES, units * BAND_OUT), lambda s: (0, s)),
            pl.BlockSpec((width, cols), lambda s: (0, s)),
            pl.BlockSpec((cols, queries), lambda s: (s, 0)),
        ],
        out_specs=[whole((count, cap, width)), whole((copies, rows, queries))],
        out_shape=[
            jax.ShapeDtypeStruct((count, cap, width), bf16),
            jax.ShapeDtypeStruct((copies, rows, queries), f32),
        ],
        scratch_shapes=[
            pltpu.VMEM((units * BAND_OUT, GROUPS * queries), bf16),
            pltpu.VMEM((LANES, GROUPS * queries), f32),
            pltpu.VMEM((filts, BAND_OUT, LANES), f32),
            pltpu.VMEM((ext.shape[1], queries), f32),
        ],
        compiler_params=params("arbitrary", mib=28),
        cost_estimate=cost(6e9, 2e7, 2.5e6),
        name="back",
    )(orow, ext, codes, qgt, img, band_t, weight_t, pre)


def tail_kernel(
    cand, core_ref, tails_ref, mate_ref, scand_ref, mcand_ref, numbers_ref, vecs_ref, own_ref, other_ref
):
    tails = jnp.concatenate([tails_ref[...], mate_ref[...]], axis=0)
    scand = jnp.concatenate([scand_ref[...], mcand_ref[...]], axis=0)
    cap = tails_ref.shape[0]
    own = jnp.zeros(own_ref.shape, f32)
    other = jnp.zeros(own_ref.shape, f32)
    for group in pairs(vecs_ref.shape[0]):
        qvt = beside(vecs_ref[p, 1] for p in group)
        pos = beside(numbers_ref[2 * p + core_ref[0], 3:4, :] for p in group)
        score = mm(tails, qvt)
        target = jnp.where(scand == pos, 1.0 - smooth + smooth / cand, smooth / cand)
        grad = ((sigmoid(score) - target) * loss_weight).astype(bf16)
        own = own + mm(qvt, grad[:cap, :], NT)
        other = other + mm(qvt, grad[cap:, :], NT)
    own_ref[...] = own
    other_ref[...] = other


def tail_part(core, tails, mate, scand, mcand, numbers, vecs, cand):
    cap, width = tails.shape
    half = jax.ShapeDtypeStruct((width, cap), f32)
    return pl.pallas_call(
        functools.partial(tail_kernel, cand),
        in_specs=[SMEM] + [VMEM] * 6,
        out_shape=[half, half],
        compiler_params=params(mib=24),
        cost_estimate=cost(2e9, 3e6, 1e6),
        name="tail_grad",
    )(core, tails, mate, scand, mcand, numbers, vecs)


def proj_kernel(
    core_ref, rtab_ref, ext_ref, band_ref, mate_ref, numbers_ref, vecs_ref, grads_ref,
    own_ref, other_ref, pick, hmat, rmat,
):
    width, rels = rtab_ref.shape
    units = band_ref.shape[0] // BAND_OUT
    flat = GROUPS * BAND_OUT
    cols = units * flat
    entry = iota((width, ext_ref.shape[1]), 0)
    for part, mat in ((0, hmat), (width, rmat)):
        pick[...] = jnp.where(entry + part == ext_ref[...], 1.0, 0.0).T.astype(bf16)
        for k, source in enumerate((band_ref, mate_ref)):
            for g in range(GROUPS):
                rows = mm(source[...], pick[g * BAND_OUT : g * BAND_OUT + LANES, :]).astype(bf16)
                for f in range(units):
                    first = k * cols + f * flat + g * BAND_OUT
                    mat[first : first + BAND_OUT, :] = rows[f * BAND_OUT : (f + 1) * BAND_OUT, :]
    for k, out in enumerate((own_ref, other_ref)):
        out[...] = jnp.zeros_like(out)
    for group in pairs(vecs_ref.shape[0]):
        hvt = beside(vecs_ref[p, 0] for p in group)
        qgt = beside(grads_ref[p] for p in group)
        rel = beside(numbers_ref[2 * p + core_ref[0], 2:3, :] for p in group)
        rvt = mm(rtab_ref[...], onehot(iota((rels, rel.shape[1]), 0) == rel)).astype(bf16)
        for k, out in enumerate((own_ref, other_ref)):
            rows = slice(k * cols, (k + 1) * cols)
            pre = mm(hmat[rows, :], hvt) + mm(rmat[rows, :], rvt)
            out[...] += mm(qgt, (pre * sigmoid(pre)).astype(bf16), NT)


def proj_part(core, rtab_t, ext, band, mate, numbers, vecs, grads):
    width = rtab_t.shape[0]
    rows = band.shape[0]
    cols = rows * GROUPS
    half = jax.ShapeDtypeStruct((width, cols), f32)
    return pl.pallas_call(
        proj_kernel,
        in_specs=[SMEM] + [VMEM] * 7,
        out_shape=[half, half],
        scratch_shapes=[
            pltpu.VMEM((ext.shape[1], width), bf16),
            pltpu.VMEM((2 * cols, width), bf16),
            pltpu.VMEM((2 * cols, width), bf16),
        ],
        compiler_params=params(mib=28),
        cost_estimate=cost(6e9, 6e6, 2.5e6),
        name="proj_grad",
    )(core, rtab_t, ext, band, mate, numbers, vecs, grads)


def proj_columns(first, cols, filters, chequer_perm, relation_table, numbers, heads, grads):
    ks = filters.shape[-1]
    rim = ks // 2
    flat = IMG * IMG
    column = first + jnp.arange(cols, dtype=i32)
    f = column // flat
    i = (column % flat) // IMG
    j = column % IMG
    spot = jnp.arange(flat, dtype=i32)
    a = (spot[:, None] // IMG - i[None, :] + rim) % IMG
    b = (spot[:, None] % IMG - j[None, :] + rim) % IMG
    tap = filters[f[None, :], jnp.minimum(a, ks - 1), jnp.minimum(b, ks - 1)]
    matrix = jnp.where((a < ks) & (b < ks), tap, jnp.zeros((), bf16))
    width = heads.shape[1]
    head = heads.transpose(0, 2, 1).reshape(-1, width)
    qg = grads.transpose(0, 2, 1).reshape(-1, width)
    joined = jnp.concatenate([head, relation_table[numbers[:, 2].reshape(-1)]], axis=1)
    pre = mm(joined[:, chequer_perm], matrix)
    return mm(qg, (pre * sigmoid(pre)).astype(bf16), TN)


def rel_kernel(width, core_ref, numbers_ref, sums_ref, rel_ref, filt_ref):
    total = jnp.zeros(rel_ref.shape, f32)
    filt = jnp.zeros(filt_ref.shape, f32)
    for group in pairs(sums_ref.shape[0]):
        rel = beside(numbers_ref[2 * p + core_ref[0], 2:3, :] for p in group)
        pick = onehot(iota((rel_ref.shape[1], rel.shape[1]), 0) == rel)
        high, low = split(beside(sums_ref[p, :width, :] for p in group))
        total = total + mm(high, pick, NT) + mm(low, pick, NT)
        for p in group:
            filt = filt + sums_ref[p, width:, :]
    rel_ref[...] = total
    filt_ref[...] = filt


def rel_part(core, numbers, sums, width, rels):
    rows, queries = sums.shape[1:]
    return pl.pallas_call(
        functools.partial(rel_kernel, width),
        in_specs=[SMEM] + [VMEM] * 2,
        out_shape=[
            jax.ShapeDtypeStruct((width, rels), f32),
            jax.ShapeDtypeStruct((rows - width, queries), f32),
        ],
        compiler_params=params(mib=24),
        cost_estimate=cost(2e9, 3e6),
        name="rel_grad",
    )(core, numbers, sums)


def entity_kernel(want_ref, srow_ref, own_ref, recv_ref, incoming_ref, out_ref):
    rows = out_ref.shape[1]
    grads = jnp.concatenate([incoming_ref[d] for d in range(incoming_ref.shape[0])], axis=0)
    total = mm(grads, onehot(iota((want_ref.shape[0], rows), 1) == want_ref[...]), TN)
    pick = onehot(iota((srow_ref.shape[0], rows), 1) == srow_ref[...])
    high, low = split(own_ref[...] + recv_ref[...])
    out_ref[...] = total + mm(high, pick) + mm(low, pick)


def entity_sum(want, srow, own, recv, incoming, rows):
    return pl.pallas_call(
        entity_kernel,
        out_shape=jax.ShapeDtypeStruct((own.shape[0], rows), f32),
        compiler_params=params(mib=24),
        cost_estimate=cost(1.5e9, 4e6),
        name="entity_grad",
    )(want, srow, own, recv, incoming)


def shards(
    entity_table,
    relation_table,
    filters,
    proj_weight,
    chequer_perm,
    head_owner,
    head_row,
    rel_ids,
    pos_index,
    tail_owner,
    tail_row,
):
    count = lax.axis_size("shard")
    me = lax.axis_index("shard")
    assert count % 2 == 0
    direct = count <= 16
    queries = head_row.shape[0]
    cand = tail_row.shape[0]
    rows, width = entity_table.shape
    rels = relation_table.shape[0]
    filts, ks, _ = filters.shape
    head_cap = 2 * queries // count
    tail_cap = 2 * cand // count
    same_core = [list(range(c, count, 2)) for c in range(2)]
    copies = count // 2 if direct else 1

    def swap(x):
        return lax.ppermute(x, "shard", [(d, d ^ 1) for d in range(count)])

    def exchange(x):
        return lax.all_to_all(x, "shard", split_axis=0, concat_axis=0, tiled=True)

    def gather_core(x):
        if direct:
            return lax.all_to_all(
                x, "shard", split_axis=0, concat_axis=0, axis_index_groups=same_core, tiled=True
            )
        return lax.all_gather(x, "shard", axis=0, axis_index_groups=same_core, tiled=True)

    me1 = me.reshape(1)
    core = (me & 1).reshape(1)
    heads = head_owner[:, 0]
    tail_owners = tail_owner[:, 0]
    table_t, rtab_t, weight_t = entity_table.T, relation_table.T, proj_weight.T
    numbers = jnp.stack([heads, head_row, rel_ids, pos_index])[None]
    numbers = exchange(jnp.broadcast_to(numbers, (count,) + numbers.shape[1:]))

    tails, tails_t, slot_cand, slot_row = pack_tails(me1, tail_owners, tail_row, table_t, tail_cap)
    all_tails = lax.all_gather(tails_t, "shard", axis=0, tiled=True)
    mate_tails, mate_cand = swap(tails), swap(slot_cand)
    found, want = find_heads(me1, numbers, table_t, head_cap)
    fetched = exchange(found)
    pos = pos_slots(tail_owners, pos_index, tail_cap)

    codes = jnp.asarray(band_codes(ks))
    band, band_t = build_band(filters, codes)
    extra = BAND_OUT * (GROUPS - 1) + LANES - IMG * IMG - BAND_OUT
    ext = jnp.concatenate([chequer_perm[-BAND_OUT:], chequer_perm, chequer_perm[:extra]])[None]
    orow = heads[None, :]
    pre, img, qv, vecs = front(
        fetched, orow, rel_ids[None, :], rtab_t, ext, band, weight_t, head_cap, copies
    )
    core_vecs = gather_core(vecs)

    qgt = score_part(qv, pos, all_tails, cand, copies)
    core_qgt = gather_core(qgt)
    outgoing, sums = back(
        qgt, orow, ext, codes, img, band_t, weight_t, pre, count, head_cap, ks * ks, copies
    )
    core_sums = gather_core(sums)
    incoming = exchange(outgoing)

    own, other = tail_part(core, tails, mate_tails, slot_cand, mate_cand, numbers, core_vecs, cand)
    entity_grad = entity_sum(want, slot_row, own, swap(other), incoming, rows).T

    cols = filts * IMG * IMG // count
    if direct and cols % (IMG * IMG) == 0:
        unit = cols // (IMG * IMG) * BAND_OUT
        mine, mate = (
            lax.dynamic_slice_in_dim(band, d * unit, unit, axis=0) for d in (me, me ^ 1)
        )
        own, other = proj_part(core, rtab_t, ext, mine, mate, numbers, core_vecs, core_qgt)
    else:
        own, other = (
            proj_columns(
                d * cols, cols, filters, chequer_perm, relation_table,
                lax.dynamic_index_in_dim(
                    numbers.reshape(count // 2, 2, 4, queries), me & 1, 1, keepdims=False
                ),
                core_vecs[:, 0], core_qgt,
            )
            for d in (me, me ^ 1)
        )
    proj_grad = (own + swap(other)).T

    part, filt = rel_part(core, numbers, core_sums, width, rels)
    relation_grad = (part + swap(part)).T
    filter_grad = (filt + swap(filt))[: ks * ks, :filts].T.reshape(filts, ks, ks)
    return (entity_grad, relation_grad, filter_grad, proj_grad)


def solution(mesh):
    placed = (
        P("shard", None),
        P(),
        P(),
        P(),
        P(),
        P(("parts", "shard"), None),
        P(("parts", "shard")),
        P(("parts", "shard")),
        P(("parts", "shard")),
        P("parts", None),
        P("parts"),
    )
    return jax.shard_map(
        shards,
        mesh=mesh,
        in_specs=placed,
        out_specs=(
            P(("parts", "shard"), None),
            P("parts", None),
            P("parts", None, None),
            P(("parts", "shard"), None),
        ),
        check_vma=False,
    )
```

```python
import functools
import math

import jax
import jax.numpy as jnp
import numpy as np
from jax import lax
from jax.experimental import pallas as pl
from jax.experimental.pallas import tpu as pltpu
from jax.sharding import PartitionSpec as P

IMG = 20
BAND = 4
GROUPS = IMG // BAND
BAND_OUT = BAND * IMG
LANES = 256

loss_weight = 0.015625
smooth = 0.1

f32 = jnp.float32
bf16 = jnp.bfloat16
i32 = jnp.int32

NN = (((1,), (0,)), ((), ()))
NT = (((1,), (1,)), ((), ()))
TN = (((0,), (0,)), ((), ()))


def mm(a, b, dims=NN):
    return lax.dot_general(a, b, dims, preferred_element_type=f32)


def iota(shape, axis):
    return lax.broadcasted_iota(i32, shape, axis)


def onehot(mask):
    return jnp.where(mask, 1.0, 0.0).astype(bf16)


def split(value):
    high = value.astype(bf16)
    return high, (value - high.astype(f32)).astype(bf16)


def sigmoid(v):
    return 0.5 * jnp.tanh(0.5 * v) + 0.5


def params(*semantics):
    return pltpu.CompilerParams(
        dimension_semantics=semantics or None, vmem_limit_bytes=60 << 20
    )


def cost(flops, nbytes, trans=0):
    return pl.CostEstimate(flops=int(flops), bytes_accessed=int(nbytes), transcendentals=int(trans))


def whole(shape):
    return pl.BlockSpec(shape, lambda *_: (0,) * len(shape))


SMEM = pl.BlockSpec(memory_space=pltpu.SMEM)


def band_codes(ks):
    codes = np.full((IMG, LANES), -1, np.int32)
    for j in range(IMG):
        for r in range(ks):
            for x in range(IMG):
                b = (x - j + ks // 2) % IMG
                if b < ks:
                    codes[j, r * IMG + x] = r * ks + b
    return codes


def band_kernel(codes_ref, filt_ref, out_ref, out_t_ref, scr):
    count, taps = filt_ref.shape
    filt = filt_ref[...]
    for j in range(IMG):
        pick = onehot(iota((taps, LANES), 0) == codes_ref[j : j + 1, :])
        row = mm(filt, pick)
        for di in range(BAND):
            scr[:, di * IMG + j, :] = row if di == 0 else pltpu.roll(row, di * IMG, 1)
    full = scr[...].reshape(count * BAND_OUT, LANES)
    out_ref[...] = full.astype(bf16)
    out_t_ref[...] = full.T.astype(bf16)


def build_band(filters, codes):
    count, ks, _ = filters.shape
    return pl.pallas_call(
        band_kernel,
        out_shape=[
            jax.ShapeDtypeStruct((count * BAND_OUT, LANES), bf16),
            jax.ShapeDtypeStruct((LANES, count * BAND_OUT), bf16),
        ],
        scratch_shapes=[pltpu.VMEM((count, BAND_OUT, LANES), f32)],
        compiler_params=params(),
        cost_estimate=cost(4e7, 4e6),
        name="band",
    )(codes, filters.reshape(count, ks * ks))


VMEM = pl.BlockSpec(memory_space=pltpu.VMEM)


def pairs(count):
    step = 2 if count % 2 == 0 else 1
    return [range(i, i + step) for i in range(0, count, step)]


def beside(blocks):
    return jnp.concatenate(list(blocks), axis=1)


def pack_kernel(shift, me_ref, owner_ref, row_ref, table_ref, tails_ref, tails_t_ref, cand_ref, srow_ref):
    cap = tails_ref.shape[0]
    lines = owner_ref.shape[0]
    mine = owner_ref[...] == me_ref[0]
    mine_b = onehot(mine)
    before = onehot(iota((128, 128), 0) < iota((128, 128), 1))
    rank = mm(mine_b, before)
    totals = mm(mine_b, jnp.ones((128, 128), bf16))
    upper = onehot(iota((lines, lines), 1) < iota((lines, lines), 0))
    offset = mm(upper, totals.astype(bf16))
    key = jnp.where(mine, (rank + offset).astype(i32), -1)
    code = row_ref[...] * (1 << shift) + iota((lines, 128), 0) * 128 + iota((lines, 128), 1) + 1
    code = code.astype(f32)
    slots = iota((cap, 128), 0)
    total = jnp.zeros((cap, 128), f32)
    for r in range(lines):
        total = total + jnp.where(slots == key[r : r + 1, :], code[r : r + 1, :], 0.0)
    found = jnp.sum(total, axis=1, keepdims=True).astype(i32) - 1
    live = found >= 0
    srow = jnp.where(live, lax.shift_right_arithmetic(found, shift), -1)
    cand_ref[...] = jnp.where(live, found & ((1 << shift) - 1), -1)
    srow_ref[...] = srow
    pick = onehot(iota((cap, table_ref.shape[1]), 1) == srow)
    tails_ref[...] = mm(pick, table_ref[...], NT).astype(bf16)
    tails_t_ref[0] = mm(table_ref[...], pick, NT).astype(bf16)


def pack_tails(me, tail_owners, tail_row, table_t, cap):
    cand = tail_row.shape[0]
    shift = int(math.log2(cand))
    width, rows = table_t.shape
    assert 1 << shift == cand and cand * rows < 1 << 24 and cand % 128 == 0
    return pl.pallas_call(
        functools.partial(pack_kernel, shift),
        in_specs=[SMEM] + [VMEM] * 3,
        out_shape=[
            jax.ShapeDtypeStruct((cap, width), bf16),
            jax.ShapeDtypeStruct((1, width, cap), bf16),
            jax.ShapeDtypeStruct((cap, 1), i32),
            jax.ShapeDtypeStruct((cap, 1), i32),
        ],
        compiler_params=params(),
        cost_estimate=cost(1e9, 2e6),
        name="pack_tails",
    )(me, tail_owners.reshape(-1, 128), tail_row.reshape(-1, 128), table_t)


def found_kernel(cap, me_ref, table_ref, numbers_ref, found_ref, want_ref, scr):
    count, _, queries = numbers_ref.shape
    owners = jnp.concatenate([numbers_ref[d, 0:1, :] for d in range(count)], axis=0)
    mine = owners == me_ref[0]
    before = onehot(iota((queries, queries), 0) < iota((queries, queries), 1))
    rank = mm(onehot(mine), before)
    key = jnp.where(mine, rank.astype(i32), -1)
    slots = iota((cap, queries), 0)
    for d in range(count):
        code = (numbers_ref[d, 1:2, :] + 1).astype(f32)
        picked = jnp.where(slots == key[d : d + 1, :], code, 0.0)
        scr[d * cap : (d + 1) * cap, :] = jnp.sum(picked, axis=1, keepdims=True)
    want = scr[...].astype(i32) - 1
    want_ref[...] = want
    pick = onehot(iota((count * cap, table_ref.shape[1]), 1) == want)
    found = mm(pick, table_ref[...], NT).astype(bf16)
    for d in range(count):
        found_ref[d] = found[d * cap : (d + 1) * cap, :]


def find_heads(me, numbers, table_t, cap):
    width = table_t.shape[0]
    count = numbers.shape[0]
    return pl.pallas_call(
        functools.partial(found_kernel, cap),
        in_specs=[SMEM] + [VMEM] * 2,
        out_shape=[
            jax.ShapeDtypeStruct((count, cap, width), bf16),
            jax.ShapeDtypeStruct((count * cap, 1), i32),
        ],
        scratch_shapes=[pltpu.VMEM((count * cap, 1), f32)],
        compiler_params=params(),
        cost_estimate=cost(3e8, 2e6),
        name="find_heads",
    )(me, table_t, numbers)


def pos_kernel(cap, owner_ref, pos_ref, out_ref):
    cand = owner_ref.shape[1]
    queries = pos_ref.shape[1]
    eye = iota((queries, queries), 0) == iota((queries, queries), 1)
    step = min(512, cand)
    row = pos_ref[...].astype(f32)
    pos = jnp.sum(jnp.where(eye, row, 0.0), axis=1, keepdims=True).astype(i32)
    owner = jnp.zeros((queries, step), f32)
    for c in range(0, cand, step):
        here = iota((queries, step), 1) + c
        value = owner_ref[:, c : c + step].astype(f32)
        owner = owner + jnp.where(here == pos, value, 0.0)
    owner = jnp.sum(owner, axis=1, keepdims=True).astype(i32)
    ahead = jnp.zeros((queries, step), f32)
    for c in range(0, cand, step):
        here = iota((queries, step), 1) + c
        same = (owner_ref[:, c : c + step] == owner) & (here < pos)
        ahead = ahead + jnp.where(same, 1.0, 0.0)
    ahead = jnp.sum(ahead, axis=1, keepdims=True).astype(i32)
    out_ref[...] = owner * cap + ahead


def pos_slots(tail_owners, pos_index, cap):
    queries = pos_index.shape[0]
    return pl.pallas_call(
        functools.partial(pos_kernel, cap),
        out_shape=jax.ShapeDtypeStruct((queries, 1), i32),
        compiler_params=params(),
        cost_estimate=cost(1e7, 1e5),
        name="pos_slots",
    )(tail_owners.reshape(1, -1), pos_index.reshape(1, -1))


def slot_picks(cap, slots, orow):
    count = slots // cap
    queries = orow.shape[1]
    member = iota((count, queries), 0) == orow
    before = onehot(iota((queries, queries), 0) < iota((queries, queries), 1))
    rank = mm(onehot(member), before)
    rank = jnp.sum(jnp.where(member, rank, 0.0), axis=0, keepdims=True).astype(i32)
    return onehot(iota((slots, queries), 0) == orow * cap + rank)


def front_kernel(
    cap, fetched_ref, orow_ref, rel_ref, rtab_ref, ext_ref, band_ref, w_ref,
    pre_ref, img_ref, qv_ref, vecs_ref, feats, acc, ext,
):
    s = pl.program_id(0)
    width, queries = acc.shape

    @pl.when(s == 0)
    def _():
        rows = jnp.concatenate([fetched_ref[d] for d in range(fetched_ref.shape[0])], axis=0)
        pick = slot_picks(cap, rows.shape[0], orow_ref[...])
        hvt = mm(rows, pick, TN).astype(bf16)
        vecs_ref[0] = hvt
        rels = rtab_ref.shape[1]
        rvt = mm(rtab_ref[...], onehot(iota((rels, queries), 0) == rel_ref[...])).astype(bf16)
        entry = iota((width, ext_ref.shape[1]), 0)
        image = mm(onehot(entry == ext_ref[...]), hvt, TN)
        image = image + mm(onehot(entry + width == ext_ref[...]), rvt, TN)
        ext[...] = image.astype(bf16)
        for g in range(GROUPS):
            img_ref[:, g * queries : (g + 1) * queries] = ext[g * BAND_OUT : g * BAND_OUT + LANES, :]
        acc[...] = jnp.zeros_like(acc)

    units = band_ref.shape[0] // BAND_OUT
    flat = GROUPS * BAND_OUT
    pre = mm(band_ref[...], img_ref[...])
    act = (pre * sigmoid(pre)).astype(bf16)
    for f in range(units):
        for g in range(GROUPS):
            rows = slice(f * flat + g * BAND_OUT, f * flat + (g + 1) * BAND_OUT)
            part = slice(f * BAND_OUT, (f + 1) * BAND_OUT)
            lanes = slice(g * queries, (g + 1) * queries)
            pre_ref[rows, :] = pre[part, lanes]
            feats[rows, :] = act[part, lanes]
    acc[...] += mm(w_ref[...], feats[...])

    @pl.when(s == pl.num_programs(0) - 1)
    def _():
        query = acc[...]
        qv_ref[...] = query.T.astype(bf16)
        vecs_ref[1] = query.astype(bf16)


def filter_block(filts):
    return math.gcd(filts, 8)


def front(fetched, orow, rel_row, rtab_t, ext, band, weight_t, cap):
    queries = orow.shape[1]
    width, flat = weight_t.shape
    filts = band.shape[0] // BAND_OUT
    units = filter_block(filts)
    cols = flat // filts * units
    return pl.pallas_call(
        functools.partial(front_kernel, cap),
        grid=(filts // units,),
        in_specs=[
            whole(fetched.shape),
            whole(orow.shape),
            whole(rel_row.shape),
            whole(rtab_t.shape),
            whole(ext.shape),
            pl.BlockSpec((units * BAND_OUT, LANES), lambda s: (s, 0)),
            pl.BlockSpec((width, cols), lambda s: (0, s)),
        ],
        out_specs=[
            pl.BlockSpec((cols, queries), lambda s: (s, 0)),
            whole((LANES, GROUPS * queries)),
            whole((queries, width)),
            whole((2, width, queries)),
        ],
        out_shape=[
            jax.ShapeDtypeStruct((flat, queries), f32),
            jax.ShapeDtypeStruct((LANES, GROUPS * queries), bf16),
            jax.ShapeDtypeStruct((queries, width), bf16),
            jax.ShapeDtypeStruct((2, width, queries), bf16),
        ],
        scratch_shapes=[
            pltpu.VMEM((cols, queries), bf16),
            pltpu.VMEM((width, queries), f32),
            pltpu.VMEM((ext.shape[1], queries), bf16),
        ],
        compiler_params=params("arbitrary"),
        cost_estimate=cost(4e9, 2.4e7, 2.5e6),
        name="front",
    )(fetched, orow, rel_row, rtab_t, ext, band, weight_t)


def score_kernel(cand, pos_ref, qv_ref, tails_ref, vecs_ref, out_ref):
    qv = qv_ref[...]
    queries = qv.shape[0]
    owners, _, cap = tails_ref.shape
    total = jnp.zeros(qv.shape, f32)
    for b in range(owners):
        block = tails_ref[b]
        score = mm(qv, block)
        here = iota((queries, cap), 1) + b * cap
        target = jnp.where(here == pos_ref[...], 1.0 - smooth + smooth / cand, smooth / cand)
        grad = ((sigmoid(score) - target) * loss_weight).astype(bf16)
        total = total + mm(grad, block, NT)
    qgt = total.T.astype(bf16)
    for d in range(out_ref.shape[0]):
        out_ref[d, 0] = qgt
        out_ref[d, 1] = vecs_ref[0]
        out_ref[d, 2] = vecs_ref[1]


def score_part(qv, pos, tails, vecs, cand, copies):
    queries, width = qv.shape
    return pl.pallas_call(
        functools.partial(score_kernel, cand),
        out_shape=jax.ShapeDtypeStruct((copies, 3, width, queries), bf16),
        compiler_params=params(),
        cost_estimate=cost(1e9, 3e6, 5e5),
        name="score",
    )(pos, qv, tails, vecs)


def back_kernel(
    cap, orow_ref, ext_ref, qgt_ref, img_ref, bandt_ref, w_ref, pre_ref,
    out_ref, sums_ref, corr_ref, turned, fgrad, spread, ext,
):
    s = pl.program_id(0)
    width, queries = qgt_ref.shape[2:]

    @pl.when(s == 0)
    def _():
        spread[...] = jnp.zeros_like(spread)

    units = bandt_ref.shape[1] // BAND_OUT
    flat = GROUPS * BAND_OUT
    eye = onehot(iota((128, 128), 0) == iota((128, 128), 1))
    for c in range(0, turned.shape[0], 128):
        turned[c : c + 128, :] = mm(eye, w_ref[:, c : c + 128], NT).astype(bf16)
    linear = mm(turned[...], qgt_ref[0, 0])
    for f in range(units):
        cols = slice(f * flat, (f + 1) * flat)
        v = pre_ref[cols, :]
        sig = sigmoid(v)
        grad = (linear[cols, :] * (sig * (1.0 + v * (1.0 - sig)))).astype(bf16)
        for g in range(GROUPS):
            fgrad[f * BAND_OUT : (f + 1) * BAND_OUT, g * queries : (g + 1) * queries] = grad[
                g * BAND_OUT : (g + 1) * BAND_OUT, :
            ]
    spread[...] += mm(bandt_ref[...], fgrad[...])
    corr_ref[...] = mm(fgrad[...], img_ref[...], NT).reshape(units, BAND_OUT, LANES)

    @pl.when(s == pl.num_programs(0) - 1)
    def _():
        ext[...] = jnp.zeros_like(ext)
        for g in range(GROUPS):
            ext[g * BAND_OUT : g * BAND_OUT + LANES, :] += spread[:, g * queries : (g + 1) * queries]
        entry = iota((width, ext.shape[0]), 0)
        high, low = split(ext[...])
        hpick = onehot(entry == ext_ref[...])
        rpick = onehot(entry + width == ext_ref[...])
        hgrad = (mm(hpick, high) + mm(hpick, low)).astype(bf16)
        sums_ref[0] = mm(rpick, high) + mm(rpick, low)
        blocks = out_ref.shape[0]
        pick = slot_picks(cap, blocks * cap, orow_ref[...])
        rows = mm(pick, hgrad, NT).astype(bf16)
        for d in range(blocks):
            out_ref[d] = rows[d * cap : (d + 1) * cap, :]


def back(vecs, orow, ext, img, band_t, weight_t, pre, count, cap):
    width, queries = vecs.shape[2:]
    flat = weight_t.shape[1]
    filts = band_t.shape[1] // BAND_OUT
    units = filter_block(filts)
    cols = flat // filts * units
    assert cols % 128 == 0
    return pl.pallas_call(
        functools.partial(back_kernel, cap),
        grid=(filts // units,),
        in_specs=[
            whole(orow.shape),
            whole(ext.shape),
            whole((1, 1, width, queries)),
            whole(img.shape),
            pl.BlockSpec((LANES, units * BAND_OUT), lambda s: (0, s)),
            pl.BlockSpec((width, cols), lambda s: (0, s)),
            pl.BlockSpec((cols, queries), lambda s: (s, 0)),
        ],
        out_specs=[
            whole((count, cap, width)),
            whole((1, width, queries)),
            pl.BlockSpec((units, BAND_OUT, LANES), lambda s: (s, 0, 0)),
        ],
        out_shape=[
            jax.ShapeDtypeStruct((count, cap, width), bf16),
            jax.ShapeDtypeStruct((1, width, queries), f32),
            jax.ShapeDtypeStruct((filts, BAND_OUT, LANES), f32),
        ],
        scratch_shapes=[
            pltpu.VMEM((cols, width), bf16),
            pltpu.VMEM((units * BAND_OUT, GROUPS * queries), bf16),
            pltpu.VMEM((LANES, GROUPS * queries), f32),
            pltpu.VMEM((ext.shape[1], queries), f32),
        ],
        compiler_params=params("arbitrary"),
        cost_estimate=cost(6e9, 2e7, 2.5e6),
        name="back",
    )(orow, ext, vecs, img, band_t, weight_t, pre)


def diag_kernel(taps, codes_ref, corr_ref, out_ref):
    filts = corr_ref.shape[0]
    total = jnp.zeros((taps, filts), f32)
    for j in range(IMG):
        rows = corr_ref[:, j, :]
        for di in range(1, BAND):
            rows = rows + pltpu.roll(corr_ref[:, di * IMG + j, :], LANES - di * IMG, 1)
        pick = onehot(iota((taps, LANES), 0) == codes_ref[j : j + 1, :])
        high, low = split(rows)
        total = total + mm(pick, high, NT) + mm(pick, low, NT)
    for d in range(out_ref.shape[0]):
        out_ref[d] = total


def filter_sums(corr, codes, taps, copies):
    return pl.pallas_call(
        functools.partial(diag_kernel, taps),
        out_shape=jax.ShapeDtypeStruct((copies, taps, corr.shape[0]), f32),
        compiler_params=params(),
        cost_estimate=cost(1e8, 4e6),
        name="filter_sums",
    )(codes, corr)


def tail_kernel(
    cand, core_ref, tails_ref, mate_ref, scand_ref, mcand_ref, numbers_ref, vecs_ref, own_ref, other_ref
):
    tails = jnp.concatenate([tails_ref[...], mate_ref[...]], axis=0)
    scand = jnp.concatenate([scand_ref[...], mcand_ref[...]], axis=0)
    cap = tails_ref.shape[0]
    own = jnp.zeros(own_ref.shape, f32)
    other = jnp.zeros(own_ref.shape, f32)
    for group in pairs(vecs_ref.shape[0]):
        qvt = beside(vecs_ref[p, 2] for p in group)
        pos = beside(numbers_ref[2 * p + core_ref[0], 3:4, :] for p in group)
        score = mm(tails, qvt)
        target = jnp.where(scand == pos, 1.0 - smooth + smooth / cand, smooth / cand)
        grad = ((sigmoid(score) - target) * loss_weight).astype(bf16)
        own = own + mm(qvt, grad[:cap, :], NT)
        other = other + mm(qvt, grad[cap:, :], NT)
    own_ref[...] = own
    other_ref[...] = other


def tail_part(core, tails, mate, scand, mcand, numbers, vecs, cand):
    cap, width = tails.shape
    half = jax.ShapeDtypeStruct((width, cap), f32)
    return pl.pallas_call(
        functools.partial(tail_kernel, cand),
        in_specs=[SMEM] + [VMEM] * 6,
        out_shape=[half, half],
        compiler_params=params(),
        cost_estimate=cost(2e9, 3e6, 1e6),
        name="tail_grad",
    )(core, tails, mate, scand, mcand, numbers, vecs)


def proj_kernel(
    core_ref, rtab_ref, ext_ref, band_ref, mate_ref, numbers_ref, vecs_ref,
    own_ref, other_ref, pick, hmat, rmat,
):
    width, rels = rtab_ref.shape
    units = band_ref.shape[0] // BAND_OUT
    flat = GROUPS * BAND_OUT
    cols = units * flat
    entry = iota((width, ext_ref.shape[1]), 0)
    for part, mat in ((0, hmat), (width, rmat)):
        pick[...] = jnp.where(entry + part == ext_ref[...], 1.0, 0.0).T.astype(bf16)
        for k, source in enumerate((band_ref, mate_ref)):
            for g in range(GROUPS):
                rows = mm(source[...], pick[g * BAND_OUT : g * BAND_OUT + LANES, :]).astype(bf16)
                for f in range(units):
                    first = k * cols + f * flat + g * BAND_OUT
                    mat[first : first + BAND_OUT, :] = rows[f * BAND_OUT : (f + 1) * BAND_OUT, :]
    for k, out in enumerate((own_ref, other_ref)):
        out[...] = jnp.zeros_like(out)
    for group in pairs(vecs_ref.shape[0]):
        hvt = beside(vecs_ref[p, 1] for p in group)
        qgt = beside(vecs_ref[p, 0] for p in group)
        rel = beside(numbers_ref[2 * p + core_ref[0], 2:3, :] for p in group)
        rvt = mm(rtab_ref[...], onehot(iota((rels, rel.shape[1]), 0) == rel)).astype(bf16)
        for k, out in enumerate((own_ref, other_ref)):
            rows = slice(k * cols, (k + 1) * cols)
            pre = mm(hmat[rows, :], hvt) + mm(rmat[rows, :], rvt)
            out[...] += mm(qgt, (pre * sigmoid(pre)).astype(bf16), NT)


def proj_part(core, rtab_t, ext, band, mate, numbers, vecs):
    width = rtab_t.shape[0]
    rows = band.shape[0]
    cols = rows * GROUPS
    half = jax.ShapeDtypeStruct((width, cols), f32)
    return pl.pallas_call(
        proj_kernel,
        in_specs=[SMEM] + [VMEM] * 6,
        out_shape=[half, half],
        scratch_shapes=[
            pltpu.VMEM((ext.shape[1], width), bf16),
            pltpu.VMEM((2 * cols, width), bf16),
            pltpu.VMEM((2 * cols, width), bf16),
        ],
        compiler_params=params(),
        cost_estimate=cost(6e9, 6e6, 2.5e6),
        name="proj_grad",
    )(core, rtab_t, ext, band, mate, numbers, vecs)


def proj_columns(first, cols, filters, chequer_perm, relation_table, numbers, heads, grads):
    ks = filters.shape[-1]
    rim = ks // 2
    flat = IMG * IMG
    column = first + jnp.arange(cols, dtype=i32)
    f = column // flat
    i = (column % flat) // IMG
    j = column % IMG
    spot = jnp.arange(flat, dtype=i32)
    a = (spot[:, None] // IMG - i[None, :] + rim) % IMG
    b = (spot[:, None] % IMG - j[None, :] + rim) % IMG
    tap = filters[f[None, :], jnp.minimum(a, ks - 1), jnp.minimum(b, ks - 1)]
    matrix = jnp.where((a < ks) & (b < ks), tap, jnp.zeros((), bf16))
    width = heads.shape[1]
    head = heads.transpose(0, 2, 1).reshape(-1, width)
    qg = grads.transpose(0, 2, 1).reshape(-1, width)
    joined = jnp.concatenate([head, relation_table[numbers[:, 2].reshape(-1)]], axis=1)
    pre = mm(joined[:, chequer_perm], matrix)
    return mm(qg, (pre * sigmoid(pre)).astype(bf16), TN)


def rel_kernel(numbers_ref, sums_ref, filt_ref, rel_ref, out_ref):
    total = jnp.zeros(rel_ref.shape, f32)
    for group in pairs(sums_ref.shape[0]):
        rel = beside(numbers_ref[p, 2:3, :] for p in group)
        pick = onehot(iota((rel_ref.shape[1], rel.shape[1]), 0) == rel)
        high, low = split(beside(sums_ref[p] for p in group))
        total = total + mm(high, pick, NT) + mm(low, pick, NT)
    rel_ref[...] = total
    filt = filt_ref[0]
    for d in range(1, filt_ref.shape[0]):
        filt = filt + filt_ref[d]
    out_ref[...] = filt


def rel_part(numbers, sums, filt, rels):
    return pl.pallas_call(
        rel_kernel,
        out_shape=[
            jax.ShapeDtypeStruct((sums.shape[1], rels), f32),
            jax.ShapeDtypeStruct(filt.shape[1:], f32),
        ],
        compiler_params=params(),
        cost_estimate=cost(2e9, 3e6),
        name="rel_grad",
    )(numbers, sums, filt)


def entity_kernel(want_ref, srow_ref, own_ref, recv_ref, incoming_ref, out_ref):
    rows = out_ref.shape[1]
    grads = jnp.concatenate([incoming_ref[d] for d in range(incoming_ref.shape[0])], axis=0)
    total = mm(grads, onehot(iota((want_ref.shape[0], rows), 1) == want_ref[...]), TN)
    pick = onehot(iota((srow_ref.shape[0], rows), 1) == srow_ref[...])
    high, low = split(own_ref[...] + recv_ref[...])
    out_ref[...] = total + mm(high, pick) + mm(low, pick)


def entity_sum(want, srow, own, recv, incoming, rows):
    return pl.pallas_call(
        entity_kernel,
        out_shape=jax.ShapeDtypeStruct((own.shape[0], rows), f32),
        compiler_params=params(),
        cost_estimate=cost(1.5e9, 4e6),
        name="entity_grad",
    )(want, srow, own, recv, incoming)


def shards(
    entity_table,
    relation_table,
    filters,
    proj_weight,
    chequer_perm,
    head_owner,
    head_row,
    rel_ids,
    pos_index,
    tail_owner,
    tail_row,
):
    count = lax.axis_size("shard")
    me = lax.axis_index("shard")
    assert count % 2 == 0
    direct = count <= 16
    queries = head_row.shape[0]
    cand = tail_row.shape[0]
    rows, width = entity_table.shape
    rels = relation_table.shape[0]
    filts, ks, _ = filters.shape
    head_cap = 2 * queries // count
    tail_cap = 2 * cand // count
    same_core = [list(range(c, count, 2)) for c in range(2)]
    copies = count // 2 if direct else 1

    def swap(x):
        return lax.ppermute(x, "shard", [(d, d ^ 1) for d in range(count)])

    def exchange(x):
        return lax.all_to_all(x, "shard", split_axis=0, concat_axis=0, tiled=True)

    def gather_core(x):
        if direct:
            return lax.all_to_all(
                x, "shard", split_axis=0, concat_axis=0, axis_index_groups=same_core, tiled=True
            )
        return lax.all_gather(x, "shard", axis=0, axis_index_groups=same_core, tiled=True)

    me1 = me.reshape(1)
    core = (me & 1).reshape(1)
    heads = head_owner[:, 0]
    tail_owners = tail_owner[:, 0]
    table_t, rtab_t, weight_t = entity_table.T, relation_table.T, proj_weight.T
    numbers = jnp.stack([heads, head_row, rel_ids, pos_index])[None]
    numbers = exchange(jnp.broadcast_to(numbers, (count,) + numbers.shape[1:]))

    tails, tails_t, slot_cand, slot_row = pack_tails(me1, tail_owners, tail_row, table_t, tail_cap)
    all_tails = lax.all_gather(tails_t, "shard", axis=0, tiled=True)
    mate_tails, mate_cand = swap(tails), swap(slot_cand)
    found, want = find_heads(me1, numbers, table_t, head_cap)
    fetched = exchange(found)
    pos = pos_slots(tail_owners, pos_index, tail_cap)

    codes = jnp.asarray(band_codes(ks))
    band, band_t = build_band(filters, codes)
    extra = BAND_OUT * (GROUPS - 1) + LANES - IMG * IMG - BAND_OUT
    ext = jnp.concatenate([chequer_perm[-BAND_OUT:], chequer_perm, chequer_perm[:extra]])[None]
    orow = heads[None, :]
    pre, img, qv, vecs = front(
        fetched, orow, rel_ids[None, :], rtab_t, ext, band, weight_t, head_cap
    )

    vecs = score_part(qv, pos, all_tails, vecs, cand, copies)
    core_vecs = gather_core(vecs)
    outgoing, sums, corr = back(vecs, orow, ext, img, band_t, weight_t, pre, count, head_cap)
    all_sums = lax.all_gather(sums, "shard", axis=0, tiled=True)
    incoming = exchange(outgoing)
    filt = exchange(filter_sums(corr, codes, ks * ks, count))

    own, other = tail_part(core, tails, mate_tails, slot_cand, mate_cand, numbers, core_vecs, cand)
    entity_grad = entity_sum(want, slot_row, own, swap(other), incoming, rows).T

    cols = filts * IMG * IMG // count
    if direct and cols % (IMG * IMG) == 0:
        unit = cols // (IMG * IMG) * BAND_OUT
        mine, mate = (
            lax.dynamic_slice_in_dim(band, d * unit, unit, axis=0) for d in (me, me ^ 1)
        )
        own, other = proj_part(core, rtab_t, ext, mine, mate, numbers, core_vecs)
    else:
        own, other = (
            proj_columns(
                d * cols, cols, filters, chequer_perm, relation_table,
                lax.dynamic_index_in_dim(
                    numbers.reshape(count // 2, 2, 4, queries), me & 1, 1, keepdims=False
                ),
                core_vecs[:, 1], core_vecs[:, 0],
            )
            for d in (me, me ^ 1)
        )
    proj_grad = (own + swap(other)).T

    relation_grad, filter_grad = rel_part(numbers, all_sums, filt, rels)
    filter_grad = filter_grad.T.reshape(filts, ks, ks)
    return (entity_grad, relation_grad.T, filter_grad, proj_grad)


def solution(mesh):
    placed = (
        P("shard", None),
        P(),
        P(),
        P(),
        P(),
        P(("parts", "shard"), None),
        P(("parts", "shard")),
        P(("parts", "shard")),
        P(("parts", "shard")),
        P("parts", None),
        P("parts"),
    )
    return jax.shard_map(
        shards,
        mesh=mesh,
        in_specs=placed,
        out_specs=(
            P(("parts", "shard"), None),
            P("parts", None),
            P("parts", None, None),
            P(("parts", "shard"), None),
        ),
        check_vma=False,
    )
```

```python
import functools
import math

import jax
import jax.numpy as jnp
import numpy as np
from jax import lax
from jax.experimental import pallas as pl
from jax.experimental.pallas import tpu as pltpu
from jax.sharding import PartitionSpec as P

IMG = 20
BAND = 4
GROUPS = IMG // BAND
BAND_OUT = BAND * IMG
LANES = 256

loss_weight = 0.015625
smooth = 0.1

f32 = jnp.float32
bf16 = jnp.bfloat16
i32 = jnp.int32

NN = (((1,), (0,)), ((), ()))
NT = (((1,), (1,)), ((), ()))
TN = (((0,), (0,)), ((), ()))


def mm(a, b, dims=NN):
    return lax.dot_general(a, b, dims, preferred_element_type=f32)


def iota(shape, axis):
    return lax.broadcasted_iota(i32, shape, axis)


def onehot(mask):
    return jnp.where(mask, 1.0, 0.0).astype(bf16)


def split(value):
    high = value.astype(bf16)
    return high, (value - high.astype(f32)).astype(bf16)


def sigmoid(v):
    return 0.5 * jnp.tanh(0.5 * v) + 0.5


def params(*semantics):
    return pltpu.CompilerParams(
        dimension_semantics=semantics or None, vmem_limit_bytes=60 << 20
    )


def cost(flops, nbytes, trans=0):
    return pl.CostEstimate(flops=int(flops), bytes_accessed=int(nbytes), transcendentals=int(trans))


def whole(shape):
    return pl.BlockSpec(shape, lambda *_: (0,) * len(shape))


SMEM = pl.BlockSpec(memory_space=pltpu.SMEM)


def band_codes(ks):
    codes = np.full((IMG, LANES), -1, np.int32)
    for j in range(IMG):
        for r in range(ks):
            for x in range(IMG):
                b = (x - j + ks // 2) % IMG
                if b < ks:
                    codes[j, r * IMG + x] = r * ks + b
    return codes


def band_kernel(codes_ref, filt_ref, out_ref, out_t_ref, scr):
    count, taps = filt_ref.shape
    filt = filt_ref[...]
    for j in range(IMG):
        pick = onehot(iota((taps, LANES), 0) == codes_ref[j : j + 1, :])
        row = mm(filt, pick)
        for di in range(BAND):
            scr[:, di * IMG + j, :] = row if di == 0 else pltpu.roll(row, di * IMG, 1)
    full = scr[...].reshape(count * BAND_OUT, LANES)
    out_ref[...] = full.astype(bf16)
    out_t_ref[...] = full.T.astype(bf16)


def build_band(filters, codes):
    count, ks, _ = filters.shape
    return pl.pallas_call(
        band_kernel,
        out_shape=[
            jax.ShapeDtypeStruct((count * BAND_OUT, LANES), bf16),
            jax.ShapeDtypeStruct((LANES, count * BAND_OUT), bf16),
        ],
        scratch_shapes=[pltpu.VMEM((count, BAND_OUT, LANES), f32)],
        compiler_params=params(),
        cost_estimate=cost(4e7, 4e6),
        name="band",
    )(codes, filters.reshape(count, ks * ks))


VMEM = pl.BlockSpec(memory_space=pltpu.VMEM)


def pairs(count):
    step = 2 if count % 2 == 0 else 1
    return [range(i, i + step) for i in range(0, count, step)]


def beside(blocks):
    return jnp.concatenate(list(blocks), axis=1)


def slot_values(owner, device, value, cap):
    lines = owner.shape[0]
    mine = owner == device
    mine_b = onehot(mine)
    before = onehot(iota((128, 128), 0) < iota((128, 128), 1))
    rank = mm(mine_b, before)
    totals = mm(mine_b, jnp.ones((128, 128), bf16))
    upper = onehot(iota((lines, lines), 1) < iota((lines, lines), 0))
    offset = mm(upper, totals.astype(bf16))
    key = jnp.where(mine, (rank + offset).astype(i32), -1)
    value = (value + 1).astype(f32)
    slots = iota((cap, 128), 0)
    total = jnp.zeros((cap, 128), f32)
    for r in range(lines):
        total = total + jnp.where(slots == key[r : r + 1, :], value[r : r + 1, :], 0.0)
    return jnp.sum(total, axis=1, keepdims=True).astype(i32) - 1


def pack_kernel(me_ref, owner_ref, row_ref, table_ref, tails_t_ref, srow_ref):
    cap = srow_ref.shape[0]
    srow = slot_values(owner_ref[...], me_ref[0], row_ref[...], cap)
    srow_ref[...] = srow
    pick = onehot(iota((cap, table_ref.shape[1]), 1) == srow)
    tails_t_ref[0] = mm(table_ref[...], pick, NT).astype(bf16)


def pack_tails(me, tail_owners, tail_row, table_t, cap):
    assert tail_row.shape[0] % 128 == 0
    return pl.pallas_call(
        pack_kernel,
        in_specs=[SMEM] + [VMEM] * 3,
        out_shape=[
            jax.ShapeDtypeStruct((1, table_t.shape[0], cap), bf16),
            jax.ShapeDtypeStruct((cap, 1), i32),
        ],
        compiler_params=params(),
        cost_estimate=cost(1e9, 2e6),
        name="pack_tails",
    )(me, tail_owners.reshape(-1, 128), tail_row.reshape(-1, 128), table_t)


def cand_kernel(me_ref, owner_ref, out_ref):
    cap = out_ref.shape[1]
    owner = owner_ref[...]
    index = iota(owner.shape, 0) * 128 + iota(owner.shape, 1)
    for k in range(2):
        out_ref[k] = slot_values(owner, me_ref[0] ^ k, index, cap)


def slot_cands(me, tail_owners, cap):
    return pl.pallas_call(
        cand_kernel,
        in_specs=[SMEM, VMEM],
        out_shape=jax.ShapeDtypeStruct((2, cap, 1), i32),
        compiler_params=params(),
        cost_estimate=cost(1e8, 1e6),
        name="slot_cands",
    )(me, tail_owners.reshape(-1, 128))


def found_kernel(cap, me_ref, table_ref, numbers_ref, found_ref, want_ref, scr):
    count, _, queries = numbers_ref.shape
    owners = jnp.concatenate([numbers_ref[d, 0:1, :] for d in range(count)], axis=0)
    mine = owners == me_ref[0]
    before = onehot(iota((queries, queries), 0) < iota((queries, queries), 1))
    rank = mm(onehot(mine), before)
    key = jnp.where(mine, rank.astype(i32), -1)
    slots = iota((cap, queries), 0)
    for d in range(count):
        code = (numbers_ref[d, 1:2, :] + 1).astype(f32)
        picked = jnp.where(slots == key[d : d + 1, :], code, 0.0)
        scr[d * cap : (d + 1) * cap, :] = jnp.sum(picked, axis=1, keepdims=True)
    want = scr[...].astype(i32) - 1
    want_ref[...] = want
    pick = onehot(iota((count * cap, table_ref.shape[1]), 1) == want)
    found = mm(pick, table_ref[...], NT).astype(bf16)
    for d in range(count):
        found_ref[d] = found[d * cap : (d + 1) * cap, :]


def find_heads(me, numbers, table_t, cap):
    width = table_t.shape[0]
    count = numbers.shape[0]
    return pl.pallas_call(
        functools.partial(found_kernel, cap),
        in_specs=[SMEM] + [VMEM] * 2,
        out_shape=[
            jax.ShapeDtypeStruct((count, cap, width), bf16),
            jax.ShapeDtypeStruct((count * cap, 1), i32),
        ],
        scratch_shapes=[pltpu.VMEM((count * cap, 1), f32)],
        compiler_params=params(),
        cost_estimate=cost(3e8, 2e6),
        name="find_heads",
    )(me, table_t, numbers)


def pos_kernel(cap, owner_ref, pos_ref, out_ref):
    cand = owner_ref.shape[1]
    queries = pos_ref.shape[1]
    eye = iota((queries, queries), 0) == iota((queries, queries), 1)
    step = min(512, cand)
    row = pos_ref[...].astype(f32)
    pos = jnp.sum(jnp.where(eye, row, 0.0), axis=1, keepdims=True).astype(i32)
    owner = jnp.zeros((queries, step), f32)
    for c in range(0, cand, step):
        here = iota((queries, step), 1) + c
        value = owner_ref[:, c : c + step].astype(f32)
        owner = owner + jnp.where(here == pos, value, 0.0)
    owner = jnp.sum(owner, axis=1, keepdims=True).astype(i32)
    ahead = jnp.zeros((queries, step), f32)
    for c in range(0, cand, step):
        here = iota((queries, step), 1) + c
        same = (owner_ref[:, c : c + step] == owner) & (here < pos)
        ahead = ahead + jnp.where(same, 1.0, 0.0)
    ahead = jnp.sum(ahead, axis=1, keepdims=True).astype(i32)
    out_ref[...] = owner * cap + ahead


def pos_slots(tail_owners, pos_index, cap):
    queries = pos_index.shape[0]
    return pl.pallas_call(
        functools.partial(pos_kernel, cap),
        out_shape=jax.ShapeDtypeStruct((queries, 1), i32),
        compiler_params=params(),
        cost_estimate=cost(1e7, 1e5),
        name="pos_slots",
    )(tail_owners.reshape(1, -1), pos_index.reshape(1, -1))


def slot_picks(cap, slots, orow):
    count = slots // cap
    queries = orow.shape[1]
    member = iota((count, queries), 0) == orow
    before = onehot(iota((queries, queries), 0) < iota((queries, queries), 1))
    rank = mm(onehot(member), before)
    rank = jnp.sum(jnp.where(member, rank, 0.0), axis=0, keepdims=True).astype(i32)
    return onehot(iota((slots, queries), 0) == orow * cap + rank)


def front_kernel(
    cap, fetched_ref, orow_ref, rel_ref, rtab_ref, ext_ref, band_ref, w_ref,
    slope_ref, turned_ref, img_ref, qv_ref, vecs_ref, feats, acc, ext,
):
    s = pl.program_id(0)
    width, queries = acc.shape

    @pl.when(s == 0)
    def _():
        rows = jnp.concatenate([fetched_ref[d] for d in range(fetched_ref.shape[0])], axis=0)
        pick = slot_picks(cap, rows.shape[0], orow_ref[...])
        hvt = mm(rows, pick, TN).astype(bf16)
        for d in range(vecs_ref.shape[0]):
            vecs_ref[d, 0] = hvt
        rels = rtab_ref.shape[1]
        rvt = mm(rtab_ref[...], onehot(iota((rels, queries), 0) == rel_ref[...])).astype(bf16)
        entry = iota((width, ext_ref.shape[1]), 0)
        image = mm(onehot(entry == ext_ref[...]), hvt, TN)
        image = image + mm(onehot(entry + width == ext_ref[...]), rvt, TN)
        ext[...] = image.astype(bf16)
        for g in range(GROUPS):
            img_ref[:, g * queries : (g + 1) * queries] = ext[g * BAND_OUT : g * BAND_OUT + LANES, :]
        acc[...] = jnp.zeros_like(acc)

    units = band_ref.shape[0] // BAND_OUT
    flat = GROUPS * BAND_OUT
    pre = mm(band_ref[...], img_ref[...])
    sig = sigmoid(pre)
    act = (pre * sig).astype(bf16)
    slope = sig * (1.0 + pre * (1.0 - sig))
    for f in range(units):
        for g in range(GROUPS):
            rows = slice(f * flat + g * BAND_OUT, f * flat + (g + 1) * BAND_OUT)
            part = slice(f * BAND_OUT, (f + 1) * BAND_OUT)
            lanes = slice(g * queries, (g + 1) * queries)
            slope_ref[rows, :] = slope[part, lanes]
            feats[rows, :] = act[part, lanes]
    acc[...] += mm(w_ref[...], feats[...])
    eye = onehot(iota((128, 128), 0) == iota((128, 128), 1))
    for c in range(0, turned_ref.shape[0], 128):
        turned_ref[c : c + 128, :] = mm(eye, w_ref[:, c : c + 128], NT).astype(bf16)

    @pl.when(s == pl.num_programs(0) - 1)
    def _():
        query = acc[...]
        qv_ref[...] = query.T.astype(bf16)
        qvt = query.astype(bf16)
        for d in range(vecs_ref.shape[0]):
            vecs_ref[d, 1] = qvt


def filter_block(filts):
    return math.gcd(filts, 8)


def front(fetched, orow, rel_row, rtab_t, ext, band, weight_t, cap, copies):
    queries = orow.shape[1]
    width, flat = weight_t.shape
    filts = band.shape[0] // BAND_OUT
    units = filter_block(filts)
    cols = flat // filts * units
    assert cols % 128 == 0
    return pl.pallas_call(
        functools.partial(front_kernel, cap),
        grid=(filts // units,),
        in_specs=[
            whole(fetched.shape),
            whole(orow.shape),
            whole(rel_row.shape),
            whole(rtab_t.shape),
            whole(ext.shape),
            pl.BlockSpec((units * BAND_OUT, LANES), lambda s: (s, 0)),
            pl.BlockSpec((width, cols), lambda s: (0, s)),
        ],
        out_specs=[
            pl.BlockSpec((cols, queries), lambda s: (s, 0)),
            pl.BlockSpec((cols, width), lambda s: (s, 0)),
            whole((LANES, GROUPS * queries)),
            whole((queries, width)),
            whole((copies, 2, width, queries)),
        ],
        out_shape=[
            jax.ShapeDtypeStruct((flat, queries), f32),
            jax.ShapeDtypeStruct((flat, width), bf16),
            jax.ShapeDtypeStruct((LANES, GROUPS * queries), bf16),
            jax.ShapeDtypeStruct((queries, width), bf16),
            jax.ShapeDtypeStruct((copies, 2, width, queries), bf16),
        ],
        scratch_shapes=[
            pltpu.VMEM((cols, queries), bf16),
            pltpu.VMEM((width, queries), f32),
            pltpu.VMEM((ext.shape[1], queries), bf16),
        ],
        compiler_params=params("arbitrary"),
        cost_estimate=cost(4e9, 2.4e7, 2.5e6),
        name="front",
    )(fetched, orow, rel_row, rtab_t, ext, band, weight_t)


def score_kernel(cand, pos_ref, qv_ref, tails_ref, out_ref, acc):
    step = pl.program_id(0)

    @pl.when(step == 0)
    def _():
        acc[...] = jnp.zeros_like(acc)

    qv = qv_ref[...]
    queries = qv.shape[0]
    blocks, _, cap = tails_ref.shape
    total = acc[...]
    for b in range(blocks):
        block = tails_ref[b]
        score = mm(qv, block)
        here = iota((queries, cap), 1) + (step * blocks + b) * cap
        target = jnp.where(here == pos_ref[...], 1.0 - smooth + smooth / cand, smooth / cand)
        grad = ((sigmoid(score) - target) * loss_weight).astype(bf16)
        total = total + mm(grad, block, NT)
    acc[...] = total

    @pl.when(step == pl.num_programs(0) - 1)
    def _():
        out_ref[0] = total.T.astype(bf16)


def score_part(qv, pos, tails, cand):
    queries, width = qv.shape
    owners, _, cap = tails.shape
    blocks = math.gcd(owners, max(1, 2048 // cap))
    return pl.pallas_call(
        functools.partial(score_kernel, cand),
        grid=(owners // blocks,),
        in_specs=[
            whole(pos.shape),
            whole(qv.shape),
            pl.BlockSpec((blocks, width, cap), lambda s: (s, 0, 0)),
        ],
        out_specs=whole((1, width, queries)),
        out_shape=jax.ShapeDtypeStruct((1, width, queries), bf16),
        scratch_shapes=[pltpu.VMEM((queries, width), f32)],
        compiler_params=params("arbitrary"),
        cost_estimate=cost(1e9, 3e6, 5e5),
        name="score",
    )(pos, qv, tails)


def back_kernel(
    cap, orow_ref, ext_ref, qgt_ref, img_ref, bandt_ref, w_ref, slope_ref,
    out_ref, sums_ref, corr_ref, fgrad, spread, ext,
):
    s = pl.program_id(0)
    _, width, queries = qgt_ref.shape

    @pl.when(s == 0)
    def _():
        spread[...] = jnp.zeros_like(spread)

    units = bandt_ref.shape[1] // BAND_OUT
    flat = GROUPS * BAND_OUT
    qgt = qgt_ref[0]
    for f in range(units):
        cols = slice(f * flat, (f + 1) * flat)
        grad = (mm(w_ref[cols, :], qgt) * slope_ref[cols, :]).astype(bf16)
        for g in range(GROUPS):
            fgrad[f * BAND_OUT : (f + 1) * BAND_OUT, g * queries : (g + 1) * queries] = grad[
                g * BAND_OUT : (g + 1) * BAND_OUT, :
            ]
    spread[...] += mm(bandt_ref[...], fgrad[...])
    corr_ref[...] = mm(fgrad[...], img_ref[...], NT).reshape(units, BAND_OUT, LANES)

    @pl.when(s == pl.num_programs(0) - 1)
    def _():
        ext[...] = jnp.zeros_like(ext)
        for g in range(GROUPS):
            ext[g * BAND_OUT : g * BAND_OUT + LANES, :] += spread[:, g * queries : (g + 1) * queries]
        entry = iota((width, ext.shape[0]), 0)
        high, low = split(ext[...])
        hpick = onehot(entry == ext_ref[...])
        rpick = onehot(entry + width == ext_ref[...])
        hgrad = (mm(hpick, high) + mm(hpick, low)).astype(bf16)
        rgrad = mm(rpick, high) + mm(rpick, low)
        for d in range(sums_ref.shape[0]):
            sums_ref[d] = rgrad
        blocks = out_ref.shape[0]
        pick = slot_picks(cap, blocks * cap, orow_ref[...])
        rows = mm(pick, hgrad, NT).astype(bf16)
        for d in range(blocks):
            out_ref[d] = rows[d * cap : (d + 1) * cap, :]


def back(qgt, orow, ext, img, band_t, weight, slope, count, cap, copies):
    _, width, queries = qgt.shape
    flat = weight.shape[0]
    filts = band_t.shape[1] // BAND_OUT
    units = filter_block(filts)
    cols = flat // filts * units
    return pl.pallas_call(
        functools.partial(back_kernel, cap),
        grid=(filts // units,),
        in_specs=[
            whole(orow.shape),
            whole(ext.shape),
            whole(qgt.shape),
            whole(img.shape),
            pl.BlockSpec((LANES, units * BAND_OUT), lambda s: (0, s)),
            pl.BlockSpec((cols, width), lambda s: (s, 0)),
            pl.BlockSpec((cols, queries), lambda s: (s, 0)),
        ],
        out_specs=[
            whole((count, cap, width)),
            whole((copies, width, queries)),
            pl.BlockSpec((units, BAND_OUT, LANES), lambda s: (s, 0, 0)),
        ],
        out_shape=[
            jax.ShapeDtypeStruct((count, cap, width), bf16),
            jax.ShapeDtypeStruct((copies, width, queries), f32),
            jax.ShapeDtypeStruct((filts, BAND_OUT, LANES), f32),
        ],
        scratch_shapes=[
            pltpu.VMEM((units * BAND_OUT, GROUPS * queries), bf16),
            pltpu.VMEM((LANES, GROUPS * queries), f32),
            pltpu.VMEM((ext.shape[1], queries), f32),
        ],
        compiler_params=params("arbitrary"),
        cost_estimate=cost(6e9, 2e7, 2.5e6),
        name="back",
    )(orow, ext, qgt, img, band_t, weight, slope)


def half_taps(taps):
    return -(-taps // 32) * 16


def diag_kernel(taps, codes_ref, corr_ref, rows_ref, out_ref):
    filts = corr_ref.shape[0]
    cap, width = rows_ref.shape[1:]
    half = half_taps(taps)
    total = jnp.zeros((2 * half, filts), f32)
    for j in range(IMG):
        rows = corr_ref[:, j, :]
        for di in range(1, BAND):
            rows = rows + pltpu.roll(corr_ref[:, di * IMG + j, :], LANES - di * IMG, 1)
        pick = onehot(iota((2 * half, LANES), 0) == codes_ref[j : j + 1, :])
        high, low = split(rows)
        total = total + mm(pick, high, NT) + mm(pick, low, NT)
    packed = jnp.zeros((half, width), f32)
    for k in range(2):
        for i, piece in enumerate(split(total[k * half : (k + 1) * half, :])):
            place = onehot(iota((filts, width), 1) == iota((filts, width), 0) + (2 * k + i) * filts)
            packed = packed + mm(piece, place)
    packed = packed.astype(bf16)
    for d in range(out_ref.shape[0]):
        out_ref[d, :cap, :] = rows_ref[d]
        out_ref[d, cap:, :] = packed


def filter_sums(corr, codes, rows, taps):
    count, cap, width = rows.shape
    assert 4 * corr.shape[0] <= width
    return pl.pallas_call(
        functools.partial(diag_kernel, taps),
        out_shape=jax.ShapeDtypeStruct((count, cap + half_taps(taps), width), bf16),
        compiler_params=params(),
        cost_estimate=cost(1e8, 4e6),
        name="filter_sums",
    )(codes, corr, rows)


def tail_kernel(cand, ids_ref, tails_ref, mate_ref, scand_ref, numbers_ref, vecs_ref, own_ref, other_ref):
    cap = own_ref.shape[1]
    tails = jnp.concatenate([ref[0].astype(f32).T for ref in (tails_ref, mate_ref)], axis=0).astype(bf16)
    scand = jnp.concatenate([scand_ref[0], scand_ref[1]], axis=0)
    own = jnp.zeros(own_ref.shape, f32)
    other = jnp.zeros(own_ref.shape, f32)
    for group in pairs(vecs_ref.shape[0]):
        qvt = beside(vecs_ref[p, 1] for p in group)
        pos = beside(numbers_ref[2 * p + ids_ref[2], 3:4, :] for p in group)
        score = mm(tails, qvt)
        target = jnp.where(scand == pos, 1.0 - smooth + smooth / cand, smooth / cand)
        grad = ((sigmoid(score) - target) * loss_weight).astype(bf16)
        own = own + mm(qvt, grad[:cap, :], NT)
        other = other + mm(qvt, grad[cap:, :], NT)
    own_ref[...] = own
    other_ref[...] = other


def tail_part(ids, tails, scand, numbers, vecs, cand):
    _, width, cap = tails.shape
    half = jax.ShapeDtypeStruct((width, cap), f32)
    return pl.pallas_call(
        functools.partial(tail_kernel, cand),
        grid_spec=pltpu.PrefetchScalarGridSpec(
            num_scalar_prefetch=1,
            grid=(1,),
            in_specs=[
                pl.BlockSpec((1, width, cap), lambda s, ids: (ids[0], 0, 0)),
                pl.BlockSpec((1, width, cap), lambda s, ids: (ids[1], 0, 0)),
                whole(scand.shape),
                whole(numbers.shape),
                whole(vecs.shape),
            ],
            out_specs=[whole(half.shape)] * 2,
        ),
        out_shape=[half, half],
        compiler_params=params("arbitrary"),
        cost_estimate=cost(2e9, 3e6, 1e6),
        name="tail_grad",
    )(ids, tails, tails, scand, numbers, vecs)


def feats_kernel(
    ids_ref, rtab_ref, ext_ref, band_ref, mate_ref, numbers_ref, vecs_ref, out_ref, pick, hmat, rmat
):
    width, rels = rtab_ref.shape
    units = band_ref.shape[0] // BAND_OUT
    flat = GROUPS * BAND_OUT
    cols = units * flat
    entry = iota((width, ext_ref.shape[1]), 0)
    for part, mat in ((0, hmat), (width, rmat)):
        pick[...] = jnp.where(entry + part == ext_ref[...], 1.0, 0.0).T.astype(bf16)
        for k, source in enumerate((band_ref, mate_ref)):
            for g in range(GROUPS):
                rows = mm(source[...], pick[g * BAND_OUT : g * BAND_OUT + LANES, :]).astype(bf16)
                for f in range(units):
                    first = k * cols + f * flat + g * BAND_OUT
                    mat[first : first + BAND_OUT, :] = rows[f * BAND_OUT : (f + 1) * BAND_OUT, :]
    queries = vecs_ref.shape[3]
    for group in pairs(vecs_ref.shape[0]):
        hvt = beside(vecs_ref[p, 0] for p in group)
        rel = beside(numbers_ref[2 * p + ids_ref[2], 2:3, :] for p in group)
        rvt = mm(rtab_ref[...], onehot(iota((rels, rel.shape[1]), 0) == rel)).astype(bf16)
        lanes = slice(group[0] * queries, (group[-1] + 1) * queries)
        for k in range(2):
            rows = slice(k * cols, (k + 1) * cols)
            pre = mm(hmat[rows, :], hvt) + mm(rmat[rows, :], rvt)
            out_ref[rows, lanes] = (pre * sigmoid(pre)).astype(bf16)


def column_feats(ids, rtab_t, ext, band, numbers, vecs, cols):
    width = rtab_t.shape[0]
    unit = cols // GROUPS
    gathered, _, _, queries = vecs.shape
    return pl.pallas_call(
        feats_kernel,
        grid_spec=pltpu.PrefetchScalarGridSpec(
            num_scalar_prefetch=1,
            grid=(1,),
            in_specs=[
                whole(rtab_t.shape),
                whole(ext.shape),
                pl.BlockSpec((unit, LANES), lambda s, ids: (ids[0], 0)),
                pl.BlockSpec((unit, LANES), lambda s, ids: (ids[1], 0)),
                whole(numbers.shape),
                whole(vecs.shape),
            ],
            out_specs=whole((2 * cols, gathered * queries)),
            scratch_shapes=[
                pltpu.VMEM((ext.shape[1], width), bf16),
                pltpu.VMEM((2 * cols, width), bf16),
                pltpu.VMEM((2 * cols, width), bf16),
            ],
        ),
        out_shape=jax.ShapeDtypeStruct((2 * cols, gathered * queries), bf16),
        compiler_params=params("arbitrary"),
        cost_estimate=cost(6e9, 6e6, 2.5e6),
        name="column_feats",
    )(ids, rtab_t, ext, band, band, numbers, vecs)


def proj_kernel(core_ref, feats_ref, grads_ref, own_ref, other_ref):
    count = grads_ref.shape[0]
    cols = own_ref.shape[1]
    qgt = beside(grads_ref[2 * p + core_ref[0]] for p in range(count // 2))
    own_ref[...] = mm(qgt, feats_ref[:cols, :], NT)
    other_ref[...] = mm(qgt, feats_ref[cols:, :], NT)


def proj_part(core, feats, grads):
    half = jax.ShapeDtypeStruct((grads.shape[1], feats.shape[0] // 2), f32)
    return pl.pallas_call(
        proj_kernel,
        in_specs=[SMEM] + [VMEM] * 2,
        out_shape=[half, half],
        compiler_params=params(),
        cost_estimate=cost(1e9, 8e6),
        name="proj_grad",
    )(core, feats, grads)


def proj_columns(first, cols, filters, chequer_perm, relation_table, numbers, heads, grads):
    ks = filters.shape[-1]
    rim = ks // 2
    flat = IMG * IMG
    column = first + jnp.arange(cols, dtype=i32)
    f = column // flat
    i = (column % flat) // IMG
    j = column % IMG
    spot = jnp.arange(flat, dtype=i32)
    a = (spot[:, None] // IMG - i[None, :] + rim) % IMG
    b = (spot[:, None] % IMG - j[None, :] + rim) % IMG
    tap = filters[f[None, :], jnp.minimum(a, ks - 1), jnp.minimum(b, ks - 1)]
    matrix = jnp.where((a < ks) & (b < ks), tap, jnp.zeros((), bf16))
    width = heads.shape[1]
    head = heads.transpose(0, 2, 1).reshape(-1, width)
    qg = grads.transpose(0, 2, 1).reshape(-1, width)
    joined = jnp.concatenate([head, relation_table[numbers[:, 2].reshape(-1)]], axis=1)
    pre = mm(joined[:, chequer_perm], matrix)
    return mm(qg, (pre * sigmoid(pre)).astype(bf16), TN)


def rel_kernel(core_ref, numbers_ref, sums_ref, rel_ref):
    width, rels = rel_ref.shape
    total = jnp.zeros((2 * width, rels), f32)
    for group in pairs(sums_ref.shape[0]):
        rel = beside(numbers_ref[2 * p + core_ref[0], 2:3, :] for p in group)
        pick = onehot(iota((rels, rel.shape[1]), 0) == rel)
        parts = jnp.concatenate(split(beside(sums_ref[p] for p in group)), axis=0)
        total = total + mm(parts, pick, NT)
    rel_ref[...] = total[:width, :] + total[width:, :]


def rel_part(core, numbers, sums, rels):
    return pl.pallas_call(
        rel_kernel,
        in_specs=[SMEM] + [VMEM] * 2,
        out_shape=jax.ShapeDtypeStruct((sums.shape[1], rels), f32),
        compiler_params=params(),
        cost_estimate=cost(2e9, 3e6),
        name="rel_grad",
    )(core, numbers, sums)


def entity_kernel(cap, want_ref, srow_ref, own_ref, recv_ref, incoming_ref, out_ref, filt_ref):
    rows = out_ref.shape[1]
    count, _, width = incoming_ref.shape
    half, filts = filt_ref.shape[0] // 2, filt_ref.shape[1]
    grads = jnp.concatenate([incoming_ref[d, :cap, :] for d in range(count)], axis=0)
    total = mm(grads, onehot(iota((want_ref.shape[0], rows), 1) == want_ref[...]), TN)
    pick = onehot(iota((srow_ref.shape[0], rows), 1) == srow_ref[...])
    high, low = split(own_ref[...] + recv_ref[...])
    out_ref[...] = total + mm(high, pick) + mm(low, pick)
    packed = incoming_ref[0, cap:, :].astype(f32)
    for d in range(1, count):
        packed = packed + incoming_ref[d, cap:, :].astype(f32)
    high, low = split(packed)
    for k in range(2):
        lane = iota((width, filts), 0) - 2 * k * filts
        unit = iota((width, filts), 1)
        place = onehot((lane == unit) | (lane == unit + filts))
        filt_ref[k * half : (k + 1) * half, :] = mm(high, place) + mm(low, place)


def entity_sum(want, srow, own, recv, incoming, rows, cap, filts):
    half = incoming.shape[1] - cap
    return pl.pallas_call(
        functools.partial(entity_kernel, cap),
        out_shape=[
            jax.ShapeDtypeStruct((own.shape[0], rows), f32),
            jax.ShapeDtypeStruct((2 * half, filts), f32),
        ],
        compiler_params=params(),
        cost_estimate=cost(1.5e9, 4e6),
        name="entity_grad",
    )(want, srow, own, recv, incoming)


def shards(
    entity_table,
    relation_table,
    filters,
    proj_weight,
    chequer_perm,
    head_owner,
    head_row,
    rel_ids,
    pos_index,
    tail_owner,
    tail_row,
):
    count = lax.axis_size("shard")
    me = lax.axis_index("shard")
    assert count % 2 == 0
    direct = count <= 16
    queries = head_row.shape[0]
    cand = tail_row.shape[0]
    rows, width = entity_table.shape
    rels = relation_table.shape[0]
    filts, ks, _ = filters.shape
    head_cap = 2 * queries // count
    tail_cap = 2 * cand // count
    same_core = [list(range(c, count, 2)) for c in range(2)]
    copies = count // 2 if direct else 1

    def swap(x):
        return lax.ppermute(x, "shard", [(d, d ^ 1) for d in range(count)])

    def exchange(x):
        return lax.all_to_all(x, "shard", split_axis=0, concat_axis=0, tiled=True)

    def gather_core(x):
        if direct:
            return lax.all_to_all(
                x, "shard", split_axis=0, concat_axis=0, axis_index_groups=same_core, tiled=True
            )
        return lax.all_gather(x, "shard", axis=0, axis_index_groups=same_core, tiled=True)

    me1 = me.reshape(1)
    core = (me & 1).reshape(1)
    heads = head_owner[:, 0]
    tail_owners = tail_owner[:, 0]
    table_t, rtab_t, weight_t = entity_table.T, relation_table.T, proj_weight.T
    numbers = jnp.stack([heads, head_row, rel_ids, pos_index])[None]
    numbers = exchange(jnp.broadcast_to(numbers, (count,) + numbers.shape[1:]))

    ids = jnp.stack([me, me ^ 1, me & 1])
    tails_t, slot_row = pack_tails(me1, tail_owners, tail_row, table_t, tail_cap)
    all_tails = lax.all_gather(tails_t, "shard", axis=0, tiled=True)
    scand = slot_cands(me1, tail_owners, tail_cap)
    found, want = find_heads(me1, numbers, table_t, head_cap)
    fetched = exchange(found)
    pos = pos_slots(tail_owners, pos_index, tail_cap)

    codes = jnp.asarray(band_codes(ks))
    band, band_t = build_band(filters, codes)
    extra = BAND_OUT * (GROUPS - 1) + LANES - IMG * IMG - BAND_OUT
    ext = jnp.concatenate([chequer_perm[-BAND_OUT:], chequer_perm, chequer_perm[:extra]])[None]
    orow = heads[None, :]
    slope, weight, img, qv, vecs = front(
        fetched, orow, rel_ids[None, :], rtab_t, ext, band, weight_t, head_cap, copies
    )
    core_vecs = gather_core(vecs)

    qgt = score_part(qv, pos, all_tails, cand)
    all_qgt = lax.all_gather(qgt, "shard", axis=0, tiled=True)
    outgoing, sums, corr = back(qgt, orow, ext, img, band_t, weight, slope, count, head_cap, copies)
    core_sums = gather_core(sums)
    incoming = exchange(filter_sums(corr, codes, outgoing, ks * ks))

    own, other = tail_part(ids, all_tails, scand, numbers, core_vecs, cand)
    entity_grad, filter_grad = entity_sum(
        want, slot_row, own, swap(other), incoming, rows, head_cap, filts
    )
    filter_grad = filter_grad[: ks * ks].T.reshape(filts, ks, ks)

    cols = filts * IMG * IMG // count
    if direct and cols % (IMG * IMG) == 0:
        feats = column_feats(ids, rtab_t, ext, band, numbers, core_vecs, cols)
        own, other = proj_part(core, feats, all_qgt)
    else:
        core_numbers, core_qgt = (
            lax.dynamic_index_in_dim(
                x.reshape((count // 2, 2) + x.shape[1:]), me & 1, 1, keepdims=False
            )
            for x in (numbers, all_qgt)
        )
        own, other = (
            proj_columns(
                d * cols, cols, filters, chequer_perm, relation_table,
                core_numbers, core_vecs[:, 0], core_qgt,
            )
            for d in (me, me ^ 1)
        )
    proj_grad = (own + swap(other)).T

    part = rel_part(core, numbers, core_sums, rels)
    relation_grad = (part + swap(part)).T
    return (entity_grad.T, relation_grad, filter_grad, proj_grad)


def solution(mesh):
    placed = (
        P("shard", None),
        P(),
        P(),
        P(),
        P(),
        P(("parts", "shard"), None),
        P(("parts", "shard")),
        P(("parts", "shard")),
        P(("parts", "shard")),
        P("parts", None),
        P("parts"),
    )
    return jax.shard_map(
        shards,
        mesh=mesh,
        in_specs=placed,
        out_specs=(
            P(("parts", "shard"), None),
            P("parts", None),
            P("parts", None, None),
            P(("parts", "shard"), None),
        ),
        check_vma=False,
    )
```

```python
import functools
import math

import jax
import jax.numpy as jnp
import numpy as np
from jax import lax
from jax.experimental import pallas as pl
from jax.experimental.pallas import tpu as pltpu
from jax.sharding import PartitionSpec as P

IMG = 20
BAND = 4
GROUPS = IMG // BAND
BAND_OUT = BAND * IMG
LANES = 256

loss_weight = 0.015625
smooth = 0.1

f32 = jnp.float32
bf16 = jnp.bfloat16
i32 = jnp.int32

NN = (((1,), (0,)), ((), ()))
NT = (((1,), (1,)), ((), ()))
TN = (((0,), (0,)), ((), ()))


def mm(a, b, dims=NN):
    return lax.dot_general(a, b, dims, preferred_element_type=f32)


def iota(shape, axis):
    return lax.broadcasted_iota(i32, shape, axis)


def onehot(mask):
    return jnp.where(mask, 1.0, 0.0).astype(bf16)


def split(value):
    high = value.astype(bf16)
    return high, (value - high.astype(f32)).astype(bf16)


def sigmoid(v):
    return 0.5 * jnp.tanh(0.5 * v) + 0.5


def params(*semantics):
    return pltpu.CompilerParams(
        dimension_semantics=semantics or None, vmem_limit_bytes=60 << 20
    )


def cost(flops, nbytes, trans=0):
    return pl.CostEstimate(flops=int(flops), bytes_accessed=int(nbytes), transcendentals=int(trans))


def whole(shape):
    return pl.BlockSpec(shape, lambda *_: (0,) * len(shape))


SMEM = pl.BlockSpec(memory_space=pltpu.SMEM)


def band_codes(ks):
    codes = np.full((IMG, LANES), -1, np.int32)
    for j in range(IMG):
        for r in range(ks):
            for x in range(IMG):
                b = (x - j + ks // 2) % IMG
                if b < ks:
                    codes[j, r * IMG + x] = r * ks + b
    return codes


def band_kernel(codes_ref, filt_ref, out_ref, out_t_ref, scr):
    count, taps = filt_ref.shape
    filt = filt_ref[...]
    for j in range(IMG):
        pick = onehot(iota((taps, LANES), 0) == codes_ref[j : j + 1, :])
        row = mm(filt, pick)
        for di in range(BAND):
            scr[:, di * IMG + j, :] = row if di == 0 else pltpu.roll(row, di * IMG, 1)
    full = scr[...].reshape(count * BAND_OUT, LANES)
    out_ref[...] = full.astype(bf16)
    out_t_ref[...] = full.T.astype(bf16)


def build_band(filters, codes):
    count, ks, _ = filters.shape
    return pl.pallas_call(
        band_kernel,
        out_shape=[
            jax.ShapeDtypeStruct((count * BAND_OUT, LANES), bf16),
            jax.ShapeDtypeStruct((LANES, count * BAND_OUT), bf16),
        ],
        scratch_shapes=[pltpu.VMEM((count, BAND_OUT, LANES), f32)],
        compiler_params=params(),
        cost_estimate=cost(4e7, 4e6),
        name="band",
    )(codes, filters.reshape(count, ks * ks))


VMEM = pl.BlockSpec(memory_space=pltpu.VMEM)


def pairs(count):
    step = 2 if count % 2 == 0 else 1
    return [range(i, i + step) for i in range(0, count, step)]


def beside(blocks):
    return jnp.concatenate(list(blocks), axis=1)


def spans(size, step):
    return [slice(i, min(i + step, size)) for i in range(0, size, step)]


def fill_picks(ref, index):
    rows, lanes = ref.shape
    for r in spans(rows, 64):
        for c in spans(lanes, 256):
            here = iota((r.stop - r.start, c.stop - c.start), 1) + c.start
            ref[r, c] = onehot(here == index[r, :])


def slot_values(owner, device, value, cap):
    lines = owner.shape[0]
    mine = owner == device
    mine_b = onehot(mine)
    before = onehot(iota((128, 128), 0) < iota((128, 128), 1))
    rank = mm(mine_b, before)
    totals = mm(mine_b, jnp.ones((128, 128), bf16))
    upper = onehot(iota((lines, lines), 1) < iota((lines, lines), 0))
    offset = mm(upper, totals.astype(bf16))
    key = jnp.where(mine, (rank + offset).astype(i32), -1)
    value = (value + 1).astype(f32)
    found = []
    for s in spans(cap, 128):
        slots = iota((s.stop - s.start, 128), 0) + s.start
        total = jnp.zeros(slots.shape, f32)
        for r in range(lines):
            total = total + jnp.where(slots == key[r : r + 1, :], value[r : r + 1, :], 0.0)
        found.append(jnp.sum(total, axis=1, keepdims=True))
    return jnp.concatenate(found, axis=0).astype(i32) - 1


def pack_kernel(me_ref, owner_ref, row_ref, table_ref, tails_t_ref, srow_ref, picks):
    cap = srow_ref.shape[0]
    srow = slot_values(owner_ref[...], me_ref[0], row_ref[...], cap)
    srow_ref[...] = srow
    fill_picks(picks, srow)
    tails_t_ref[0] = mm(table_ref[...], picks[...], NT).astype(bf16)


def pack_tails(me, tail_owners, tail_row, table_t, cap):
    assert tail_row.shape[0] % 128 == 0
    return pl.pallas_call(
        pack_kernel,
        in_specs=[SMEM] + [VMEM] * 3,
        out_shape=[
            jax.ShapeDtypeStruct((1, table_t.shape[0], cap), bf16),
            jax.ShapeDtypeStruct((cap, 1), i32),
        ],
        scratch_shapes=[pltpu.VMEM((cap, table_t.shape[1]), bf16)],
        compiler_params=params(),
        cost_estimate=cost(1e9, 2e6),
        name="pack_tails",
    )(me, tail_owners.reshape(-1, 128), tail_row.reshape(-1, 128), table_t)


def cand_kernel(me_ref, owner_ref, out_ref):
    cap = out_ref.shape[1]
    owner = owner_ref[...]
    index = iota(owner.shape, 0) * 128 + iota(owner.shape, 1)
    for k in range(2):
        out_ref[k] = slot_values(owner, me_ref[0] ^ k, index, cap)


def slot_cands(me, tail_owners, cap):
    return pl.pallas_call(
        cand_kernel,
        in_specs=[SMEM, VMEM],
        out_shape=jax.ShapeDtypeStruct((2, cap, 1), i32),
        compiler_params=params(),
        cost_estimate=cost(1e8, 1e6),
        name="slot_cands",
    )(me, tail_owners.reshape(-1, 128))


def found_kernel(cap, me_ref, table_ref, numbers_ref, found_ref, want_ref, scr, picks):
    count, _, queries = numbers_ref.shape
    owners = jnp.concatenate([numbers_ref[d, 0:1, :] for d in range(count)], axis=0)
    mine = owners == me_ref[0]
    before = onehot(iota((queries, queries), 0) < iota((queries, queries), 1))
    rank = mm(onehot(mine), before)
    key = jnp.where(mine, rank.astype(i32), -1)
    slots = iota((cap, queries), 0)
    for d in range(count):
        code = (numbers_ref[d, 1:2, :] + 1).astype(f32)
        picked = jnp.where(slots == key[d : d + 1, :], code, 0.0)
        scr[d * cap : (d + 1) * cap, :] = jnp.sum(picked, axis=1, keepdims=True)
    want = scr[...].astype(i32) - 1
    want_ref[...] = want
    fill_picks(picks, want)
    found = mm(picks[...], table_ref[...], NT).astype(bf16)
    for d in range(count):
        found_ref[d] = found[d * cap : (d + 1) * cap, :]


def find_heads(me, numbers, table_t, cap):
    width = table_t.shape[0]
    count = numbers.shape[0]
    return pl.pallas_call(
        functools.partial(found_kernel, cap),
        in_specs=[SMEM] + [VMEM] * 2,
        out_shape=[
            jax.ShapeDtypeStruct((count, cap, width), bf16),
            jax.ShapeDtypeStruct((count * cap, 1), i32),
        ],
        scratch_shapes=[
            pltpu.VMEM((count * cap, 1), f32),
            pltpu.VMEM((count * cap, table_t.shape[1]), bf16),
        ],
        compiler_params=params(),
        cost_estimate=cost(3e8, 2e6),
        name="find_heads",
    )(me, table_t, numbers)


def pos_kernel(cap, owner_ref, pos_ref, out_ref):
    cand = owner_ref.shape[1]
    queries = pos_ref.shape[1]
    eye = iota((queries, queries), 0) == iota((queries, queries), 1)
    step = min(128, cand)
    row = pos_ref[...].astype(f32)
    pos = jnp.sum(jnp.where(eye, row, 0.0), axis=1, keepdims=True).astype(i32)
    owner = jnp.zeros((queries, step), f32)
    for c in range(0, cand, step):
        here = iota((queries, step), 1) + c
        value = owner_ref[:, c : c + step].astype(f32)
        owner = owner + jnp.where(here == pos, value, 0.0)
    owner = jnp.sum(owner, axis=1, keepdims=True).astype(i32)
    ahead = jnp.zeros((queries, step), f32)
    for c in range(0, cand, step):
        here = iota((queries, step), 1) + c
        same = (owner_ref[:, c : c + step] == owner) & (here < pos)
        ahead = ahead + jnp.where(same, 1.0, 0.0)
    ahead = jnp.sum(ahead, axis=1, keepdims=True).astype(i32)
    out_ref[...] = owner * cap + ahead


def pos_slots(tail_owners, pos_index, cap):
    queries = pos_index.shape[0]
    return pl.pallas_call(
        functools.partial(pos_kernel, cap),
        out_shape=jax.ShapeDtypeStruct((queries, 1), i32),
        compiler_params=params(),
        cost_estimate=cost(1e7, 1e5),
        name="pos_slots",
    )(tail_owners.reshape(1, -1), pos_index.reshape(1, -1))


def slot_picks(cap, slots, orow):
    count = slots // cap
    queries = orow.shape[1]
    member = iota((count, queries), 0) == orow
    before = onehot(iota((queries, queries), 0) < iota((queries, queries), 1))
    rank = mm(onehot(member), before)
    rank = jnp.sum(jnp.where(member, rank, 0.0), axis=0, keepdims=True).astype(i32)
    return onehot(iota((slots, queries), 0) == orow * cap + rank)


def front_kernel(
    cap, fetched_ref, orow_ref, rel_ref, rtab_ref, ext_ref, band_ref, w_ref,
    img_ref, qv_ref, vecs_ref, feats, acc, ext, pre,
):
    s = pl.program_id(0)
    width, queries = acc.shape

    @pl.when(s == 0)
    def _():
        rows = jnp.concatenate([fetched_ref[d] for d in range(fetched_ref.shape[0])], axis=0)
        pick = slot_picks(cap, rows.shape[0], orow_ref[...])
        hvt = mm(rows, pick, TN).astype(bf16)
        for d in range(vecs_ref.shape[0]):
            vecs_ref[d, 0] = hvt
        rels = rtab_ref.shape[1]
        rvt = mm(rtab_ref[...], onehot(iota((rels, queries), 0) == rel_ref[...])).astype(bf16)
        entry = iota((width, ext_ref.shape[1]), 0)
        image = mm(onehot(entry == ext_ref[...]), hvt, TN)
        image = image + mm(onehot(entry + width == ext_ref[...]), rvt, TN)
        ext[...] = image.astype(bf16)
        for g in range(GROUPS):
            img_ref[:, g * queries : (g + 1) * queries] = ext[g * BAND_OUT : g * BAND_OUT + LANES, :]
        acc[...] = jnp.zeros_like(acc)

    units = band_ref.shape[0] // BAND_OUT
    flat = GROUPS * BAND_OUT
    pre[...] = mm(band_ref[...], img_ref[...])
    for f in range(units):
        for g in range(GROUPS):
            rows = slice(f * flat + g * BAND_OUT, f * flat + (g + 1) * BAND_OUT)
            v = pre[f * BAND_OUT : (f + 1) * BAND_OUT, g * queries : (g + 1) * queries]
            feats[rows, :] = (v * sigmoid(v)).astype(bf16)
    acc[...] += mm(w_ref[...], feats[...])

    @pl.when(s == pl.num_programs(0) - 1)
    def _():
        query = acc[...]
        qv_ref[...] = query.T.astype(bf16)
        qvt = query.astype(bf16)
        for d in range(vecs_ref.shape[0]):
            vecs_ref[d, 1] = qvt


def filter_block(filts):
    return math.gcd(filts, 8)


def front(fetched, orow, rel_row, rtab_t, ext, band, weight_t, cap, copies):
    queries = orow.shape[1]
    width, flat = weight_t.shape
    filts = band.shape[0] // BAND_OUT
    units = filter_block(filts)
    cols = flat // filts * units
    return pl.pallas_call(
        functools.partial(front_kernel, cap),
        grid=(filts // units,),
        in_specs=[
            whole(fetched.shape),
            whole(orow.shape),
            whole(rel_row.shape),
            whole(rtab_t.shape),
            whole(ext.shape),
            pl.BlockSpec((units * BAND_OUT, LANES), lambda s: (s, 0)),
            pl.BlockSpec((width, cols), lambda s: (0, s)),
        ],
        out_specs=[
            whole((LANES, GROUPS * queries)),
            whole((queries, width)),
            whole((copies, 2, width, queries)),
        ],
        out_shape=[
            jax.ShapeDtypeStruct((LANES, GROUPS * queries), bf16),
            jax.ShapeDtypeStruct((queries, width), bf16),
            jax.ShapeDtypeStruct((copies, 2, width, queries), bf16),
        ],
        scratch_shapes=[
            pltpu.VMEM((cols, queries), bf16),
            pltpu.VMEM((width, queries), f32),
            pltpu.VMEM((ext.shape[1], queries), bf16),
            pltpu.VMEM((units * BAND_OUT, GROUPS * queries), f32),
        ],
        compiler_params=params("arbitrary"),
        cost_estimate=cost(4e9, 2.4e7, 2.5e6),
        name="front",
    )(fetched, orow, rel_row, rtab_t, ext, band, weight_t)


def score_kernel(cand, pos_ref, qv_ref, tails_ref, out_ref, acc, scores, grads):
    step = pl.program_id(0)

    @pl.when(step == 0)
    def _():
        acc[...] = jnp.zeros_like(acc)

    qv = qv_ref[...]
    queries = qv.shape[0]
    blocks, _, cap = tails_ref.shape
    total = acc[...]
    for b in range(blocks):
        block = tails_ref[b]
        scores[b] = mm(qv, block)
        for r in spans(queries, 16):
            here = iota((r.stop - r.start, cap), 1) + (step * blocks + b) * cap
            target = jnp.where(here == pos_ref[r, :], 1.0 - smooth + smooth / cand, smooth / cand)
            grads[b, r, :] = ((sigmoid(scores[b, r, :]) - target) * loss_weight).astype(bf16)
        total = total + mm(grads[b], block, NT)
    acc[...] = total

    @pl.when(step == pl.num_programs(0) - 1)
    def _():
        qgt = total.T.astype(bf16)
        for d in range(out_ref.shape[0]):
            out_ref[d] = qgt


def score_part(qv, pos, tails, cand, copies):
    queries, width = qv.shape
    owners, _, cap = tails.shape
    blocks = math.gcd(owners, max(1, 2048 // cap))
    return pl.pallas_call(
        functools.partial(score_kernel, cand),
        grid=(owners // blocks,),
        in_specs=[
            whole(pos.shape),
            whole(qv.shape),
            pl.BlockSpec((blocks, width, cap), lambda s: (s, 0, 0)),
        ],
        out_specs=whole((copies, width, queries)),
        out_shape=jax.ShapeDtypeStruct((copies, width, queries), bf16),
        scratch_shapes=[
            pltpu.VMEM((queries, width), f32),
            pltpu.VMEM((blocks, queries, cap), f32),
            pltpu.VMEM((blocks, queries, cap), bf16),
        ],
        compiler_params=params("arbitrary"),
        cost_estimate=cost(1e9, 3e6, 5e5),
        name="score",
    )(pos, qv, tails)


def back_kernel(
    cap, orow_ref, ext_ref, qgt_ref, img_ref, band_ref, bandt_ref, w_ref,
    out_ref, sums_ref, corr_ref, fgrad, spread, ext, pre, linear,
):
    s = pl.program_id(0)
    _, width, queries = qgt_ref.shape

    @pl.when(s == 0)
    def _():
        spread[...] = jnp.zeros_like(spread)

    units = bandt_ref.shape[1] // BAND_OUT
    flat = GROUPS * BAND_OUT
    pre[...] = mm(band_ref[...], img_ref[...])
    linear[...] = mm(w_ref[...], qgt_ref[0], TN)
    for f in range(units):
        for g in range(GROUPS):
            rows = slice(f * flat + g * BAND_OUT, f * flat + (g + 1) * BAND_OUT)
            part = slice(f * BAND_OUT, (f + 1) * BAND_OUT)
            lanes = slice(g * queries, (g + 1) * queries)
            v = pre[part, lanes]
            sig = sigmoid(v)
            fgrad[part, lanes] = (linear[rows, :] * (sig * (1.0 + v * (1.0 - sig)))).astype(bf16)
    spread[...] += mm(bandt_ref[...], fgrad[...])
    corr_ref[...] = mm(fgrad[...], img_ref[...], NT).reshape(units, BAND_OUT, LANES)

    @pl.when(s == pl.num_programs(0) - 1)
    def _():
        ext[...] = jnp.zeros_like(ext)
        for g in range(GROUPS):
            ext[g * BAND_OUT : g * BAND_OUT + LANES, :] += spread[:, g * queries : (g + 1) * queries]
        entry = iota((width, ext.shape[0]), 0)
        high, low = split(ext[...])
        hpick = onehot(entry == ext_ref[...])
        rpick = onehot(entry + width == ext_ref[...])
        hgrad = (mm(hpick, high) + mm(hpick, low)).astype(bf16)
        rgrad = mm(rpick, high) + mm(rpick, low)
        sums_ref[0] = rgrad
        blocks = out_ref.shape[0]
        pick = slot_picks(cap, blocks * cap, orow_ref[...])
        rows = mm(pick, hgrad, NT).astype(bf16)
        for d in range(blocks):
            out_ref[d] = rows[d * cap : (d + 1) * cap, :]


def back(qgt, orow, ext, img, band, band_t, weight_t, count, cap):
    _, width, queries = qgt.shape
    flat = weight_t.shape[1]
    filts = band_t.shape[1] // BAND_OUT
    units = filter_block(filts)
    cols = flat // filts * units
    return pl.pallas_call(
        functools.partial(back_kernel, cap),
        grid=(filts // units,),
        in_specs=[
            whole(orow.shape),
            whole(ext.shape),
            whole((1, width, queries)),
            whole(img.shape),
            pl.BlockSpec((units * BAND_OUT, LANES), lambda s: (s, 0)),
            pl.BlockSpec((LANES, units * BAND_OUT), lambda s: (0, s)),
            pl.BlockSpec((width, cols), lambda s: (0, s)),
        ],
        out_specs=[
            whole((count, cap, width)),
            whole((1, width, queries)),
            pl.BlockSpec((units, BAND_OUT, LANES), lambda s: (s, 0, 0)),
        ],
        out_shape=[
            jax.ShapeDtypeStruct((count, cap, width), bf16),
            jax.ShapeDtypeStruct((1, width, queries), f32),
            jax.ShapeDtypeStruct((filts, BAND_OUT, LANES), f32),
        ],
        scratch_shapes=[
            pltpu.VMEM((units * BAND_OUT, GROUPS * queries), bf16),
            pltpu.VMEM((LANES, GROUPS * queries), f32),
            pltpu.VMEM((ext.shape[1], queries), f32),
            pltpu.VMEM((units * BAND_OUT, GROUPS * queries), f32),
            pltpu.VMEM((cols, queries), f32),
        ],
        compiler_params=params("arbitrary"),
        cost_estimate=cost(6e9, 2e7, 2.5e6),
        name="back",
    )(orow, ext, qgt, img, band, band_t, weight_t)


def half_taps(taps):
    return -(-taps // 32) * 16


def diag_kernel(taps, codes_ref, corr_ref, rows_ref, out_ref):
    filts = corr_ref.shape[0]
    cap, width = rows_ref.shape[1:]
    half = half_taps(taps)
    total = jnp.zeros((2 * half, filts), f32)
    for j in range(IMG):
        rows = corr_ref[:, j, :]
        for di in range(1, BAND):
            rows = rows + pltpu.roll(corr_ref[:, di * IMG + j, :], LANES - di * IMG, 1)
        pick = onehot(iota((2 * half, LANES), 0) == codes_ref[j : j + 1, :])
        high, low = split(rows)
        total = total + mm(pick, high, NT) + mm(pick, low, NT)
    packed = jnp.zeros((half, width), f32)
    for k in range(2):
        for i, piece in enumerate(split(total[k * half : (k + 1) * half, :])):
            place = onehot(iota((filts, width), 1) == iota((filts, width), 0) + (2 * k + i) * filts)
            packed = packed + mm(piece, place)
    packed = packed.astype(bf16)
    for d in range(out_ref.shape[0]):
        out_ref[d, :cap, :] = rows_ref[d]
        out_ref[d, cap:, :] = packed


def filter_sums(corr, codes, rows, taps):
    count, cap, width = rows.shape
    assert 4 * corr.shape[0] <= width
    return pl.pallas_call(
        functools.partial(diag_kernel, taps),
        out_shape=jax.ShapeDtypeStruct((count, cap + half_taps(taps), width), bf16),
        compiler_params=params(),
        cost_estimate=cost(1e8, 4e6),
        name="filter_sums",
    )(codes, corr, rows)


def tail_kernel(
    cand, ids_ref, tails_ref, mate_ref, scand_ref, numbers_ref, vecs_ref, own_ref, other_ref, scores, grads
):
    cap = own_ref.shape[1]
    tails = jnp.concatenate([ref[0].astype(f32).T for ref in (tails_ref, mate_ref)], axis=0).astype(bf16)
    scand = jnp.concatenate([scand_ref[0], scand_ref[1]], axis=0)
    own = jnp.zeros(own_ref.shape, f32)
    other = jnp.zeros(own_ref.shape, f32)
    for i, group in enumerate(pairs(vecs_ref.shape[0])):
        qvt = beside(vecs_ref[p, 1] for p in group)
        pos = beside(numbers_ref[2 * p + ids_ref[2], 3:4, :] for p in group)
        score, grad = scores.at[i % 2], grads.at[i % 2]
        score[...] = mm(tails, qvt)
        for r in spans(2 * cap, 64):
            target = jnp.where(scand[r, :] == pos, 1.0 - smooth + smooth / cand, smooth / cand)
            grad[r, :] = ((sigmoid(score[r, :]) - target) * loss_weight).astype(bf16)
        own = own + mm(qvt, grad[:cap, :], NT)
        other = other + mm(qvt, grad[cap:, :], NT)
    own_ref[...] = own
    other_ref[...] = other


def tail_part(ids, tails, scand, numbers, vecs, cand):
    _, width, cap = tails.shape
    half = jax.ShapeDtypeStruct((width, cap), f32)
    return pl.pallas_call(
        functools.partial(tail_kernel, cand),
        grid_spec=pltpu.PrefetchScalarGridSpec(
            num_scalar_prefetch=1,
            grid=(1,),
            in_specs=[
                pl.BlockSpec((1, width, cap), lambda s, ids: (ids[0], 0, 0)),
                pl.BlockSpec((1, width, cap), lambda s, ids: (ids[1], 0, 0)),
                whole(scand.shape),
                whole(numbers.shape),
                whole(vecs.shape),
            ],
            out_specs=[whole(half.shape)] * 2,
            scratch_shapes=[
                pltpu.VMEM((2, 2 * cap, 2 * vecs.shape[3]), f32),
                pltpu.VMEM((2, 2 * cap, 2 * vecs.shape[3]), bf16),
            ],
        ),
        out_shape=[half, half],
        compiler_params=params("arbitrary"),
        cost_estimate=cost(2e9, 3e6, 1e6),
        name="tail_grad",
    )(ids, tails, tails, scand, numbers, vecs)


def feats_kernel(
    ids_ref, rtab_ref, ext_ref, band_ref, mate_ref, numbers_ref, vecs_ref, out_ref, pick, hmat, rmat, pre, rpick
):
    width, rels = rtab_ref.shape
    units = band_ref.shape[0] // BAND_OUT
    flat = GROUPS * BAND_OUT
    cols = units * flat
    entry = iota((width, ext_ref.shape[1]), 0)
    for part, mat in ((0, hmat), (width, rmat)):
        pick[...] = jnp.where(entry + part == ext_ref[...], 1.0, 0.0).T.astype(bf16)
        for k, source in enumerate((band_ref, mate_ref)):
            for g in range(GROUPS):
                rows = mm(source[...], pick[g * BAND_OUT : g * BAND_OUT + LANES, :]).astype(bf16)
                for f in range(units):
                    first = k * cols + f * flat + g * BAND_OUT
                    mat[first : first + BAND_OUT, :] = rows[f * BAND_OUT : (f + 1) * BAND_OUT, :]
    queries = vecs_ref.shape[3]
    for group in pairs(vecs_ref.shape[0]):
        hvt = beside(vecs_ref[p, 0] for p in group)
        rel = beside(numbers_ref[2 * p + ids_ref[2], 2:3, :] for p in group)
        for r in spans(rels, 64):
            rpick[r, :] = onehot(iota((r.stop - r.start, rel.shape[1]), 0) + r.start == rel)
        rvt = mm(rtab_ref[...], rpick[...]).astype(bf16)
        lanes = slice(group[0] * queries, (group[-1] + 1) * queries)
        for k in range(2):
            rows = slice(k * cols, (k + 1) * cols)
            pre[k] = mm(hmat[rows, :], hvt) + mm(rmat[rows, :], rvt)
            for r in spans(cols, 80):
                v = pre[k, r, :]
                out_ref[k * cols + r.start : k * cols + r.stop, lanes] = (v * sigmoid(v)).astype(bf16)


def column_feats(ids, rtab_t, ext, band, numbers, vecs, cols):
    width = rtab_t.shape[0]
    unit = cols // GROUPS
    gathered, _, _, queries = vecs.shape
    return pl.pallas_call(
        feats_kernel,
        grid_spec=pltpu.PrefetchScalarGridSpec(
            num_scalar_prefetch=1,
            grid=(1,),
            in_specs=[
                whole(rtab_t.shape),
                whole(ext.shape),
                pl.BlockSpec((unit, LANES), lambda s, ids: (ids[0], 0)),
                pl.BlockSpec((unit, LANES), lambda s, ids: (ids[1], 0)),
                whole(numbers.shape),
                whole(vecs.shape),
            ],
            out_specs=whole((2 * cols, gathered * queries)),
            scratch_shapes=[
                pltpu.VMEM((ext.shape[1], width), bf16),
                pltpu.VMEM((2 * cols, width), bf16),
                pltpu.VMEM((2 * cols, width), bf16),
                pltpu.VMEM((2, cols, 2 * queries), f32),
                pltpu.VMEM((rtab_t.shape[1], 2 * queries), bf16),
            ],
        ),
        out_shape=jax.ShapeDtypeStruct((2 * cols, gathered * queries), bf16),
        compiler_params=params("arbitrary"),
        cost_estimate=cost(6e9, 6e6, 2.5e6),
        name="column_feats",
    )(ids, rtab_t, ext, band, band, numbers, vecs)


def proj_kernel(feats_ref, grads_ref, own_ref, other_ref):
    cols = own_ref.shape[1]
    qgt = beside(grads_ref[p] for p in range(grads_ref.shape[0]))
    own_ref[...] = mm(qgt, feats_ref[:cols, :], NT)
    other_ref[...] = mm(qgt, feats_ref[cols:, :], NT)


def proj_part(feats, grads):
    half = jax.ShapeDtypeStruct((grads.shape[1], feats.shape[0] // 2), f32)
    return pl.pallas_call(
        proj_kernel,
        out_shape=[half, half],
        compiler_params=params(),
        cost_estimate=cost(1e9, 8e6),
        name="proj_grad",
    )(feats, grads)


def proj_columns(first, cols, filters, chequer_perm, relation_table, numbers, heads, grads):
    ks = filters.shape[-1]
    rim = ks // 2
    flat = IMG * IMG
    column = first + jnp.arange(cols, dtype=i32)
    f = column // flat
    i = (column % flat) // IMG
    j = column % IMG
    spot = jnp.arange(flat, dtype=i32)
    a = (spot[:, None] // IMG - i[None, :] + rim) % IMG
    b = (spot[:, None] % IMG - j[None, :] + rim) % IMG
    tap = filters[f[None, :], jnp.minimum(a, ks - 1), jnp.minimum(b, ks - 1)]
    matrix = jnp.where((a < ks) & (b < ks), tap, jnp.zeros((), bf16))
    width = heads.shape[1]
    head = heads.transpose(0, 2, 1).reshape(-1, width)
    qg = grads.transpose(0, 2, 1).reshape(-1, width)
    joined = jnp.concatenate([head, relation_table[numbers[:, 2].reshape(-1)]], axis=1)
    pre = mm(joined[:, chequer_perm], matrix)
    return mm(qg, (pre * sigmoid(pre)).astype(bf16), TN)


def rel_kernel(numbers_ref, sums_ref, rel_ref, picks):
    width, rels = rel_ref.shape
    queries = sums_ref.shape[2]
    total = None
    for block in spans(sums_ref.shape[0], picks.shape[1] // queries):
        members = range(block.start, block.stop)
        for i, p in enumerate(members):
            rel = numbers_ref[p, 2:3, :]
            for r in spans(rels, 128):
                here = iota((r.stop - r.start, queries), 0) + r.start
                picks[r, i * queries : (i + 1) * queries] = onehot(here == rel)
        parts = jnp.concatenate(split(beside(sums_ref[p] for p in members)), axis=0)
        part = mm(parts, picks[...], NT)
        total = part if total is None else total + part
    rel_ref[...] = total[:width, :] + total[width:, :]


def rel_part(numbers, sums, rels):
    count, width, queries = sums.shape
    return pl.pallas_call(
        rel_kernel,
        out_shape=jax.ShapeDtypeStruct((width, rels), f32),
        scratch_shapes=[pltpu.VMEM((rels, math.gcd(count, 16) * queries), bf16)],
        compiler_params=params(),
        cost_estimate=cost(2e9, 3e6),
        name="rel_grad",
    )(numbers, sums)


def entity_kernel(cap, want_ref, srow_ref, own_ref, recv_ref, incoming_ref, out_ref, filt_ref):
    rows = out_ref.shape[1]
    count, _, width = incoming_ref.shape
    half, filts = filt_ref.shape[0] // 2, filt_ref.shape[1]
    grads = jnp.concatenate([incoming_ref[d, :cap, :] for d in range(count)], axis=0)
    turned = grads.astype(f32).T.astype(bf16)
    high, low = split(own_ref[...] + recv_ref[...])
    for c in spans(rows, 256):
        here = iota((want_ref.shape[0], c.stop - c.start), 1) + c.start
        total = mm(turned, onehot(here == want_ref[...]))
        here = iota((srow_ref.shape[0], c.stop - c.start), 1) + c.start
        pick = onehot(here == srow_ref[...])
        out_ref[:, c] = total + mm(high, pick) + mm(low, pick)
    packed = incoming_ref[0, cap:, :].astype(f32)
    for d in range(1, count):
        packed = packed + incoming_ref[d, cap:, :].astype(f32)
    high, low = split(packed)
    for k in range(2):
        lane = iota((width, filts), 0) - 2 * k * filts
        unit = iota((width, filts), 1)
        place = onehot((lane == unit) | (lane == unit + filts))
        filt_ref[k * half : (k + 1) * half, :] = mm(high, place) + mm(low, place)


def entity_sum(want, srow, own, recv, incoming, rows, cap, filts):
    half = incoming.shape[1] - cap
    return pl.pallas_call(
        functools.partial(entity_kernel, cap),
        out_shape=[
            jax.ShapeDtypeStruct((own.shape[0], rows), f32),
            jax.ShapeDtypeStruct((2 * half, filts), f32),
        ],
        compiler_params=params(),
        cost_estimate=cost(1.5e9, 4e6),
        name="entity_grad",
    )(want, srow, own, recv, incoming)


def shards(
    entity_table,
    relation_table,
    filters,
    proj_weight,
    chequer_perm,
    head_owner,
    head_row,
    rel_ids,
    pos_index,
    tail_owner,
    tail_row,
):
    count = lax.axis_size("shard")
    me = lax.axis_index("shard")
    assert count % 2 == 0
    direct = count <= 16
    queries = head_row.shape[0]
    cand = tail_row.shape[0]
    rows, width = entity_table.shape
    rels = relation_table.shape[0]
    filts, ks, _ = filters.shape
    head_cap = 2 * queries // count
    tail_cap = 2 * cand // count
    same_core = [list(range(c, count, 2)) for c in range(2)]
    copies = count // 2 if direct else 1

    def swap(x):
        return lax.ppermute(x, "shard", [(d, d ^ 1) for d in range(count)])

    def exchange(x):
        return lax.all_to_all(x, "shard", split_axis=0, concat_axis=0, tiled=True)

    def gather_core(x):
        if direct:
            return lax.all_to_all(
                x, "shard", split_axis=0, concat_axis=0, axis_index_groups=same_core, tiled=True
            )
        return lax.all_gather(x, "shard", axis=0, axis_index_groups=same_core, tiled=True)

    me1 = me.reshape(1)
    heads = head_owner[:, 0]
    tail_owners = tail_owner[:, 0]
    table_t, rtab_t, weight_t = entity_table.T, relation_table.T, proj_weight.T
    numbers = jnp.stack([heads, head_row, rel_ids, pos_index])[None]
    numbers = exchange(jnp.broadcast_to(numbers, (count,) + numbers.shape[1:]))

    ids = jnp.stack([me, me ^ 1, me & 1])
    tails_t, slot_row = pack_tails(me1, tail_owners, tail_row, table_t, tail_cap)
    all_tails = lax.all_gather(tails_t, "shard", axis=0, tiled=True)
    scand = slot_cands(me1, tail_owners, tail_cap)
    found, want = find_heads(me1, numbers, table_t, head_cap)
    fetched = exchange(found)
    pos = pos_slots(tail_owners, pos_index, tail_cap)

    codes = jnp.asarray(band_codes(ks))
    band, band_t = build_band(filters, codes)
    extra = BAND_OUT * (GROUPS - 1) + LANES - IMG * IMG - BAND_OUT
    ext = jnp.concatenate([chequer_perm[-BAND_OUT:], chequer_perm, chequer_perm[:extra]])[None]
    orow = heads[None, :]
    img, qv, vecs = front(
        fetched, orow, rel_ids[None, :], rtab_t, ext, band, weight_t, head_cap, copies
    )
    core_vecs = gather_core(vecs)

    qgt = score_part(qv, pos, all_tails, cand, copies)
    outgoing, sums, corr = back(qgt, orow, ext, img, band, band_t, weight_t, count, head_cap)
    all_sums = lax.all_gather(sums, "shard", axis=0, tiled=True)
    qgt, _ = lax.optimization_barrier((qgt, outgoing))
    core_qgt = gather_core(qgt)
    incoming = exchange(filter_sums(corr, codes, outgoing, ks * ks))

    own, other = tail_part(ids, all_tails, scand, numbers, core_vecs, cand)
    entity_grad, filter_grad = entity_sum(
        want, slot_row, own, swap(other), incoming, rows, head_cap, filts
    )
    filter_grad = filter_grad[: ks * ks].T.reshape(filts, ks, ks)

    cols = filts * IMG * IMG // count
    if direct and cols % (IMG * IMG) == 0:
        feats = column_feats(ids, rtab_t, ext, band, numbers, core_vecs, cols)
        own, other = proj_part(feats, core_qgt)
    else:
        core_numbers = lax.dynamic_index_in_dim(
            numbers.reshape(count // 2, 2, 4, queries), me & 1, 1, keepdims=False
        )
        own, other = (
            proj_columns(
                d * cols, cols, filters, chequer_perm, relation_table,
                core_numbers, core_vecs[:, 0], core_qgt,
            )
            for d in (me, me ^ 1)
        )
    proj_grad = (own + swap(other)).T

    relation_grad = rel_part(numbers, all_sums, rels).T
    return (entity_grad.T, relation_grad, filter_grad, proj_grad)


def solution(mesh):
    placed = (
        P("shard", None),
        P(),
        P(),
        P(),
        P(),
        P(("parts", "shard"), None),
        P(("parts", "shard")),
        P(("parts", "shard")),
        P(("parts", "shard")),
        P("parts", None),
        P("parts"),
    )
    return jax.shard_map(
        shards,
        mesh=mesh,
        in_specs=placed,
        out_specs=(
            P(("parts", "shard"), None),
            P("parts", None),
            P("parts", None, None),
            P(("parts", "shard"), None),
        ),
        check_vma=False,
    )
```

```python
import functools
import math

import jax
import jax.numpy as jnp
import numpy as np
from jax import lax
from jax.experimental import pallas as pl
from jax.experimental.pallas import tpu as pltpu
from jax.sharding import PartitionSpec as P

IMG = 20
BAND = 4
GROUPS = IMG // BAND
BAND_OUT = BAND * IMG
LANES = 256

loss_weight = 0.015625
smooth = 0.1

f32 = jnp.float32
bf16 = jnp.bfloat16
i32 = jnp.int32

NN = (((1,), (0,)), ((), ()))
NT = (((1,), (1,)), ((), ()))
TN = (((0,), (0,)), ((), ()))


def mm(a, b, dims=NN):
    return lax.dot_general(a, b, dims, preferred_element_type=f32)


def iota(shape, axis):
    return lax.broadcasted_iota(i32, shape, axis)


def onehot(mask):
    return jnp.where(mask, 1.0, 0.0).astype(bf16)


def split(value):
    high = value.astype(bf16)
    return high, (value - high.astype(f32)).astype(bf16)


def sigmoid(v):
    return 0.5 * jnp.tanh(0.5 * v) + 0.5


def params(*semantics):
    return pltpu.CompilerParams(
        dimension_semantics=semantics or None, vmem_limit_bytes=60 << 20
    )


def cost(flops, nbytes, trans=0):
    return pl.CostEstimate(flops=int(flops), bytes_accessed=int(nbytes), transcendentals=int(trans))


def whole(shape):
    return pl.BlockSpec(shape, lambda *_: (0,) * len(shape))


SMEM = pl.BlockSpec(memory_space=pltpu.SMEM)


def band_codes(ks):
    codes = np.full((IMG, LANES), -1, np.int32)
    for j in range(IMG):
        for r in range(ks):
            for x in range(IMG):
                b = (x - j + ks // 2) % IMG
                if b < ks:
                    codes[j, r * IMG + x] = r * ks + b
    return codes


def band_kernel(codes_ref, filt_ref, out_ref, out_t_ref, scr):
    count, taps = filt_ref.shape
    filt = filt_ref[...]
    for j in range(IMG):
        pick = onehot(iota((taps, LANES), 0) == codes_ref[j : j + 1, :])
        row = mm(filt, pick)
        for di in range(BAND):
            scr[:, di * IMG + j, :] = row if di == 0 else pltpu.roll(row, di * IMG, 1)
    full = scr[...].reshape(count * BAND_OUT, LANES)
    out_ref[...] = full.astype(bf16)
    out_t_ref[...] = full.T.astype(bf16)


def build_band(filters, codes):
    count, ks, _ = filters.shape
    return pl.pallas_call(
        band_kernel,
        out_shape=[
            jax.ShapeDtypeStruct((count * BAND_OUT, LANES), bf16),
            jax.ShapeDtypeStruct((LANES, count * BAND_OUT), bf16),
        ],
        scratch_shapes=[pltpu.VMEM((count, BAND_OUT, LANES), f32)],
        compiler_params=params(),
        cost_estimate=cost(4e7, 4e6),
        name="band",
    )(codes, filters.reshape(count, ks * ks))


VMEM = pl.BlockSpec(memory_space=pltpu.VMEM)


def pairs(count):
    step = 2 if count % 2 == 0 else 1
    return [range(i, i + step) for i in range(0, count, step)]


def beside(blocks):
    return jnp.concatenate(list(blocks), axis=1)


def spans(size, step):
    return [slice(i, min(i + step, size)) for i in range(0, size, step)]


def fill_picks(ref, index):
    rows, lanes = ref.shape
    for r in spans(rows, 64):
        for c in spans(lanes, 256):
            here = iota((r.stop - r.start, c.stop - c.start), 1) + c.start
            ref[r, c] = onehot(here == index[r, :])


def field(ref, d, k):
    queries = ref.shape[2] // 4
    return ref[d, :, k * queries : (k + 1) * queries]


def slot_values(owner, device, value, cap):
    lines = owner.shape[0]
    mine = owner == device
    mine_b = onehot(mine)
    before = onehot(iota((128, 128), 0) < iota((128, 128), 1))
    rank = mm(mine_b, before)
    totals = mm(mine_b, jnp.ones((128, 128), bf16))
    upper = onehot(iota((lines, lines), 1) < iota((lines, lines), 0))
    offset = mm(upper, totals.astype(bf16))
    key = jnp.where(mine, (rank + offset).astype(i32), -1)
    value = (value + 1).astype(f32)
    found = []
    for s in spans(cap, 128):
        slots = iota((s.stop - s.start, 128), 0) + s.start
        total = jnp.zeros(slots.shape, f32)
        for r in range(lines):
            total = total + jnp.where(slots == key[r : r + 1, :], value[r : r + 1, :], 0.0)
        found.append(jnp.sum(total, axis=1, keepdims=True))
    return jnp.concatenate(found, axis=0).astype(i32) - 1


def pack_kernel(me_ref, owner_ref, row_ref, table_ref, tails_t_ref, srow_ref, picks):
    cap = srow_ref.shape[0]
    srow = slot_values(owner_ref[...], me_ref[0], row_ref[...], cap)
    srow_ref[...] = srow
    fill_picks(picks, srow)
    tails_t_ref[0] = mm(table_ref[...], picks[...], NT).astype(bf16)


def pack_tails(me, tail_owners, tail_row, table_t, cap):
    assert tail_row.shape[0] % 128 == 0
    return pl.pallas_call(
        pack_kernel,
        in_specs=[SMEM] + [VMEM] * 3,
        out_shape=[
            jax.ShapeDtypeStruct((1, table_t.shape[0], cap), bf16),
            jax.ShapeDtypeStruct((cap, 1), i32),
        ],
        scratch_shapes=[pltpu.VMEM((cap, table_t.shape[1]), bf16)],
        compiler_params=params(),
        cost_estimate=cost(1e9, 2e6),
        name="pack_tails",
    )(me, tail_owners.reshape(-1, 128), tail_row.reshape(-1, 128), table_t)


def found_kernel(cap, me_ref, table_ref, numbers_ref, found_ref, want_ref, scr, picks):
    count = numbers_ref.shape[0]
    owners = jnp.concatenate([field(numbers_ref, d, 0) for d in range(count)], axis=0)
    queries = owners.shape[1]
    mine = owners == me_ref[0]
    before = onehot(iota((queries, queries), 0) < iota((queries, queries), 1))
    rank = mm(onehot(mine), before)
    key = jnp.where(mine, rank.astype(i32), -1)
    slots = iota((cap, queries), 0)
    for d in range(count):
        code = (field(numbers_ref, d, 1) + 1).astype(f32)
        picked = jnp.where(slots == key[d : d + 1, :], code, 0.0)
        scr[d * cap : (d + 1) * cap, :] = jnp.sum(picked, axis=1, keepdims=True)
    want = scr[...].astype(i32) - 1
    want_ref[...] = want
    fill_picks(picks, want)
    found = mm(picks[...], table_ref[...], NT).astype(bf16)
    for d in range(count):
        found_ref[d] = found[d * cap : (d + 1) * cap, :]


def find_heads(me, numbers, table_t, cap):
    width = table_t.shape[0]
    count = numbers.shape[0]
    return pl.pallas_call(
        functools.partial(found_kernel, cap),
        in_specs=[SMEM] + [VMEM] * 2,
        out_shape=[
            jax.ShapeDtypeStruct((count, cap, width), bf16),
            jax.ShapeDtypeStruct((count * cap, 1), i32),
        ],
        scratch_shapes=[
            pltpu.VMEM((count * cap, 1), f32),
            pltpu.VMEM((count * cap, table_t.shape[1]), bf16),
        ],
        compiler_params=params(),
        cost_estimate=cost(3e8, 2e6),
        name="find_heads",
    )(me, table_t, numbers)


def slots_kernel(me_ref, owner_ref, row_ref, pos_ref, cand_ref, out_ref):
    cap = cand_ref.shape[1]
    owner = owner_ref[...]
    index = iota(owner.shape, 0) * 128 + iota(owner.shape, 1)
    for k in range(2):
        cand_ref[k] = slot_values(owner, me_ref[0] ^ k, index, cap)
    queries = pos_ref.shape[1]
    eye = iota((queries, queries), 0) == iota((queries, queries), 1)
    row = pos_ref[...].astype(f32)
    pos = jnp.sum(jnp.where(eye, row, 0.0), axis=1, keepdims=True).astype(i32)
    lanes = spans(row_ref.shape[1], 128)
    owner = jnp.zeros((queries, 128), f32)
    for c in lanes:
        here = iota((queries, 128), 1) + c.start
        owner = owner + jnp.where(here == pos, row_ref[:, c].astype(f32), 0.0)
    owner = jnp.sum(owner, axis=1, keepdims=True).astype(i32)
    ahead = jnp.zeros((queries, 128), f32)
    for c in lanes:
        here = iota((queries, 128), 1) + c.start
        ahead = ahead + jnp.where((row_ref[:, c] == owner) & (here < pos), 1.0, 0.0)
    ahead = jnp.sum(ahead, axis=1, keepdims=True).astype(i32)
    out_ref[...] = owner * cap + ahead


def slot_tables(me, tail_owners, pos_index, cap):
    return pl.pallas_call(
        slots_kernel,
        in_specs=[SMEM] + [VMEM] * 3,
        out_shape=[
            jax.ShapeDtypeStruct((2, cap, 1), i32),
            jax.ShapeDtypeStruct((pos_index.shape[0], 1), i32),
        ],
        compiler_params=params(),
        cost_estimate=cost(1e9, 1e6),
        name="slot_tables",
    )(me, tail_owners.reshape(-1, 128), tail_owners.reshape(1, -1), pos_index.reshape(1, -1))


def slot_picks(cap, slots, orow):
    count = slots // cap
    queries = orow.shape[1]
    member = iota((count, queries), 0) == orow
    before = onehot(iota((queries, queries), 0) < iota((queries, queries), 1))
    rank = mm(onehot(member), before)
    rank = jnp.sum(jnp.where(member, rank, 0.0), axis=0, keepdims=True).astype(i32)
    return onehot(iota((slots, queries), 0) == orow * cap + rank)


def front_kernel(
    cap, fetched_ref, orow_ref, rel_ref, rtab_ref, ext_ref, band_ref, w_ref,
    slope_ref, img_ref, qv_ref, vecs_ref, feats, acc, ext, pre,
):
    s = pl.program_id(0)
    width, queries = acc.shape

    @pl.when(s == 0)
    def _():
        rows = jnp.concatenate([fetched_ref[d] for d in range(fetched_ref.shape[0])], axis=0)
        pick = slot_picks(cap, rows.shape[0], orow_ref[...])
        hvt = mm(rows, pick, TN).astype(bf16)
        for d in range(vecs_ref.shape[0]):
            vecs_ref[d, 0] = hvt
        rels = rtab_ref.shape[1]
        rvt = mm(rtab_ref[...], onehot(iota((rels, queries), 0) == rel_ref[...])).astype(bf16)
        entry = iota((width, ext_ref.shape[1]), 0)
        image = mm(onehot(entry == ext_ref[...]), hvt, TN)
        image = image + mm(onehot(entry + width == ext_ref[...]), rvt, TN)
        ext[...] = image.astype(bf16)
        for g in range(GROUPS):
            img_ref[:, g * queries : (g + 1) * queries] = ext[g * BAND_OUT : g * BAND_OUT + LANES, :]
        acc[...] = jnp.zeros_like(acc)

    units = band_ref.shape[0] // BAND_OUT
    flat = GROUPS * BAND_OUT
    pre[...] = mm(band_ref[...], img_ref[...])
    for f in range(units):
        for g in range(GROUPS):
            rows = slice(f * flat + g * BAND_OUT, f * flat + (g + 1) * BAND_OUT)
            v = pre[f * BAND_OUT : (f + 1) * BAND_OUT, g * queries : (g + 1) * queries]
            sig = sigmoid(v)
            feats[rows, :] = (v * sig).astype(bf16)
            slope_ref[rows, :] = sig * (1.0 + v * (1.0 - sig))
    acc[...] += mm(w_ref[...], feats[...])

    @pl.when(s == pl.num_programs(0) - 1)
    def _():
        query = acc[...]
        qv_ref[...] = query.T.astype(bf16)
        qvt = query.astype(bf16)
        for d in range(vecs_ref.shape[0]):
            vecs_ref[d, 1] = qvt


def filter_block(filts):
    return math.gcd(filts, 8)


def front(fetched, orow, rel_row, rtab_t, ext, band, weight_t, cap, copies):
    queries = orow.shape[1]
    width, flat = weight_t.shape
    filts = band.shape[0] // BAND_OUT
    units = filter_block(filts)
    cols = flat // filts * units
    return pl.pallas_call(
        functools.partial(front_kernel, cap),
        grid=(filts // units,),
        in_specs=[
            whole(fetched.shape),
            whole(orow.shape),
            whole(rel_row.shape),
            whole(rtab_t.shape),
            whole(ext.shape),
            pl.BlockSpec((units * BAND_OUT, LANES), lambda s: (s, 0)),
            pl.BlockSpec((width, cols), lambda s: (0, s)),
        ],
        out_specs=[
            pl.BlockSpec((cols, queries), lambda s: (s, 0)),
            whole((LANES, GROUPS * queries)),
            whole((queries, width)),
            whole((copies, 2, width, queries)),
        ],
        out_shape=[
            jax.ShapeDtypeStruct((flat, queries), f32),
            jax.ShapeDtypeStruct((LANES, GROUPS * queries), bf16),
            jax.ShapeDtypeStruct((queries, width), bf16),
            jax.ShapeDtypeStruct((copies, 2, width, queries), bf16),
        ],
        scratch_shapes=[
            pltpu.VMEM((cols, queries), bf16),
            pltpu.VMEM((width, queries), f32),
            pltpu.VMEM((ext.shape[1], queries), bf16),
            pltpu.VMEM((units * BAND_OUT, GROUPS * queries), f32),
        ],
        compiler_params=params("arbitrary"),
        cost_estimate=cost(4e9, 2.4e7, 2.5e6),
        name="front",
    )(fetched, orow, rel_row, rtab_t, ext, band, weight_t)


def score_kernel(cand, pos_ref, qv_ref, tails_ref, out_ref, acc, scores, grads):
    step = pl.program_id(0)

    @pl.when(step == 0)
    def _():
        acc[...] = jnp.zeros_like(acc)

    qv = qv_ref[...]
    queries = qv.shape[0]
    blocks, _, cap = tails_ref.shape
    total = acc[...]
    for b in range(blocks):
        block = tails_ref[b]
        scores[b] = mm(qv, block)
        for r in spans(queries, 16):
            here = iota((r.stop - r.start, cap), 1) + (step * blocks + b) * cap
            target = jnp.where(here == pos_ref[r, :], 1.0 - smooth + smooth / cand, smooth / cand)
            grads[b, r, :] = ((sigmoid(scores[b, r, :]) - target) * loss_weight).astype(bf16)
        total = total + mm(grads[b], block, NT)
    acc[...] = total

    @pl.when(step == pl.num_programs(0) - 1)
    def _():
        out_ref[0] = total.T


def score_part(qv, pos, tails, cand):
    queries, width = qv.shape
    owners, _, cap = tails.shape
    blocks = math.gcd(owners, max(1, 2048 // cap))
    return pl.pallas_call(
        functools.partial(score_kernel, cand),
        grid=(owners // blocks,),
        in_specs=[
            whole(pos.shape),
            whole(qv.shape),
            pl.BlockSpec((blocks, width, cap), lambda s: (s, 0, 0)),
        ],
        out_specs=whole((1, width, queries)),
        out_shape=jax.ShapeDtypeStruct((1, width, queries), f32),
        scratch_shapes=[
            pltpu.VMEM((queries, width), f32),
            pltpu.VMEM((blocks, queries, cap), f32),
            pltpu.VMEM((blocks, queries, cap), bf16),
        ],
        compiler_params=params("arbitrary"),
        cost_estimate=cost(1e9, 3e6, 5e5),
        name="score",
    )(pos, qv, tails)


def back_kernel(
    cap, orow_ref, ext_ref, qgt_ref, bandt_ref, w_ref, slope_ref,
    out_ref, sums_ref, fgrad_ref, spread, ext, linear,
):
    s = pl.program_id(0)
    _, width, queries = qgt_ref.shape

    @pl.when(s == 0)
    def _():
        spread[...] = jnp.zeros_like(spread)

    units = bandt_ref.shape[1] // BAND_OUT
    flat = GROUPS * BAND_OUT
    linear[...] = mm(w_ref[...], qgt_ref[0].astype(bf16), TN)
    for f in range(units):
        for g in range(GROUPS):
            rows = slice(f * flat + g * BAND_OUT, f * flat + (g + 1) * BAND_OUT)
            part = slice(f * BAND_OUT, (f + 1) * BAND_OUT)
            lanes = slice(g * queries, (g + 1) * queries)
            fgrad_ref[part, lanes] = (linear[rows, :] * slope_ref[rows, :]).astype(bf16)
    spread[...] += mm(bandt_ref[...], fgrad_ref[...])

    @pl.when(s == pl.num_programs(0) - 1)
    def _():
        ext[...] = jnp.zeros_like(ext)
        for g in range(GROUPS):
            ext[g * BAND_OUT : g * BAND_OUT + LANES, :] += spread[:, g * queries : (g + 1) * queries]
        entry = iota((width, ext.shape[0]), 0)
        high, low = split(ext[...])
        hpick = onehot(entry == ext_ref[...])
        rpick = onehot(entry + width == ext_ref[...])
        hgrad = (mm(hpick, high) + mm(hpick, low)).astype(bf16)
        rgrad = mm(rpick, high) + mm(rpick, low)
        for d in range(sums_ref.shape[0]):
            sums_ref[d] = rgrad
        blocks = out_ref.shape[0]
        pick = slot_picks(cap, blocks * cap, orow_ref[...])
        rows = mm(pick, hgrad, NT).astype(bf16)
        for d in range(blocks):
            out_ref[d] = rows[d * cap : (d + 1) * cap, :]


def back(qgt, orow, ext, band_t, weight_t, slope, count, cap, copies):
    _, width, queries = qgt.shape
    flat = weight_t.shape[1]
    filts = band_t.shape[1] // BAND_OUT
    units = math.gcd(filts, 16)
    cols = flat // filts * units
    return pl.pallas_call(
        functools.partial(back_kernel, cap),
        grid=(filts // units,),
        in_specs=[
            whole(orow.shape),
            whole(ext.shape),
            whole(qgt.shape),
            pl.BlockSpec((LANES, units * BAND_OUT), lambda s: (0, s)),
            pl.BlockSpec((width, cols), lambda s: (0, s)),
            pl.BlockSpec((cols, queries), lambda s: (s, 0)),
        ],
        out_specs=[
            whole((count, cap, width)),
            whole((copies, width, queries)),
            pl.BlockSpec((units * BAND_OUT, GROUPS * queries), lambda s: (s, 0)),
        ],
        out_shape=[
            jax.ShapeDtypeStruct((count, cap, width), bf16),
            jax.ShapeDtypeStruct((copies, width, queries), f32),
            jax.ShapeDtypeStruct((filts * BAND_OUT, GROUPS * queries), bf16),
        ],
        scratch_shapes=[
            pltpu.VMEM((LANES, GROUPS * queries), f32),
            pltpu.VMEM((ext.shape[1], queries), f32),
            pltpu.VMEM((cols, queries), f32),
        ],
        compiler_params=params("arbitrary"),
        cost_estimate=cost(6e9, 2e7),
        name="back",
    )(orow, ext, qgt, band_t, weight_t, slope)


def half_taps(taps):
    return -(-taps // 32) * 16


def diag_kernel(taps, codes_ref, fgrad_ref, img_ref, rows_ref, out_ref, corr_ref):
    s = pl.program_id(0)
    units = fgrad_ref.shape[0] // BAND_OUT
    part = mm(fgrad_ref[...], img_ref[...], NT)
    corr_ref[pl.ds(s * units, units)] = part.reshape(units, BAND_OUT, LANES)

    @pl.when(s == pl.num_programs(0) - 1)
    def _():
        diag_sums(taps, codes_ref, corr_ref, rows_ref, out_ref)


def diag_sums(taps, codes_ref, corr_ref, rows_ref, out_ref):
    filts = corr_ref.shape[0]
    cap, width = rows_ref.shape[1:]
    half = half_taps(taps)
    total = jnp.zeros((2 * half, filts), f32)
    for j in range(IMG):
        rows = corr_ref[:, j, :]
        for di in range(1, BAND):
            rows = rows + pltpu.roll(corr_ref[:, di * IMG + j, :], LANES - di * IMG, 1)
        pick = onehot(iota((2 * half, LANES), 0) == codes_ref[j : j + 1, :])
        high, low = split(rows)
        total = total + mm(pick, high, NT) + mm(pick, low, NT)
    packed = jnp.zeros((half, width), f32)
    for k in range(2):
        for i, piece in enumerate(split(total[k * half : (k + 1) * half, :])):
            place = onehot(iota((filts, width), 1) == iota((filts, width), 0) + (2 * k + i) * filts)
            packed = packed + mm(piece, place)
    packed = packed.astype(bf16)
    for d in range(out_ref.shape[0]):
        out_ref[d, :cap, :] = rows_ref[d]
        out_ref[d, cap:, :] = packed


def filter_sums(fgrad, img, codes, rows, taps):
    count, cap, width = rows.shape
    filts = fgrad.shape[0] // BAND_OUT
    units = filter_block(filts)
    assert 4 * filts <= width
    out = (count, cap + half_taps(taps), width)
    return pl.pallas_call(
        functools.partial(diag_kernel, taps),
        grid=(filts // units,),
        in_specs=[
            whole(codes.shape),
            pl.BlockSpec((units * BAND_OUT, fgrad.shape[1]), lambda s: (s, 0)),
            whole(img.shape),
            whole(rows.shape),
        ],
        out_specs=whole(out),
        out_shape=jax.ShapeDtypeStruct(out, bf16),
        scratch_shapes=[pltpu.VMEM((filts, BAND_OUT, LANES), f32)],
        compiler_params=params("arbitrary"),
        cost_estimate=cost(2e9, 6e6),
        name="filter_sums",
    )(codes, fgrad, img, rows)


def tail_kernel(
    cand, ids_ref, tails_ref, mate_ref, scand_ref, numbers_ref, vecs_ref, own_ref, other_ref, scores, grads
):
    cap = own_ref.shape[1]
    tails = jnp.concatenate([ref[0].astype(f32).T for ref in (tails_ref, mate_ref)], axis=0).astype(bf16)
    scand = jnp.concatenate([scand_ref[0], scand_ref[1]], axis=0)
    own = jnp.zeros(own_ref.shape, f32)
    other = jnp.zeros(own_ref.shape, f32)
    for i, group in enumerate(pairs(vecs_ref.shape[0])):
        qvt = beside(vecs_ref[p, 1] for p in group)
        pos = beside(field(numbers_ref, 2 * p + ids_ref[2], 3) for p in group)
        score, grad = scores.at[i % 2], grads.at[i % 2]
        score[...] = mm(tails, qvt)
        for r in spans(2 * cap, 64):
            target = jnp.where(scand[r, :] == pos, 1.0 - smooth + smooth / cand, smooth / cand)
            grad[r, :] = ((sigmoid(score[r, :]) - target) * loss_weight).astype(bf16)
        own = own + mm(qvt, grad[:cap, :], NT)
        other = other + mm(qvt, grad[cap:, :], NT)
    own_ref[...] = own
    other_ref[...] = other


def tail_part(ids, tails, scand, numbers, vecs, cand):
    _, width, cap = tails.shape
    half = jax.ShapeDtypeStruct((width, cap), f32)
    return pl.pallas_call(
        functools.partial(tail_kernel, cand),
        grid_spec=pltpu.PrefetchScalarGridSpec(
            num_scalar_prefetch=1,
            grid=(1,),
            in_specs=[
                pl.BlockSpec((1, width, cap), lambda s, ids: (ids[0], 0, 0)),
                pl.BlockSpec((1, width, cap), lambda s, ids: (ids[1], 0, 0)),
                whole(scand.shape),
                whole(numbers.shape),
                whole(vecs.shape),
            ],
            out_specs=[whole(half.shape)] * 2,
            scratch_shapes=[
                pltpu.VMEM((2, 2 * cap, 2 * vecs.shape[3]), f32),
                pltpu.VMEM((2, 2 * cap, 2 * vecs.shape[3]), bf16),
            ],
        ),
        out_shape=[half, half],
        compiler_params=params("arbitrary"),
        cost_estimate=cost(2e9, 3e6, 1e6),
        name="tail_grad",
    )(ids, tails, tails, scand, numbers, vecs)


def feats_kernel(
    ids_ref, rtab_ref, ext_ref, band_ref, mate_ref, numbers_ref, vecs_ref, out_ref, hpick, rpick, rels_hot, ext, pre
):
    width, rels = rtab_ref.shape
    units = band_ref.shape[0] // BAND_OUT
    flat = GROUPS * BAND_OUT
    cols = units * flat
    entry = iota((width, ext_ref.shape[1]), 0)
    hpick[...] = jnp.where(entry == ext_ref[...], 1.0, 0.0).T.astype(bf16)
    rpick[...] = jnp.where(entry + width == ext_ref[...], 1.0, 0.0).T.astype(bf16)
    queries = vecs_ref.shape[3]
    for i, group in enumerate(pairs(vecs_ref.shape[0])):
        hvt = beside(vecs_ref[p, 0] for p in group)
        rel = beside(field(numbers_ref, 2 * p + ids_ref[2], 2) for p in group)
        for r in spans(rels, 64):
            rels_hot[r, :] = onehot(iota((r.stop - r.start, rel.shape[1]), 0) + r.start == rel)
        rvt = mm(rtab_ref[...], rels_hot[...]).astype(bf16)
        image = ext.at[i % 2]
        image[...] = (mm(hpick[...], hvt) + mm(rpick[...], rvt)).astype(bf16)
        lanes = slice(group[0] * queries, (group[-1] + 1) * queries)
        for k, source in enumerate((band_ref, mate_ref)):
            for g in range(GROUPS):
                slot = (k * GROUPS + g) % 2
                pre[slot] = mm(source[...], image[g * BAND_OUT : g * BAND_OUT + LANES, :])
                for f in range(units):
                    v = pre[slot, f * BAND_OUT : (f + 1) * BAND_OUT, :]
                    first = k * cols + f * flat + g * BAND_OUT
                    out_ref[first : first + BAND_OUT, lanes] = (v * sigmoid(v)).astype(bf16)


def column_feats(ids, rtab_t, ext, band, numbers, vecs, cols):
    width, rels = rtab_t.shape
    unit = cols // GROUPS
    gathered, _, _, queries = vecs.shape
    return pl.pallas_call(
        feats_kernel,
        grid_spec=pltpu.PrefetchScalarGridSpec(
            num_scalar_prefetch=1,
            grid=(1,),
            in_specs=[
                whole(rtab_t.shape),
                whole(ext.shape),
                pl.BlockSpec((unit, LANES), lambda s, ids: (ids[0], 0)),
                pl.BlockSpec((unit, LANES), lambda s, ids: (ids[1], 0)),
                whole(numbers.shape),
                whole(vecs.shape),
            ],
            out_specs=whole((2 * cols, gathered * queries)),
            scratch_shapes=[
                pltpu.VMEM((ext.shape[1], width), bf16),
                pltpu.VMEM((ext.shape[1], width), bf16),
                pltpu.VMEM((rels, 2 * queries), bf16),
                pltpu.VMEM((2, ext.shape[1], 2 * queries), bf16),
                pltpu.VMEM((2, unit, 2 * queries), f32),
            ],
        ),
        out_shape=jax.ShapeDtypeStruct((2 * cols, gathered * queries), bf16),
        compiler_params=params("arbitrary"),
        cost_estimate=cost(5e9, 6e6, 2.5e6),
        name="column_feats",
    )(ids, rtab_t, ext, band, band, numbers, vecs)


def proj_kernel(core_ref, feats_ref, grads_ref, own_ref, other_ref):
    cols = own_ref.shape[1]
    count = grads_ref.shape[0] // 2
    qgt = beside(grads_ref[2 * p + core_ref[0]].astype(bf16) for p in range(count))
    own_ref[...] = mm(qgt, feats_ref[:cols, :], NT)
    other_ref[...] = mm(qgt, feats_ref[cols:, :], NT)


def proj_part(core, feats, grads):
    half = jax.ShapeDtypeStruct((grads.shape[1], feats.shape[0] // 2), f32)
    return pl.pallas_call(
        proj_kernel,
        in_specs=[SMEM] + [VMEM] * 2,
        out_shape=[half, half],
        compiler_params=params(),
        cost_estimate=cost(1e9, 8e6),
        name="proj_grad",
    )(core, feats, grads)


def proj_columns(first, cols, filters, chequer_perm, relation_table, numbers, heads, grads):
    ks = filters.shape[-1]
    rim = ks // 2
    flat = IMG * IMG
    column = first + jnp.arange(cols, dtype=i32)
    f = column // flat
    i = (column % flat) // IMG
    j = column % IMG
    spot = jnp.arange(flat, dtype=i32)
    a = (spot[:, None] // IMG - i[None, :] + rim) % IMG
    b = (spot[:, None] % IMG - j[None, :] + rim) % IMG
    tap = filters[f[None, :], jnp.minimum(a, ks - 1), jnp.minimum(b, ks - 1)]
    matrix = jnp.where((a < ks) & (b < ks), tap, jnp.zeros((), bf16))
    width = heads.shape[1]
    head = heads.transpose(0, 2, 1).reshape(-1, width)
    qg = grads.transpose(0, 2, 1).reshape(-1, width)
    joined = jnp.concatenate([head, relation_table[numbers[:, 2].reshape(-1)]], axis=1)
    pre = mm(joined[:, chequer_perm], matrix)
    return mm(qg, (pre * sigmoid(pre)).astype(bf16), TN)


def rel_kernel(core_ref, numbers_ref, sums_ref, rel_ref, picks):
    width, rels = rel_ref.shape
    queries = sums_ref.shape[2]
    total = None
    for block in spans(sums_ref.shape[0], picks.shape[1] // queries):
        members = range(block.start, block.stop)
        for i, p in enumerate(members):
            rel = field(numbers_ref, 2 * p + core_ref[0], 2)
            for r in spans(rels, 128):
                here = iota((r.stop - r.start, queries), 0) + r.start
                picks[r, i * queries : (i + 1) * queries] = onehot(here == rel)
        parts = jnp.concatenate(split(beside(sums_ref[p] for p in members)), axis=0)
        part = mm(parts, picks[...], NT)
        total = part if total is None else total + part
    rel_ref[...] = total[:width, :] + total[width:, :]


def rel_part(core, numbers, sums, rels):
    count, width, queries = sums.shape
    return pl.pallas_call(
        rel_kernel,
        in_specs=[SMEM] + [VMEM] * 2,
        out_shape=jax.ShapeDtypeStruct((width, rels), f32),
        scratch_shapes=[pltpu.VMEM((rels, math.gcd(count, 8) * queries), bf16)],
        compiler_params=params(),
        cost_estimate=cost(2e9, 3e6),
        name="rel_grad",
    )(core, numbers, sums)


def entity_kernel(cap, want_ref, srow_ref, own_ref, recv_ref, incoming_ref, out_ref, filt_ref):
    rows = out_ref.shape[1]
    count, _, width = incoming_ref.shape
    half, filts = filt_ref.shape[0] // 2, filt_ref.shape[1]
    grads = jnp.concatenate([incoming_ref[d, :cap, :] for d in range(count)], axis=0)
    turned = grads.astype(f32).T.astype(bf16)
    high, low = split(own_ref[...] + recv_ref[...])
    for c in spans(rows, 256):
        here = iota((want_ref.shape[0], c.stop - c.start), 1) + c.start
        total = mm(turned, onehot(here == want_ref[...]))
        here = iota((srow_ref.shape[0], c.stop - c.start), 1) + c.start
        pick = onehot(here == srow_ref[...])
        out_ref[:, c] = total + mm(high, pick) + mm(low, pick)
    packed = incoming_ref[0, cap:, :].astype(f32)
    for d in range(1, count):
        packed = packed + incoming_ref[d, cap:, :].astype(f32)
    high, low = split(packed)
    for k in range(2):
        lane = iota((width, filts), 0) - 2 * k * filts
        unit = iota((width, filts), 1)
        place = onehot((lane == unit) | (lane == unit + filts))
        filt_ref[k * half : (k + 1) * half, :] = mm(high, place) + mm(low, place)


def entity_sum(want, srow, own, recv, incoming, rows, cap, filts):
    half = incoming.shape[1] - cap
    return pl.pallas_call(
        functools.partial(entity_kernel, cap),
        out_shape=[
            jax.ShapeDtypeStruct((own.shape[0], rows), f32),
            jax.ShapeDtypeStruct((2 * half, filts), f32),
        ],
        compiler_params=params(),
        cost_estimate=cost(1.5e9, 4e6),
        name="entity_grad",
    )(want, srow, own, recv, incoming)


def shards(
    entity_table,
    relation_table,
    filters,
    proj_weight,
    chequer_perm,
    head_owner,
    head_row,
    rel_ids,
    pos_index,
    tail_owner,
    tail_row,
):
    count = lax.axis_size("shard")
    me = lax.axis_index("shard")
    assert count % 2 == 0
    direct = count <= 16
    queries = head_row.shape[0]
    cand = tail_row.shape[0]
    rows, width = entity_table.shape
    rels = relation_table.shape[0]
    filts, ks, _ = filters.shape
    head_cap = 2 * queries // count
    tail_cap = 2 * cand // count
    same_core = [list(range(c, count, 2)) for c in range(2)]
    copies = count // 2 if direct else 1

    def swap(x):
        return lax.ppermute(x, "shard", [(d, d ^ 1) for d in range(count)])

    def exchange(x):
        return lax.all_to_all(x, "shard", split_axis=0, concat_axis=0, tiled=True)

    def gather_core(x):
        if direct:
            return lax.all_to_all(
                x, "shard", split_axis=0, concat_axis=0, axis_index_groups=same_core, tiled=True
            )
        return lax.all_gather(x, "shard", axis=0, axis_index_groups=same_core, tiled=True)

    me1 = me.reshape(1)
    core = (me & 1).reshape(1)
    heads = head_owner[:, 0]
    tail_owners = tail_owner[:, 0]
    table_t, rtab_t, weight_t = entity_table.T, relation_table.T, proj_weight.T
    numbers = jnp.concatenate([heads, head_row, rel_ids, pos_index])
    numbers = exchange(jnp.broadcast_to(numbers, (count, 1, 4 * queries)))

    ids = jnp.stack([me, me ^ 1, me & 1])
    tails_t, slot_row = pack_tails(me1, tail_owners, tail_row, table_t, tail_cap)
    all_tails = lax.all_gather(tails_t, "shard", axis=0, tiled=True)
    scand, pos = slot_tables(me1, tail_owners, pos_index, tail_cap)
    found, want = find_heads(me1, numbers, table_t, head_cap)
    fetched = exchange(found)

    codes = jnp.asarray(band_codes(ks))
    band, band_t = build_band(filters, codes)
    extra = BAND_OUT * (GROUPS - 1) + LANES - IMG * IMG - BAND_OUT
    ext = jnp.concatenate([chequer_perm[-BAND_OUT:], chequer_perm, chequer_perm[:extra]])[None]
    orow = heads[None, :]
    slope, img, qv, vecs = front(
        fetched, orow, rel_ids[None, :], rtab_t, ext, band, weight_t, head_cap, copies
    )
    core_vecs = gather_core(vecs)

    qgt = score_part(qv, pos, all_tails, cand)
    all_qgt = lax.all_gather(qgt, "shard", axis=0, tiled=True)
    outgoing, sums, fgrad = back(qgt, orow, ext, band_t, weight_t, slope, count, head_cap, copies)
    core_sums = gather_core(sums)
    incoming = exchange(filter_sums(fgrad, img, codes, outgoing, ks * ks))

    own, other = tail_part(ids, all_tails, scand, numbers, core_vecs, cand)
    entity_grad, filter_grad = entity_sum(
        want, slot_row, own, swap(other), incoming, rows, head_cap, filts
    )
    filter_grad = filter_grad[: ks * ks].T.reshape(filts, ks, ks)

    cols = filts * IMG * IMG // count
    if direct and cols % (IMG * IMG) == 0:
        feats = column_feats(ids, rtab_t, ext, band, numbers, core_vecs, cols)
        own, other = proj_part(core, feats, all_qgt)
    else:
        core_numbers, core_qgt = (
            lax.dynamic_index_in_dim(
                x.reshape((count // 2, 2) + x.shape[1:]), me & 1, 1, keepdims=False
            )
            for x in (numbers.reshape(count, 4, queries), all_qgt.astype(bf16))
        )
        own, other = (
            proj_columns(
                d * cols, cols, filters, chequer_perm, relation_table,
                core_numbers, core_vecs[:, 0], core_qgt,
            )
            for d in (me, me ^ 1)
        )
    proj_grad = (own + swap(other)).T

    part = rel_part(core, numbers, core_sums, rels)
    relation_grad = (part + swap(part)).T
    return (entity_grad.T, relation_grad, filter_grad, proj_grad)


def solution(mesh):
    placed = (
        P("shard", None),
        P(),
        P(),
        P(),
        P(),
        P(("parts", "shard"), None),
        P(("parts", "shard")),
        P(("parts", "shard")),
        P(("parts", "shard")),
        P("parts", None),
        P("parts"),
    )
    return jax.shard_map(
        shards,
        mesh=mesh,
        in_specs=placed,
        out_specs=(
            P(("parts", "shard"), None),
            P("parts", None),
            P("parts", None, None),
            P(("parts", "shard"), None),
        ),
        check_vma=False,
    )
```

```python
import functools
import math

import jax
import jax.numpy as jnp
import numpy as np
from jax import lax
from jax.experimental import pallas as pl
from jax.experimental.pallas import tpu as pltpu
from jax.sharding import PartitionSpec as P

IMG = 20
BAND = 4
GROUPS = IMG // BAND
BAND_OUT = BAND * IMG
LANES = 256

loss_weight = 0.015625
smooth = 0.1

f32 = jnp.float32
bf16 = jnp.bfloat16
i32 = jnp.int32

NN = (((1,), (0,)), ((), ()))
NT = (((1,), (1,)), ((), ()))
TN = (((0,), (0,)), ((), ()))


def mm(a, b, dims=NN):
    return lax.dot_general(a, b, dims, preferred_element_type=f32)


def iota(shape, axis):
    return lax.broadcasted_iota(i32, shape, axis)


def onehot(mask):
    return jnp.where(mask, 1.0, 0.0).astype(bf16)


def split(value):
    high = value.astype(bf16)
    return high, (value - high.astype(f32)).astype(bf16)


def sigmoid(v):
    return 0.5 * jnp.tanh(0.5 * v) + 0.5


def params(*semantics):
    return pltpu.CompilerParams(
        dimension_semantics=semantics or None, vmem_limit_bytes=60 << 20
    )


def cost(flops, nbytes, trans=0):
    return pl.CostEstimate(flops=int(flops), bytes_accessed=int(nbytes), transcendentals=int(trans))


def whole(shape):
    return pl.BlockSpec(shape, lambda *_: (0,) * len(shape))


SMEM = pl.BlockSpec(memory_space=pltpu.SMEM)


def band_codes(ks):
    codes = np.full((IMG, LANES), -1, np.int32)
    for j in range(IMG):
        for r in range(ks):
            for x in range(IMG):
                b = (x - j + ks // 2) % IMG
                if b < ks:
                    codes[j, r * IMG + x] = r * ks + b
    return codes


def band_kernel(codes_ref, filt_ref, out_ref, out_t_ref, scr):
    count, taps = filt_ref.shape
    filt = filt_ref[...]
    for j in range(IMG):
        pick = onehot(iota((taps, LANES), 0) == codes_ref[j : j + 1, :])
        row = mm(filt, pick)
        for di in range(BAND):
            scr[:, di * IMG + j, :] = row if di == 0 else pltpu.roll(row, di * IMG, 1)
    full = scr[...].reshape(count * BAND_OUT, LANES)
    out_ref[...] = full.astype(bf16)
    out_t_ref[...] = full.T.astype(bf16)


def build_band(filters, codes):
    count, ks, _ = filters.shape
    return pl.pallas_call(
        band_kernel,
        out_shape=[
            jax.ShapeDtypeStruct((count * BAND_OUT, LANES), bf16),
            jax.ShapeDtypeStruct((LANES, count * BAND_OUT), bf16),
        ],
        scratch_shapes=[pltpu.VMEM((count, BAND_OUT, LANES), f32)],
        compiler_params=params(),
        cost_estimate=cost(4e7, 4e6),
        name="band",
    )(codes, filters.reshape(count, ks * ks))


VMEM = pl.BlockSpec(memory_space=pltpu.VMEM)


def pairs(count):
    step = 2 if count % 2 == 0 else 1
    return [range(i, i + step) for i in range(0, count, step)]


def beside(blocks):
    return jnp.concatenate(list(blocks), axis=1)


def spans(size, step):
    return [slice(i, min(i + step, size)) for i in range(0, size, step)]


def fill_picks(ref, index):
    rows, lanes = ref.shape
    for r in spans(rows, 64):
        for c in spans(lanes, 256):
            here = iota((r.stop - r.start, c.stop - c.start), 1) + c.start
            ref[r, c] = onehot(here == index[r, :])


def field(ref, d, k):
    queries = ref.shape[2] // 4
    return ref[d, :, k * queries : (k + 1) * queries]


def slot_values(owner, device, value, cap):
    lines = owner.shape[0]
    mine = owner == device
    mine_b = onehot(mine)
    before = onehot(iota((128, 128), 0) < iota((128, 128), 1))
    rank = mm(mine_b, before)
    totals = mm(mine_b, jnp.ones((128, 128), bf16))
    upper = onehot(iota((lines, lines), 1) < iota((lines, lines), 0))
    offset = mm(upper, totals.astype(bf16))
    key = jnp.where(mine, (rank + offset).astype(i32), -1)
    value = (value + 1).astype(f32)
    found = []
    for s in spans(cap, 128):
        slots = iota((s.stop - s.start, 128), 0) + s.start
        total = jnp.zeros(slots.shape, f32)
        for r in range(lines):
            total = total + jnp.where(slots == key[r : r + 1, :], value[r : r + 1, :], 0.0)
        found.append(jnp.sum(total, axis=1, keepdims=True))
    return jnp.concatenate(found, axis=0).astype(i32) - 1


def pack_kernel(me_ref, owner_ref, row_ref, table_ref, tails_t_ref, srow_ref, picks):
    cap = srow_ref.shape[0]
    srow = slot_values(owner_ref[...], me_ref[0], row_ref[...], cap)
    srow_ref[...] = srow
    fill_picks(picks, srow)
    tails_t_ref[0] = mm(table_ref[...], picks[...], NT).astype(bf16)


def pack_tails(me, tail_owners, tail_row, table_t, cap):
    assert tail_row.shape[0] % 128 == 0
    return pl.pallas_call(
        pack_kernel,
        in_specs=[SMEM] + [VMEM] * 3,
        out_shape=[
            jax.ShapeDtypeStruct((1, table_t.shape[0], cap), bf16),
            jax.ShapeDtypeStruct((cap, 1), i32),
        ],
        scratch_shapes=[pltpu.VMEM((cap, table_t.shape[1]), bf16)],
        compiler_params=params(),
        cost_estimate=cost(1e9, 2e6),
        name="pack_tails",
    )(me, tail_owners.reshape(-1, 128), tail_row.reshape(-1, 128), table_t)


def found_kernel(cap, me_ref, table_ref, numbers_ref, found_ref, want_ref, scr, picks):
    count = numbers_ref.shape[0]
    owners = jnp.concatenate([field(numbers_ref, d, 0) for d in range(count)], axis=0)
    queries = owners.shape[1]
    mine = owners == me_ref[0]
    before = onehot(iota((queries, queries), 0) < iota((queries, queries), 1))
    rank = mm(onehot(mine), before)
    key = jnp.where(mine, rank.astype(i32), -1)
    slots = iota((cap, queries), 0)
    for d in range(count):
        code = (field(numbers_ref, d, 1) + 1).astype(f32)
        picked = jnp.where(slots == key[d : d + 1, :], code, 0.0)
        scr[d * cap : (d + 1) * cap, :] = jnp.sum(picked, axis=1, keepdims=True)
    want = scr[...].astype(i32) - 1
    want_ref[...] = want
    fill_picks(picks, want)
    found = mm(picks[...], table_ref[...], NT).astype(bf16)
    for d in range(count):
        found_ref[d] = found[d * cap : (d + 1) * cap, :]


def find_heads(me, numbers, table_t, cap):
    width = table_t.shape[0]
    count = numbers.shape[0]
    return pl.pallas_call(
        functools.partial(found_kernel, cap),
        in_specs=[SMEM] + [VMEM] * 2,
        out_shape=[
            jax.ShapeDtypeStruct((count, cap, width), bf16),
            jax.ShapeDtypeStruct((count * cap, 1), i32),
        ],
        scratch_shapes=[
            pltpu.VMEM((count * cap, 1), f32),
            pltpu.VMEM((count * cap, table_t.shape[1]), bf16),
        ],
        compiler_params=params(),
        cost_estimate=cost(3e8, 2e6),
        name="find_heads",
    )(me, table_t, numbers)


def slots_kernel(me_ref, owner_ref, row_ref, pos_ref, cand_ref, out_ref):
    cap = cand_ref.shape[1]
    owner = owner_ref[...]
    index = iota(owner.shape, 0) * 128 + iota(owner.shape, 1)
    for k in range(2):
        cand_ref[k] = slot_values(owner, me_ref[0] ^ k, index, cap)
    queries = pos_ref.shape[1]
    eye = iota((queries, queries), 0) == iota((queries, queries), 1)
    row = pos_ref[...].astype(f32)
    pos = jnp.sum(jnp.where(eye, row, 0.0), axis=1, keepdims=True).astype(i32)
    lanes = spans(row_ref.shape[1], 128)
    owner = jnp.zeros((queries, 128), f32)
    for c in lanes:
        here = iota((queries, 128), 1) + c.start
        owner = owner + jnp.where(here == pos, row_ref[:, c].astype(f32), 0.0)
    owner = jnp.sum(owner, axis=1, keepdims=True).astype(i32)
    ahead = jnp.zeros((queries, 128), f32)
    for c in lanes:
        here = iota((queries, 128), 1) + c.start
        ahead = ahead + jnp.where((row_ref[:, c] == owner) & (here < pos), 1.0, 0.0)
    ahead = jnp.sum(ahead, axis=1, keepdims=True).astype(i32)
    out_ref[...] = owner * cap + ahead


def slot_tables(me, tail_owners, pos_index, cap):
    return pl.pallas_call(
        slots_kernel,
        in_specs=[SMEM] + [VMEM] * 3,
        out_shape=[
            jax.ShapeDtypeStruct((2, cap, 1), i32),
            jax.ShapeDtypeStruct((pos_index.shape[0], 1), i32),
        ],
        compiler_params=params(),
        cost_estimate=cost(1e9, 1e6),
        name="slot_tables",
    )(me, tail_owners.reshape(-1, 128), tail_owners.reshape(1, -1), pos_index.reshape(1, -1))


def slot_picks(cap, slots, orow):
    count = slots // cap
    queries = orow.shape[1]
    member = iota((count, queries), 0) == orow
    before = onehot(iota((queries, queries), 0) < iota((queries, queries), 1))
    rank = mm(onehot(member), before)
    rank = jnp.sum(jnp.where(member, rank, 0.0), axis=0, keepdims=True).astype(i32)
    return onehot(iota((slots, queries), 0) == orow * cap + rank)


def front_kernel(
    cap, fetched_ref, orow_ref, rel_ref, rtab_ref, ext_ref, band_ref, w_ref,
    slope_ref, img_ref, qv_ref, vecs_ref, feats, acc, ext, pre,
):
    s = pl.program_id(0)
    width, queries = acc.shape

    @pl.when(s == 0)
    def _():
        rows = jnp.concatenate([fetched_ref[d] for d in range(fetched_ref.shape[0])], axis=0)
        pick = slot_picks(cap, rows.shape[0], orow_ref[...])
        hvt = mm(rows, pick, TN).astype(bf16)
        for d in range(vecs_ref.shape[0]):
            vecs_ref[d, 0] = hvt
        rels = rtab_ref.shape[1]
        rvt = mm(rtab_ref[...], onehot(iota((rels, queries), 0) == rel_ref[...])).astype(bf16)
        entry = iota((width, ext_ref.shape[1]), 0)
        image = mm(onehot(entry == ext_ref[...]), hvt, TN)
        image = image + mm(onehot(entry + width == ext_ref[...]), rvt, TN)
        ext[...] = image.astype(bf16)
        for g in range(GROUPS):
            img_ref[:, g * queries : (g + 1) * queries] = ext[g * BAND_OUT : g * BAND_OUT + LANES, :]
        acc[...] = jnp.zeros_like(acc)

    units = band_ref.shape[0] // BAND_OUT
    flat = GROUPS * BAND_OUT
    pre[...] = mm(band_ref[...], img_ref[...])
    for f in range(units):
        for g in range(GROUPS):
            rows = slice(f * flat + g * BAND_OUT, f * flat + (g + 1) * BAND_OUT)
            v = pre[f * BAND_OUT : (f + 1) * BAND_OUT, g * queries : (g + 1) * queries]
            sig = sigmoid(v)
            feats[rows, :] = (v * sig).astype(bf16)
            slope_ref[rows, :] = sig * (1.0 + v * (1.0 - sig))
    acc[...] += mm(w_ref[...], feats[...])

    @pl.when(s == pl.num_programs(0) - 1)
    def _():
        query = acc[...]
        qv_ref[...] = query.T.astype(bf16)
        qvt = query.astype(bf16)
        for d in range(vecs_ref.shape[0]):
            vecs_ref[d, 1] = qvt


def filter_block(filts):
    return math.gcd(filts, 8)


def front(fetched, orow, rel_row, rtab_t, ext, band, weight_t, cap, copies):
    queries = orow.shape[1]
    width, flat = weight_t.shape
    filts = band.shape[0] // BAND_OUT
    units = filter_block(filts)
    cols = flat // filts * units
    return pl.pallas_call(
        functools.partial(front_kernel, cap),
        grid=(filts // units,),
        in_specs=[
            whole(fetched.shape),
            whole(orow.shape),
            whole(rel_row.shape),
            whole(rtab_t.shape),
            whole(ext.shape),
            pl.BlockSpec((units * BAND_OUT, LANES), lambda s: (s, 0)),
            pl.BlockSpec((width, cols), lambda s: (0, s)),
        ],
        out_specs=[
            pl.BlockSpec((cols, queries), lambda s: (s, 0)),
            whole((LANES, GROUPS * queries)),
            whole((queries, width)),
            whole((copies, 2, width, queries)),
        ],
        out_shape=[
            jax.ShapeDtypeStruct((flat, queries), f32),
            jax.ShapeDtypeStruct((LANES, GROUPS * queries), bf16),
            jax.ShapeDtypeStruct((queries, width), bf16),
            jax.ShapeDtypeStruct((copies, 2, width, queries), bf16),
        ],
        scratch_shapes=[
            pltpu.VMEM((cols, queries), bf16),
            pltpu.VMEM((width, queries), f32),
            pltpu.VMEM((ext.shape[1], queries), bf16),
            pltpu.VMEM((units * BAND_OUT, GROUPS * queries), f32),
        ],
        compiler_params=params("arbitrary"),
        cost_estimate=cost(4e9, 2.4e7, 2.5e6),
        name="front",
    )(fetched, orow, rel_row, rtab_t, ext, band, weight_t)


def middle_kernel(
    cap, cand, pos_ref, qv_ref, orow_ref, ext_ref, bandt_ref, tails_hbm, w_hbm, slope_hbm,
    out_ref, sums_ref, qgt_ref, fgrad_hbm,
    tails, w, slope, fgrad, scores, grads, spread, ext, linear, tail_sems, w_sems, slope_sems, out_sems,
):
    owners, width, slots = tails.shape
    steps, _, cols = w.shape
    queries = qv_ref.shape[0]
    chunks = tail_sems.shape[0]
    blocks = owners // chunks
    part_rows = fgrad.shape[1]

    def tail_copy(i):
        span = pl.ds(i * blocks, blocks)
        return pltpu.make_async_copy(tails_hbm.at[span], tails.at[span], tail_sems.at[i])

    def w_copy(k):
        return pltpu.make_async_copy(w_hbm.at[:, pl.ds(k * cols, cols)], w.at[k], w_sems.at[k])

    def slope_copy(k):
        return pltpu.make_async_copy(slope_hbm.at[pl.ds(k * cols, cols)], slope.at[k], slope_sems.at[k])

    def out_copy(k):
        span = pl.ds(k * part_rows, part_rows)
        return pltpu.make_async_copy(fgrad.at[k], fgrad_hbm.at[span], out_sems.at[k])

    for i in range(chunks):
        tail_copy(i).start()
    for k in range(steps):
        w_copy(k).start()
        slope_copy(k).start()

    qv = qv_ref[...]
    total = jnp.zeros((queries, width), f32)
    for i in range(chunks):
        tail_copy(i).wait()
        for b in range(blocks):
            o = i * blocks + b
            block = tails[o]
            slot = o % scores.shape[0]
            scores[slot] = mm(qv, block)
            for r in spans(queries, 16):
                here = iota((r.stop - r.start, slots), 1) + o * slots
                target = jnp.where(here == pos_ref[r, :], 1.0 - smooth + smooth / cand, smooth / cand)
                grads[slot, r, :] = ((sigmoid(scores[slot, r, :]) - target) * loss_weight).astype(bf16)
            total = total + mm(grads[slot], block, NT)
    qgt = total.T.astype(bf16)
    for d in range(qgt_ref.shape[0]):
        qgt_ref[d] = qgt

    units = part_rows // BAND_OUT
    flat = GROUPS * BAND_OUT
    for k in range(steps):
        lin = linear.at[k % 2]
        w_copy(k).wait()
        lin[...] = mm(w[k], qgt, TN)
        slope_copy(k).wait()
        for f in range(units):
            for g in range(GROUPS):
                rows = slice(f * flat + g * BAND_OUT, f * flat + (g + 1) * BAND_OUT)
                part = slice(f * BAND_OUT, (f + 1) * BAND_OUT)
                lanes = slice(g * queries, (g + 1) * queries)
                fgrad[k, part, lanes] = (lin[rows, :] * slope[k, rows, :]).astype(bf16)
        out_copy(k).start()
        spread_k = mm(bandt_ref[:, k * part_rows : (k + 1) * part_rows], fgrad[k])
        if k == 0:
            spread[...] = spread_k
        else:
            spread[...] += spread_k

    ext[...] = jnp.zeros_like(ext)
    for g in range(GROUPS):
        ext[g * BAND_OUT : g * BAND_OUT + LANES, :] += spread[:, g * queries : (g + 1) * queries]
    entry = iota((width, ext.shape[0]), 0)
    high, low = split(ext[...])
    hpick = onehot(entry == ext_ref[...])
    rpick = onehot(entry + width == ext_ref[...])
    hgrad = (mm(hpick, high) + mm(hpick, low)).astype(bf16)
    sums_ref[0] = mm(rpick, high) + mm(rpick, low)
    count = out_ref.shape[0]
    pick = slot_picks(cap, count * cap, orow_ref[...])
    rows = mm(pick, hgrad, NT).astype(bf16)
    for d in range(count):
        out_ref[d] = rows[d * cap : (d + 1) * cap, :]
    for k in range(steps):
        out_copy(k).wait()


def middle(pos, qv, orow, ext, band_t, tails, weight_t, slope, cand, cap, copies):
    queries, width = qv.shape
    owners, _, slots = tails.shape
    flat = weight_t.shape[1]
    filts = band_t.shape[1] // BAND_OUT
    units = math.gcd(filts, 16)
    steps = filts // units
    cols = flat // steps
    rows = units * BAND_OUT
    blocks = math.gcd(owners, max(1, 2048 // slots))
    ring = min(owners, 4)
    hbm = pl.BlockSpec(memory_space=pl.ANY)
    return pl.pallas_call(
        functools.partial(middle_kernel, cap, cand),
        in_specs=[VMEM] * 5 + [hbm] * 3,
        out_specs=[VMEM] * 3 + [hbm],
        out_shape=[
            jax.ShapeDtypeStruct((owners, cap, width), bf16),
            jax.ShapeDtypeStruct((1, width, queries), f32),
            jax.ShapeDtypeStruct((copies, width, queries), bf16),
            jax.ShapeDtypeStruct((filts * BAND_OUT, GROUPS * queries), bf16),
        ],
        scratch_shapes=[
            pltpu.VMEM(tails.shape, bf16),
            pltpu.VMEM((steps, width, cols), bf16),
            pltpu.VMEM((steps, cols, queries), f32),
            pltpu.VMEM((steps, rows, GROUPS * queries), bf16),
            pltpu.VMEM((ring, queries, slots), f32),
            pltpu.VMEM((ring, queries, slots), bf16),
            pltpu.VMEM((LANES, GROUPS * queries), f32),
            pltpu.VMEM((ext.shape[1], queries), f32),
            pltpu.VMEM((2, cols, queries), f32),
            pltpu.SemaphoreType.DMA((owners // blocks,)),
            pltpu.SemaphoreType.DMA((steps,)),
            pltpu.SemaphoreType.DMA((steps,)),
            pltpu.SemaphoreType.DMA((steps,)),
        ],
        compiler_params=params(),
        cost_estimate=cost(6e9, 2.5e7, 5e5),
        name="middle",
    )(pos, qv, orow, ext, band_t, tails, weight_t, slope)


def half_taps(taps):
    return -(-taps // 32) * 16


def diag_kernel(taps, codes_ref, fgrad_ref, img_ref, rows_ref, out_ref, corr_ref):
    s = pl.program_id(0)
    units = fgrad_ref.shape[0] // BAND_OUT
    part = mm(fgrad_ref[...], img_ref[...], NT)
    corr_ref[pl.ds(s * units, units)] = part.reshape(units, BAND_OUT, LANES)

    @pl.when(s == pl.num_programs(0) - 1)
    def _():
        diag_sums(taps, codes_ref, corr_ref, rows_ref, out_ref)


def diag_sums(taps, codes_ref, corr_ref, rows_ref, out_ref):
    filts = corr_ref.shape[0]
    cap, width = rows_ref.shape[1:]
    half = half_taps(taps)
    total = jnp.zeros((2 * half, filts), f32)
    for j in range(IMG):
        rows = corr_ref[:, j, :]
        for di in range(1, BAND):
            rows = rows + pltpu.roll(corr_ref[:, di * IMG + j, :], LANES - di * IMG, 1)
        pick = onehot(iota((2 * half, LANES), 0) == codes_ref[j : j + 1, :])
        high, low = split(rows)
        total = total + mm(pick, high, NT) + mm(pick, low, NT)
    packed = jnp.zeros((half, width), f32)
    for k in range(2):
        for i, piece in enumerate(split(total[k * half : (k + 1) * half, :])):
            place = onehot(iota((filts, width), 1) == iota((filts, width), 0) + (2 * k + i) * filts)
            packed = packed + mm(piece, place)
    packed = packed.astype(bf16)
    for d in range(out_ref.shape[0]):
        out_ref[d, :cap, :] = rows_ref[d]
        out_ref[d, cap:, :] = packed


def filter_sums(fgrad, img, codes, rows, taps):
    count, cap, width = rows.shape
    filts = fgrad.shape[0] // BAND_OUT
    units = filter_block(filts)
    assert 4 * filts <= width
    out = (count, cap + half_taps(taps), width)
    return pl.pallas_call(
        functools.partial(diag_kernel, taps),
        grid=(filts // units,),
        in_specs=[
            whole(codes.shape),
            pl.BlockSpec((units * BAND_OUT, fgrad.shape[1]), lambda s: (s, 0)),
            whole(img.shape),
            whole(rows.shape),
        ],
        out_specs=whole(out),
        out_shape=jax.ShapeDtypeStruct(out, bf16),
        scratch_shapes=[pltpu.VMEM((filts, BAND_OUT, LANES), f32)],
        compiler_params=params("arbitrary"),
        cost_estimate=cost(2e9, 6e6),
        name="filter_sums",
    )(codes, fgrad, img, rows)


def tail_kernel(
    cand, ids_ref, tails_ref, mate_ref, scand_ref, numbers_ref, vecs_ref, own_ref, other_ref, scores, grads
):
    cap = own_ref.shape[1]
    tails = jnp.concatenate([ref[0].astype(f32).T for ref in (tails_ref, mate_ref)], axis=0).astype(bf16)
    scand = jnp.concatenate([scand_ref[0], scand_ref[1]], axis=0)
    own = jnp.zeros(own_ref.shape, f32)
    other = jnp.zeros(own_ref.shape, f32)
    for i, group in enumerate(pairs(vecs_ref.shape[0])):
        qvt = beside(vecs_ref[p, 1] for p in group)
        pos = beside(field(numbers_ref, 2 * p + ids_ref[2], 3) for p in group)
        score, grad = scores.at[i % 2], grads.at[i % 2]
        score[...] = mm(tails, qvt)
        for r in spans(2 * cap, 64):
            target = jnp.where(scand[r, :] == pos, 1.0 - smooth + smooth / cand, smooth / cand)
            grad[r, :] = ((sigmoid(score[r, :]) - target) * loss_weight).astype(bf16)
        own = own + mm(qvt, grad[:cap, :], NT)
        other = other + mm(qvt, grad[cap:, :], NT)
    own_ref[...] = own
    other_ref[...] = other


def tail_part(ids, tails, scand, numbers, vecs, cand):
    _, width, cap = tails.shape
    half = jax.ShapeDtypeStruct((width, cap), f32)
    return pl.pallas_call(
        functools.partial(tail_kernel, cand),
        grid_spec=pltpu.PrefetchScalarGridSpec(
            num_scalar_prefetch=1,
            grid=(1,),
            in_specs=[
                pl.BlockSpec((1, width, cap), lambda s, ids: (ids[0], 0, 0)),
                pl.BlockSpec((1, width, cap), lambda s, ids: (ids[1], 0, 0)),
                whole(scand.shape),
                whole(numbers.shape),
                whole(vecs.shape),
            ],
            out_specs=[whole(half.shape)] * 2,
            scratch_shapes=[
                pltpu.VMEM((2, 2 * cap, 2 * vecs.shape[3]), f32),
                pltpu.VMEM((2, 2 * cap, 2 * vecs.shape[3]), bf16),
            ],
        ),
        out_shape=[half, half],
        compiler_params=params("arbitrary"),
        cost_estimate=cost(2e9, 3e6, 1e6),
        name="tail_grad",
    )(ids, tails, tails, scand, numbers, vecs)


def feats_kernel(
    ids_ref, rtab_ref, ext_ref, band_ref, mate_ref, numbers_ref, vecs_ref, out_ref, hpick, rpick, rels_hot, ext, pre
):
    width, rels = rtab_ref.shape
    units = band_ref.shape[0] // BAND_OUT
    flat = GROUPS * BAND_OUT
    cols = units * flat
    entry = iota((width, ext_ref.shape[1]), 0)
    hpick[...] = jnp.where(entry == ext_ref[...], 1.0, 0.0).T.astype(bf16)
    rpick[...] = jnp.where(entry + width == ext_ref[...], 1.0, 0.0).T.astype(bf16)
    queries = vecs_ref.shape[3]
    for i, group in enumerate(pairs(vecs_ref.shape[0])):
        hvt = beside(vecs_ref[p, 0] for p in group)
        rel = beside(field(numbers_ref, 2 * p + ids_ref[2], 2) for p in group)
        for r in spans(rels, 64):
            rels_hot[r, :] = onehot(iota((r.stop - r.start, rel.shape[1]), 0) + r.start == rel)
        rvt = mm(rtab_ref[...], rels_hot[...]).astype(bf16)
        image = ext.at[i % 2]
        image[...] = (mm(hpick[...], hvt) + mm(rpick[...], rvt)).astype(bf16)
        lanes = slice(group[0] * queries, (group[-1] + 1) * queries)
        for k, source in enumerate((band_ref, mate_ref)):
            for g in range(GROUPS):
                slot = (k * GROUPS + g) % 2
                pre[slot] = mm(source[...], image[g * BAND_OUT : g * BAND_OUT + LANES, :])
                for f in range(units):
                    v = pre[slot, f * BAND_OUT : (f + 1) * BAND_OUT, :]
                    first = k * cols + f * flat + g * BAND_OUT
                    out_ref[first : first + BAND_OUT, lanes] = (v * sigmoid(v)).astype(bf16)


def column_feats(ids, rtab_t, ext, band, numbers, vecs, cols):
    width, rels = rtab_t.shape
    unit = cols // GROUPS
    gathered, _, _, queries = vecs.shape
    return pl.pallas_call(
        feats_kernel,
        grid_spec=pltpu.PrefetchScalarGridSpec(
            num_scalar_prefetch=1,
            grid=(1,),
            in_specs=[
                whole(rtab_t.shape),
                whole(ext.shape),
                pl.BlockSpec((unit, LANES), lambda s, ids: (ids[0], 0)),
                pl.BlockSpec((unit, LANES), lambda s, ids: (ids[1], 0)),
                whole(numbers.shape),
                whole(vecs.shape),
            ],
            out_specs=whole((2 * cols, gathered * queries)),
            scratch_shapes=[
                pltpu.VMEM((ext.shape[1], width), bf16),
                pltpu.VMEM((ext.shape[1], width), bf16),
                pltpu.VMEM((rels, 2 * queries), bf16),
                pltpu.VMEM((2, ext.shape[1], 2 * queries), bf16),
                pltpu.VMEM((2, unit, 2 * queries), f32),
            ],
        ),
        out_shape=jax.ShapeDtypeStruct((2 * cols, gathered * queries), bf16),
        compiler_params=params("arbitrary"),
        cost_estimate=cost(5e9, 6e6, 2.5e6),
        name="column_feats",
    )(ids, rtab_t, ext, band, band, numbers, vecs)


def proj_kernel(feats_ref, grads_ref, own_ref, other_ref):
    cols = own_ref.shape[1]
    qgt = beside(grads_ref[p] for p in range(grads_ref.shape[0]))
    own_ref[...] = mm(qgt, feats_ref[:cols, :], NT)
    other_ref[...] = mm(qgt, feats_ref[cols:, :], NT)


def proj_part(feats, grads):
    half = jax.ShapeDtypeStruct((grads.shape[1], feats.shape[0] // 2), f32)
    return pl.pallas_call(
        proj_kernel,
        out_shape=[half, half],
        compiler_params=params(),
        cost_estimate=cost(1e9, 8e6),
        name="proj_grad",
    )(feats, grads)


def proj_columns(first, cols, filters, chequer_perm, relation_table, numbers, heads, grads):
    ks = filters.shape[-1]
    rim = ks // 2
    flat = IMG * IMG
    column = first + jnp.arange(cols, dtype=i32)
    f = column // flat
    i = (column % flat) // IMG
    j = column % IMG
    spot = jnp.arange(flat, dtype=i32)
    a = (spot[:, None] // IMG - i[None, :] + rim) % IMG
    b = (spot[:, None] % IMG - j[None, :] + rim) % IMG
    tap = filters[f[None, :], jnp.minimum(a, ks - 1), jnp.minimum(b, ks - 1)]
    matrix = jnp.where((a < ks) & (b < ks), tap, jnp.zeros((), bf16))
    width = heads.shape[1]
    head = heads.transpose(0, 2, 1).reshape(-1, width)
    qg = grads.transpose(0, 2, 1).reshape(-1, width)
    joined = jnp.concatenate([head, relation_table[numbers[:, 2].reshape(-1)]], axis=1)
    pre = mm(joined[:, chequer_perm], matrix)
    return mm(qg, (pre * sigmoid(pre)).astype(bf16), TN)


def rel_kernel(numbers_ref, sums_ref, rel_ref, picks):
    width, rels = rel_ref.shape
    queries = sums_ref.shape[2]
    total = None
    for block in spans(sums_ref.shape[0], picks.shape[1] // queries):
        members = range(block.start, block.stop)
        for i, p in enumerate(members):
            rel = field(numbers_ref, p, 2)
            for r in spans(rels, 128):
                here = iota((r.stop - r.start, queries), 0) + r.start
                picks[r, i * queries : (i + 1) * queries] = onehot(here == rel)
        parts = jnp.concatenate(split(beside(sums_ref[p] for p in members)), axis=0)
        part = mm(parts, picks[...], NT)
        total = part if total is None else total + part
    rel_ref[...] = total[:width, :] + total[width:, :]


def rel_part(numbers, sums, rels):
    count, width, queries = sums.shape
    return pl.pallas_call(
        rel_kernel,
        out_shape=jax.ShapeDtypeStruct((width, rels), f32),
        scratch_shapes=[pltpu.VMEM((rels, math.gcd(count, 16) * queries), bf16)],
        compiler_params=params(),
        cost_estimate=cost(2e9, 3e6),
        name="rel_grad",
    )(numbers, sums)


def entity_kernel(cap, want_ref, srow_ref, own_ref, recv_ref, incoming_ref, out_ref, filt_ref):
    rows = out_ref.shape[1]
    count, _, width = incoming_ref.shape
    half, filts = filt_ref.shape[0] // 2, filt_ref.shape[1]
    grads = jnp.concatenate([incoming_ref[d, :cap, :] for d in range(count)], axis=0)
    turned = grads.astype(f32).T.astype(bf16)
    high, low = split(own_ref[...] + recv_ref[...])
    for c in spans(rows, 256):
        here = iota((want_ref.shape[0], c.stop - c.start), 1) + c.start
        total = mm(turned, onehot(here == want_ref[...]))
        here = iota((srow_ref.shape[0], c.stop - c.start), 1) + c.start
        pick = onehot(here == srow_ref[...])
        out_ref[:, c] = total + mm(high, pick) + mm(low, pick)
    packed = incoming_ref[0, cap:, :].astype(f32)
    for d in range(1, count):
        packed = packed + incoming_ref[d, cap:, :].astype(f32)
    high, low = split(packed)
    for k in range(2):
        lane = iota((width, filts), 0) - 2 * k * filts
        unit = iota((width, filts), 1)
        place = onehot((lane == unit) | (lane == unit + filts))
        filt_ref[k * half : (k + 1) * half, :] = mm(high, place) + mm(low, place)


def entity_sum(want, srow, own, recv, incoming, rows, cap, filts):
    half = incoming.shape[1] - cap
    return pl.pallas_call(
        functools.partial(entity_kernel, cap),
        out_shape=[
            jax.ShapeDtypeStruct((own.shape[0], rows), f32),
            jax.ShapeDtypeStruct((2 * half, filts), f32),
        ],
        compiler_params=params(),
        cost_estimate=cost(1.5e9, 4e6),
        name="entity_grad",
    )(want, srow, own, recv, incoming)


def shards(
    entity_table,
    relation_table,
    filters,
    proj_weight,
    chequer_perm,
    head_owner,
    head_row,
    rel_ids,
    pos_index,
    tail_owner,
    tail_row,
):
    count = lax.axis_size("shard")
    me = lax.axis_index("shard")
    assert count % 2 == 0
    direct = count <= 16
    queries = head_row.shape[0]
    cand = tail_row.shape[0]
    rows, width = entity_table.shape
    rels = relation_table.shape[0]
    filts, ks, _ = filters.shape
    head_cap = 2 * queries // count
    tail_cap = 2 * cand // count
    same_core = [list(range(c, count, 2)) for c in range(2)]
    copies = count // 2 if direct else 1

    def swap(x):
        return lax.ppermute(x, "shard", [(d, d ^ 1) for d in range(count)])

    def exchange(x):
        return lax.all_to_all(x, "shard", split_axis=0, concat_axis=0, tiled=True)

    def gather_core(x):
        if direct:
            return lax.all_to_all(
                x, "shard", split_axis=0, concat_axis=0, axis_index_groups=same_core, tiled=True
            )
        return lax.all_gather(x, "shard", axis=0, axis_index_groups=same_core, tiled=True)

    me1 = me.reshape(1)
    heads = head_owner[:, 0]
    tail_owners = tail_owner[:, 0]
    table_t, rtab_t, weight_t = entity_table.T, relation_table.T, proj_weight.T
    numbers = jnp.concatenate([heads, head_row, rel_ids, pos_index])
    numbers = exchange(jnp.broadcast_to(numbers, (count, 1, 4 * queries)))

    ids = jnp.stack([me, me ^ 1, me & 1])
    tails_t, slot_row = pack_tails(me1, tail_owners, tail_row, table_t, tail_cap)
    all_tails = lax.all_gather(tails_t, "shard", axis=0, tiled=True)
    scand, pos = slot_tables(me1, tail_owners, pos_index, tail_cap)
    found, want = find_heads(me1, numbers, table_t, head_cap)
    fetched = exchange(found)

    codes = jnp.asarray(band_codes(ks))
    band, band_t = build_band(filters, codes)
    extra = BAND_OUT * (GROUPS - 1) + LANES - IMG * IMG - BAND_OUT
    ext = jnp.concatenate([chequer_perm[-BAND_OUT:], chequer_perm, chequer_perm[:extra]])[None]
    orow = heads[None, :]
    slope, img, qv, vecs = front(
        fetched, orow, rel_ids[None, :], rtab_t, ext, band, weight_t, head_cap, copies
    )
    core_vecs = gather_core(vecs)

    outgoing, sums, qgt, fgrad = middle(
        pos, qv, orow, ext, band_t, all_tails, weight_t, slope, cand, head_cap, copies
    )
    all_sums = lax.all_gather(sums, "shard", axis=0, tiled=True)
    qgt, core_vecs = lax.optimization_barrier((qgt, core_vecs))
    core_qgt = gather_core(qgt)
    outgoing = filter_sums(fgrad, img, codes, outgoing, ks * ks)
    outgoing, core_qgt = lax.optimization_barrier((outgoing, core_qgt))
    incoming = exchange(outgoing)

    own, other = tail_part(ids, all_tails, scand, numbers, core_vecs, cand)
    entity_grad, filter_grad = entity_sum(
        want, slot_row, own, swap(other), incoming, rows, head_cap, filts
    )
    filter_grad = filter_grad[: ks * ks].T.reshape(filts, ks, ks)

    cols = filts * IMG * IMG // count
    if direct and cols % (IMG * IMG) == 0:
        feats = column_feats(ids, rtab_t, ext, band, numbers, core_vecs, cols)
        own, other = proj_part(feats, core_qgt)
    else:
        core_numbers = lax.dynamic_index_in_dim(
            numbers.reshape(count // 2, 2, 4, queries), me & 1, 1, keepdims=False
        )
        own, other = (
            proj_columns(
                d * cols, cols, filters, chequer_perm, relation_table,
                core_numbers, core_vecs[:, 0], core_qgt,
            )
            for d in (me, me ^ 1)
        )
    proj_grad = (own + swap(other)).T

    relation_grad = rel_part(numbers, all_sums, rels).T
    return (entity_grad.T, relation_grad, filter_grad, proj_grad)


def solution(mesh):
    placed = (
        P("shard", None),
        P(),
        P(),
        P(),
        P(),
        P(("parts", "shard"), None),
        P(("parts", "shard")),
        P(("parts", "shard")),
        P(("parts", "shard")),
        P("parts", None),
        P("parts"),
    )
    return jax.shard_map(
        shards,
        mesh=mesh,
        in_specs=placed,
        out_specs=(
            P(("parts", "shard"), None),
            P("parts", None),
            P("parts", None, None),
            P(("parts", "shard"), None),
        ),
        check_vma=False,
    )
```

```python
import functools
import math

import jax
import jax.numpy as jnp
import numpy as np
from jax import lax
from jax.experimental import pallas as pl
from jax.experimental.pallas import tpu as pltpu
from jax.sharding import PartitionSpec as P

IMG = 20
BAND = 4
GROUPS = IMG // BAND
BAND_OUT = BAND * IMG
LANES = 256

loss_weight = 0.015625
smooth = 0.1

f32 = jnp.float32
bf16 = jnp.bfloat16
i32 = jnp.int32

NN = (((1,), (0,)), ((), ()))
NT = (((1,), (1,)), ((), ()))
TN = (((0,), (0,)), ((), ()))


def mm(a, b, dims=NN):
    return lax.dot_general(a, b, dims, preferred_element_type=f32)


def iota(shape, axis):
    return lax.broadcasted_iota(i32, shape, axis)


def onehot(mask):
    return jnp.where(mask, 1.0, 0.0).astype(bf16)


def split(value):
    high = value.astype(bf16)
    return high, (value - high.astype(f32)).astype(bf16)


def sigmoid(v):
    return 0.5 * jnp.tanh(0.5 * v) + 0.5


def params(*semantics):
    return pltpu.CompilerParams(
        dimension_semantics=semantics or None, vmem_limit_bytes=60 << 20
    )


def cost(flops, nbytes, trans=0):
    return pl.CostEstimate(flops=int(flops), bytes_accessed=int(nbytes), transcendentals=int(trans))


def whole(shape):
    return pl.BlockSpec(shape, lambda *_: (0,) * len(shape))


SMEM = pl.BlockSpec(memory_space=pltpu.SMEM)


def band_codes(ks):
    codes = np.full((IMG, LANES), -1, np.int32)
    for j in range(IMG):
        for r in range(ks):
            for x in range(IMG):
                b = (x - j + ks // 2) % IMG
                if b < ks:
                    codes[j, r * IMG + x] = r * ks + b
    return codes


def band_kernel(codes_ref, filt_ref, out_ref, out_t_ref, scr):
    count, taps = filt_ref.shape
    filt = filt_ref[...]
    for j in range(IMG):
        pick = onehot(iota((taps, LANES), 0) == codes_ref[j : j + 1, :])
        row = mm(filt, pick)
        for di in range(BAND):
            scr[:, di * IMG + j, :] = row if di == 0 else pltpu.roll(row, di * IMG, 1)
    full = scr[...].reshape(count * BAND_OUT, LANES)
    out_ref[...] = full.astype(bf16)
    out_t_ref[...] = full.T.astype(bf16)


def build_band(filters, codes):
    count, ks, _ = filters.shape
    return pl.pallas_call(
        band_kernel,
        out_shape=[
            jax.ShapeDtypeStruct((count * BAND_OUT, LANES), bf16),
            jax.ShapeDtypeStruct((LANES, count * BAND_OUT), bf16),
        ],
        scratch_shapes=[pltpu.VMEM((count, BAND_OUT, LANES), f32)],
        compiler_params=params(),
        cost_estimate=cost(4e7, 4e6),
        name="band",
    )(codes, filters.reshape(count, ks * ks))


VMEM = pl.BlockSpec(memory_space=pltpu.VMEM)


def pairs(count):
    step = 2 if count % 2 == 0 else 1
    return [range(i, i + step) for i in range(0, count, step)]


def beside(blocks):
    return jnp.concatenate(list(blocks), axis=1)


def spans(size, step):
    return [slice(i, min(i + step, size)) for i in range(0, size, step)]


def fill_picks(ref, index):
    rows, lanes = ref.shape
    for r in spans(rows, 64):
        for c in spans(lanes, 256):
            here = iota((r.stop - r.start, c.stop - c.start), 1) + c.start
            ref[r, c] = onehot(here == index[r, :])


def field(ref, d, k):
    queries = ref.shape[2] // 4
    return ref[d, :, k * queries : (k + 1) * queries]


def slot_values(owner, device, value, cap):
    lines = owner.shape[0]
    mine = owner == device
    mine_b = onehot(mine)
    before = onehot(iota((128, 128), 0) < iota((128, 128), 1))
    rank = mm(mine_b, before)
    totals = mm(mine_b, jnp.ones((128, 128), bf16))
    upper = onehot(iota((lines, lines), 1) < iota((lines, lines), 0))
    offset = mm(upper, totals.astype(bf16))
    key = jnp.where(mine, (rank + offset).astype(i32), -1)
    value = (value + 1).astype(f32)
    found = []
    for s in spans(cap, 128):
        slots = iota((s.stop - s.start, 128), 0) + s.start
        total = jnp.zeros(slots.shape, f32)
        for r in range(lines):
            total = total + jnp.where(slots == key[r : r + 1, :], value[r : r + 1, :], 0.0)
        found.append(jnp.sum(total, axis=1, keepdims=True))
    return jnp.concatenate(found, axis=0).astype(i32) - 1


def pack_kernel(me_ref, owner_ref, row_ref, table_ref, tails_t_ref, srow_ref, picks):
    cap = srow_ref.shape[0]
    srow = slot_values(owner_ref[...], me_ref[0], row_ref[...], cap)
    srow_ref[...] = srow
    fill_picks(picks, srow)
    tails_t_ref[0] = mm(table_ref[...], picks[...], NT).astype(bf16)


def pack_tails(me, tail_owners, tail_row, table_t, cap):
    assert tail_row.shape[0] % 128 == 0
    return pl.pallas_call(
        pack_kernel,
        in_specs=[SMEM] + [VMEM] * 3,
        out_shape=[
            jax.ShapeDtypeStruct((1, table_t.shape[0], cap), bf16),
            jax.ShapeDtypeStruct((cap, 1), i32),
        ],
        scratch_shapes=[pltpu.VMEM((cap, table_t.shape[1]), bf16)],
        compiler_params=params(),
        cost_estimate=cost(1e9, 2e6),
        name="pack_tails",
    )(me, tail_owners.reshape(-1, 128), tail_row.reshape(-1, 128), table_t)


def found_kernel(cap, me_ref, table_ref, numbers_ref, found_ref, want_ref, scr, picks):
    count = numbers_ref.shape[0]
    owners = jnp.concatenate([field(numbers_ref, d, 0) for d in range(count)], axis=0)
    queries = owners.shape[1]
    mine = owners == me_ref[0]
    before = onehot(iota((queries, queries), 0) < iota((queries, queries), 1))
    rank = mm(onehot(mine), before)
    key = jnp.where(mine, rank.astype(i32), -1)
    slots = iota((cap, queries), 0)
    for d in range(count):
        code = (field(numbers_ref, d, 1) + 1).astype(f32)
        picked = jnp.where(slots == key[d : d + 1, :], code, 0.0)
        scr[d * cap : (d + 1) * cap, :] = jnp.sum(picked, axis=1, keepdims=True)
    want = scr[...].astype(i32) - 1
    want_ref[...] = want
    fill_picks(picks, want)
    found = mm(picks[...], table_ref[...], NT).astype(bf16)
    for d in range(count):
        found_ref[d] = found[d * cap : (d + 1) * cap, :]


def find_heads(me, numbers, table_t, cap):
    width = table_t.shape[0]
    count = numbers.shape[0]
    return pl.pallas_call(
        functools.partial(found_kernel, cap),
        in_specs=[SMEM] + [VMEM] * 2,
        out_shape=[
            jax.ShapeDtypeStruct((count, cap, width), bf16),
            jax.ShapeDtypeStruct((count * cap, 1), i32),
        ],
        scratch_shapes=[
            pltpu.VMEM((count * cap, 1), f32),
            pltpu.VMEM((count * cap, table_t.shape[1]), bf16),
        ],
        compiler_params=params(),
        cost_estimate=cost(3e8, 2e6),
        name="find_heads",
    )(me, table_t, numbers)


def slots_kernel(me_ref, owner_ref, row_ref, pos_ref, cand_ref, out_ref):
    cap = cand_ref.shape[1]
    owner = owner_ref[...]
    index = iota(owner.shape, 0) * 128 + iota(owner.shape, 1)
    for k in range(2):
        cand_ref[k] = slot_values(owner, me_ref[0] ^ k, index, cap)
    queries = pos_ref.shape[1]
    eye = iota((queries, queries), 0) == iota((queries, queries), 1)
    row = pos_ref[...].astype(f32)
    pos = jnp.sum(jnp.where(eye, row, 0.0), axis=1, keepdims=True).astype(i32)
    lanes = spans(row_ref.shape[1], 128)
    owner = jnp.zeros((queries, 128), f32)
    for c in lanes:
        here = iota((queries, 128), 1) + c.start
        owner = owner + jnp.where(here == pos, row_ref[:, c].astype(f32), 0.0)
    owner = jnp.sum(owner, axis=1, keepdims=True).astype(i32)
    ahead = jnp.zeros((queries, 128), f32)
    for c in lanes:
        here = iota((queries, 128), 1) + c.start
        ahead = ahead + jnp.where((row_ref[:, c] == owner) & (here < pos), 1.0, 0.0)
    ahead = jnp.sum(ahead, axis=1, keepdims=True).astype(i32)
    out_ref[...] = owner * cap + ahead


def slot_tables(me, tail_owners, pos_index, cap):
    return pl.pallas_call(
        slots_kernel,
        in_specs=[SMEM] + [VMEM] * 3,
        out_shape=[
            jax.ShapeDtypeStruct((2, cap, 1), i32),
            jax.ShapeDtypeStruct((pos_index.shape[0], 1), i32),
        ],
        compiler_params=params(),
        cost_estimate=cost(1e9, 1e6),
        name="slot_tables",
    )(me, tail_owners.reshape(-1, 128), tail_owners.reshape(1, -1), pos_index.reshape(1, -1))


def slot_picks(cap, slots, orow):
    count = slots // cap
    queries = orow.shape[1]
    member = iota((count, queries), 0) == orow
    before = onehot(iota((queries, queries), 0) < iota((queries, queries), 1))
    rank = mm(onehot(member), before)
    rank = jnp.sum(jnp.where(member, rank, 0.0), axis=0, keepdims=True).astype(i32)
    return onehot(iota((slots, queries), 0) == orow * cap + rank)


def front_kernel(
    cap, fetched_ref, orow_ref, rel_ref, rtab_ref, ext_ref, band_ref, w_ref,
    slope_ref, img_ref, qv_ref, vecs_ref, feats, acc, ext, pre,
):
    s = pl.program_id(0)
    width, queries = acc.shape

    @pl.when(s == 0)
    def _():
        rows = jnp.concatenate([fetched_ref[d] for d in range(fetched_ref.shape[0])], axis=0)
        pick = slot_picks(cap, rows.shape[0], orow_ref[...])
        hvt = mm(rows, pick, TN).astype(bf16)
        for d in range(vecs_ref.shape[0]):
            vecs_ref[d, 0] = hvt
        rels = rtab_ref.shape[1]
        rvt = mm(rtab_ref[...], onehot(iota((rels, queries), 0) == rel_ref[...])).astype(bf16)
        entry = iota((width, ext_ref.shape[1]), 0)
        image = mm(onehot(entry == ext_ref[...]), hvt, TN)
        image = image + mm(onehot(entry + width == ext_ref[...]), rvt, TN)
        ext[...] = image.astype(bf16)
        for g in range(GROUPS):
            img_ref[:, g * queries : (g + 1) * queries] = ext[g * BAND_OUT : g * BAND_OUT + LANES, :]
        acc[...] = jnp.zeros_like(acc)

    units = band_ref.shape[0] // BAND_OUT
    flat = GROUPS * BAND_OUT
    pre[...] = mm(band_ref[...], img_ref[...])
    for f in range(units):
        for g in range(GROUPS):
            rows = slice(f * flat + g * BAND_OUT, f * flat + (g + 1) * BAND_OUT)
            v = pre[f * BAND_OUT : (f + 1) * BAND_OUT, g * queries : (g + 1) * queries]
            sig = sigmoid(v)
            feats[rows, :] = (v * sig).astype(bf16)
            slope_ref[rows, :] = sig * (1.0 + v * (1.0 - sig))
    acc[...] += mm(w_ref[...], feats[...])

    @pl.when(s == pl.num_programs(0) - 1)
    def _():
        query = acc[...]
        qv_ref[...] = query.T.astype(bf16)
        qvt = query.astype(bf16)
        for d in range(vecs_ref.shape[0]):
            vecs_ref[d, 1] = qvt


def filter_block(filts):
    return math.gcd(filts, 8)


def front(fetched, orow, rel_row, rtab_t, ext, band, weight_t, cap, copies):
    queries = orow.shape[1]
    width, flat = weight_t.shape
    filts = band.shape[0] // BAND_OUT
    units = filter_block(filts)
    cols = flat // filts * units
    return pl.pallas_call(
        functools.partial(front_kernel, cap),
        grid=(filts // units,),
        in_specs=[
            whole(fetched.shape),
            whole(orow.shape),
            whole(rel_row.shape),
            whole(rtab_t.shape),
            whole(ext.shape),
            pl.BlockSpec((units * BAND_OUT, LANES), lambda s: (s, 0)),
            pl.BlockSpec((width, cols), lambda s: (0, s)),
        ],
        out_specs=[
            pl.BlockSpec((cols, queries), lambda s: (s, 0)),
            whole((LANES, GROUPS * queries)),
            whole((queries, width)),
            whole((copies, 2, width, queries)),
        ],
        out_shape=[
            jax.ShapeDtypeStruct((flat, queries), f32),
            jax.ShapeDtypeStruct((LANES, GROUPS * queries), bf16),
            jax.ShapeDtypeStruct((queries, width), bf16),
            jax.ShapeDtypeStruct((copies, 2, width, queries), bf16),
        ],
        scratch_shapes=[
            pltpu.VMEM((cols, queries), bf16),
            pltpu.VMEM((width, queries), f32),
            pltpu.VMEM((ext.shape[1], queries), bf16),
            pltpu.VMEM((units * BAND_OUT, GROUPS * queries), f32),
        ],
        compiler_params=params("arbitrary"),
        cost_estimate=cost(4e9, 2.4e7, 2.5e6),
        name="front",
    )(fetched, orow, rel_row, rtab_t, ext, band, weight_t)


def middle_kernel(
    cap, cand, pos_ref, qv_ref, orow_ref, ext_ref, bandt_hbm, tails_hbm, w_hbm, slope_hbm,
    out_ref, sums_ref, qgt_ref, fgrad_hbm,
    bandt, tails, w, slope, fgrad, scores, grads, spread, ext, linear,
    band_sem, tail_sems, w_sems, slope_sems, out_sems,
):
    owners, width, slots = tails.shape
    steps, _, cols = w.shape
    queries = qv_ref.shape[0]
    chunks = tail_sems.shape[0]
    blocks = owners // chunks
    part_rows = fgrad.shape[1]

    def tail_copy(i):
        span = pl.ds(i * blocks, blocks)
        return pltpu.make_async_copy(tails_hbm.at[span], tails.at[span], tail_sems.at[i])

    def w_copy(k):
        return pltpu.make_async_copy(w_hbm.at[:, pl.ds(k * cols, cols)], w.at[k], w_sems.at[k])

    def slope_copy(k):
        return pltpu.make_async_copy(slope_hbm.at[pl.ds(k * cols, cols)], slope.at[k], slope_sems.at[k])

    def out_copy(k):
        span = pl.ds(k * part_rows, part_rows)
        return pltpu.make_async_copy(fgrad.at[k], fgrad_hbm.at[span], out_sems.at[k])

    for i in range(chunks):
        tail_copy(i).start()
    band_copy = pltpu.make_async_copy(bandt_hbm, bandt, band_sem)
    for k in range(steps):
        w_copy(k).start()
        slope_copy(k).start()
        if k == 0:
            band_copy.start()

    qv = qv_ref[...]
    total = jnp.zeros((queries, width), f32)
    for i in range(chunks):
        tail_copy(i).wait()
        for b in range(blocks):
            o = i * blocks + b
            block = tails[o]
            slot = o % scores.shape[0]
            scores[slot] = mm(qv, block)
            for r in spans(queries, 16):
                here = iota((r.stop - r.start, slots), 1) + o * slots
                target = jnp.where(here == pos_ref[r, :], 1.0 - smooth + smooth / cand, smooth / cand)
                grads[slot, r, :] = ((sigmoid(scores[slot, r, :]) - target) * loss_weight).astype(bf16)
            total = total + mm(grads[slot], block, NT)
    qgt = total.T.astype(bf16)
    for d in range(qgt_ref.shape[0]):
        qgt_ref[d] = qgt

    units = part_rows // BAND_OUT
    flat = GROUPS * BAND_OUT
    for k in range(steps):
        lin = linear.at[k % 2]
        w_copy(k).wait()
        lin[...] = mm(w[k], qgt, TN)
        slope_copy(k).wait()
        for f in range(units):
            for g in range(GROUPS):
                rows = slice(f * flat + g * BAND_OUT, f * flat + (g + 1) * BAND_OUT)
                part = slice(f * BAND_OUT, (f + 1) * BAND_OUT)
                lanes = slice(g * queries, (g + 1) * queries)
                fgrad[k, part, lanes] = (lin[rows, :] * slope[k, rows, :]).astype(bf16)
        out_copy(k).start()
        if k == 0:
            band_copy.wait()
        spread_k = mm(bandt[:, k * part_rows : (k + 1) * part_rows], fgrad[k])
        if k == 0:
            spread[...] = spread_k
        else:
            spread[...] += spread_k

    ext[...] = jnp.zeros_like(ext)
    for g in range(GROUPS):
        ext[g * BAND_OUT : g * BAND_OUT + LANES, :] += spread[:, g * queries : (g + 1) * queries]
    entry = iota((width, ext.shape[0]), 0)
    high, low = split(ext[...])
    hpick = onehot(entry == ext_ref[...])
    rpick = onehot(entry + width == ext_ref[...])
    hgrad = (mm(hpick, high) + mm(hpick, low)).astype(bf16)
    sums_ref[0] = mm(rpick, high) + mm(rpick, low)
    count = out_ref.shape[0]
    pick = slot_picks(cap, count * cap, orow_ref[...])
    rows = mm(pick, hgrad, NT).astype(bf16)
    for d in range(count):
        out_ref[d] = rows[d * cap : (d + 1) * cap, :]
    for k in range(steps):
        out_copy(k).wait()


def middle(pos, qv, orow, ext, band_t, tails, weight_t, slope, cand, cap, copies):
    queries, width = qv.shape
    owners, _, slots = tails.shape
    flat = weight_t.shape[1]
    filts = band_t.shape[1] // BAND_OUT
    units = math.gcd(filts, 16)
    steps = filts // units
    cols = flat // steps
    rows = units * BAND_OUT
    blocks = math.gcd(owners, max(1, 2048 // slots))
    ring = min(owners, 4)
    hbm = pl.BlockSpec(memory_space=pl.ANY)
    return pl.pallas_call(
        functools.partial(middle_kernel, cap, cand),
        in_specs=[VMEM] * 4 + [hbm] * 4,
        out_specs=[VMEM] * 3 + [hbm],
        out_shape=[
            jax.ShapeDtypeStruct((owners, cap, width), bf16),
            jax.ShapeDtypeStruct((1, width, queries), f32),
            jax.ShapeDtypeStruct((copies, width, queries), bf16),
            jax.ShapeDtypeStruct((filts * BAND_OUT, GROUPS * queries), bf16),
        ],
        scratch_shapes=[
            pltpu.VMEM(band_t.shape, bf16),
            pltpu.VMEM(tails.shape, bf16),
            pltpu.VMEM((steps, width, cols), bf16),
            pltpu.VMEM((steps, cols, queries), f32),
            pltpu.VMEM((steps, rows, GROUPS * queries), bf16),
            pltpu.VMEM((ring, queries, slots), f32),
            pltpu.VMEM((ring, queries, slots), bf16),
            pltpu.VMEM((LANES, GROUPS * queries), f32),
            pltpu.VMEM((ext.shape[1], queries), f32),
            pltpu.VMEM((2, cols, queries), f32),
            pltpu.SemaphoreType.DMA,
            pltpu.SemaphoreType.DMA((owners // blocks,)),
            pltpu.SemaphoreType.DMA((steps,)),
            pltpu.SemaphoreType.DMA((steps,)),
            pltpu.SemaphoreType.DMA((steps,)),
        ],
        compiler_params=params(),
        cost_estimate=cost(6e9, 2.5e7, 5e5),
        name="middle",
    )(pos, qv, orow, ext, band_t, tails, weight_t, slope)


def half_taps(taps):
    return -(-taps // 32) * 16


def diag_kernel(taps, codes_ref, fgrad_ref, img_ref, rows_ref, out_ref, corr_ref):
    s = pl.program_id(0)
    units = fgrad_ref.shape[0] // BAND_OUT
    part = mm(fgrad_ref[...], img_ref[...], NT)
    corr_ref[pl.ds(s * units, units)] = part.reshape(units, BAND_OUT, LANES)

    @pl.when(s == pl.num_programs(0) - 1)
    def _():
        diag_sums(taps, codes_ref, corr_ref, rows_ref, out_ref)


def diag_sums(taps, codes_ref, corr_ref, rows_ref, out_ref):
    filts = corr_ref.shape[0]
    cap, width = rows_ref.shape[1:]
    half = half_taps(taps)
    total = jnp.zeros((2 * half, filts), f32)
    for j in range(IMG):
        rows = corr_ref[:, j, :]
        for di in range(1, BAND):
            rows = rows + pltpu.roll(corr_ref[:, di * IMG + j, :], LANES - di * IMG, 1)
        pick = onehot(iota((2 * half, LANES), 0) == codes_ref[j : j + 1, :])
        high, low = split(rows)
        total = total + mm(pick, high, NT) + mm(pick, low, NT)
    packed = jnp.zeros((half, width), f32)
    for k in range(2):
        for i, piece in enumerate(split(total[k * half : (k + 1) * half, :])):
            place = onehot(iota((filts, width), 1) == iota((filts, width), 0) + (2 * k + i) * filts)
            packed = packed + mm(piece, place)
    packed = packed.astype(bf16)
    for d in range(out_ref.shape[0]):
        out_ref[d, :cap, :] = rows_ref[d]
        out_ref[d, cap:, :] = packed


def filter_sums(fgrad, img, codes, rows, taps):
    count, cap, width = rows.shape
    filts = fgrad.shape[0] // BAND_OUT
    units = filter_block(filts)
    assert 4 * filts <= width
    out = (count, cap + half_taps(taps), width)
    return pl.pallas_call(
        functools.partial(diag_kernel, taps),
        grid=(filts // units,),
        in_specs=[
            whole(codes.shape),
            pl.BlockSpec((units * BAND_OUT, fgrad.shape[1]), lambda s: (s, 0)),
            whole(img.shape),
            whole(rows.shape),
        ],
        out_specs=whole(out),
        out_shape=jax.ShapeDtypeStruct(out, bf16),
        scratch_shapes=[pltpu.VMEM((filts, BAND_OUT, LANES), f32)],
        compiler_params=params("arbitrary"),
        cost_estimate=cost(2e9, 6e6),
        name="filter_sums",
    )(codes, fgrad, img, rows)


def tail_kernel(
    cand, ids_ref, tails_ref, mate_ref, scand_ref, numbers_ref, vecs_ref, own_ref, other_ref, scores, grads
):
    cap = own_ref.shape[1]
    tails = jnp.concatenate([ref[0].astype(f32).T for ref in (tails_ref, mate_ref)], axis=0).astype(bf16)
    scand = jnp.concatenate([scand_ref[0], scand_ref[1]], axis=0)
    own = jnp.zeros(own_ref.shape, f32)
    other = jnp.zeros(own_ref.shape, f32)
    for i, group in enumerate(pairs(vecs_ref.shape[0])):
        qvt = beside(vecs_ref[p, 1] for p in group)
        pos = beside(field(numbers_ref, 2 * p + ids_ref[2], 3) for p in group)
        score, grad = scores.at[i % 2], grads.at[i % 2]
        score[...] = mm(tails, qvt)
        for r in spans(2 * cap, 64):
            target = jnp.where(scand[r, :] == pos, 1.0 - smooth + smooth / cand, smooth / cand)
            grad[r, :] = ((sigmoid(score[r, :]) - target) * loss_weight).astype(bf16)
        own = own + mm(qvt, grad[:cap, :], NT)
        other = other + mm(qvt, grad[cap:, :], NT)
    own_ref[...] = own
    other_ref[...] = other


def tail_part(ids, tails, scand, numbers, vecs, cand):
    _, width, cap = tails.shape
    half = jax.ShapeDtypeStruct((width, cap), f32)
    return pl.pallas_call(
        functools.partial(tail_kernel, cand),
        grid_spec=pltpu.PrefetchScalarGridSpec(
            num_scalar_prefetch=1,
            grid=(1,),
            in_specs=[
                pl.BlockSpec((1, width, cap), lambda s, ids: (ids[0], 0, 0)),
                pl.BlockSpec((1, width, cap), lambda s, ids: (ids[1], 0, 0)),
                whole(scand.shape),
                whole(numbers.shape),
                whole(vecs.shape),
            ],
            out_specs=[whole(half.shape)] * 2,
            scratch_shapes=[
                pltpu.VMEM((2, 2 * cap, 2 * vecs.shape[3]), f32),
                pltpu.VMEM((2, 2 * cap, 2 * vecs.shape[3]), bf16),
            ],
        ),
        out_shape=[half, half],
        compiler_params=params("arbitrary"),
        cost_estimate=cost(2e9, 3e6, 1e6),
        name="tail_grad",
    )(ids, tails, tails, scand, numbers, vecs)


def proj_kernel(
    ids_ref, rtab_ref, ext_ref, band_ref, mate_ref, numbers_ref, vecs_ref, grads_ref,
    own_ref, other_ref, feats, hpick, rpick, rels_hot, ext, pre,
):
    width, rels = rtab_ref.shape
    units = band_ref.shape[0] // BAND_OUT
    flat = GROUPS * BAND_OUT
    cols = units * flat
    entry = iota((width, ext_ref.shape[1]), 0)
    hpick[...] = jnp.where(entry == ext_ref[...], 1.0, 0.0).T.astype(bf16)
    rpick[...] = jnp.where(entry + width == ext_ref[...], 1.0, 0.0).T.astype(bf16)
    queries = vecs_ref.shape[3]
    for i, group in enumerate(pairs(vecs_ref.shape[0])):
        hvt = beside(vecs_ref[p, 0] for p in group)
        rel = beside(field(numbers_ref, 2 * p + ids_ref[2], 2) for p in group)
        for r in spans(rels, 64):
            rels_hot[r, :] = onehot(iota((r.stop - r.start, rel.shape[1]), 0) + r.start == rel)
        rvt = mm(rtab_ref[...], rels_hot[...]).astype(bf16)
        image = ext.at[i % 2]
        image[...] = (mm(hpick[...], hvt) + mm(rpick[...], rvt)).astype(bf16)
        lanes = slice(group[0] * queries, (group[-1] + 1) * queries)
        for k, source in enumerate((band_ref, mate_ref)):
            for g in range(GROUPS):
                slot = (k * GROUPS + g) % 2
                pre[slot] = mm(source[...], image[g * BAND_OUT : g * BAND_OUT + LANES, :])
                for f in range(units):
                    v = pre[slot, f * BAND_OUT : (f + 1) * BAND_OUT, :]
                    first = k * cols + f * flat + g * BAND_OUT
                    feats[first : first + BAND_OUT, lanes] = (v * sigmoid(v)).astype(bf16)
    qgt = beside(grads_ref[p] for p in range(grads_ref.shape[0]))
    own_ref[...] = mm(qgt, feats[:cols, :], NT)
    other_ref[...] = mm(qgt, feats[cols:, :], NT)


def proj_part(ids, rtab_t, ext, band, numbers, vecs, grads, cols):
    width, rels = rtab_t.shape
    unit = cols // GROUPS
    gathered, _, _, queries = vecs.shape
    half = jax.ShapeDtypeStruct((width, cols), f32)
    return pl.pallas_call(
        proj_kernel,
        grid_spec=pltpu.PrefetchScalarGridSpec(
            num_scalar_prefetch=1,
            grid=(1,),
            in_specs=[
                whole(rtab_t.shape),
                whole(ext.shape),
                pl.BlockSpec((unit, LANES), lambda s, ids: (ids[0], 0)),
                pl.BlockSpec((unit, LANES), lambda s, ids: (ids[1], 0)),
                whole(numbers.shape),
                whole(vecs.shape),
                whole(grads.shape),
            ],
            out_specs=[whole(half.shape)] * 2,
            scratch_shapes=[
                pltpu.VMEM((2 * cols, gathered * queries), bf16),
                pltpu.VMEM((ext.shape[1], width), bf16),
                pltpu.VMEM((ext.shape[1], width), bf16),
                pltpu.VMEM((rels, 2 * queries), bf16),
                pltpu.VMEM((2, ext.shape[1], 2 * queries), bf16),
                pltpu.VMEM((2, unit, 2 * queries), f32),
            ],
        ),
        out_shape=[half, half],
        compiler_params=params("arbitrary"),
        cost_estimate=cost(6e9, 6e6, 2.5e6),
        name="proj_grad",
    )(ids, rtab_t, ext, band, band, numbers, vecs, grads)


def proj_columns(first, cols, filters, chequer_perm, relation_table, numbers, heads, grads):
    ks = filters.shape[-1]
    rim = ks // 2
    flat = IMG * IMG
    column = first + jnp.arange(cols, dtype=i32)
    f = column // flat
    i = (column % flat) // IMG
    j = column % IMG
    spot = jnp.arange(flat, dtype=i32)
    a = (spot[:, None] // IMG - i[None, :] + rim) % IMG
    b = (spot[:, None] % IMG - j[None, :] + rim) % IMG
    tap = filters[f[None, :], jnp.minimum(a, ks - 1), jnp.minimum(b, ks - 1)]
    matrix = jnp.where((a < ks) & (b < ks), tap, jnp.zeros((), bf16))
    width = heads.shape[1]
    head = heads.transpose(0, 2, 1).reshape(-1, width)
    qg = grads.transpose(0, 2, 1).reshape(-1, width)
    joined = jnp.concatenate([head, relation_table[numbers[:, 2].reshape(-1)]], axis=1)
    pre = mm(joined[:, chequer_perm], matrix)
    return mm(qg, (pre * sigmoid(pre)).astype(bf16), TN)


def rel_kernel(numbers_ref, sums_hbm, rel_ref, sums_ref, picks, sem):
    copy = pltpu.make_async_copy(sums_hbm, sums_ref, sem)
    copy.start()
    width, rels = rel_ref.shape
    queries = sums_ref.shape[2]
    total = None
    for block in spans(sums_ref.shape[0], picks.shape[1] // queries):
        members = range(block.start, block.stop)
        for i, p in enumerate(members):
            rel = field(numbers_ref, p, 2)
            for r in spans(rels, 128):
                here = iota((r.stop - r.start, queries), 0) + r.start
                picks[r, i * queries : (i + 1) * queries] = onehot(here == rel)
        if block.start == 0:
            copy.wait()
        parts = jnp.concatenate(split(beside(sums_ref[p] for p in members)), axis=0)
        part = mm(parts, picks[...], NT)
        total = part if total is None else total + part
    rel_ref[...] = total[:width, :] + total[width:, :]


def rel_part(numbers, sums, rels):
    count, width, queries = sums.shape
    return pl.pallas_call(
        rel_kernel,
        in_specs=[VMEM, pl.BlockSpec(memory_space=pl.ANY)],
        out_shape=jax.ShapeDtypeStruct((width, rels), f32),
        scratch_shapes=[
            pltpu.VMEM(sums.shape, f32),
            pltpu.VMEM((rels, math.gcd(count, 16) * queries), bf16),
            pltpu.SemaphoreType.DMA,
        ],
        compiler_params=params(),
        cost_estimate=cost(2e9, 3e6),
        name="rel_grad",
    )(numbers, sums)


def entity_kernel(cap, want_ref, srow_ref, own_ref, recv_ref, incoming_ref, out_ref, filt_ref):
    rows = out_ref.shape[1]
    count, _, width = incoming_ref.shape
    half, filts = filt_ref.shape[0] // 2, filt_ref.shape[1]
    grads = jnp.concatenate([incoming_ref[d, :cap, :] for d in range(count)], axis=0)
    turned = grads.astype(f32).T.astype(bf16)
    high, low = split(own_ref[...] + recv_ref[...])
    for c in spans(rows, 256):
        here = iota((want_ref.shape[0], c.stop - c.start), 1) + c.start
        total = mm(turned, onehot(here == want_ref[...]))
        here = iota((srow_ref.shape[0], c.stop - c.start), 1) + c.start
        pick = onehot(here == srow_ref[...])
        out_ref[:, c] = total + mm(high, pick) + mm(low, pick)
    packed = incoming_ref[0, cap:, :].astype(f32)
    for d in range(1, count):
        packed = packed + incoming_ref[d, cap:, :].astype(f32)
    high, low = split(packed)
    for k in range(2):
        lane = iota((width, filts), 0) - 2 * k * filts
        unit = iota((width, filts), 1)
        place = onehot((lane == unit) | (lane == unit + filts))
        filt_ref[k * half : (k + 1) * half, :] = mm(high, place) + mm(low, place)


def entity_sum(want, srow, own, recv, incoming, rows, cap, filts):
    half = incoming.shape[1] - cap
    return pl.pallas_call(
        functools.partial(entity_kernel, cap),
        out_shape=[
            jax.ShapeDtypeStruct((own.shape[0], rows), f32),
            jax.ShapeDtypeStruct((2 * half, filts), f32),
        ],
        compiler_params=params(),
        cost_estimate=cost(1.5e9, 4e6),
        name="entity_grad",
    )(want, srow, own, recv, incoming)


def shards(
    entity_table,
    relation_table,
    filters,
    proj_weight,
    chequer_perm,
    head_owner,
    head_row,
    rel_ids,
    pos_index,
    tail_owner,
    tail_row,
):
    count = lax.axis_size("shard")
    me = lax.axis_index("shard")
    assert count % 2 == 0
    direct = count <= 16
    queries = head_row.shape[0]
    cand = tail_row.shape[0]
    rows, width = entity_table.shape
    rels = relation_table.shape[0]
    filts, ks, _ = filters.shape
    head_cap = 2 * queries // count
    tail_cap = 2 * cand // count
    same_core = [list(range(c, count, 2)) for c in range(2)]
    copies = count // 2 if direct else 1

    def swap(x):
        return lax.ppermute(x, "shard", [(d, d ^ 1) for d in range(count)])

    def exchange(x):
        return lax.all_to_all(x, "shard", split_axis=0, concat_axis=0, tiled=True)

    def gather_core(x):
        if direct:
            return lax.all_to_all(
                x, "shard", split_axis=0, concat_axis=0, axis_index_groups=same_core, tiled=True
            )
        return lax.all_gather(x, "shard", axis=0, axis_index_groups=same_core, tiled=True)

    me1 = me.reshape(1)
    heads = head_owner[:, 0]
    tail_owners = tail_owner[:, 0]
    table_t, rtab_t, weight_t = entity_table.T, relation_table.T, proj_weight.T
    numbers = jnp.concatenate([heads, head_row, rel_ids, pos_index])
    numbers = exchange(jnp.broadcast_to(numbers, (count, 1, 4 * queries)))

    ids = jnp.stack([me, me ^ 1, me & 1])
    tails_t, slot_row = pack_tails(me1, tail_owners, tail_row, table_t, tail_cap)
    all_tails = lax.all_gather(tails_t, "shard", axis=0, tiled=True)
    scand, pos = slot_tables(me1, tail_owners, pos_index, tail_cap)
    codes = jnp.asarray(band_codes(ks))
    band, band_t = build_band(filters, codes)
    numbers, scand, pos, band, band_t = lax.optimization_barrier((numbers, scand, pos, band, band_t))
    found, want = find_heads(me1, numbers, table_t, head_cap)
    fetched = exchange(found)

    extra = BAND_OUT * (GROUPS - 1) + LANES - IMG * IMG - BAND_OUT
    ext = jnp.concatenate([chequer_perm[-BAND_OUT:], chequer_perm, chequer_perm[:extra]])[None]
    orow = heads[None, :]
    slope, img, qv, vecs = front(
        fetched, orow, rel_ids[None, :], rtab_t, ext, band, weight_t, head_cap, copies
    )
    core_vecs = gather_core(vecs)

    outgoing, sums, qgt, fgrad = middle(
        pos, qv, orow, ext, band_t, all_tails, weight_t, slope, cand, head_cap, copies
    )
    all_sums = lax.all_gather(sums, "shard", axis=0, tiled=True)
    qgt, core_vecs = lax.optimization_barrier((qgt, core_vecs))
    core_qgt = gather_core(qgt)
    outgoing = filter_sums(fgrad, img, codes, outgoing, ks * ks)
    outgoing, core_qgt = lax.optimization_barrier((outgoing, core_qgt))
    incoming = exchange(outgoing)

    own, other = tail_part(ids, all_tails, scand, numbers, core_vecs, cand)
    entity_grad, filter_grad = entity_sum(
        want, slot_row, own, swap(other), incoming, rows, head_cap, filts
    )
    filter_grad = filter_grad[: ks * ks].T.reshape(filts, ks, ks)

    cols = filts * IMG * IMG // count
    if direct and cols % (IMG * IMG) == 0:
        own, other = proj_part(ids, rtab_t, ext, band, numbers, core_vecs, core_qgt, cols)
    else:
        core_numbers = lax.dynamic_index_in_dim(
            numbers.reshape(count // 2, 2, 4, queries), me & 1, 1, keepdims=False
        )
        own, other = (
            proj_columns(
                d * cols, cols, filters, chequer_perm, relation_table,
                core_numbers, core_vecs[:, 0], core_qgt,
            )
            for d in (me, me ^ 1)
        )
    proj_grad = (own + swap(other)).T

    relation_grad = rel_part(numbers, all_sums, rels).T
    return (entity_grad.T, relation_grad, filter_grad, proj_grad)


def solution(mesh):
    placed = (
        P("shard", None),
        P(),
        P(),
        P(),
        P(),
        P(("parts", "shard"), None),
        P(("parts", "shard")),
        P(("parts", "shard")),
        P(("parts", "shard")),
        P("parts", None),
        P("parts"),
    )
    return jax.shard_map(
        shards,
        mesh=mesh,
        in_specs=placed,
        out_specs=(
            P(("parts", "shard"), None),
            P("parts", None),
            P("parts", None, None),
            P(("parts", "shard"), None),
        ),
        check_vma=False,
    )
```

```python
import functools
import math

import jax
import jax.numpy as jnp
import numpy as np
from jax import lax
from jax.experimental import pallas as pl
from jax.experimental.pallas import tpu as pltpu
from jax.sharding import PartitionSpec as P

IMG = 20
BAND = 4
GROUPS = IMG // BAND
BAND_OUT = BAND * IMG
LANES = 256

loss_weight = 0.015625
smooth = 0.1

f32 = jnp.float32
bf16 = jnp.bfloat16
i32 = jnp.int32

NN = (((1,), (0,)), ((), ()))
NT = (((1,), (1,)), ((), ()))
TN = (((0,), (0,)), ((), ()))


def mm(a, b, dims=NN):
    return lax.dot_general(a, b, dims, preferred_element_type=f32)


def iota(shape, axis):
    return lax.broadcasted_iota(i32, shape, axis)


def onehot(mask):
    return jnp.where(mask, 1.0, 0.0).astype(bf16)


def split(value):
    high = value.astype(bf16)
    return high, (value - high.astype(f32)).astype(bf16)


def sigmoid(v):
    return 0.5 * jnp.tanh(0.5 * v) + 0.5


def params(*semantics):
    return pltpu.CompilerParams(
        dimension_semantics=semantics or None, vmem_limit_bytes=60 << 20
    )


def cost(flops, nbytes, trans=0):
    return pl.CostEstimate(flops=int(flops), bytes_accessed=int(nbytes), transcendentals=int(trans))


def whole(shape):
    return pl.BlockSpec(shape, lambda *_: (0,) * len(shape))


SMEM = pl.BlockSpec(memory_space=pltpu.SMEM)


def band_codes(ks):
    codes = np.full((IMG, LANES), -1, np.int32)
    for j in range(IMG):
        for r in range(ks):
            for x in range(IMG):
                b = (x - j + ks // 2) % IMG
                if b < ks:
                    codes[j, r * IMG + x] = r * ks + b
    return codes


def band_kernel(codes_ref, filt_ref, out_ref, out_t_ref, scr):
    count, taps = filt_ref.shape
    filt = filt_ref[...]
    for j in range(IMG):
        pick = onehot(iota((taps, LANES), 0) == codes_ref[j : j + 1, :])
        row = mm(filt, pick)
        for di in range(BAND):
            scr[:, di * IMG + j, :] = row if di == 0 else pltpu.roll(row, di * IMG, 1)
    full = scr[...].reshape(count * BAND_OUT, LANES)
    out_ref[...] = full.astype(bf16)
    out_t_ref[...] = full.T.astype(bf16)


def build_band(filters, codes):
    count, ks, _ = filters.shape
    return pl.pallas_call(
        band_kernel,
        out_shape=[
            jax.ShapeDtypeStruct((count * BAND_OUT, LANES), bf16),
            jax.ShapeDtypeStruct((LANES, count * BAND_OUT), bf16),
        ],
        scratch_shapes=[pltpu.VMEM((count, BAND_OUT, LANES), f32)],
        compiler_params=params(),
        cost_estimate=cost(4e7, 4e6),
        name="band",
    )(codes, filters.reshape(count, ks * ks))


VMEM = pl.BlockSpec(memory_space=pltpu.VMEM)


def pairs(count):
    step = 2 if count % 2 == 0 else 1
    return [range(i, i + step) for i in range(0, count, step)]


def beside(blocks):
    return jnp.concatenate(list(blocks), axis=1)


def spans(size, step):
    return [slice(i, min(i + step, size)) for i in range(0, size, step)]


def fill_picks(ref, index):
    rows, lanes = ref.shape
    for r in spans(rows, 64):
        for c in spans(lanes, 256):
            here = iota((r.stop - r.start, c.stop - c.start), 1) + c.start
            ref[r, c] = onehot(here == index[r, :])


def field(ref, d, k):
    queries = ref.shape[2] // 4
    return ref[d, :, k * queries : (k + 1) * queries]


def slot_values(owner, device, value, cap):
    lines = owner.shape[0]
    mine = owner == device
    mine_b = onehot(mine)
    before = onehot(iota((128, 128), 0) < iota((128, 128), 1))
    rank = mm(mine_b, before)
    totals = mm(mine_b, jnp.ones((128, 128), bf16))
    upper = onehot(iota((lines, lines), 1) < iota((lines, lines), 0))
    offset = mm(upper, totals.astype(bf16))
    key = jnp.where(mine, (rank + offset).astype(i32), -1)
    value = (value + 1).astype(f32)
    found = []
    for s in spans(cap, 128):
        slots = iota((s.stop - s.start, 128), 0) + s.start
        total = jnp.zeros(slots.shape, f32)
        for r in range(lines):
            total = total + jnp.where(slots == key[r : r + 1, :], value[r : r + 1, :], 0.0)
        found.append(jnp.sum(total, axis=1, keepdims=True))
    return jnp.concatenate(found, axis=0).astype(i32) - 1


def pack_kernel(me_ref, owner_ref, row_ref, table_hbm, tails_t_ref, srow_ref, picks, table, sem):
    copy = pltpu.make_async_copy(table_hbm, table, sem)
    copy.start()
    cap = srow_ref.shape[0]
    srow = slot_values(owner_ref[...], me_ref[0], row_ref[...], cap)
    srow_ref[...] = srow
    fill_picks(picks, srow)
    copy.wait()
    tails_t_ref[0] = mm(table[...], picks[...], NT).astype(bf16)


def pack_tails(me, tail_owners, tail_row, table_t, cap):
    assert tail_row.shape[0] % 128 == 0
    return pl.pallas_call(
        pack_kernel,
        in_specs=[SMEM, VMEM, VMEM, pl.BlockSpec(memory_space=pl.ANY)],
        out_shape=[
            jax.ShapeDtypeStruct((1, table_t.shape[0], cap), bf16),
            jax.ShapeDtypeStruct((cap, 1), i32),
        ],
        scratch_shapes=[
            pltpu.VMEM((cap, table_t.shape[1]), bf16),
            pltpu.VMEM(table_t.shape, bf16),
            pltpu.SemaphoreType.DMA,
        ],
        compiler_params=params(),
        cost_estimate=cost(1e9, 2e6),
        name="pack_tails",
    )(me, tail_owners.reshape(-1, 128), tail_row.reshape(-1, 128), table_t)


def found_kernel(cap, me_ref, table_ref, numbers_ref, found_ref, want_ref, scr, picks):
    count = numbers_ref.shape[0]
    owners = jnp.concatenate([field(numbers_ref, d, 0) for d in range(count)], axis=0)
    queries = owners.shape[1]
    mine = owners == me_ref[0]
    before = onehot(iota((queries, queries), 0) < iota((queries, queries), 1))
    rank = mm(onehot(mine), before)
    key = jnp.where(mine, rank.astype(i32), -1)
    slots = iota((cap, queries), 0)
    for d in range(count):
        code = (field(numbers_ref, d, 1) + 1).astype(f32)
        picked = jnp.where(slots == key[d : d + 1, :], code, 0.0)
        scr[d * cap : (d + 1) * cap, :] = jnp.sum(picked, axis=1, keepdims=True)
    want = scr[...].astype(i32) - 1
    want_ref[...] = want
    fill_picks(picks, want)
    found = mm(picks[...], table_ref[...], NT).astype(bf16)
    for d in range(count):
        found_ref[d] = found[d * cap : (d + 1) * cap, :]


def find_heads(me, numbers, table_t, cap):
    width = table_t.shape[0]
    count = numbers.shape[0]
    return pl.pallas_call(
        functools.partial(found_kernel, cap),
        in_specs=[SMEM] + [VMEM] * 2,
        out_shape=[
            jax.ShapeDtypeStruct((count, cap, width), bf16),
            jax.ShapeDtypeStruct((count * cap, 1), i32),
        ],
        scratch_shapes=[
            pltpu.VMEM((count * cap, 1), f32),
            pltpu.VMEM((count * cap, table_t.shape[1]), bf16),
        ],
        compiler_params=params(),
        cost_estimate=cost(3e8, 2e6),
        name="find_heads",
    )(me, table_t, numbers)


def cand_kernel(me_ref, owner_ref, out_ref):
    cap = out_ref.shape[1]
    owner = owner_ref[...]
    index = iota(owner.shape, 0) * 128 + iota(owner.shape, 1)
    for k in range(2):
        out_ref[k] = slot_values(owner, me_ref[0] ^ k, index, cap)


def slot_cands(me, tail_owners, cap):
    return pl.pallas_call(
        cand_kernel,
        in_specs=[SMEM, VMEM],
        out_shape=jax.ShapeDtypeStruct((2, cap, 1), i32),
        compiler_params=params(),
        cost_estimate=cost(1e8, 1e6),
        name="slot_cands",
    )(me, tail_owners.reshape(-1, 128))


def pos_kernel(cap, row_ref, pos_ref, out_ref):
    queries = pos_ref.shape[1]
    eye = iota((queries, queries), 0) == iota((queries, queries), 1)
    row = pos_ref[...].astype(f32)
    pos = jnp.sum(jnp.where(eye, row, 0.0), axis=1, keepdims=True).astype(i32)
    lanes = spans(row_ref.shape[1], 128)
    owner = jnp.zeros((queries, 128), f32)
    for c in lanes:
        here = iota((queries, 128), 1) + c.start
        owner = owner + jnp.where(here == pos, row_ref[:, c].astype(f32), 0.0)
    owner = jnp.sum(owner, axis=1, keepdims=True).astype(i32)
    ahead = jnp.zeros((queries, 128), f32)
    for c in lanes:
        here = iota((queries, 128), 1) + c.start
        ahead = ahead + jnp.where((row_ref[:, c] == owner) & (here < pos), 1.0, 0.0)
    ahead = jnp.sum(ahead, axis=1, keepdims=True).astype(i32)
    out_ref[...] = owner * cap + ahead


def pos_slots(tail_owners, pos_index, cap):
    return pl.pallas_call(
        functools.partial(pos_kernel, cap),
        out_shape=jax.ShapeDtypeStruct((pos_index.shape[0], 1), i32),
        compiler_params=params(),
        cost_estimate=cost(1e8, 1e5),
        name="pos_slots",
    )(tail_owners.reshape(1, -1), pos_index.reshape(1, -1))


def slot_picks(cap, slots, orow):
    count = slots // cap
    queries = orow.shape[1]
    member = iota((count, queries), 0) == orow
    before = onehot(iota((queries, queries), 0) < iota((queries, queries), 1))
    rank = mm(onehot(member), before)
    rank = jnp.sum(jnp.where(member, rank, 0.0), axis=0, keepdims=True).astype(i32)
    return onehot(iota((slots, queries), 0) == orow * cap + rank)


def front_kernel(
    cap, fetched_ref, orow_ref, rel_ref, rtab_ref, ext_ref, band_ref, w_ref,
    slope_ref, img_ref, qv_ref, vecs_ref, feats, acc, ext, pre,
):
    s = pl.program_id(0)
    width, queries = acc.shape

    @pl.when(s == 0)
    def _():
        rows = jnp.concatenate([fetched_ref[d] for d in range(fetched_ref.shape[0])], axis=0)
        pick = slot_picks(cap, rows.shape[0], orow_ref[...])
        hvt = mm(rows, pick, TN).astype(bf16)
        for d in range(vecs_ref.shape[0]):
            vecs_ref[d, 0] = hvt
        rels = rtab_ref.shape[1]
        rvt = mm(rtab_ref[...], onehot(iota((rels, queries), 0) == rel_ref[...])).astype(bf16)
        entry = iota((width, ext_ref.shape[1]), 0)
        image = mm(onehot(entry == ext_ref[...]), hvt, TN)
        image = image + mm(onehot(entry + width == ext_ref[...]), rvt, TN)
        ext[...] = image.astype(bf16)
        for g in range(GROUPS):
            img_ref[:, g * queries : (g + 1) * queries] = ext[g * BAND_OUT : g * BAND_OUT + LANES, :]
        acc[...] = jnp.zeros_like(acc)

    units = band_ref.shape[0] // BAND_OUT
    flat = GROUPS * BAND_OUT
    pre[...] = mm(band_ref[...], img_ref[...])
    for f in range(units):
        for g in range(GROUPS):
            rows = slice(f * flat + g * BAND_OUT, f * flat + (g + 1) * BAND_OUT)
            v = pre[f * BAND_OUT : (f + 1) * BAND_OUT, g * queries : (g + 1) * queries]
            sig = sigmoid(v)
            feats[rows, :] = (v * sig).astype(bf16)
            slope_ref[rows, :] = sig * (1.0 + v * (1.0 - sig))
    acc[...] += mm(w_ref[...], feats[...])

    @pl.when(s == pl.num_programs(0) - 1)
    def _():
        query = acc[...]
        qv_ref[...] = query.T.astype(bf16)
        qvt = query.astype(bf16)
        for d in range(vecs_ref.shape[0]):
            vecs_ref[d, 1] = qvt


def filter_block(filts):
    return math.gcd(filts, 8)


def front(fetched, orow, rel_row, rtab_t, ext, band, weight_t, cap, copies):
    queries = orow.shape[1]
    width, flat = weight_t.shape
    filts = band.shape[0] // BAND_OUT
    units = filter_block(filts)
    cols = flat // filts * units
    return pl.pallas_call(
        functools.partial(front_kernel, cap),
        grid=(filts // units,),
        in_specs=[
            whole(fetched.shape),
            whole(orow.shape),
            whole(rel_row.shape),
            whole(rtab_t.shape),
            whole(ext.shape),
            pl.BlockSpec((units * BAND_OUT, LANES), lambda s: (s, 0)),
            pl.BlockSpec((width, cols), lambda s: (0, s)),
        ],
        out_specs=[
            pl.BlockSpec((cols, queries), lambda s: (s, 0)),
            whole((LANES, GROUPS * queries)),
            whole((queries, width)),
            whole((copies, 2, width, queries)),
        ],
        out_shape=[
            jax.ShapeDtypeStruct((flat, queries), f32),
            jax.ShapeDtypeStruct((LANES, GROUPS * queries), bf16),
            jax.ShapeDtypeStruct((queries, width), bf16),
            jax.ShapeDtypeStruct((copies, 2, width, queries), bf16),
        ],
        scratch_shapes=[
            pltpu.VMEM((cols, queries), bf16),
            pltpu.VMEM((width, queries), f32),
            pltpu.VMEM((ext.shape[1], queries), bf16),
            pltpu.VMEM((units * BAND_OUT, GROUPS * queries), f32),
        ],
        compiler_params=params("arbitrary"),
        cost_estimate=cost(4e9, 2.4e7, 2.5e6),
        name="front",
    )(fetched, orow, rel_row, rtab_t, ext, band, weight_t)


def middle_kernel(
    cand, pos_ref, qv_ref, ext_ref, bandt_hbm, tails_hbm, w_hbm, slope_hbm,
    ext, sums_ref, qgt_ref, fgrad_hbm,
    bandt, tails, w, slope, fgrad, scores, grads, spread, linear,
    band_sem, tail_sems, w_sems, slope_sems, out_sems,
):
    owners, width, slots = tails.shape
    steps, _, cols = w.shape
    queries = qv_ref.shape[0]
    chunks = tail_sems.shape[0]
    blocks = owners // chunks
    part_rows = fgrad.shape[1]

    def tail_copy(i):
        span = pl.ds(i * blocks, blocks)
        return pltpu.make_async_copy(tails_hbm.at[span], tails.at[span], tail_sems.at[i])

    def w_copy(k):
        return pltpu.make_async_copy(w_hbm.at[:, pl.ds(k * cols, cols)], w.at[k], w_sems.at[k])

    def slope_copy(k):
        return pltpu.make_async_copy(slope_hbm.at[pl.ds(k * cols, cols)], slope.at[k], slope_sems.at[k])

    def out_copy(k):
        span = pl.ds(k * part_rows, part_rows)
        return pltpu.make_async_copy(fgrad.at[k], fgrad_hbm.at[span], out_sems.at[k])

    for i in range(chunks):
        tail_copy(i).start()
    band_copy = pltpu.make_async_copy(bandt_hbm, bandt, band_sem)
    for k in range(steps):
        w_copy(k).start()
        slope_copy(k).start()
        if k == 0:
            band_copy.start()

    qv = qv_ref[...]
    total = jnp.zeros((queries, width), f32)
    for i in range(chunks):
        tail_copy(i).wait()
        for b in range(blocks):
            o = i * blocks + b
            block = tails[o]
            slot = o % scores.shape[0]
            scores[slot] = mm(qv, block)
            for r in spans(queries, 16):
                here = iota((r.stop - r.start, slots), 1) + o * slots
                target = jnp.where(here == pos_ref[r, :], 1.0 - smooth + smooth / cand, smooth / cand)
                grads[slot, r, :] = ((sigmoid(scores[slot, r, :]) - target) * loss_weight).astype(bf16)
            total = total + mm(grads[slot], block, NT)
    qgt = total.T.astype(bf16)
    for d in range(qgt_ref.shape[0]):
        qgt_ref[d] = qgt

    units = part_rows // BAND_OUT
    flat = GROUPS * BAND_OUT
    for k in range(steps):
        lin = linear.at[k % 2]
        w_copy(k).wait()
        lin[...] = mm(w[k], qgt, TN)
        slope_copy(k).wait()
        for f in range(units):
            for g in range(GROUPS):
                rows = slice(f * flat + g * BAND_OUT, f * flat + (g + 1) * BAND_OUT)
                part = slice(f * BAND_OUT, (f + 1) * BAND_OUT)
                lanes = slice(g * queries, (g + 1) * queries)
                fgrad[k, part, lanes] = (lin[rows, :] * slope[k, rows, :]).astype(bf16)
        out_copy(k).start()
        if k == 0:
            band_copy.wait()
        spread_k = mm(bandt[:, k * part_rows : (k + 1) * part_rows], fgrad[k])
        if k == 0:
            spread[...] = spread_k
        else:
            spread[...] += spread_k

    ext[...] = jnp.zeros_like(ext)
    for g in range(GROUPS):
        ext[g * BAND_OUT : g * BAND_OUT + LANES, :] += spread[:, g * queries : (g + 1) * queries]
    high, low = split(ext[...])
    rpick = onehot(iota((width, ext.shape[0]), 0) + width == ext_ref[...])
    sums_ref[0] = mm(rpick, high) + mm(rpick, low)
    for k in range(steps):
        out_copy(k).wait()


def middle(pos, qv, ext, band_t, tails, weight_t, slope, cand, copies):
    queries, width = qv.shape
    owners, _, slots = tails.shape
    flat = weight_t.shape[1]
    filts = band_t.shape[1] // BAND_OUT
    units = math.gcd(filts, 16)
    steps = filts // units
    cols = flat // steps
    rows = units * BAND_OUT
    blocks = math.gcd(owners, max(1, 2048 // slots))
    ring = min(owners, 4)
    hbm = pl.BlockSpec(memory_space=pl.ANY)
    return pl.pallas_call(
        functools.partial(middle_kernel, cand),
        in_specs=[VMEM] * 3 + [hbm] * 4,
        out_specs=[VMEM] * 3 + [hbm],
        out_shape=[
            jax.ShapeDtypeStruct((ext.shape[1], queries), f32),
            jax.ShapeDtypeStruct((1, width, queries), f32),
            jax.ShapeDtypeStruct((copies, width, queries), bf16),
            jax.ShapeDtypeStruct((filts * BAND_OUT, GROUPS * queries), bf16),
        ],
        scratch_shapes=[
            pltpu.VMEM(band_t.shape, bf16),
            pltpu.VMEM(tails.shape, bf16),
            pltpu.VMEM((steps, width, cols), bf16),
            pltpu.VMEM((steps, cols, queries), f32),
            pltpu.VMEM((steps, rows, GROUPS * queries), bf16),
            pltpu.VMEM((ring, queries, slots), f32),
            pltpu.VMEM((ring, queries, slots), bf16),
            pltpu.VMEM((LANES, GROUPS * queries), f32),
            pltpu.VMEM((2, cols, queries), f32),
            pltpu.SemaphoreType.DMA,
            pltpu.SemaphoreType.DMA((owners // blocks,)),
            pltpu.SemaphoreType.DMA((steps,)),
            pltpu.SemaphoreType.DMA((steps,)),
            pltpu.SemaphoreType.DMA((steps,)),
        ],
        compiler_params=params(),
        cost_estimate=cost(6e9, 2.5e7, 5e5),
        name="middle",
    )(pos, qv, ext, band_t, tails, weight_t, slope)


def half_taps(taps):
    return -(-taps // 32) * 16


def diag_kernel(
    cap, taps, codes_ref, orow_ref, ext_ref, spread_ref, fgrad_ref, img_ref, out_ref, corr_ref
):
    s = pl.program_id(0)
    units = fgrad_ref.shape[0] // BAND_OUT
    part = mm(fgrad_ref[...], img_ref[...], NT)
    corr_ref[pl.ds(s * units, units)] = part.reshape(units, BAND_OUT, LANES)

    @pl.when(s == pl.num_programs(0) - 1)
    def _():
        width = out_ref.shape[2]
        high, low = split(spread_ref[...])
        hpick = onehot(iota((width, spread_ref.shape[0]), 0) == ext_ref[...])
        hgrad = (mm(hpick, high) + mm(hpick, low)).astype(bf16)
        pick = slot_picks(cap, out_ref.shape[0] * cap, orow_ref[...])
        rows = mm(pick, hgrad, NT).astype(bf16)
        diag_sums(cap, taps, codes_ref, corr_ref, rows, out_ref)


def diag_sums(cap, taps, codes_ref, corr_ref, rows, out_ref):
    filts = corr_ref.shape[0]
    width = out_ref.shape[2]
    half = half_taps(taps)
    total = jnp.zeros((2 * half, filts), f32)
    for j in range(IMG):
        line = corr_ref[:, j, :]
        for di in range(1, BAND):
            line = line + pltpu.roll(corr_ref[:, di * IMG + j, :], LANES - di * IMG, 1)
        pick = onehot(iota((2 * half, LANES), 0) == codes_ref[j : j + 1, :])
        high, low = split(line)
        total = total + mm(pick, high, NT) + mm(pick, low, NT)
    packed = jnp.zeros((half, width), f32)
    for k in range(2):
        for i, piece in enumerate(split(total[k * half : (k + 1) * half, :])):
            place = onehot(iota((filts, width), 1) == iota((filts, width), 0) + (2 * k + i) * filts)
            packed = packed + mm(piece, place)
    packed = packed.astype(bf16)
    for d in range(out_ref.shape[0]):
        out_ref[d, :cap, :] = rows[d * cap : (d + 1) * cap, :]
        out_ref[d, cap:, :] = packed


def filter_sums(fgrad, img, codes, orow, ext, spread, count, width, cap, taps):
    filts = fgrad.shape[0] // BAND_OUT
    units = filter_block(filts)
    assert 4 * filts <= width
    out = (count, cap + half_taps(taps), width)
    return pl.pallas_call(
        functools.partial(diag_kernel, cap, taps),
        grid=(filts // units,),
        in_specs=[
            whole(codes.shape),
            whole(orow.shape),
            whole(ext.shape),
            whole(spread.shape),
            pl.BlockSpec((units * BAND_OUT, fgrad.shape[1]), lambda s: (s, 0)),
            whole(img.shape),
        ],
        out_specs=whole(out),
        out_shape=jax.ShapeDtypeStruct(out, bf16),
        scratch_shapes=[pltpu.VMEM((filts, BAND_OUT, LANES), f32)],
        compiler_params=params("arbitrary"),
        cost_estimate=cost(2e9, 6e6),
        name="filter_sums",
    )(codes, orow, ext, spread, fgrad, img)


def tail_kernel(
    cand, ids_ref, tails_ref, mate_ref, scand_ref, numbers_ref, vecs_ref, own_ref, other_ref, scores, grads
):
    cap = own_ref.shape[1]
    tails = jnp.concatenate([ref[0].astype(f32).T for ref in (tails_ref, mate_ref)], axis=0).astype(bf16)
    scand = jnp.concatenate([scand_ref[0], scand_ref[1]], axis=0)
    own = jnp.zeros(own_ref.shape, f32)
    other = jnp.zeros(own_ref.shape, f32)
    for i, group in enumerate(pairs(vecs_ref.shape[0])):
        qvt = beside(vecs_ref[p, 1] for p in group)
        pos = beside(field(numbers_ref, 2 * p + ids_ref[2], 3) for p in group)
        score, grad = scores.at[i % 2], grads.at[i % 2]
        score[...] = mm(tails, qvt)
        for r in spans(2 * cap, 64):
            target = jnp.where(scand[r, :] == pos, 1.0 - smooth + smooth / cand, smooth / cand)
            grad[r, :] = ((sigmoid(score[r, :]) - target) * loss_weight).astype(bf16)
        own = own + mm(qvt, grad[:cap, :], NT)
        other = other + mm(qvt, grad[cap:, :], NT)
    own_ref[...] = own
    other_ref[...] = other


def tail_part(ids, tails, scand, numbers, vecs, cand):
    _, width, cap = tails.shape
    half = jax.ShapeDtypeStruct((width, cap), f32)
    return pl.pallas_call(
        functools.partial(tail_kernel, cand),
        grid_spec=pltpu.PrefetchScalarGridSpec(
            num_scalar_prefetch=1,
            grid=(1,),
            in_specs=[
                pl.BlockSpec((1, width, cap), lambda s, ids: (ids[0], 0, 0)),
                pl.BlockSpec((1, width, cap), lambda s, ids: (ids[1], 0, 0)),
                whole(scand.shape),
                whole(numbers.shape),
                whole(vecs.shape),
            ],
            out_specs=[whole(half.shape)] * 2,
            scratch_shapes=[
                pltpu.VMEM((2, 2 * cap, 2 * vecs.shape[3]), f32),
                pltpu.VMEM((2, 2 * cap, 2 * vecs.shape[3]), bf16),
            ],
        ),
        out_shape=[half, half],
        compiler_params=params("arbitrary"),
        cost_estimate=cost(2e9, 3e6, 1e6),
        name="tail_grad",
    )(ids, tails, tails, scand, numbers, vecs)


def proj_kernel(
    ids_ref, rtab_ref, ext_ref, band_ref, mate_ref, numbers_ref, vecs_ref, grads_ref,
    own_ref, other_ref, feats, hpick, rpick, rels_hot, ext, pre,
):
    width, rels = rtab_ref.shape
    units = band_ref.shape[0] // BAND_OUT
    flat = GROUPS * BAND_OUT
    cols = units * flat
    entry = iota((width, ext_ref.shape[1]), 0)
    hpick[...] = jnp.where(entry == ext_ref[...], 1.0, 0.0).T.astype(bf16)
    rpick[...] = jnp.where(entry + width == ext_ref[...], 1.0, 0.0).T.astype(bf16)
    queries = vecs_ref.shape[3]
    for i, group in enumerate(pairs(vecs_ref.shape[0])):
        hvt = beside(vecs_ref[p, 0] for p in group)
        rel = beside(field(numbers_ref, 2 * p + ids_ref[2], 2) for p in group)
        for r in spans(rels, 64):
            rels_hot[r, :] = onehot(iota((r.stop - r.start, rel.shape[1]), 0) + r.start == rel)
        rvt = mm(rtab_ref[...], rels_hot[...]).astype(bf16)
        image = ext.at[i % 2]
        image[...] = (mm(hpick[...], hvt) + mm(rpick[...], rvt)).astype(bf16)
        lanes = slice(group[0] * queries, (group[-1] + 1) * queries)
        for k, source in enumerate((band_ref, mate_ref)):
            for g in range(GROUPS):
                slot = (k * GROUPS + g) % 2
                pre[slot] = mm(source[...], image[g * BAND_OUT : g * BAND_OUT + LANES, :])
                for f in range(units):
                    v = pre[slot, f * BAND_OUT : (f + 1) * BAND_OUT, :]
                    first = k * cols + f * flat + g * BAND_OUT
                    feats[first : first + BAND_OUT, lanes] = (v * sigmoid(v)).astype(bf16)
    qgt = beside(grads_ref[p] for p in range(grads_ref.shape[0]))
    own_ref[...] = mm(qgt, feats[:cols, :], NT)
    other_ref[...] = mm(qgt, feats[cols:, :], NT)


def proj_part(ids, rtab_t, ext, band, numbers, vecs, grads, cols):
    width, rels = rtab_t.shape
    unit = cols // GROUPS
    gathered, _, _, queries = vecs.shape
    half = jax.ShapeDtypeStruct((width, cols), f32)
    return pl.pallas_call(
        proj_kernel,
        grid_spec=pltpu.PrefetchScalarGridSpec(
            num_scalar_prefetch=1,
            grid=(1,),
            in_specs=[
                whole(rtab_t.shape),
                whole(ext.shape),
                pl.BlockSpec((unit, LANES), lambda s, ids: (ids[0], 0)),
                pl.BlockSpec((unit, LANES), lambda s, ids: (ids[1], 0)),
                whole(numbers.shape),
                whole(vecs.shape),
                whole(grads.shape),
            ],
            out_specs=[whole(half.shape)] * 2,
            scratch_shapes=[
                pltpu.VMEM((2 * cols, gathered * queries), bf16),
                pltpu.VMEM((ext.shape[1], width), bf16),
                pltpu.VMEM((ext.shape[1], width), bf16),
                pltpu.VMEM((rels, 2 * queries), bf16),
                pltpu.VMEM((2, ext.shape[1], 2 * queries), bf16),
                pltpu.VMEM((2, unit, 2 * queries), f32),
            ],
        ),
        out_shape=[half, half],
        compiler_params=params("arbitrary"),
        cost_estimate=cost(6e9, 6e6, 2.5e6),
        name="proj_grad",
    )(ids, rtab_t, ext, band, band, numbers, vecs, grads)


def proj_columns(first, cols, filters, chequer_perm, relation_table, numbers, heads, grads):
    ks = filters.shape[-1]
    rim = ks // 2
    flat = IMG * IMG
    column = first + jnp.arange(cols, dtype=i32)
    f = column // flat
    i = (column % flat) // IMG
    j = column % IMG
    spot = jnp.arange(flat, dtype=i32)
    a = (spot[:, None] // IMG - i[None, :] + rim) % IMG
    b = (spot[:, None] % IMG - j[None, :] + rim) % IMG
    tap = filters[f[None, :], jnp.minimum(a, ks - 1), jnp.minimum(b, ks - 1)]
    matrix = jnp.where((a < ks) & (b < ks), tap, jnp.zeros((), bf16))
    width = heads.shape[1]
    head = heads.transpose(0, 2, 1).reshape(-1, width)
    qg = grads.transpose(0, 2, 1).reshape(-1, width)
    joined = jnp.concatenate([head, relation_table[numbers[:, 2].reshape(-1)]], axis=1)
    pre = mm(joined[:, chequer_perm], matrix)
    return mm(qg, (pre * sigmoid(pre)).astype(bf16), TN)


def rel_kernel(numbers_ref, sums_ref, rel_ref, picks):
    width, rels = rel_ref.shape
    queries = sums_ref.shape[2]
    total = None
    for block in spans(sums_ref.shape[0], picks.shape[1] // queries):
        members = range(block.start, block.stop)
        for i, p in enumerate(members):
            rel = field(numbers_ref, p, 2)
            for r in spans(rels, 128):
                here = iota((r.stop - r.start, queries), 0) + r.start
                picks[r, i * queries : (i + 1) * queries] = onehot(here == rel)
        parts = jnp.concatenate(split(beside(sums_ref[p] for p in members)), axis=0)
        part = mm(parts, picks[...], NT)
        total = part if total is None else total + part
    rel_ref[...] = total[:width, :] + total[width:, :]


def rel_part(numbers, sums, rels):
    count, width, queries = sums.shape
    return pl.pallas_call(
        rel_kernel,
        out_shape=jax.ShapeDtypeStruct((width, rels), f32),
        scratch_shapes=[pltpu.VMEM((rels, math.gcd(count, 16) * queries), bf16)],
        compiler_params=params(),
        cost_estimate=cost(2e9, 3e6),
        name="rel_grad",
    )(numbers, sums)


def entity_kernel(cap, want_ref, srow_ref, own_ref, recv_ref, incoming_ref, out_ref, filt_ref):
    rows = out_ref.shape[1]
    count, _, width = incoming_ref.shape
    half, filts = filt_ref.shape[0] // 2, filt_ref.shape[1]
    grads = jnp.concatenate([incoming_ref[d, :cap, :] for d in range(count)], axis=0)
    turned = grads.astype(f32).T.astype(bf16)
    high, low = split(own_ref[...] + recv_ref[...])
    for c in spans(rows, 256):
        here = iota((want_ref.shape[0], c.stop - c.start), 1) + c.start
        total = mm(turned, onehot(here == want_ref[...]))
        here = iota((srow_ref.shape[0], c.stop - c.start), 1) + c.start
        pick = onehot(here == srow_ref[...])
        out_ref[:, c] = total + mm(high, pick) + mm(low, pick)
    packed = incoming_ref[0, cap:, :].astype(f32)
    for d in range(1, count):
        packed = packed + incoming_ref[d, cap:, :].astype(f32)
    high, low = split(packed)
    for k in range(2):
        lane = iota((width, filts), 0) - 2 * k * filts
        unit = iota((width, filts), 1)
        place = onehot((lane == unit) | (lane == unit + filts))
        filt_ref[k * half : (k + 1) * half, :] = mm(high, place) + mm(low, place)


def entity_sum(want, srow, own, recv, incoming, rows, cap, filts):
    half = incoming.shape[1] - cap
    return pl.pallas_call(
        functools.partial(entity_kernel, cap),
        out_shape=[
            jax.ShapeDtypeStruct((own.shape[0], rows), f32),
            jax.ShapeDtypeStruct((2 * half, filts), f32),
        ],
        compiler_params=params(),
        cost_estimate=cost(1.5e9, 4e6),
        name="entity_grad",
    )(want, srow, own, recv, incoming)


def shards(
    entity_table,
    relation_table,
    filters,
    proj_weight,
    chequer_perm,
    head_owner,
    head_row,
    rel_ids,
    pos_index,
    tail_owner,
    tail_row,
):
    count = lax.axis_size("shard")
    me = lax.axis_index("shard")
    assert count % 2 == 0
    direct = count <= 16
    queries = head_row.shape[0]
    cand = tail_row.shape[0]
    rows, width = entity_table.shape
    rels = relation_table.shape[0]
    filts, ks, _ = filters.shape
    head_cap = 2 * queries // count
    tail_cap = 2 * cand // count
    same_core = [list(range(c, count, 2)) for c in range(2)]
    copies = count // 2 if direct else 1

    def swap(x):
        return lax.ppermute(x, "shard", [(d, d ^ 1) for d in range(count)])

    def exchange(x):
        return lax.all_to_all(x, "shard", split_axis=0, concat_axis=0, tiled=True)

    def gather_core(x):
        if direct:
            return lax.all_to_all(
                x, "shard", split_axis=0, concat_axis=0, axis_index_groups=same_core, tiled=True
            )
        return lax.all_gather(x, "shard", axis=0, axis_index_groups=same_core, tiled=True)

    me1 = me.reshape(1)
    heads = head_owner[:, 0]
    tail_owners = tail_owner[:, 0]
    table_t, rtab_t, weight_t = entity_table.T, relation_table.T, proj_weight.T
    numbers = jnp.concatenate([heads, head_row, rel_ids, pos_index])
    numbers = exchange(jnp.broadcast_to(numbers, (count, 1, 4 * queries)))

    ids = jnp.stack([me, me ^ 1, me & 1])
    tails_t, slot_row = pack_tails(me1, tail_owners, tail_row, table_t, tail_cap)
    all_tails = lax.all_gather(tails_t, "shard", axis=0, tiled=True)
    scand = slot_cands(me1, tail_owners, tail_cap)
    found, want = find_heads(me1, numbers, table_t, head_cap)
    fetched = exchange(found)
    pos = pos_slots(tail_owners, pos_index, tail_cap)

    codes = jnp.asarray(band_codes(ks))
    band, band_t = build_band(filters, codes)
    extra = BAND_OUT * (GROUPS - 1) + LANES - IMG * IMG - BAND_OUT
    ext = jnp.concatenate([chequer_perm[-BAND_OUT:], chequer_perm, chequer_perm[:extra]])[None]
    orow = heads[None, :]
    slope, img, qv, vecs = front(
        fetched, orow, rel_ids[None, :], rtab_t, ext, band, weight_t, head_cap, copies
    )
    core_vecs = gather_core(vecs)

    spread, sums, qgt, fgrad = middle(
        pos, qv, ext, band_t, all_tails, weight_t, slope, cand, copies
    )
    all_sums = lax.all_gather(sums, "shard", axis=0, tiled=True)
    qgt, core_vecs = lax.optimization_barrier((qgt, core_vecs))
    core_qgt = gather_core(qgt)
    outgoing = filter_sums(
        fgrad, img, codes, orow, ext, spread, count, width, head_cap, ks * ks
    )
    own, other = tail_part(ids, all_tails, scand, numbers, core_vecs, cand)
    outgoing, core_qgt, own, other = lax.optimization_barrier((outgoing, core_qgt, own, other))
    incoming = exchange(outgoing)
    entity_grad, filter_grad = entity_sum(
        want, slot_row, own, swap(other), incoming, rows, head_cap, filts
    )
    filter_grad = filter_grad[: ks * ks].T.reshape(filts, ks, ks)

    cols = filts * IMG * IMG // count
    if direct and cols % (IMG * IMG) == 0:
        own, other = proj_part(ids, rtab_t, ext, band, numbers, core_vecs, core_qgt, cols)
    else:
        core_numbers = lax.dynamic_index_in_dim(
            numbers.reshape(count // 2, 2, 4, queries), me & 1, 1, keepdims=False
        )
        own, other = (
            proj_columns(
                d * cols, cols, filters, chequer_perm, relation_table,
                core_numbers, core_vecs[:, 0], core_qgt,
            )
            for d in (me, me ^ 1)
        )
    proj_grad = (own + swap(other)).T

    relation_grad = rel_part(numbers, all_sums, rels).T
    return (entity_grad.T, relation_grad, filter_grad, proj_grad)


def solution(mesh):
    placed = (
        P("shard", None),
        P(),
        P(),
        P(),
        P(),
        P(("parts", "shard"), None),
        P(("parts", "shard")),
        P(("parts", "shard")),
        P(("parts", "shard")),
        P("parts", None),
        P("parts"),
    )
    return jax.shard_map(
        shards,
        mesh=mesh,
        in_specs=placed,
        out_specs=(
            P(("parts", "shard"), None),
            P("parts", None),
            P("parts", None, None),
            P(("parts", "shard"), None),
        ),
        check_vma=False,
    )
```

```python
import functools
import math

import jax
import jax.numpy as jnp
import numpy as np
from jax import lax
from jax.experimental import pallas as pl
from jax.experimental.pallas import tpu as pltpu
from jax.sharding import PartitionSpec as P

IMG = 20
BAND = 4
GROUPS = IMG // BAND
BAND_OUT = BAND * IMG
LANES = 256

loss_weight = 0.015625
smooth = 0.1

f32 = jnp.float32
bf16 = jnp.bfloat16
i32 = jnp.int32

NN = (((1,), (0,)), ((), ()))
NT = (((1,), (1,)), ((), ()))
TN = (((0,), (0,)), ((), ()))


def mm(a, b, dims=NN):
    return lax.dot_general(a, b, dims, preferred_element_type=f32)


def iota(shape, axis):
    return lax.broadcasted_iota(i32, shape, axis)


def onehot(mask):
    return jnp.where(mask, 1.0, 0.0).astype(bf16)


def split(value):
    high = value.astype(bf16)
    return high, (value - high.astype(f32)).astype(bf16)


def sigmoid(v):
    return 0.5 * jnp.tanh(0.5 * v) + 0.5


def params(*semantics):
    return pltpu.CompilerParams(
        dimension_semantics=semantics or None, vmem_limit_bytes=60 << 20
    )


def cost(flops, nbytes, trans=0):
    return pl.CostEstimate(flops=int(flops), bytes_accessed=int(nbytes), transcendentals=int(trans))


def whole(shape):
    return pl.BlockSpec(shape, lambda *_: (0,) * len(shape))


SMEM = pl.BlockSpec(memory_space=pltpu.SMEM)


def band_codes(ks):
    codes = np.full((IMG, LANES), -1, np.int32)
    for j in range(IMG):
        for r in range(ks):
            for x in range(IMG):
                b = (x - j + ks // 2) % IMG
                if b < ks:
                    codes[j, r * IMG + x] = r * ks + b
    return codes


def band_kernel(codes_ref, filt_ref, out_ref, out_t_ref, scr):
    count, taps = filt_ref.shape
    filt = filt_ref[...]
    for j in range(IMG):
        pick = onehot(iota((taps, LANES), 0) == codes_ref[j : j + 1, :])
        row = mm(filt, pick)
        for di in range(BAND):
            scr[:, di * IMG + j, :] = row if di == 0 else pltpu.roll(row, di * IMG, 1)
    full = scr[...].reshape(count * BAND_OUT, LANES)
    out_ref[...] = full.astype(bf16)
    out_t_ref[...] = full.T.astype(bf16)


def build_band(filters, codes):
    count, ks, _ = filters.shape
    return pl.pallas_call(
        band_kernel,
        out_shape=[
            jax.ShapeDtypeStruct((count * BAND_OUT, LANES), bf16),
            jax.ShapeDtypeStruct((LANES, count * BAND_OUT), bf16),
        ],
        scratch_shapes=[pltpu.VMEM((count, BAND_OUT, LANES), f32)],
        compiler_params=params(),
        cost_estimate=cost(4e7, 4e6),
        name="band",
    )(codes, filters.reshape(count, ks * ks))


VMEM = pl.BlockSpec(memory_space=pltpu.VMEM)


def pairs(count):
    step = 2 if count % 2 == 0 else 1
    return [range(i, i + step) for i in range(0, count, step)]


def beside(blocks):
    return jnp.concatenate(list(blocks), axis=1)


def spans(size, step):
    return [slice(i, min(i + step, size)) for i in range(0, size, step)]


def fill_picks(ref, index):
    rows, lanes = ref.shape
    for r in spans(rows, 64):
        for c in spans(lanes, 256):
            here = iota((r.stop - r.start, c.stop - c.start), 1) + c.start
            ref[r, c] = onehot(here == index[r, :])


def field(ref, d, k):
    queries = ref.shape[2] // 4
    return ref[d, :, k * queries : (k + 1) * queries]


def slot_values(owner, device, value, cap):
    lines = owner.shape[0]
    mine = owner == device
    mine_b = onehot(mine)
    before = onehot(iota((128, 128), 0) < iota((128, 128), 1))
    rank = mm(mine_b, before)
    totals = mm(mine_b, jnp.ones((128, 128), bf16))
    upper = onehot(iota((lines, lines), 1) < iota((lines, lines), 0))
    offset = mm(upper, totals.astype(bf16))
    key = jnp.where(mine, (rank + offset).astype(i32), -1)
    value = (value + 1).astype(f32)
    found = []
    for s in spans(cap, 128):
        slots = iota((s.stop - s.start, 128), 0) + s.start
        total = jnp.zeros(slots.shape, f32)
        for r in range(lines):
            total = total + jnp.where(slots == key[r : r + 1, :], value[r : r + 1, :], 0.0)
        found.append(jnp.sum(total, axis=1, keepdims=True))
    return jnp.concatenate(found, axis=0).astype(i32) - 1


def pack_kernel(me_ref, owner_ref, row_ref, table_hbm, tails_t_ref, srow_ref, picks, table, sem):
    copy = pltpu.make_async_copy(table_hbm, table, sem)
    copy.start()
    cap = srow_ref.shape[0]
    srow = slot_values(owner_ref[...], me_ref[0], row_ref[...], cap)
    srow_ref[...] = srow
    fill_picks(picks, srow)
    copy.wait()
    tails_t_ref[0] = mm(table[...], picks[...], NT).astype(bf16)


def pack_tails(me, tail_owners, tail_row, table_t, cap):
    assert tail_row.shape[0] % 128 == 0
    return pl.pallas_call(
        pack_kernel,
        in_specs=[SMEM, VMEM, VMEM, pl.BlockSpec(memory_space=pl.ANY)],
        out_shape=[
            jax.ShapeDtypeStruct((1, table_t.shape[0], cap), bf16),
            jax.ShapeDtypeStruct((cap, 1), i32),
        ],
        scratch_shapes=[
            pltpu.VMEM((cap, table_t.shape[1]), bf16),
            pltpu.VMEM(table_t.shape, bf16),
            pltpu.SemaphoreType.DMA,
        ],
        compiler_params=params(),
        cost_estimate=cost(1e9, 2e6),
        name="pack_tails",
    )(me, tail_owners.reshape(-1, 128), tail_row.reshape(-1, 128), table_t)


def found_kernel(cap, me_ref, table_ref, numbers_ref, found_ref, want_ref, scr, picks):
    count = numbers_ref.shape[0]
    owners = jnp.concatenate([field(numbers_ref, d, 0) for d in range(count)], axis=0)
    queries = owners.shape[1]
    mine = owners == me_ref[0]
    before = onehot(iota((queries, queries), 0) < iota((queries, queries), 1))
    rank = mm(onehot(mine), before)
    key = jnp.where(mine, rank.astype(i32), -1)
    slots = iota((cap, queries), 0)
    for d in range(count):
        code = (field(numbers_ref, d, 1) + 1).astype(f32)
        picked = jnp.where(slots == key[d : d + 1, :], code, 0.0)
        scr[d * cap : (d + 1) * cap, :] = jnp.sum(picked, axis=1, keepdims=True)
    want = scr[...].astype(i32) - 1
    want_ref[...] = want
    fill_picks(picks, want)
    found = mm(picks[...], table_ref[...], NT).astype(bf16)
    for d in range(count):
        found_ref[d] = found[d * cap : (d + 1) * cap, :]


def find_heads(me, numbers, table_t, cap):
    width = table_t.shape[0]
    count = numbers.shape[0]
    return pl.pallas_call(
        functools.partial(found_kernel, cap),
        in_specs=[SMEM] + [VMEM] * 2,
        out_shape=[
            jax.ShapeDtypeStruct((count, cap, width), bf16),
            jax.ShapeDtypeStruct((count * cap, 1), i32),
        ],
        scratch_shapes=[
            pltpu.VMEM((count * cap, 1), f32),
            pltpu.VMEM((count * cap, table_t.shape[1]), bf16),
        ],
        compiler_params=params(),
        cost_estimate=cost(3e8, 2e6),
        name="find_heads",
    )(me, table_t, numbers)


def cand_kernel(me_ref, owner_ref, out_ref):
    cap = out_ref.shape[1]
    owner = owner_ref[...]
    index = iota(owner.shape, 0) * 128 + iota(owner.shape, 1)
    for k in range(2):
        out_ref[k] = slot_values(owner, me_ref[0] ^ k, index, cap)


def slot_cands(me, tail_owners, cap):
    return pl.pallas_call(
        cand_kernel,
        in_specs=[SMEM, VMEM],
        out_shape=jax.ShapeDtypeStruct((2, cap, 1), i32),
        compiler_params=params(),
        cost_estimate=cost(1e8, 1e6),
        name="slot_cands",
    )(me, tail_owners.reshape(-1, 128))


def pos_kernel(cap, row_ref, pos_ref, out_ref):
    queries = pos_ref.shape[1]
    eye = iota((queries, queries), 0) == iota((queries, queries), 1)
    row = pos_ref[...].astype(f32)
    pos = jnp.sum(jnp.where(eye, row, 0.0), axis=1, keepdims=True).astype(i32)
    lanes = spans(row_ref.shape[1], 128)
    owner = jnp.zeros((queries, 128), f32)
    for c in lanes:
        here = iota((queries, 128), 1) + c.start
        owner = owner + jnp.where(here == pos, row_ref[:, c].astype(f32), 0.0)
    owner = jnp.sum(owner, axis=1, keepdims=True).astype(i32)
    ahead = jnp.zeros((queries, 128), f32)
    for c in lanes:
        here = iota((queries, 128), 1) + c.start
        ahead = ahead + jnp.where((row_ref[:, c] == owner) & (here < pos), 1.0, 0.0)
    ahead = jnp.sum(ahead, axis=1, keepdims=True).astype(i32)
    out_ref[...] = owner * cap + ahead


def pos_slots(tail_owners, pos_index, cap):
    return pl.pallas_call(
        functools.partial(pos_kernel, cap),
        out_shape=jax.ShapeDtypeStruct((pos_index.shape[0], 1), i32),
        compiler_params=params(),
        cost_estimate=cost(1e8, 1e5),
        name="pos_slots",
    )(tail_owners.reshape(1, -1), pos_index.reshape(1, -1))


def slot_picks(cap, slots, orow):
    count = slots // cap
    queries = orow.shape[1]
    member = iota((count, queries), 0) == orow
    before = onehot(iota((queries, queries), 0) < iota((queries, queries), 1))
    rank = mm(onehot(member), before)
    rank = jnp.sum(jnp.where(member, rank, 0.0), axis=0, keepdims=True).astype(i32)
    return onehot(iota((slots, queries), 0) == orow * cap + rank)


def front_kernel(
    cap, fetched_ref, orow_ref, rel_ref, rtab_ref, ext_ref, band_ref, w_ref,
    slope_ref, img_ref, qv_ref, vecs_ref, feats, acc, ext, pre,
):
    s = pl.program_id(0)
    width, queries = acc.shape

    @pl.when(s == 0)
    def _():
        rows = jnp.concatenate([fetched_ref[d] for d in range(fetched_ref.shape[0])], axis=0)
        pick = slot_picks(cap, rows.shape[0], orow_ref[...])
        hvt = mm(rows, pick, TN).astype(bf16)
        for d in range(vecs_ref.shape[0]):
            vecs_ref[d, 0] = hvt
        rels = rtab_ref.shape[1]
        rvt = mm(rtab_ref[...], onehot(iota((rels, queries), 0) == rel_ref[...])).astype(bf16)
        entry = iota((width, ext_ref.shape[1]), 0)
        image = mm(onehot(entry == ext_ref[...]), hvt, TN)
        image = image + mm(onehot(entry + width == ext_ref[...]), rvt, TN)
        ext[...] = image.astype(bf16)
        for g in range(GROUPS):
            img_ref[:, g * queries : (g + 1) * queries] = ext[g * BAND_OUT : g * BAND_OUT + LANES, :]
        acc[...] = jnp.zeros_like(acc)

    units = band_ref.shape[0] // BAND_OUT
    flat = GROUPS * BAND_OUT
    pre[...] = mm(band_ref[...], img_ref[...])
    for f in range(units):
        for g in range(GROUPS):
            rows = slice(f * flat + g * BAND_OUT, f * flat + (g + 1) * BAND_OUT)
            v = pre[f * BAND_OUT : (f + 1) * BAND_OUT, g * queries : (g + 1) * queries]
            sig = sigmoid(v)
            feats[rows, :] = (v * sig).astype(bf16)
            slope_ref[rows, :] = sig * (1.0 + v * (1.0 - sig))
    acc[...] += mm(w_ref[...], feats[...])

    @pl.when(s == pl.num_programs(0) - 1)
    def _():
        query = acc[...]
        qv_ref[...] = query.T.astype(bf16)
        qvt = query.astype(bf16)
        for d in range(vecs_ref.shape[0]):
            vecs_ref[d, 1] = qvt


def filter_block(filts):
    return math.gcd(filts, 8)


def front(fetched, orow, rel_row, rtab_t, ext, band, weight_t, cap, copies):
    queries = orow.shape[1]
    width, flat = weight_t.shape
    filts = band.shape[0] // BAND_OUT
    units = filter_block(filts)
    cols = flat // filts * units
    return pl.pallas_call(
        functools.partial(front_kernel, cap),
        grid=(filts // units,),
        in_specs=[
            whole(fetched.shape),
            whole(orow.shape),
            whole(rel_row.shape),
            whole(rtab_t.shape),
            whole(ext.shape),
            pl.BlockSpec((units * BAND_OUT, LANES), lambda s: (s, 0)),
            pl.BlockSpec((width, cols), lambda s: (0, s)),
        ],
        out_specs=[
            pl.BlockSpec((cols, queries), lambda s: (s, 0)),
            whole((LANES, GROUPS * queries)),
            whole((queries, width)),
            whole((copies, 2, width, queries)),
        ],
        out_shape=[
            jax.ShapeDtypeStruct((flat, queries), f32),
            jax.ShapeDtypeStruct((LANES, GROUPS * queries), bf16),
            jax.ShapeDtypeStruct((queries, width), bf16),
            jax.ShapeDtypeStruct((copies, 2, width, queries), bf16),
        ],
        scratch_shapes=[
            pltpu.VMEM((cols, queries), bf16),
            pltpu.VMEM((width, queries), f32),
            pltpu.VMEM((ext.shape[1], queries), bf16),
            pltpu.VMEM((units * BAND_OUT, GROUPS * queries), f32),
        ],
        compiler_params=params("arbitrary"),
        cost_estimate=cost(4e9, 2.4e7, 2.5e6),
        name="front",
    )(fetched, orow, rel_row, rtab_t, ext, band, weight_t)


def middle_kernel(
    cand, pos_ref, qv_ref, ext_ref, bandt_hbm, tails_hbm, w_hbm, slope_hbm,
    ext, sums_ref, qgt_ref, fgrad_hbm,
    bandt, tails, w, slope, fgrad, scores, grads, spread, linear,
    band_sem, tail_sems, w_sems, slope_sems, out_sems,
):
    owners, width, slots = tails.shape
    steps, _, cols = w.shape
    queries = qv_ref.shape[0]
    chunks = tail_sems.shape[0]
    blocks = owners // chunks
    part_rows = fgrad.shape[1]

    def tail_copy(i):
        span = pl.ds(i * blocks, blocks)
        return pltpu.make_async_copy(tails_hbm.at[span], tails.at[span], tail_sems.at[i])

    def w_copy(k):
        return pltpu.make_async_copy(w_hbm.at[:, pl.ds(k * cols, cols)], w.at[k], w_sems.at[k])

    def slope_copy(k):
        return pltpu.make_async_copy(slope_hbm.at[pl.ds(k * cols, cols)], slope.at[k], slope_sems.at[k])

    def out_copy(k):
        span = pl.ds(k * part_rows, part_rows)
        return pltpu.make_async_copy(fgrad.at[k], fgrad_hbm.at[span], out_sems.at[k])

    for i in range(chunks):
        tail_copy(i).start()
    band_copy = pltpu.make_async_copy(bandt_hbm, bandt, band_sem)
    for k in range(steps):
        w_copy(k).start()
        slope_copy(k).start()
        if k == 0:
            band_copy.start()

    qv = qv_ref[...]
    total = jnp.zeros((queries, width), f32)
    for i in range(chunks):
        tail_copy(i).wait()
        for b in range(blocks):
            o = i * blocks + b
            block = tails[o]
            slot = o % scores.shape[0]
            scores[slot] = mm(qv, block)
            for r in spans(queries, 16):
                here = iota((r.stop - r.start, slots), 1) + o * slots
                target = jnp.where(here == pos_ref[r, :], 1.0 - smooth + smooth / cand, smooth / cand)
                grads[slot, r, :] = ((sigmoid(scores[slot, r, :]) - target) * loss_weight).astype(bf16)
            total = total + mm(grads[slot], block, NT)
    qgt = total.T.astype(bf16)
    for d in range(qgt_ref.shape[0]):
        qgt_ref[d] = qgt

    units = part_rows // BAND_OUT
    flat = GROUPS * BAND_OUT
    for k in range(steps):
        lin = linear.at[k % 2]
        w_copy(k).wait()
        lin[...] = mm(w[k], qgt, TN)
        slope_copy(k).wait()
        for f in range(units):
            for g in range(GROUPS):
                rows = slice(f * flat + g * BAND_OUT, f * flat + (g + 1) * BAND_OUT)
                part = slice(f * BAND_OUT, (f + 1) * BAND_OUT)
                lanes = slice(g * queries, (g + 1) * queries)
                fgrad[k, part, lanes] = (lin[rows, :] * slope[k, rows, :]).astype(bf16)
        out_copy(k).start()
        if k == 0:
            band_copy.wait()
        spread_k = mm(bandt[:, k * part_rows : (k + 1) * part_rows], fgrad[k])
        if k == 0:
            spread[...] = spread_k
        else:
            spread[...] += spread_k

    ext[...] = jnp.zeros_like(ext)
    for g in range(GROUPS):
        ext[g * BAND_OUT : g * BAND_OUT + LANES, :] += spread[:, g * queries : (g + 1) * queries]
    high, low = split(ext[...])
    rpick = onehot(iota((width, ext.shape[0]), 0) + width == ext_ref[...])
    sums_ref[0] = mm(rpick, high) + mm(rpick, low)
    for k in range(steps):
        out_copy(k).wait()


def middle(pos, qv, ext, band_t, tails, weight_t, slope, cand, copies):
    queries, width = qv.shape
    owners, _, slots = tails.shape
    flat = weight_t.shape[1]
    filts = band_t.shape[1] // BAND_OUT
    units = math.gcd(filts, 16)
    steps = filts // units
    cols = flat // steps
    rows = units * BAND_OUT
    blocks = math.gcd(owners, max(1, 2048 // slots))
    ring = min(owners, 4)
    hbm = pl.BlockSpec(memory_space=pl.ANY)
    return pl.pallas_call(
        functools.partial(middle_kernel, cand),
        in_specs=[VMEM] * 3 + [hbm] * 4,
        out_specs=[VMEM] * 3 + [hbm],
        out_shape=[
            jax.ShapeDtypeStruct((ext.shape[1], queries), f32),
            jax.ShapeDtypeStruct((1, width, queries), f32),
            jax.ShapeDtypeStruct((copies, width, queries), bf16),
            jax.ShapeDtypeStruct((filts * BAND_OUT, GROUPS * queries), bf16),
        ],
        scratch_shapes=[
            pltpu.VMEM(band_t.shape, bf16),
            pltpu.VMEM(tails.shape, bf16),
            pltpu.VMEM((steps, width, cols), bf16),
            pltpu.VMEM((steps, cols, queries), f32),
            pltpu.VMEM((steps, rows, GROUPS * queries), bf16),
            pltpu.VMEM((ring, queries, slots), f32),
            pltpu.VMEM((ring, queries, slots), bf16),
            pltpu.VMEM((LANES, GROUPS * queries), f32),
            pltpu.VMEM((2, cols, queries), f32),
            pltpu.SemaphoreType.DMA,
            pltpu.SemaphoreType.DMA((owners // blocks,)),
            pltpu.SemaphoreType.DMA((steps,)),
            pltpu.SemaphoreType.DMA((steps,)),
            pltpu.SemaphoreType.DMA((steps,)),
        ],
        compiler_params=params(),
        cost_estimate=cost(6e9, 2.5e7, 5e5),
        name="middle",
    )(pos, qv, ext, band_t, tails, weight_t, slope)


def half_taps(taps):
    return -(-taps // 32) * 16


def diag_kernel(
    cap, taps, codes_ref, orow_ref, ext_ref, spread_ref, fgrad_ref, img_ref, out_ref, corr_ref
):
    s = pl.program_id(0)
    units = fgrad_ref.shape[0] // BAND_OUT
    part = mm(fgrad_ref[...], img_ref[...], NT)
    corr_ref[pl.ds(s * units, units)] = part.reshape(units, BAND_OUT, LANES)

    @pl.when(s == pl.num_programs(0) - 1)
    def _():
        width = out_ref.shape[2]
        high, low = split(spread_ref[...])
        hpick = onehot(iota((width, spread_ref.shape[0]), 0) == ext_ref[...])
        hgrad = (mm(hpick, high) + mm(hpick, low)).astype(bf16)
        pick = slot_picks(cap, out_ref.shape[0] * cap, orow_ref[...])
        rows = mm(pick, hgrad, NT).astype(bf16)
        diag_sums(cap, taps, codes_ref, corr_ref, rows, out_ref)


def diag_sums(cap, taps, codes_ref, corr_ref, rows, out_ref):
    filts = corr_ref.shape[0]
    width = out_ref.shape[2]
    half = half_taps(taps)
    total = jnp.zeros((2 * half, filts), f32)
    for j in range(IMG):
        line = corr_ref[:, j, :]
        for di in range(1, BAND):
            line = line + pltpu.roll(corr_ref[:, di * IMG + j, :], LANES - di * IMG, 1)
        pick = onehot(iota((2 * half, LANES), 0) == codes_ref[j : j + 1, :])
        high, low = split(line)
        total = total + mm(pick, high, NT) + mm(pick, low, NT)
    packed = jnp.zeros((half, width), f32)
    for k in range(2):
        for i, piece in enumerate(split(total[k * half : (k + 1) * half, :])):
            place = onehot(iota((filts, width), 1) == iota((filts, width), 0) + (2 * k + i) * filts)
            packed = packed + mm(piece, place)
    packed = packed.astype(bf16)
    for d in range(out_ref.shape[0]):
        out_ref[d, :cap, :] = rows[d * cap : (d + 1) * cap, :]
        out_ref[d, cap:, :] = packed


def filter_sums(fgrad, img, codes, orow, ext, spread, count, width, cap, taps):
    filts = fgrad.shape[0] // BAND_OUT
    units = filter_block(filts)
    assert 4 * filts <= width
    out = (count, cap + half_taps(taps), width)
    return pl.pallas_call(
        functools.partial(diag_kernel, cap, taps),
        grid=(filts // units,),
        in_specs=[
            whole(codes.shape),
            whole(orow.shape),
            whole(ext.shape),
            whole(spread.shape),
            pl.BlockSpec((units * BAND_OUT, fgrad.shape[1]), lambda s: (s, 0)),
            whole(img.shape),
        ],
        out_specs=whole(out),
        out_shape=jax.ShapeDtypeStruct(out, bf16),
        scratch_shapes=[pltpu.VMEM((filts, BAND_OUT, LANES), f32)],
        compiler_params=params("arbitrary"),
        cost_estimate=cost(2e9, 6e6),
        name="filter_sums",
    )(codes, orow, ext, spread, fgrad, img)


def tail_kernel(
    cand, ids_ref, tails_ref, mate_ref, scand_ref, numbers_ref, vecs_ref, own_ref, other_ref, scores, grads
):
    cap = own_ref.shape[1]
    tails = jnp.concatenate([ref[0].astype(f32).T for ref in (tails_ref, mate_ref)], axis=0).astype(bf16)
    scand = jnp.concatenate([scand_ref[0], scand_ref[1]], axis=0)
    own = jnp.zeros(own_ref.shape, f32)
    other = jnp.zeros(own_ref.shape, f32)
    for i, group in enumerate(pairs(vecs_ref.shape[0])):
        qvt = beside(vecs_ref[p, 1] for p in group)
        pos = beside(field(numbers_ref, 2 * p + ids_ref[2], 3) for p in group)
        score, grad = scores.at[i % 2], grads.at[i % 2]
        score[...] = mm(tails, qvt)
        for r in spans(2 * cap, 64):
            target = jnp.where(scand[r, :] == pos, 1.0 - smooth + smooth / cand, smooth / cand)
            grad[r, :] = ((sigmoid(score[r, :]) - target) * loss_weight).astype(bf16)
        own = own + mm(qvt, grad[:cap, :], NT)
        other = other + mm(qvt, grad[cap:, :], NT)
    own_ref[...] = own
    other_ref[...] = other


def tail_part(ids, tails, scand, numbers, vecs, cand):
    _, width, cap = tails.shape
    half = jax.ShapeDtypeStruct((width, cap), f32)
    return pl.pallas_call(
        functools.partial(tail_kernel, cand),
        grid_spec=pltpu.PrefetchScalarGridSpec(
            num_scalar_prefetch=1,
            grid=(1,),
            in_specs=[
                pl.BlockSpec((1, width, cap), lambda s, ids: (ids[0], 0, 0)),
                pl.BlockSpec((1, width, cap), lambda s, ids: (ids[1], 0, 0)),
                whole(scand.shape),
                whole(numbers.shape),
                whole(vecs.shape),
            ],
            out_specs=[whole(half.shape)] * 2,
            scratch_shapes=[
                pltpu.VMEM((2, 2 * cap, 2 * vecs.shape[3]), f32),
                pltpu.VMEM((2, 2 * cap, 2 * vecs.shape[3]), bf16),
            ],
        ),
        out_shape=[half, half],
        compiler_params=params("arbitrary"),
        cost_estimate=cost(2e9, 3e6, 1e6),
        name="tail_grad",
    )(ids, tails, tails, scand, numbers, vecs)


def proj_kernel(
    ids_ref, rtab_ref, ext_ref, band_ref, mate_ref, numbers_ref, vecs_ref, grads_ref,
    own_ref, other_ref, feats, hpick, rpick, rels_hot, ext, pre,
):
    width, rels = rtab_ref.shape
    units = band_ref.shape[0] // BAND_OUT
    flat = GROUPS * BAND_OUT
    cols = units * flat
    entry = iota((width, ext_ref.shape[1]), 0)
    hpick[...] = jnp.where(entry == ext_ref[...], 1.0, 0.0).T.astype(bf16)
    rpick[...] = jnp.where(entry + width == ext_ref[...], 1.0, 0.0).T.astype(bf16)
    queries = vecs_ref.shape[3]
    for i, group in enumerate(pairs(vecs_ref.shape[0])):
        hvt = beside(vecs_ref[p, 0] for p in group)
        rel = beside(field(numbers_ref, 2 * p + ids_ref[2], 2) for p in group)
        for r in spans(rels, 64):
            rels_hot[r, :] = onehot(iota((r.stop - r.start, rel.shape[1]), 0) + r.start == rel)
        rvt = mm(rtab_ref[...], rels_hot[...]).astype(bf16)
        image = ext.at[i % 2]
        image[...] = (mm(hpick[...], hvt) + mm(rpick[...], rvt)).astype(bf16)
        lanes = slice(group[0] * queries, (group[-1] + 1) * queries)
        for k, source in enumerate((band_ref, mate_ref)):
            for g in range(GROUPS):
                slot = (k * GROUPS + g) % 2
                pre[slot] = mm(source[...], image[g * BAND_OUT : g * BAND_OUT + LANES, :])
                for f in range(units):
                    v = pre[slot, f * BAND_OUT : (f + 1) * BAND_OUT, :]
                    first = k * cols + f * flat + g * BAND_OUT
                    feats[first : first + BAND_OUT, lanes] = (v * sigmoid(v)).astype(bf16)
    qgt = beside(grads_ref[p] for p in range(grads_ref.shape[0]))
    own_ref[...] = mm(qgt, feats[:cols, :], NT)
    other_ref[...] = mm(qgt, feats[cols:, :], NT)


def proj_part(ids, rtab_t, ext, band, numbers, vecs, grads, cols):
    width, rels = rtab_t.shape
    unit = cols // GROUPS
    gathered, _, _, queries = vecs.shape
    half = jax.ShapeDtypeStruct((width, cols), f32)
    return pl.pallas_call(
        proj_kernel,
        grid_spec=pltpu.PrefetchScalarGridSpec(
            num_scalar_prefetch=1,
            grid=(1,),
            in_specs=[
                whole(rtab_t.shape),
                whole(ext.shape),
                pl.BlockSpec((unit, LANES), lambda s, ids: (ids[0], 0)),
                pl.BlockSpec((unit, LANES), lambda s, ids: (ids[1], 0)),
                whole(numbers.shape),
                whole(vecs.shape),
                whole(grads.shape),
            ],
            out_specs=[whole(half.shape)] * 2,
            scratch_shapes=[
                pltpu.VMEM((2 * cols, gathered * queries), bf16),
                pltpu.VMEM((ext.shape[1], width), bf16),
                pltpu.VMEM((ext.shape[1], width), bf16),
                pltpu.VMEM((rels, 2 * queries), bf16),
                pltpu.VMEM((2, ext.shape[1], 2 * queries), bf16),
                pltpu.VMEM((2, unit, 2 * queries), f32),
            ],
        ),
        out_shape=[half, half],
        compiler_params=params("arbitrary"),
        cost_estimate=cost(6e9, 6e6, 2.5e6),
        name="proj_grad",
    )(ids, rtab_t, ext, band, band, numbers, vecs, grads)


def proj_columns(first, cols, filters, chequer_perm, relation_table, numbers, heads, grads):
    ks = filters.shape[-1]
    rim = ks // 2
    flat = IMG * IMG
    column = first + jnp.arange(cols, dtype=i32)
    f = column // flat
    i = (column % flat) // IMG
    j = column % IMG
    spot = jnp.arange(flat, dtype=i32)
    a = (spot[:, None] // IMG - i[None, :] + rim) % IMG
    b = (spot[:, None] % IMG - j[None, :] + rim) % IMG
    tap = filters[f[None, :], jnp.minimum(a, ks - 1), jnp.minimum(b, ks - 1)]
    matrix = jnp.where((a < ks) & (b < ks), tap, jnp.zeros((), bf16))
    width = heads.shape[1]
    head = heads.transpose(0, 2, 1).reshape(-1, width)
    qg = grads.transpose(0, 2, 1).reshape(-1, width)
    joined = jnp.concatenate([head, relation_table[numbers[:, 2].reshape(-1)]], axis=1)
    pre = mm(joined[:, chequer_perm], matrix)
    return mm(qg, (pre * sigmoid(pre)).astype(bf16), TN)


def rel_kernel(numbers_ref, sums_ref, rel_ref, picks):
    width, rels = rel_ref.shape
    queries = sums_ref.shape[2]
    total = None
    for block in spans(sums_ref.shape[0], picks.shape[1] // queries):
        members = range(block.start, block.stop)
        for i, p in enumerate(members):
            rel = field(numbers_ref, p, 2)
            for r in spans(rels, 128):
                here = iota((r.stop - r.start, queries), 0) + r.start
                picks[r, i * queries : (i + 1) * queries] = onehot(here == rel)
        parts = jnp.concatenate(split(beside(sums_ref[p] for p in members)), axis=0)
        part = mm(parts, picks[...], NT)
        total = part if total is None else total + part
    rel_ref[...] = total[:width, :] + total[width:, :]


def rel_part(numbers, sums, rels):
    count, width, queries = sums.shape
    return pl.pallas_call(
        rel_kernel,
        out_shape=jax.ShapeDtypeStruct((width, rels), f32),
        scratch_shapes=[pltpu.VMEM((rels, math.gcd(count, 16) * queries), bf16)],
        compiler_params=params(),
        cost_estimate=cost(2e9, 3e6),
        name="rel_grad",
    )(numbers, sums)


def owned_kernel(srow_ref, own_ref, recv_ref, out_ref, parts):
    slots = srow_ref.shape[0]
    width, lanes = out_ref.shape
    s = pl.program_id(0)

    @pl.when(s == 0)
    def _():
        parts[:width, :], parts[width:, :] = split(own_ref[...] + recv_ref[...])

    here = iota((slots, lanes), 1) + s * lanes
    total = mm(parts[...], onehot(here == srow_ref[...]))
    out_ref[...] = total[:width, :] + total[width:, :]


def owned_sum(srow, own, recv, rows):
    width, slots = own.shape
    lanes = math.gcd(rows, 512)
    return pl.pallas_call(
        owned_kernel,
        grid=(rows // lanes,),
        in_specs=[whole(srow.shape), whole(own.shape), whole(recv.shape)],
        out_specs=pl.BlockSpec((width, lanes), lambda s: (0, s)),
        out_shape=jax.ShapeDtypeStruct((width, rows), f32),
        scratch_shapes=[pltpu.VMEM((2 * width, slots), bf16)],
        compiler_params=params("arbitrary"),
        cost_estimate=cost(1.5e9, 4e6),
        name="owned_grad",
    )(srow, own, recv)


def entity_kernel(cap, want_ref, incoming_ref, base_ref, out_ref, filt_ref, turned):
    lanes = out_ref.shape[1]
    count, _, width = incoming_ref.shape
    half, filts = filt_ref.shape[0] // 2, filt_ref.shape[1]
    s = pl.program_id(0)

    @pl.when(s == 0)
    def _():
        grads = jnp.concatenate([incoming_ref[d, :cap, :] for d in range(count)], axis=0)
        turned[...] = grads.astype(f32).T.astype(bf16)
        packed = incoming_ref[0, cap:, :].astype(f32)
        for d in range(1, count):
            packed = packed + incoming_ref[d, cap:, :].astype(f32)
        high, low = split(packed)
        for k in range(2):
            lane = iota((width, filts), 0) - 2 * k * filts
            unit = iota((width, filts), 1)
            place = onehot((lane == unit) | (lane == unit + filts))
            filt_ref[k * half : (k + 1) * half, :] = mm(high, place) + mm(low, place)

    here = iota((want_ref.shape[0], lanes), 1) + s * lanes
    out_ref[...] = base_ref[...] + mm(turned[...], onehot(here == want_ref[...]))


def entity_sum(want, incoming, base, cap, filts):
    half = incoming.shape[1] - cap
    width, rows = base.shape
    lanes = math.gcd(rows, 512)
    block = pl.BlockSpec((width, lanes), lambda s: (0, s))
    return pl.pallas_call(
        functools.partial(entity_kernel, cap),
        grid=(rows // lanes,),
        in_specs=[whole(want.shape), whole(incoming.shape), block],
        out_specs=[block, whole((2 * half, filts))],
        out_shape=[
            jax.ShapeDtypeStruct(base.shape, f32),
            jax.ShapeDtypeStruct((2 * half, filts), f32),
        ],
        scratch_shapes=[pltpu.VMEM((width, want.shape[0]), bf16)],
        compiler_params=params("arbitrary"),
        cost_estimate=cost(1e9, 4e6),
        name="entity_grad",
    )(want, incoming, base)


def shards(
    entity_table,
    relation_table,
    filters,
    proj_weight,
    chequer_perm,
    head_owner,
    head_row,
    rel_ids,
    pos_index,
    tail_owner,
    tail_row,
):
    count = lax.axis_size("shard")
    me = lax.axis_index("shard")
    assert count % 2 == 0
    direct = count <= 16
    queries = head_row.shape[0]
    cand = tail_row.shape[0]
    rows, width = entity_table.shape
    rels = relation_table.shape[0]
    filts, ks, _ = filters.shape
    head_cap = 2 * queries // count
    tail_cap = 2 * cand // count
    same_core = [list(range(c, count, 2)) for c in range(2)]
    copies = count // 2 if direct else 1

    def swap(x):
        return lax.ppermute(x, "shard", [(d, d ^ 1) for d in range(count)])

    def exchange(x):
        return lax.all_to_all(x, "shard", split_axis=0, concat_axis=0, tiled=True)

    def gather_core(x):
        if direct:
            return lax.all_to_all(
                x, "shard", split_axis=0, concat_axis=0, axis_index_groups=same_core, tiled=True
            )
        return lax.all_gather(x, "shard", axis=0, axis_index_groups=same_core, tiled=True)

    me1 = me.reshape(1)
    heads = head_owner[:, 0]
    tail_owners = tail_owner[:, 0]
    table_t, rtab_t, weight_t = entity_table.T, relation_table.T, proj_weight.T
    numbers = jnp.concatenate([heads, head_row, rel_ids, pos_index])
    numbers = exchange(jnp.broadcast_to(numbers, (count, 1, 4 * queries)))

    ids = jnp.stack([me, me ^ 1, me & 1])
    tails_t, slot_row = pack_tails(me1, tail_owners, tail_row, table_t, tail_cap)
    all_tails = lax.all_gather(tails_t, "shard", axis=0, tiled=True)
    scand = slot_cands(me1, tail_owners, tail_cap)
    found, want = find_heads(me1, numbers, table_t, head_cap)
    fetched = exchange(found)
    pos = pos_slots(tail_owners, pos_index, tail_cap)

    codes = jnp.asarray(band_codes(ks))
    band, band_t = build_band(filters, codes)
    extra = BAND_OUT * (GROUPS - 1) + LANES - IMG * IMG - BAND_OUT
    ext = jnp.concatenate([chequer_perm[-BAND_OUT:], chequer_perm, chequer_perm[:extra]])[None]
    orow = heads[None, :]
    slope, img, qv, vecs = front(
        fetched, orow, rel_ids[None, :], rtab_t, ext, band, weight_t, head_cap, copies
    )
    core_vecs = gather_core(vecs)

    spread, sums, qgt, fgrad = middle(
        pos, qv, ext, band_t, all_tails, weight_t, slope, cand, copies
    )
    all_sums = lax.all_gather(sums, "shard", axis=0, tiled=True)
    qgt, core_vecs = lax.optimization_barrier((qgt, core_vecs))
    core_qgt = gather_core(qgt)
    outgoing = filter_sums(
        fgrad, img, codes, orow, ext, spread, count, width, head_cap, ks * ks
    )
    outgoing, core_qgt, scand = lax.optimization_barrier((outgoing, core_qgt, scand))
    incoming = exchange(outgoing)
    own, other = tail_part(ids, all_tails, scand, numbers, core_vecs, cand)
    core_qgt, own, other = lax.optimization_barrier((core_qgt, own, other))
    base = owned_sum(slot_row, own, swap(other), rows)
    entity_grad, filter_grad = entity_sum(want, incoming, base, head_cap, filts)
    filter_grad = filter_grad[: ks * ks].T.reshape(filts, ks, ks)

    cols = filts * IMG * IMG // count
    if direct and cols % (IMG * IMG) == 0:
        own, other = proj_part(ids, rtab_t, ext, band, numbers, core_vecs, core_qgt, cols)
    else:
        core_numbers = lax.dynamic_index_in_dim(
            numbers.reshape(count // 2, 2, 4, queries), me & 1, 1, keepdims=False
        )
        own, other = (
            proj_columns(
                d * cols, cols, filters, chequer_perm, relation_table,
                core_numbers, core_vecs[:, 0], core_qgt,
            )
            for d in (me, me ^ 1)
        )
    proj_grad = (own + swap(other)).T

    relation_grad = rel_part(numbers, all_sums, rels).T
    return (entity_grad.T, relation_grad, filter_grad, proj_grad)


def solution(mesh):
    placed = (
        P("shard", None),
        P(),
        P(),
        P(),
        P(),
        P(("parts", "shard"), None),
        P(("parts", "shard")),
        P(("parts", "shard")),
        P(("parts", "shard")),
        P("parts", None),
        P("parts"),
    )
    return jax.shard_map(
        shards,
        mesh=mesh,
        in_specs=placed,
        out_specs=(
            P(("parts", "shard"), None),
            P("parts", None),
            P("parts", None, None),
            P(("parts", "shard"), None),
        ),
        check_vma=False,
    )
```

```python
import functools
import math

import jax
import jax.numpy as jnp
import numpy as np
from jax import lax
from jax.experimental import pallas as pl
from jax.experimental.pallas import tpu as pltpu
from jax.sharding import PartitionSpec as P

IMG = 20
BAND = 4
GROUPS = IMG // BAND
BAND_OUT = BAND * IMG
LANES = 256

loss_weight = 0.015625
smooth = 0.1

f32 = jnp.float32
bf16 = jnp.bfloat16
i32 = jnp.int32

NN = (((1,), (0,)), ((), ()))
NT = (((1,), (1,)), ((), ()))
TN = (((0,), (0,)), ((), ()))


def mm(a, b, dims=NN):
    return lax.dot_general(a, b, dims, preferred_element_type=f32)


def iota(shape, axis):
    return lax.broadcasted_iota(i32, shape, axis)


def onehot(mask):
    return jnp.where(mask, 1.0, 0.0).astype(bf16)


def split(value):
    high = value.astype(bf16)
    return high, (value - high.astype(f32)).astype(bf16)


def sigmoid(v):
    return 0.5 * jnp.tanh(0.5 * v) + 0.5


def params(*semantics):
    return pltpu.CompilerParams(
        dimension_semantics=semantics or None, vmem_limit_bytes=60 << 20
    )


def cost(flops, nbytes, trans=0):
    return pl.CostEstimate(flops=int(flops), bytes_accessed=int(nbytes), transcendentals=int(trans))


def whole(shape):
    return pl.BlockSpec(shape, lambda *_: (0,) * len(shape))


SMEM = pl.BlockSpec(memory_space=pltpu.SMEM)


def band_codes(ks):
    codes = np.full((IMG, LANES), -1, np.int32)
    for j in range(IMG):
        for r in range(ks):
            for x in range(IMG):
                b = (x - j + ks // 2) % IMG
                if b < ks:
                    codes[j, r * IMG + x] = r * ks + b
    return codes


def band_kernel(codes_ref, filt_ref, out_ref, out_t_ref, scr):
    count, taps = filt_ref.shape
    filt = filt_ref[...]
    for j in range(IMG):
        pick = onehot(iota((taps, LANES), 0) == codes_ref[j : j + 1, :])
        row = mm(filt, pick)
        for di in range(BAND):
            scr[:, di * IMG + j, :] = row if di == 0 else pltpu.roll(row, di * IMG, 1)
    full = scr[...].reshape(count * BAND_OUT, LANES)
    out_ref[...] = full.astype(bf16)
    out_t_ref[...] = full.T.astype(bf16)


def build_band(filters, codes):
    count, ks, _ = filters.shape
    return pl.pallas_call(
        band_kernel,
        out_shape=[
            jax.ShapeDtypeStruct((count * BAND_OUT, LANES), bf16),
            jax.ShapeDtypeStruct((LANES, count * BAND_OUT), bf16),
        ],
        scratch_shapes=[pltpu.VMEM((count, BAND_OUT, LANES), f32)],
        compiler_params=params(),
        cost_estimate=cost(4e7, 4e6),
        name="band",
    )(codes, filters.reshape(count, ks * ks))


VMEM = pl.BlockSpec(memory_space=pltpu.VMEM)


def pairs(count):
    step = 2 if count % 2 == 0 else 1
    return [range(i, i + step) for i in range(0, count, step)]


def beside(blocks):
    return jnp.concatenate(list(blocks), axis=1)


def spans(size, step):
    return [slice(i, min(i + step, size)) for i in range(0, size, step)]


def fill_picks(ref, index):
    rows, lanes = ref.shape
    for r in spans(rows, 64):
        for c in spans(lanes, 256):
            here = iota((r.stop - r.start, c.stop - c.start), 1) + c.start
            ref[r, c] = onehot(here == index[r, :])


def field(ref, d, k):
    queries = ref.shape[2] // 4
    return ref[d, :, k * queries : (k + 1) * queries]


def slot_values(owner, device, value, cap):
    lines = owner.shape[0]
    mine = owner == device
    mine_b = onehot(mine)
    before = onehot(iota((128, 128), 0) < iota((128, 128), 1))
    rank = mm(mine_b, before)
    totals = mm(mine_b, jnp.ones((128, 128), bf16))
    upper = onehot(iota((lines, lines), 1) < iota((lines, lines), 0))
    offset = mm(upper, totals.astype(bf16))
    key = jnp.where(mine, (rank + offset).astype(i32), -1)
    value = (value + 1).astype(f32)
    found = []
    for s in spans(cap, 128):
        slots = iota((s.stop - s.start, 128), 0) + s.start
        total = jnp.zeros(slots.shape, f32)
        for r in range(lines):
            total = total + jnp.where(slots == key[r : r + 1, :], value[r : r + 1, :], 0.0)
        found.append(jnp.sum(total, axis=1, keepdims=True))
    return jnp.concatenate(found, axis=0).astype(i32) - 1


def pack_kernel(
    shift, me_ref, owner_ref, row_ref, table_hbm, tails_t_ref, srow_ref, cand_ref, picks, table, sem
):
    copy = pltpu.make_async_copy(table_hbm, table, sem)
    copy.start()
    cap = srow_ref.shape[0]
    lines = owner_ref.shape[0]
    index = iota((lines, 128), 0) * 128 + iota((lines, 128), 1)
    found = slot_values(owner_ref[...], me_ref[0], row_ref[...] * (1 << shift) + index, cap)
    srow = lax.shift_right_arithmetic(found, shift)
    srow_ref[...] = srow
    cand_ref[...] = jnp.where(found < 0, -1, found & ((1 << shift) - 1))
    fill_picks(picks, srow)
    copy.wait()
    tails_t_ref[0] = mm(table[...], picks[...], NT).astype(bf16)


def pack_tails(me, tail_owners, tail_row, table_t, cap):
    shift = int(math.log2(tail_row.shape[0]))
    assert shift >= 7 and 1 << shift == tail_row.shape[0]
    assert table_t.shape[1] << shift < 1 << 24
    return pl.pallas_call(
        functools.partial(pack_kernel, shift),
        in_specs=[SMEM, VMEM, VMEM, pl.BlockSpec(memory_space=pl.ANY)],
        out_shape=[
            jax.ShapeDtypeStruct((1, table_t.shape[0], cap), bf16),
            jax.ShapeDtypeStruct((cap, 1), i32),
            jax.ShapeDtypeStruct((cap, 1), i32),
        ],
        scratch_shapes=[
            pltpu.VMEM((cap, table_t.shape[1]), bf16),
            pltpu.VMEM(table_t.shape, bf16),
            pltpu.SemaphoreType.DMA,
        ],
        compiler_params=params(),
        cost_estimate=cost(1e9, 2e6),
        name="pack_tails",
    )(me, tail_owners.reshape(-1, 128), tail_row.reshape(-1, 128), table_t)


def found_kernel(cap, me_ref, table_ref, numbers_ref, found_ref, want_ref, scr, picks):
    count = numbers_ref.shape[0]
    owners = jnp.concatenate([field(numbers_ref, d, 0) for d in range(count)], axis=0)
    queries = owners.shape[1]
    mine = owners == me_ref[0]
    before = onehot(iota((queries, queries), 0) < iota((queries, queries), 1))
    rank = mm(onehot(mine), before)
    key = jnp.where(mine, rank.astype(i32), -1)
    slots = iota((cap, queries), 0)
    for d in range(count):
        code = (field(numbers_ref, d, 1) + 1).astype(f32)
        picked = jnp.where(slots == key[d : d + 1, :], code, 0.0)
        scr[d * cap : (d + 1) * cap, :] = jnp.sum(picked, axis=1, keepdims=True)
    want = scr[...].astype(i32) - 1
    want_ref[...] = want
    fill_picks(picks, want)
    found = mm(picks[...], table_ref[...], NT).astype(bf16)
    for d in range(count):
        found_ref[d] = found[d * cap : (d + 1) * cap, :]


def find_heads(me, numbers, table_t, cap):
    width = table_t.shape[0]
    count = numbers.shape[0]
    return pl.pallas_call(
        functools.partial(found_kernel, cap),
        in_specs=[SMEM] + [VMEM] * 2,
        out_shape=[
            jax.ShapeDtypeStruct((count, cap, width), bf16),
            jax.ShapeDtypeStruct((count * cap, 1), i32),
        ],
        scratch_shapes=[
            pltpu.VMEM((count * cap, 1), f32),
            pltpu.VMEM((count * cap, table_t.shape[1]), bf16),
        ],
        compiler_params=params(),
        cost_estimate=cost(3e8, 2e6),
        name="find_heads",
    )(me, table_t, numbers)


def cand_kernel(me_ref, owner_ref, out_ref):
    owner = owner_ref[...]
    index = iota(owner.shape, 0) * 128 + iota(owner.shape, 1)
    out_ref[...] = slot_values(owner, me_ref[0] ^ 1, index, out_ref.shape[0])


def mate_cands(me, tail_owners, cap):
    return pl.pallas_call(
        cand_kernel,
        in_specs=[SMEM, VMEM],
        out_shape=jax.ShapeDtypeStruct((cap, 1), i32),
        compiler_params=params(),
        cost_estimate=cost(1e8, 1e6),
        name="mate_cands",
    )(me, tail_owners.reshape(-1, 128))


def pos_kernel(cap, row_ref, pos_ref, out_ref):
    queries = pos_ref.shape[1]
    eye = iota((queries, queries), 0) == iota((queries, queries), 1)
    row = pos_ref[...].astype(f32)
    pos = jnp.sum(jnp.where(eye, row, 0.0), axis=1, keepdims=True).astype(i32)
    lanes = spans(row_ref.shape[1], 128)
    owner = jnp.zeros((queries, 128), f32)
    for c in lanes:
        here = iota((queries, 128), 1) + c.start
        owner = owner + jnp.where(here == pos, row_ref[:, c].astype(f32), 0.0)
    owner = jnp.sum(owner, axis=1, keepdims=True).astype(i32)
    ahead = jnp.zeros((queries, 128), f32)
    for c in lanes:
        here = iota((queries, 128), 1) + c.start
        ahead = ahead + jnp.where((row_ref[:, c] == owner) & (here < pos), 1.0, 0.0)
    ahead = jnp.sum(ahead, axis=1, keepdims=True).astype(i32)
    out_ref[...] = owner * cap + ahead


def pos_slots(tail_owners, pos_index, cap):
    return pl.pallas_call(
        functools.partial(pos_kernel, cap),
        out_shape=jax.ShapeDtypeStruct((pos_index.shape[0], 1), i32),
        compiler_params=params(),
        cost_estimate=cost(1e8, 1e5),
        name="pos_slots",
    )(tail_owners.reshape(1, -1), pos_index.reshape(1, -1))


def slot_picks(cap, slots, orow):
    count = slots // cap
    queries = orow.shape[1]
    member = iota((count, queries), 0) == orow
    before = onehot(iota((queries, queries), 0) < iota((queries, queries), 1))
    rank = mm(onehot(member), before)
    rank = jnp.sum(jnp.where(member, rank, 0.0), axis=0, keepdims=True).astype(i32)
    return onehot(iota((slots, queries), 0) == orow * cap + rank)


def front_kernel(
    cap, fetched_ref, orow_ref, rel_ref, rtab_ref, ext_ref, band_ref, w_ref,
    slope_ref, img_ref, qv_ref, vecs_ref, feats, acc, ext, pre,
):
    s = pl.program_id(0)
    width, queries = acc.shape

    @pl.when(s == 0)
    def _():
        rows = jnp.concatenate([fetched_ref[d] for d in range(fetched_ref.shape[0])], axis=0)
        pick = slot_picks(cap, rows.shape[0], orow_ref[...])
        hvt = mm(rows, pick, TN).astype(bf16)
        for d in range(vecs_ref.shape[0]):
            vecs_ref[d, 0] = hvt
        rels = rtab_ref.shape[1]
        rvt = mm(rtab_ref[...], onehot(iota((rels, queries), 0) == rel_ref[...])).astype(bf16)
        entry = iota((width, ext_ref.shape[1]), 0)
        image = mm(onehot(entry == ext_ref[...]), hvt, TN)
        image = image + mm(onehot(entry + width == ext_ref[...]), rvt, TN)
        ext[...] = image.astype(bf16)
        for g in range(GROUPS):
            img_ref[:, g * queries : (g + 1) * queries] = ext[g * BAND_OUT : g * BAND_OUT + LANES, :]
        acc[...] = jnp.zeros_like(acc)

    units = band_ref.shape[0] // BAND_OUT
    flat = GROUPS * BAND_OUT
    pre[...] = mm(band_ref[...], img_ref[...])
    for f in range(units):
        for g in range(GROUPS):
            rows = slice(f * flat + g * BAND_OUT, f * flat + (g + 1) * BAND_OUT)
            v = pre[f * BAND_OUT : (f + 1) * BAND_OUT, g * queries : (g + 1) * queries]
            sig = sigmoid(v)
            feats[rows, :] = (v * sig).astype(bf16)
            slope_ref[rows, :] = sig * (1.0 + v * (1.0 - sig))
    acc[...] += mm(w_ref[...], feats[...])

    @pl.when(s == pl.num_programs(0) - 1)
    def _():
        query = acc[...]
        qv_ref[...] = query.T.astype(bf16)
        qvt = query.astype(bf16)
        for d in range(vecs_ref.shape[0]):
            vecs_ref[d, 1] = qvt


def filter_block(filts):
    return math.gcd(filts, 8)


def front(fetched, orow, rel_row, rtab_t, ext, band, weight_t, cap, copies):
    queries = orow.shape[1]
    width, flat = weight_t.shape
    filts = band.shape[0] // BAND_OUT
    units = filter_block(filts)
    cols = flat // filts * units
    return pl.pallas_call(
        functools.partial(front_kernel, cap),
        grid=(filts // units,),
        in_specs=[
            whole(fetched.shape),
            whole(orow.shape),
            whole(rel_row.shape),
            whole(rtab_t.shape),
            whole(ext.shape),
            pl.BlockSpec((units * BAND_OUT, LANES), lambda s: (s, 0)),
            pl.BlockSpec((width, cols), lambda s: (0, s)),
        ],
        out_specs=[
            pl.BlockSpec((cols, queries), lambda s: (s, 0)),
            whole((LANES, GROUPS * queries)),
            whole((queries, width)),
            whole((copies, 2, width, queries)),
        ],
        out_shape=[
            jax.ShapeDtypeStruct((flat, queries), f32),
            jax.ShapeDtypeStruct((LANES, GROUPS * queries), bf16),
            jax.ShapeDtypeStruct((queries, width), bf16),
            jax.ShapeDtypeStruct((copies, 2, width, queries), bf16),
        ],
        scratch_shapes=[
            pltpu.VMEM((cols, queries), bf16),
            pltpu.VMEM((width, queries), f32),
            pltpu.VMEM((ext.shape[1], queries), bf16),
            pltpu.VMEM((units * BAND_OUT, GROUPS * queries), f32),
        ],
        compiler_params=params("arbitrary"),
        cost_estimate=cost(4e9, 2.4e7, 2.5e6),
        name="front",
    )(fetched, orow, rel_row, rtab_t, ext, band, weight_t)


def middle_kernel(
    cand, pos_ref, qv_ref, ext_ref, bandt_hbm, tails_hbm, w_hbm, slope_hbm,
    ext, sums_ref, qgt_ref, fgrad_hbm,
    bandt, tails, w, slope, fgrad, scores, grads, spread, linear,
    band_sem, tail_sems, w_sems, slope_sems, out_sems,
):
    owners, width, slots = tails.shape
    steps, _, cols = w.shape
    queries = qv_ref.shape[0]
    chunks = tail_sems.shape[0]
    blocks = owners // chunks
    part_rows = fgrad.shape[1]

    def tail_copy(i):
        span = pl.ds(i * blocks, blocks)
        return pltpu.make_async_copy(tails_hbm.at[span], tails.at[span], tail_sems.at[i])

    def w_copy(k):
        return pltpu.make_async_copy(w_hbm.at[:, pl.ds(k * cols, cols)], w.at[k], w_sems.at[k])

    def slope_copy(k):
        return pltpu.make_async_copy(slope_hbm.at[pl.ds(k * cols, cols)], slope.at[k], slope_sems.at[k])

    def out_copy(k):
        span = pl.ds(k * part_rows, part_rows)
        return pltpu.make_async_copy(fgrad.at[k], fgrad_hbm.at[span], out_sems.at[k])

    for i in range(chunks):
        tail_copy(i).start()
    band_copy = pltpu.make_async_copy(bandt_hbm, bandt, band_sem)
    for k in range(steps):
        w_copy(k).start()
        slope_copy(k).start()
        if k == 0:
            band_copy.start()

    qv = qv_ref[...]
    total = jnp.zeros((queries, width), f32)
    for i in range(chunks):
        tail_copy(i).wait()
        for b in range(blocks):
            o = i * blocks + b
            block = tails[o]
            slot = o % scores.shape[0]
            scores[slot] = mm(qv, block)
            for r in spans(queries, 16):
                here = iota((r.stop - r.start, slots), 1) + o * slots
                target = jnp.where(here == pos_ref[r, :], 1.0 - smooth + smooth / cand, smooth / cand)
                grads[slot, r, :] = ((sigmoid(scores[slot, r, :]) - target) * loss_weight).astype(bf16)
            total = total + mm(grads[slot], block, NT)
    qgt = total.T.astype(bf16)
    for d in range(qgt_ref.shape[0]):
        qgt_ref[d] = qgt

    units = part_rows // BAND_OUT
    flat = GROUPS * BAND_OUT
    for k in range(steps):
        lin = linear.at[k % 2]
        w_copy(k).wait()
        lin[...] = mm(w[k], qgt, TN)
        slope_copy(k).wait()
        for f in range(units):
            for g in range(GROUPS):
                rows = slice(f * flat + g * BAND_OUT, f * flat + (g + 1) * BAND_OUT)
                part = slice(f * BAND_OUT, (f + 1) * BAND_OUT)
                lanes = slice(g * queries, (g + 1) * queries)
                fgrad[k, part, lanes] = (lin[rows, :] * slope[k, rows, :]).astype(bf16)
        out_copy(k).start()
        if k == 0:
            band_copy.wait()
        spread_k = mm(bandt[:, k * part_rows : (k + 1) * part_rows], fgrad[k])
        if k == 0:
            spread[...] = spread_k
        else:
            spread[...] += spread_k

    ext[...] = jnp.zeros_like(ext)
    for g in range(GROUPS):
        ext[g * BAND_OUT : g * BAND_OUT + LANES, :] += spread[:, g * queries : (g + 1) * queries]
    high, low = split(ext[...])
    rpick = onehot(iota((width, ext.shape[0]), 0) + width == ext_ref[...])
    sums_ref[0] = mm(rpick, high) + mm(rpick, low)
    for k in range(steps):
        out_copy(k).wait()


def middle(pos, qv, ext, band_t, tails, weight_t, slope, cand, copies):
    queries, width = qv.shape
    owners, _, slots = tails.shape
    flat = weight_t.shape[1]
    filts = band_t.shape[1] // BAND_OUT
    units = math.gcd(filts, 16)
    steps = filts // units
    cols = flat // steps
    rows = units * BAND_OUT
    blocks = math.gcd(owners, max(1, 2048 // slots))
    ring = min(owners, 4)
    hbm = pl.BlockSpec(memory_space=pl.ANY)
    return pl.pallas_call(
        functools.partial(middle_kernel, cand),
        in_specs=[VMEM] * 3 + [hbm] * 4,
        out_specs=[VMEM] * 3 + [hbm],
        out_shape=[
            jax.ShapeDtypeStruct((ext.shape[1], queries), f32),
            jax.ShapeDtypeStruct((1, width, queries), f32),
            jax.ShapeDtypeStruct((copies, width, queries), bf16),
            jax.ShapeDtypeStruct((filts * BAND_OUT, GROUPS * queries), bf16),
        ],
        scratch_shapes=[
            pltpu.VMEM(band_t.shape, bf16),
            pltpu.VMEM(tails.shape, bf16),
            pltpu.VMEM((steps, width, cols), bf16),
            pltpu.VMEM((steps, cols, queries), f32),
            pltpu.VMEM((steps, rows, GROUPS * queries), bf16),
            pltpu.VMEM((ring, queries, slots), f32),
            pltpu.VMEM((ring, queries, slots), bf16),
            pltpu.VMEM((LANES, GROUPS * queries), f32),
            pltpu.VMEM((2, cols, queries), f32),
            pltpu.SemaphoreType.DMA,
            pltpu.SemaphoreType.DMA((owners // blocks,)),
            pltpu.SemaphoreType.DMA((steps,)),
            pltpu.SemaphoreType.DMA((steps,)),
            pltpu.SemaphoreType.DMA((steps,)),
        ],
        compiler_params=params(),
        cost_estimate=cost(6e9, 2.5e7, 5e5),
        name="middle",
    )(pos, qv, ext, band_t, tails, weight_t, slope)


def half_taps(taps):
    return -(-taps // 32) * 16


def diag_kernel(
    cap, taps, codes_ref, orow_ref, ext_ref, spread_ref, fgrad_ref, img_ref, out_ref, corr_ref
):
    s = pl.program_id(0)
    units = fgrad_ref.shape[0] // BAND_OUT
    part = mm(fgrad_ref[...], img_ref[...], NT)
    corr_ref[pl.ds(s * units, units)] = part.reshape(units, BAND_OUT, LANES)

    @pl.when(s == pl.num_programs(0) - 1)
    def _():
        width = out_ref.shape[2]
        high, low = split(spread_ref[...])
        hpick = onehot(iota((width, spread_ref.shape[0]), 0) == ext_ref[...])
        hgrad = (mm(hpick, high) + mm(hpick, low)).astype(bf16)
        pick = slot_picks(cap, out_ref.shape[0] * cap, orow_ref[...])
        rows = mm(pick, hgrad, NT).astype(bf16)
        diag_sums(cap, taps, codes_ref, corr_ref, rows, out_ref)


def diag_sums(cap, taps, codes_ref, corr_ref, rows, out_ref):
    filts = corr_ref.shape[0]
    width = out_ref.shape[2]
    half = half_taps(taps)
    total = jnp.zeros((2 * half, filts), f32)
    for j in range(IMG):
        line = corr_ref[:, j, :]
        for di in range(1, BAND):
            line = line + pltpu.roll(corr_ref[:, di * IMG + j, :], LANES - di * IMG, 1)
        pick = onehot(iota((2 * half, LANES), 0) == codes_ref[j : j + 1, :])
        high, low = split(line)
        total = total + mm(pick, high, NT) + mm(pick, low, NT)
    packed = jnp.zeros((half, width), f32)
    for k in range(2):
        for i, piece in enumerate(split(total[k * half : (k + 1) * half, :])):
            place = onehot(iota((filts, width), 1) == iota((filts, width), 0) + (2 * k + i) * filts)
            packed = packed + mm(piece, place)
    packed = packed.astype(bf16)
    for d in range(out_ref.shape[0]):
        out_ref[d, :cap, :] = rows[d * cap : (d + 1) * cap, :]
        out_ref[d, cap:, :] = packed


def filter_sums(fgrad, img, codes, orow, ext, spread, count, width, cap, taps):
    filts = fgrad.shape[0] // BAND_OUT
    units = filter_block(filts)
    assert 4 * filts <= width
    out = (count, cap + half_taps(taps), width)
    return pl.pallas_call(
        functools.partial(diag_kernel, cap, taps),
        grid=(filts // units,),
        in_specs=[
            whole(codes.shape),
            whole(orow.shape),
            whole(ext.shape),
            whole(spread.shape),
            pl.BlockSpec((units * BAND_OUT, fgrad.shape[1]), lambda s: (s, 0)),
            whole(img.shape),
        ],
        out_specs=whole(out),
        out_shape=jax.ShapeDtypeStruct(out, bf16),
        scratch_shapes=[pltpu.VMEM((filts, BAND_OUT, LANES), f32)],
        compiler_params=params("arbitrary"),
        cost_estimate=cost(2e9, 6e6),
        name="filter_sums",
    )(codes, orow, ext, spread, fgrad, img)


def tail_kernel(
    cand, ids_ref, tails_ref, mate_ref, scand_ref, mcand_ref, numbers_ref, vecs_ref, own_ref, other_ref, scores, grads
):
    cap = own_ref.shape[1]
    tails = jnp.concatenate([ref[0].astype(f32).T for ref in (tails_ref, mate_ref)], axis=0).astype(bf16)
    scand = jnp.concatenate([scand_ref[...], mcand_ref[...]], axis=0)
    own = jnp.zeros(own_ref.shape, f32)
    other = jnp.zeros(own_ref.shape, f32)
    for i, group in enumerate(pairs(vecs_ref.shape[0])):
        qvt = beside(vecs_ref[p, 1] for p in group)
        pos = beside(field(numbers_ref, 2 * p + ids_ref[2], 3) for p in group)
        score, grad = scores.at[i % 2], grads.at[i % 2]
        score[...] = mm(tails, qvt)
        for r in spans(2 * cap, 64):
            target = jnp.where(scand[r, :] == pos, 1.0 - smooth + smooth / cand, smooth / cand)
            grad[r, :] = ((sigmoid(score[r, :]) - target) * loss_weight).astype(bf16)
        own = own + mm(qvt, grad[:cap, :], NT)
        other = other + mm(qvt, grad[cap:, :], NT)
    own_ref[...] = own
    other_ref[...] = other


def tail_part(ids, tails, scand, mcand, numbers, vecs, cand):
    _, width, cap = tails.shape
    half = jax.ShapeDtypeStruct((width, cap), f32)
    return pl.pallas_call(
        functools.partial(tail_kernel, cand),
        grid_spec=pltpu.PrefetchScalarGridSpec(
            num_scalar_prefetch=1,
            grid=(1,),
            in_specs=[
                pl.BlockSpec((1, width, cap), lambda s, ids: (ids[0], 0, 0)),
                pl.BlockSpec((1, width, cap), lambda s, ids: (ids[1], 0, 0)),
                whole(scand.shape),
                whole(mcand.shape),
                whole(numbers.shape),
                whole(vecs.shape),
            ],
            out_specs=[whole(half.shape)] * 2,
            scratch_shapes=[
                pltpu.VMEM((2, 2 * cap, 2 * vecs.shape[3]), f32),
                pltpu.VMEM((2, 2 * cap, 2 * vecs.shape[3]), bf16),
            ],
        ),
        out_shape=[half, half],
        compiler_params=params("arbitrary"),
        cost_estimate=cost(2e9, 3e6, 1e6),
        name="tail_grad",
    )(ids, tails, tails, scand, mcand, numbers, vecs)


def proj_kernel(
    ids_ref, rtab_ref, ext_ref, band_ref, mate_ref, numbers_ref, vecs_ref, grads_ref,
    own_ref, other_ref, feats, hpick, rpick, rels_hot, ext, pre,
):
    width, rels = rtab_ref.shape
    units = band_ref.shape[0] // BAND_OUT
    flat = GROUPS * BAND_OUT
    cols = units * flat
    entry = iota((width, ext_ref.shape[1]), 0)
    hpick[...] = jnp.where(entry == ext_ref[...], 1.0, 0.0).T.astype(bf16)
    rpick[...] = jnp.where(entry + width == ext_ref[...], 1.0, 0.0).T.astype(bf16)
    queries = vecs_ref.shape[3]
    for i, group in enumerate(pairs(vecs_ref.shape[0])):
        hvt = beside(vecs_ref[p, 0] for p in group)
        rel = beside(field(numbers_ref, 2 * p + ids_ref[2], 2) for p in group)
        for r in spans(rels, 64):
            rels_hot[r, :] = onehot(iota((r.stop - r.start, rel.shape[1]), 0) + r.start == rel)
        rvt = mm(rtab_ref[...], rels_hot[...]).astype(bf16)
        image = ext.at[i % 2]
        image[...] = (mm(hpick[...], hvt) + mm(rpick[...], rvt)).astype(bf16)
        lanes = slice(group[0] * queries, (group[-1] + 1) * queries)
        for k, source in enumerate((band_ref, mate_ref)):
            for g in range(GROUPS):
                slot = (k * GROUPS + g) % 2
                pre[slot] = mm(source[...], image[g * BAND_OUT : g * BAND_OUT + LANES, :])
                for f in range(units):
                    v = pre[slot, f * BAND_OUT : (f + 1) * BAND_OUT, :]
                    first = k * cols + f * flat + g * BAND_OUT
                    feats[first : first + BAND_OUT, lanes] = (v * sigmoid(v)).astype(bf16)
    qgt = beside(grads_ref[p] for p in range(grads_ref.shape[0]))
    own_ref[...] = mm(qgt, feats[:cols, :], NT)
    other_ref[...] = mm(qgt, feats[cols:, :], NT)


def proj_part(ids, rtab_t, ext, band, numbers, vecs, grads, cols):
    width, rels = rtab_t.shape
    unit = cols // GROUPS
    gathered, _, _, queries = vecs.shape
    half = jax.ShapeDtypeStruct((width, cols), f32)
    return pl.pallas_call(
        proj_kernel,
        grid_spec=pltpu.PrefetchScalarGridSpec(
            num_scalar_prefetch=1,
            grid=(1,),
            in_specs=[
                whole(rtab_t.shape),
                whole(ext.shape),
                pl.BlockSpec((unit, LANES), lambda s, ids: (ids[0], 0)),
                pl.BlockSpec((unit, LANES), lambda s, ids: (ids[1], 0)),
                whole(numbers.shape),
                whole(vecs.shape),
                whole(grads.shape),
            ],
            out_specs=[whole(half.shape)] * 2,
            scratch_shapes=[
                pltpu.VMEM((2 * cols, gathered * queries), bf16),
                pltpu.VMEM((ext.shape[1], width), bf16),
                pltpu.VMEM((ext.shape[1], width), bf16),
                pltpu.VMEM((rels, 2 * queries), bf16),
                pltpu.VMEM((2, ext.shape[1], 2 * queries), bf16),
                pltpu.VMEM((2, unit, 2 * queries), f32),
            ],
        ),
        out_shape=[half, half],
        compiler_params=params("arbitrary"),
        cost_estimate=cost(6e9, 6e6, 2.5e6),
        name="proj_grad",
    )(ids, rtab_t, ext, band, band, numbers, vecs, grads)


def proj_columns(first, cols, filters, chequer_perm, relation_table, numbers, heads, grads):
    ks = filters.shape[-1]
    rim = ks // 2
    flat = IMG * IMG
    column = first + jnp.arange(cols, dtype=i32)
    f = column // flat
    i = (column % flat) // IMG
    j = column % IMG
    spot = jnp.arange(flat, dtype=i32)
    a = (spot[:, None] // IMG - i[None, :] + rim) % IMG
    b = (spot[:, None] % IMG - j[None, :] + rim) % IMG
    tap = filters[f[None, :], jnp.minimum(a, ks - 1), jnp.minimum(b, ks - 1)]
    matrix = jnp.where((a < ks) & (b < ks), tap, jnp.zeros((), bf16))
    width = heads.shape[1]
    head = heads.transpose(0, 2, 1).reshape(-1, width)
    qg = grads.transpose(0, 2, 1).reshape(-1, width)
    joined = jnp.concatenate([head, relation_table[numbers[:, 2].reshape(-1)]], axis=1)
    pre = mm(joined[:, chequer_perm], matrix)
    return mm(qg, (pre * sigmoid(pre)).astype(bf16), TN)


def rel_kernel(numbers_ref, sums_ref, rel_ref, picks):
    width, rels = rel_ref.shape
    queries = sums_ref.shape[2]
    total = None
    for block in spans(sums_ref.shape[0], picks.shape[1] // queries):
        members = range(block.start, block.stop)
        for i, p in enumerate(members):
            rel = field(numbers_ref, p, 2)
            for r in spans(rels, 128):
                here = iota((r.stop - r.start, queries), 0) + r.start
                picks[r, i * queries : (i + 1) * queries] = onehot(here == rel)
        parts = jnp.concatenate(split(beside(sums_ref[p] for p in members)), axis=0)
        part = mm(parts, picks[...], NT)
        total = part if total is None else total + part
    rel_ref[...] = total[:width, :] + total[width:, :]


def rel_part(numbers, sums, rels):
    count, width, queries = sums.shape
    return pl.pallas_call(
        rel_kernel,
        out_shape=jax.ShapeDtypeStruct((width, rels), f32),
        scratch_shapes=[pltpu.VMEM((rels, math.gcd(count, 16) * queries), bf16)],
        compiler_params=params(),
        cost_estimate=cost(2e9, 3e6),
        name="rel_grad",
    )(numbers, sums)


def entity_kernel(cap, want_ref, srow_ref, own_ref, recv_ref, incoming_ref, out_ref, filt_ref, sums):
    rows = out_ref.shape[1]
    count, _, width = incoming_ref.shape
    half = incoming_ref.shape[1] - cap
    ks, _, filts = filt_ref.shape
    grads = jnp.concatenate([incoming_ref[d, :cap, :] for d in range(count)], axis=0)
    turned = grads.astype(f32).T.astype(bf16)
    high, low = split(own_ref[...] + recv_ref[...])
    for c in spans(rows, 256):
        here = iota((want_ref.shape[0], c.stop - c.start), 1) + c.start
        total = mm(turned, onehot(here == want_ref[...]))
        here = iota((srow_ref.shape[0], c.stop - c.start), 1) + c.start
        pick = onehot(here == srow_ref[...])
        out_ref[:, c] = total + mm(high, pick) + mm(low, pick)
    packed = incoming_ref[0, cap:, :].astype(f32)
    for d in range(1, count):
        packed = packed + incoming_ref[d, cap:, :].astype(f32)
    high, low = split(packed)
    for k in range(2):
        lane = iota((width, filts), 0) - 2 * k * filts
        unit = iota((width, filts), 1)
        place = onehot((lane == unit) | (lane == unit + filts))
        sums[k * half : (k + 1) * half, :] = mm(high, place) + mm(low, place)
    for a in range(ks):
        filt_ref[a] = sums[a * ks : (a + 1) * ks, :]


def entity_sum(want, srow, own, recv, incoming, rows, cap, filts, ks):
    half = incoming.shape[1] - cap
    return pl.pallas_call(
        functools.partial(entity_kernel, cap),
        out_shape=[
            jax.ShapeDtypeStruct((own.shape[0], rows), f32),
            jax.ShapeDtypeStruct((ks, ks, filts), f32),
        ],
        scratch_shapes=[pltpu.VMEM((2 * half, filts), f32)],
        compiler_params=params(),
        cost_estimate=cost(1.5e9, 4e6),
        name="entity_grad",
    )(want, srow, own, recv, incoming)


def shards(
    entity_table,
    relation_table,
    filters,
    proj_weight,
    chequer_perm,
    head_owner,
    head_row,
    rel_ids,
    pos_index,
    tail_owner,
    tail_row,
):
    count = lax.axis_size("shard")
    me = lax.axis_index("shard")
    assert count % 2 == 0
    direct = count <= 16
    queries = head_row.shape[0]
    cand = tail_row.shape[0]
    rows, width = entity_table.shape
    rels = relation_table.shape[0]
    filts, ks, _ = filters.shape
    head_cap = 2 * queries // count
    tail_cap = 2 * cand // count
    same_core = [list(range(c, count, 2)) for c in range(2)]
    copies = count // 2 if direct else 1

    def swap(x):
        return lax.ppermute(x, "shard", [(d, d ^ 1) for d in range(count)])

    def exchange(x):
        return lax.all_to_all(x, "shard", split_axis=0, concat_axis=0, tiled=True)

    def gather_core(x):
        if direct:
            return lax.all_to_all(
                x, "shard", split_axis=0, concat_axis=0, axis_index_groups=same_core, tiled=True
            )
        return lax.all_gather(x, "shard", axis=0, axis_index_groups=same_core, tiled=True)

    me1 = me.reshape(1)
    heads = head_owner[:, 0]
    tail_owners = tail_owner[:, 0]
    table_t, rtab_t, weight_t = entity_table.T, relation_table.T, proj_weight.T
    numbers = jnp.concatenate([heads, head_row, rel_ids, pos_index])
    numbers = exchange(jnp.broadcast_to(numbers, (count, 1, 4 * queries)))

    ids = jnp.stack([me, me ^ 1, me & 1])
    tails_t, slot_row, scand = pack_tails(me1, tail_owners, tail_row, table_t, tail_cap)
    all_tails = lax.all_gather(tails_t, "shard", axis=0, tiled=True)
    mcand = mate_cands(me1, tail_owners, tail_cap)
    found, want = find_heads(me1, numbers, table_t, head_cap)
    fetched = exchange(found)
    pos = pos_slots(tail_owners, pos_index, tail_cap)

    codes = jnp.asarray(band_codes(ks))
    band, band_t = build_band(filters, codes)
    extra = BAND_OUT * (GROUPS - 1) + LANES - IMG * IMG - BAND_OUT
    ext = jnp.concatenate([chequer_perm[-BAND_OUT:], chequer_perm, chequer_perm[:extra]])[None]
    orow = heads[None, :]
    slope, img, qv, vecs = front(
        fetched, orow, rel_ids[None, :], rtab_t, ext, band, weight_t, head_cap, copies
    )
    core_vecs = gather_core(vecs)

    spread, sums, qgt, fgrad = middle(
        pos, qv, ext, band_t, all_tails, weight_t, slope, cand, copies
    )
    all_sums = lax.all_gather(sums, "shard", axis=0, tiled=True)
    qgt, core_vecs = lax.optimization_barrier((qgt, core_vecs))
    core_qgt = gather_core(qgt)
    outgoing = filter_sums(
        fgrad, img, codes, orow, ext, spread, count, width, head_cap, ks * ks
    )
    outgoing, core_qgt, mcand = lax.optimization_barrier((outgoing, core_qgt, mcand))
    incoming = exchange(outgoing)
    own, other = tail_part(ids, all_tails, scand, mcand, numbers, core_vecs, cand)
    core_qgt, own, other = lax.optimization_barrier((core_qgt, own, other))
    entity_grad, filter_grad = entity_sum(
        want, slot_row, own, swap(other), incoming, rows, head_cap, filts, ks
    )
    filter_grad = filter_grad.transpose(2, 0, 1)

    cols = filts * IMG * IMG // count
    if direct and cols % (IMG * IMG) == 0:
        own, other = proj_part(ids, rtab_t, ext, band, numbers, core_vecs, core_qgt, cols)
    else:
        core_numbers = lax.dynamic_index_in_dim(
            numbers.reshape(count // 2, 2, 4, queries), me & 1, 1, keepdims=False
        )
        own, other = (
            proj_columns(
                d * cols, cols, filters, chequer_perm, relation_table,
                core_numbers, core_vecs[:, 0], core_qgt,
            )
            for d in (me, me ^ 1)
        )
    proj_grad = (own + swap(other)).T

    relation_grad = rel_part(numbers, all_sums, rels).T
    return (entity_grad.T, relation_grad, filter_grad, proj_grad)


def solution(mesh):
    placed = (
        P("shard", None),
        P(),
        P(),
        P(),
        P(),
        P(("parts", "shard"), None),
        P(("parts", "shard")),
        P(("parts", "shard")),
        P(("parts", "shard")),
        P("parts", None),
        P("parts"),
    )
    return jax.shard_map(
        shards,
        mesh=mesh,
        in_specs=placed,
        out_specs=(
            P(("parts", "shard"), None),
            P("parts", None),
            P("parts", None, None),
            P(("parts", "shard"), None),
        ),
        check_vma=False,
    )
```
